32 devices in a mesh: tm: 8 (over y, x, core), dp: 4 (over z).
Axes of the slice: x: 2, y: 2, z: 4, core: 2. Of those that a mesh axis runs over, the one named last changes fastest.
Arguments:
- layer_in: bfloat16 [4, 1024, 2560], P('dp', 'tm'), may hold values from -6 to 6
- out_grad: bfloat16 [4, 1024, 2560], P('dp', 'tm'), may hold values from -6 to 6
- w_bc: bfloat16 [2560, 256], P('dp'), may hold values from -0.009765625 to 0.009765625
- log_decay: float32 [4, 1024, 40], P('dp', 'tm'), may hold values from -2 to 0
- step: float32 [4, 1024, 40], P('dp', 'tm'), may hold values from 0.02 to 0.2
- saved_states: bfloat16 [4, 8, 40, 64, 128], P('dp', 'tm'), may hold values from -3 to 3
- w_gate: bfloat16 [1, 2560, 7168], P(None, None, 'tm'), may hold values from -0.125 to 0.125
- w_up: bfloat16 [1, 2560, 7168], P(None, None, 'tm'), may hold values from -0.125 to 0.125
- slot_rows: int32 [4, 1, 128], P('dp', None, 'tm'), may hold values from 0 to 127, as said below
- slot_counts: int32 [4, 8], P('dp', 'tm'), may hold values from 4 to 16, as said below
- slot_gates: bfloat16 [4, 1, 128], P('dp', None, 'tm'), may hold values from 0.099609375 to 0.8984375
Outputs:
- in_grad: bfloat16 [4, 1024, 2560], P('dp', 'tm')
- decay_grad: float32 [4, 1024, 40], P('dp', 'tm')
- step_grad: float32 [4, 1024, 40], P('dp', 'tm')
- w_bc_grad: float32 [2560, 256], P(('tm', 'dp'))
- w_down_grad: bfloat16 [1, 7168, 2560], P(None, 'tm', 'dp')
The draws below stay inside these ranges and needn't reach their ends.
Inputs may be any that keep to these rules, and one draw needn't show every extreme that they name: `slot_rows`: among the used slots of one expert in one shard the frames are distinct. `slot_counts`: the count 16 is reached in some shard of every recording, and in every shard of some recording, for each expert.
All inputs are finite; a program needn't handle non-finite values.
Results may differ from the reference program's by a relative error of at most 0.009.
Values may be sent and summed in bfloat16 or wider, within the bound.
No kernel may reach another device: no remote copies, remote signals or barrier semaphores. Data moves between devices by JAX's collectives and lax.ppermute only.
A program may use at most 128 MiB of HBM per device.

```python
import math
import jax
import jax.numpy as jnp
from jax import lax

D = 2560
H = 40
P_SIZE = 64
N = 128
E = 1
F = 7168
CAP = 16
TOK_DEV = 128
TIMESTEPS_EACH = 1024
AUDIO_TOTAL = 4
N_TM = 8


def draw_log_decay(key, part):
    key = jax.random.fold_in(key, 11)
    stochastic_seeds = jax.random.split(key, 7)
    slow_share = 0.5
    is_slow = jax.random.uniform(stochastic_seeds[0], (H,)) < slow_share
    slow = jnp.exp(jax.random.uniform(stochastic_seeds[1], (H,), jnp.float32, jnp.log(0.2 / TIMESTEPS_EACH), jnp.log(0.8 / TIMESTEPS_EACH)))
    fast = jnp.exp(jax.random.uniform(stochastic_seeds[2], (H,), jnp.float32, jnp.log(2.5 / TOK_DEV), jnp.log(4.0 / TOK_DEV)))
    rate = jnp.where(is_slow, slow, fast)
    shards = TIMESTEPS_EACH // TOK_DEV
    factor = jnp.exp(jax.random.uniform(stochastic_seeds[3], (AUDIO_TOTAL, shards, 1, 1), jnp.float32, jnp.log(0.6), jnp.log(1.5)))
    factor = jnp.broadcast_to(factor, (AUDIO_TOTAL, shards, TOK_DEV, 1)).reshape(AUDIO_TOTAL, TIMESTEPS_EACH, 1)
    rough = jax.random.uniform(stochastic_seeds[4], (AUDIO_TOTAL, TIMESTEPS_EACH, H), jnp.float32, 0.5, 1.5)
    starting_position = -rate[None, None, :] * rough * factor
    span_extent = jax.random.uniform(stochastic_seeds[5], (AUDIO_TOTAL, TIMESTEPS_EACH, 1)) < 3.0 / TIMESTEPS_EACH
    stacked_levels = jnp.log(jax.random.uniform(stochastic_seeds[6], (AUDIO_TOTAL, TIMESTEPS_EACH, 1), jnp.float32, 0.5, 0.8))
    return (starting_position + jnp.where(span_extent, stacked_levels, 0.0)).astype(jnp.float32)


def draw_slot_rows(key, part):
    key = jax.random.fold_in(key, 5)
    shards = TIMESTEPS_EACH // TOK_DEV
    scores = jax.random.randint(key, (AUDIO_TOTAL, E, shards, TOK_DEV), 0, 1 << 20) * TOK_DEV + jnp.arange(TOK_DEV)
    order = jnp.argsort(scores, axis=-1, stable=True)[..., :CAP]
    return order.astype(jnp.int32).reshape(AUDIO_TOTAL, E, shards * CAP)


def draw_slot_counts(key, part):
    key = jax.random.fold_in(key, 7)
    stochastic_seeds = jax.random.split(key, 3)
    shards = TIMESTEPS_EACH // TOK_DEV
    starting_position = jax.random.randint(stochastic_seeds[0], (AUDIO_TOTAL, shards, E), CAP // 4, CAP + 1)
    full_rec = jax.random.randint(stochastic_seeds[1], (E,), 0, AUDIO_TOTAL)
    full_shard = jax.random.randint(stochastic_seeds[2], (AUDIO_TOTAL,), 0, shards)
    full = (jnp.arange(AUDIO_TOTAL)[:, None, None] == full_rec[None, None, :]) | (jnp.arange(shards)[None, :, None] == full_shard[:, None, None])
    return jnp.where(full, CAP, starting_position).astype(jnp.int32).reshape(AUDIO_TOTAL, shards * E)


def block_levels(stream_key, shape, pieces, least, high):
    def one(position, parts):
        draws = jax.random.uniform(jax.random.fold_in(jax.random.fold_in(stream_key, 6), position), (parts,), jnp.float32, least / len(pieces), high / len(pieces))
        return jnp.repeat(jnp.exp(draws), shape[position] // parts).reshape((-1,) + (1,) * (len(shape) - position - 1))

    loudness = one(*pieces[0])
    for cut in pieces[1:]:
        loudness = loudness * one(*cut)
    return loudness


def centred(key, shape, deviation, most, pieces=(), kind=jnp.bfloat16):
    drawn = deviation * jax.random.normal(key, shape, jnp.float32)
    if pieces:
        drawn = drawn * block_levels(key, shape, pieces, -0.22, 0.18)
    return jnp.clip(drawn, -most, most).astype(kind)


def setup_inputs(seed: int = 0) -> dict:
    key_of = jax.random.split(jax.random.key(seed), 12)
    layer_in = centred(key_of[0], (AUDIO_TOTAL, TIMESTEPS_EACH, D), 1.0, 6.0, ((0, 4), (1, 8)))
    out_grad = centred(key_of[1], (AUDIO_TOTAL, TIMESTEPS_EACH, D), 1.0, 6.0, ((0, 4), (1, 8)))
    w_bc = centred(key_of[2], (D, 2 * N), (D * N) ** -0.5, 0.009765625, ((0, 4),))
    log_decay = draw_log_decay(jax.random.fold_in(key_of[11], 71), 0)
    step = jnp.clip(jnp.exp(math.log(0.2) - 2.3025851 * jax.random.uniform(key_of[4], (AUDIO_TOTAL, TIMESTEPS_EACH, H), jnp.float32) ** block_levels(key_of[4], (AUDIO_TOTAL, TIMESTEPS_EACH, H), ((0, 4), (1, 8)), -0.2, 0.2)), 0.02, 0.2)
    saved_states = centred(key_of[5], (AUDIO_TOTAL, N_TM, H, P_SIZE, N), 0.5, 3.0, ((0, 4), (1, 8)))
    w_gate = centred(key_of[6], (E, D, F), D ** -0.5, 0.125, ((2, 8),))
    w_up = centred(key_of[7], (E, D, F), D ** -0.5, 0.125, ((2, 8),))
    slot_rows = draw_slot_rows(jax.random.fold_in(key_of[11], 71), 0)
    slot_counts = draw_slot_counts(jax.random.fold_in(key_of[11], 71), 0)
    slot_gates = jnp.clip(0.099609375 + 0.7988281 * jax.random.uniform(key_of[10], (AUDIO_TOTAL, E, N_TM * CAP), jnp.float32) ** block_levels(key_of[10], (AUDIO_TOTAL, E, N_TM * CAP), ((0, 4), (2, 8)), -0.2, 0.2), 0.099609375, 0.8984375).astype(jnp.bfloat16)
    return dict(layer_in=layer_in, out_grad=out_grad, w_bc=w_bc, log_decay=log_decay, step=step, saved_states=saved_states, w_gate=w_gate, w_up=w_up, slot_rows=slot_rows, slot_counts=slot_counts, slot_gates=slot_gates)


HI = lax.Precision.HIGHEST


def local_terms(layer_in, out_grad, w_bc, log_decay, step):
    length, width = layer_in.shape
    heads = log_decay.shape[1]
    size = width // heads
    bc = jnp.dot(layer_in, w_bc, preferred_element_type=jnp.float32).astype(jnp.bfloat16)
    states = bc.shape[1] // 2
    b_rows = bc[:, :states]
    c_rows = bc[:, states:]
    cum = jnp.cumsum(log_decay, axis=0)
    total = cum[-1]
    inputs = layer_in.astype(jnp.float32).reshape(length, heads, size)
    grads = out_grad.astype(jnp.float32).reshape(length, heads, size)
    into_end = jnp.exp(total[None, :] - cum) * step
    s_local = jnp.einsum('thp,tn->hpn', inputs * into_end[:, :, None], b_rows.astype(jnp.float32), precision=HI)
    g_local = jnp.einsum('thp,tn->hpn', grads * jnp.exp(cum)[:, :, None], c_rows.astype(jnp.float32), precision=HI)
    context = (layer_in, out_grad, w_bc, step, cum, b_rows, c_rows, s_local, total)
    return context, (jnp.exp(total), g_local)


def finish(context, h_in, r_grad):
    layer_in, out_grad, w_bc, step, cum, b_rows, c_rows, s_local, total = context
    length, width = layer_in.shape
    heads = step.shape[1]
    size = width // heads
    inputs = layer_in.astype(jnp.float32).reshape(length, heads, size)
    grads = out_grad.astype(jnp.float32).reshape(length, heads, size)
    b_full = b_rows.astype(jnp.float32)
    c_full = c_rows.astype(jnp.float32)
    order = jnp.arange(length)
    lower = order[:, None] >= order[None, :]
    heads_cum = cum.T
    diff = heads_cum[:, :, None] - heads_cum[:, None, :]
    seg = jnp.where(lower[None], jnp.exp(jnp.minimum(diff, 0.0)), 0.0)
    scores = jnp.dot(c_rows, b_rows.T, preferred_element_type=jnp.float32)
    kern = seg * scores[None]
    from_start = jnp.exp(cum)
    to_end = jnp.exp(total[None, :] - cum)
    produced_results = jnp.einsum('hts,shp->thp', kern * step.T[:, None, :], inputs, precision=HI)
    produced_results = produced_results + from_start[:, :, None] * jnp.einsum('hpn,tn->thp', h_in, c_full, precision=HI)
    back = jnp.einsum('hrt,rhp->thp', kern, grads, precision=HI)
    back = back + to_end[:, :, None] * jnp.einsum('hpn,tn->thp', r_grad, b_full, precision=HI)
    d_inputs = step[:, :, None] * back
    d_step = jnp.sum(inputs * back, axis=2)
    cross = jnp.einsum('ahp,bhp->hab', grads, inputs, precision=HI)
    mixed = seg * cross * step.T[:, None, :]
    carried_in = jnp.einsum('thp,hpn->thn', inputs, r_grad, precision=HI)
    d_b = jnp.einsum('hab,an->bn', mixed, c_full, precision=HI) + jnp.sum(carried_in * (to_end * step)[:, :, None], axis=1)
    carried_out = jnp.einsum('thp,hpn->thn', grads, h_in, precision=HI)
    d_c = jnp.einsum('hab,bn->an', mixed, b_full, precision=HI) + jnp.sum(carried_out * from_start[:, :, None], axis=1)
    h_last = jnp.exp(total)[:, None, None] * h_in + s_local
    edge = jnp.sum(r_grad * h_last, axis=(1, 2))
    excess = jnp.sum(grads * produced_results, axis=2) - jnp.sum(inputs * d_inputs, axis=2)
    d_decay = jnp.cumsum(excess[::-1], axis=0)[::-1] + edge[None, :]
    d_bc = jnp.concatenate([d_b, d_c], axis=1).astype(jnp.bfloat16)
    d_in = d_inputs.reshape(length, width) + jnp.einsum('tn,dn->td', d_bc, w_bc, preferred_element_type=jnp.float32)
    w_term = jnp.einsum('td,tn->dn', layer_in, d_bc, preferred_element_type=jnp.float32)
    return d_in.astype(jnp.bfloat16), d_decay, d_step, w_term


def one_recording(items):
    layer_in, out_grad, log_decay, step, saved, w_bc = items
    shards = TIMESTEPS_EACH // TOK_DEV
    width = layer_in.shape[1]
    heads = log_decay.shape[1]
    context, backward_items = jax.vmap(local_terms, in_axes=(0, 0, None, 0, 0))(
        layer_in.reshape(shards, TOK_DEV, width), out_grad.reshape(shards, TOK_DEV, width), w_bc,
        log_decay.reshape(shards, TOK_DEV, heads), step.reshape(shards, TOK_DEV, heads))
    zero_state = jnp.zeros_like(backward_items[1][0])

    def backward_turn(carry, item):
        return item[1] + item[0][:, None, None] * carry, carry

    first_grad, r_grads = lax.scan(backward_turn, zero_state, backward_items, reverse=True)
    h_ins = saved.astype(jnp.float32)
    d_in, d_decay, d_step, w_terms = jax.vmap(finish)(context, h_ins, r_grads)
    return (d_in.reshape(TIMESTEPS_EACH, width), d_decay.reshape(TIMESTEPS_EACH, heads), d_step.reshape(TIMESTEPS_EACH, heads), jnp.sum(w_terms, axis=0))


def expert_partial(layer_in, out_grad, rows, counts, gates, w_gate, w_up):
    shards = TIMESTEPS_EACH // TOK_DEV
    slots = jnp.arange(shards * CAP)
    offsets = (slots // CAP * TOK_DEV).astype(jnp.int32)
    frames = (rows + offsets[None, :]).astype(jnp.int32)
    per_shard = counts.reshape(shards, E).T
    live = (slots % CAP)[None, :] < jnp.repeat(per_shard, CAP, axis=1)
    weights = jnp.where(live, gates, jnp.zeros_like(gates)).astype(jnp.float32)
    picked_in = jnp.take(layer_in, frames, axis=0).astype(jnp.float32)
    picked_grad = jnp.take(out_grad, frames, axis=0).astype(jnp.float32)
    gate_h = jnp.einsum('ekd,edf->ekf', picked_in, w_gate.astype(jnp.float32), precision=HI)
    up_h = jnp.einsum('ekd,edf->ekf', picked_in, w_up.astype(jnp.float32), precision=HI)
    weighted = (jax.nn.silu(gate_h) * up_h * weights[:, :, None]).astype(jnp.bfloat16)
    partial_grad = jnp.einsum('ekf,ekd->efd', weighted.astype(jnp.float32), picked_grad, precision=HI)
    return partial_grad.astype(jnp.bfloat16)


def reference(layer_in, out_grad, w_bc, log_decay, step, saved_states, w_gate, w_up, slot_rows, slot_counts, slot_gates):
    recs = layer_in.shape[0]
    w_stack = jnp.broadcast_to(w_bc, (recs,) + w_bc.shape)
    in_grad, decay_grad, step_grad, w_terms = lax.map(one_recording, (layer_in, out_grad, log_decay, step, saved_states, w_stack))
    w_bc_grad = jnp.sum(w_terms, axis=0)

    def add_recording(total, items):
        partial_grad = expert_partial(items[0], items[1], items[2], items[3], items[4], w_gate, w_up)
        partial_grad = lax.optimization_barrier(partial_grad)
        return total + partial_grad.astype(jnp.float32), 0

    start = jnp.zeros((w_gate.shape[0], w_gate.shape[2], w_gate.shape[1]), jnp.float32)
    summed, ignored_value = lax.scan(add_recording, start, (layer_in, out_grad, slot_rows, slot_counts, slot_gates))
    return in_grad, decay_grad, step_grad, w_bc_grad, summed.astype(jnp.bfloat16)
```

```python
import jax
import jax.numpy as jnp
from jax import lax
from jax.sharding import PartitionSpec as P

HI = lax.Precision.HIGHEST


def local_terms(layer_in, out_grad, w_bc, log_decay, step):
    length, width = layer_in.shape
    heads = log_decay.shape[1]
    size = width // heads
    bc = jnp.dot(layer_in, w_bc, preferred_element_type=jnp.float32).astype(jnp.bfloat16)
    states = bc.shape[1] // 2
    b_rows = bc[:, :states]
    c_rows = bc[:, states:]
    cum_cols = jnp.cumsum(log_decay, axis=0).T
    total = cum_cols[:, -1]
    step_cols = step.T
    input_cols = layer_in.T.reshape(heads, size, length)
    grad_cols = out_grad.T.reshape(heads, size, length)
    inputs = input_cols.astype(jnp.float32)
    grads = grad_cols.astype(jnp.float32)
    into_end = jnp.exp(total[:, None] - cum_cols) * step_cols
    s_local = jnp.einsum(
        "hpt,tn->hpn", inputs * into_end[:, None, :], b_rows.astype(jnp.float32), precision=HI
    )
    g_local = jnp.einsum(
        "hpt,tn->hpn",
        grads * jnp.exp(cum_cols)[:, None, :],
        c_rows.astype(jnp.float32),
        precision=HI,
    )
    context = (
        input_cols,
        grad_cols,
        layer_in,
        w_bc,
        step_cols,
        cum_cols,
        b_rows,
        c_rows,
        s_local,
        total,
    )
    return (context, (jnp.exp(total), g_local))


def finish(context, h_in, r_grad):
    input_cols, grad_cols, layer_in, w_bc, step_cols, cum_cols, b_rows, c_rows, s_local, total = (
        context
    )
    heads, size, length = input_cols.shape
    width = heads * size
    inputs = input_cols.astype(jnp.float32)
    grads = grad_cols.astype(jnp.float32)
    b_full = b_rows.astype(jnp.float32)
    c_full = c_rows.astype(jnp.float32)
    order = jnp.arange(length)
    lower = order[:, None] >= order[None, :]
    diff = cum_cols[:, :, None] - cum_cols[:, None, :]
    seg = jnp.where(lower[None], jnp.exp(jnp.minimum(diff, 0.0)), 0.0)
    scores = jnp.dot(c_rows, b_rows.T, preferred_element_type=jnp.float32)
    kern = seg * scores[None]
    from_start = jnp.exp(cum_cols)
    to_end = jnp.exp(total[:, None] - cum_cols)
    produced_results = jnp.einsum(
        "hts,hps->hpt", kern * step_cols[:, None, :], inputs, precision=HI
    )
    produced_results = produced_results + from_start[:, None, :] * jnp.einsum(
        "hpn,tn->hpt", h_in, c_full, precision=HI
    )
    back = jnp.einsum("hrt,hpr->hpt", kern, grads, precision=HI)
    back = back + to_end[:, None, :] * jnp.einsum("hpn,tn->hpt", r_grad, b_full, precision=HI)
    d_inputs = step_cols[:, None, :] * back
    d_step = jnp.sum(inputs * back, axis=1).T
    cross = jnp.einsum("hpa,hpb->hab", grad_cols, input_cols, preferred_element_type=jnp.float32)
    mixed = seg * cross * step_cols[:, None, :]
    d_b = jnp.einsum("hab,an->bn", mixed, c_full, precision=HI) + jnp.einsum(
        "hpt,hpn->tn", inputs * (to_end * step_cols)[:, None, :], r_grad, precision=HI
    )
    d_c = jnp.einsum("hab,bn->an", mixed, b_full, precision=HI) + jnp.einsum(
        "hpt,hpn->tn", grads * from_start[:, None, :], h_in, precision=HI
    )
    h_last = jnp.exp(total)[:, None, None] * h_in + s_local
    edge = jnp.sum(r_grad * h_last, axis=(1, 2))
    excess = jnp.sum(grads * produced_results, axis=1) - jnp.sum(inputs * d_inputs, axis=1)
    d_decay = (jnp.cumsum(excess[:, ::-1], axis=1)[:, ::-1] + edge[:, None]).T
    d_bc = jnp.concatenate([d_b, d_c], axis=1).astype(jnp.bfloat16)
    d_in = d_inputs.reshape(width, length).T + jnp.einsum(
        "tn,dn->td", d_bc, w_bc, preferred_element_type=jnp.float32
    )
    return (d_in.astype(jnp.bfloat16), d_decay, d_step, d_bc)


def reverse_carry(decay, g_local):
    count = lax.axis_size("tm")
    heads, size, states = g_local.shape
    rows = heads * size
    parts = g_local.astype(jnp.bfloat16).reshape(count, rows // count, states)
    parts = lax.all_to_all(parts, "tm", split_axis=0, concat_axis=0)
    decays = jnp.repeat(lax.all_gather(decay, "tm"), size, axis=1)
    place = lax.axis_index("tm")
    decays = lax.dynamic_slice_in_dim(decays, place * (rows // count), rows // count, 1)
    carry = jnp.zeros((rows // count, states), jnp.float32)
    outs = [None] * count
    for k in reversed(range(count)):
        outs[k] = carry.astype(jnp.bfloat16)
        carry = parts[k].astype(jnp.float32) + decays[k][:, None] * carry
    back = lax.all_to_all(jnp.stack(outs), "tm", split_axis=0, concat_axis=0)
    return back.reshape(heads, size, states).astype(jnp.float32)


def per_device(
    layer_in,
    out_grad,
    w_bc,
    log_decay,
    step,
    saved_states,
    w_gate,
    w_up,
    slot_rows,
    slot_counts,
    slot_gates,
):
    n_tm = lax.axis_size("tm")
    n_dp = lax.axis_size("dp")
    place = lax.axis_index("tm")
    frames_in = layer_in[0]
    timestep_derivative = out_grad[0]
    length, width = frames_in.shape
    share = w_bc.shape[0] // n_tm
    w_share = lax.dynamic_slice_in_dim(w_bc, place * share, share, 0)
    w_whole = lax.all_gather(w_share, ("dp", "tm"), axis=0, tiled=True)

    chosen = slot_rows[0, 0]
    capacity = chosen.shape[0]
    live = jnp.arange(capacity) < slot_counts[0, 0]
    weights = jnp.where(live, slot_gates[0, 0], jnp.zeros_like(slot_gates[0, 0]))
    pick = (chosen[:, None] == jnp.arange(length)[None, :]).astype(jnp.bfloat16)
    rows_in = jnp.dot(pick, frames_in, preferred_element_type=jnp.float32).astype(jnp.bfloat16)
    rows_grad = jnp.dot(pick, timestep_derivative, preferred_element_type=jnp.float32)
    rows_grad = (rows_grad * weights.astype(jnp.float32)[:, None]).astype(jnp.bfloat16)
    piece = width // n_dp
    rows_grad = rows_grad.reshape(capacity, n_dp, piece).transpose(1, 0, 2)
    rows_grad = lax.all_to_all(rows_grad, "dp", split_axis=0, concat_axis=0)
    rows_in = rows_in.reshape(capacity, n_dp, piece).transpose(1, 0, 2)
    rows = lax.all_gather(jnp.stack([rows_in, rows_grad]), "tm")
    rows_in = rows[:, 0].transpose(0, 2, 1, 3).reshape(n_tm * capacity, width)
    rows_grad = rows[:, 1].transpose(1, 0, 2, 3).reshape(n_dp * n_tm * capacity, piece)
    gate_h = jnp.dot(rows_in, w_gate[0], preferred_element_type=jnp.float32)
    up_h = jnp.dot(rows_in, w_up[0], preferred_element_type=jnp.float32)
    weighted = (jax.nn.silu(gate_h) * up_h).astype(jnp.bfloat16)
    weighted = lax.all_gather(weighted, "dp", axis=0, tiled=True)
    w_down_grad = lax.dot_general(
        weighted, rows_grad, (((0,), (0,)), ((), ())), preferred_element_type=jnp.float32
    ).astype(jnp.bfloat16)

    columns = frames_in.reshape(length, n_tm, width // n_tm).transpose(1, 0, 2)
    columns = lax.all_to_all(columns, "tm", split_axis=0, concat_axis=0)
    columns = columns.reshape(n_tm * length, width // n_tm)

    context, (decay, g_local) = local_terms(
        frames_in, timestep_derivative, w_whole, log_decay[0], step[0]
    )
    r_grad = reverse_carry(decay, g_local)
    h_in = saved_states[0, 0].astype(jnp.float32)
    d_in, d_decay, d_step, d_bc = finish(context, h_in, r_grad)
    d_bc = lax.all_gather(d_bc, "tm", axis=0, tiled=True)
    w_term = lax.dot_general(
        columns, d_bc, (((0,), (0,)), ((), ())), preferred_element_type=jnp.float32
    )
    w_bc_grad = lax.psum_scatter(w_term, "dp", scatter_dimension=0, tiled=True)
    return (d_in[None], d_decay[None], d_step[None], w_bc_grad, w_down_grad[None])


def solution(mesh):
    in_specs = (
        P("dp", "tm", None),
        P("dp", "tm", None),
        P("dp", None),
        P("dp", "tm", None),
        P("dp", "tm", None),
        P("dp", "tm", None, None, None),
        P(None, None, "tm"),
        P(None, None, "tm"),
        P("dp", None, "tm"),
        P("dp", "tm"),
        P("dp", None, "tm"),
    )
    out_specs = (
        P("dp", "tm", None),
        P("dp", "tm", None),
        P("dp", "tm", None),
        P(("tm", "dp"), None),
        P(None, "tm", "dp"),
    )
    return jax.shard_map(
        per_device, mesh=mesh, in_specs=in_specs, out_specs=out_specs, check_vma=False
    )
```

```python
import jax
import jax.numpy as jnp
from jax import lax
from jax.experimental import pallas as pl
from jax.experimental.pallas import tpu as pltpu
from jax.sharding import PartitionSpec as P

HI = lax.Precision.HIGHEST
F32 = jnp.float32
BF16 = jnp.bfloat16
LANES = 128
EXTRA = 16


def dot(a, b, ca, cb, precision=None):
    return lax.dot_general(
        a, b, (((ca,), (cb,)), ((), ())), precision=precision, preferred_element_type=F32
    )


def iota(shape, axis):
    return lax.broadcasted_iota(jnp.int32, shape, axis)


def triangle(n, keep):
    return jnp.where(keep(iota((n, n), 0), iota((n, n), 1)), 1.0, 0.0).astype(F32)


def spread(table, j, size):
    per = LANES // size
    out = table[:, j * per : j * per + 1]
    lane = iota((1, LANES), 1)
    for i in range(1, per):
        out = jnp.where(lane < i * size, out, table[:, j * per + i : j * per + i + 1])
    return out


def by_head(j, size, copies):
    shape = (LANES, LANES)
    one = jnp.where(iota(shape, 0) // size + j * (LANES // size) == iota(shape, 1), 1.0, 0.0)
    return jnp.concatenate([one.astype(BF16)] * copies, axis=0)


def halves(values):
    high = values.astype(BF16)
    low = (values - high.astype(F32)).astype(BF16)
    return jnp.concatenate([high, low], axis=1)


def call(kernel, outs, flops, scratch=(), limit=40):
    size = sum(o.size * o.dtype.itemsize for o in outs)
    return pl.pallas_call(
        kernel,
        out_shape=outs,
        scratch_shapes=list(scratch),
        cost_estimate=pl.CostEstimate(
            flops=int(flops), bytes_accessed=int(2 * size), transcendentals=0
        ),
        compiler_params=pltpu.CompilerParams(vmem_limit_bytes=limit * 1024 * 1024),
    )


def shape(dims, kind):
    return jax.ShapeDtypeStruct(dims, kind)


def pick_kernel(x_ref, dy_ref, rows_ref, count_ref, gate_ref, in_ref, grad_ref, xt_ref):
    length, width = x_ref.shape
    slots = rows_ref.shape[1]
    hit = iota((length, slots), 0) == rows_ref[...]
    live = iota((1, slots), 1) < count_ref[...]
    weight = jnp.where(live, gate_ref[...].astype(F32), 0.0)
    pick = jnp.where(hit, 1.0, 0.0).astype(BF16)
    scaled = jnp.where(hit, weight, 0.0).astype(BF16)
    in_ref[...] = dot(pick, x_ref[...], 0, 0).astype(BF16)
    grads = dot(scaled, dy_ref[...], 0, 0).astype(BF16)
    piece = grad_ref.shape[2]
    for i in range(grad_ref.shape[0]):
        grad_ref[i] = grads[:, i * piece : (i + 1) * piece]
    for j in range(width // LANES):
        tile = x_ref[:, j * LANES : (j + 1) * LANES].astype(F32)
        xt_ref[j * LANES : (j + 1) * LANES, :] = tile.T.astype(BF16)


def project_kernel(n_dp, unit, *refs):
    x_ref, dy_ref, ld_ref, ldt_ref, own_ref = refs[:5]
    mine = refs[5 : 4 + n_dp]
    other = refs[4 + n_dp : 3 + 2 * n_dp]
    w_ref, bc_ref, g_ref = refs[3 + 2 * n_dp :]
    share = own_ref.shape[0]
    half = own_ref.shape[1] // 2
    place = lax.axis_index("dp")
    core = lax.rem(lax.axis_index("tm"), 2)

    def rows(shift):
        source = lax.rem(place + n_dp - shift, n_dp)
        return pl.ds(pl.multiple_of(source * share, 16), share)

    w_ref[rows(0), :] = own_ref[...]
    for i in range(n_dp - 1):
        w_ref[rows(i + 1), pl.ds(pl.multiple_of(core * half, LANES), half)] = mine[i][...]
        w_ref[rows(i + 1), pl.ds(pl.multiple_of((1 - core) * half, LANES), half)] = other[i][...]
    bc = dot(x_ref[...], w_ref[...], 1, 0).astype(BF16)
    bc_ref[...] = bc
    c_rows = bc[:, half:]
    length, width = x_ref.shape
    heads = ld_ref.shape[1]
    size = width // heads
    cum = dot(triangle(length, lambda a, b: a >= b), ld_ref[...], 1, 0, HI)
    cumt = dot(ldt_ref[...], triangle(length, lambda a, b: a <= b), 1, 0, HI)
    start = jnp.exp(cum)
    n_tm = g_ref.shape[0]
    block = g_ref.shape[1] - EXTRA
    for j in range(width // LANES):
        span = slice(j * LANES, (j + 1) * LANES)
        scaled = (dy_ref[:, span].astype(F32) * spread(start, j, size)).astype(BF16)
        tile = dot(scaled, c_rows, 0, 0).astype(BF16)
        for i in range(LANES // unit):
            row = j * LANES + i * unit
            g_ref[row // block, row % block : row % block + unit, :] = tile[
                i * unit : (i + 1) * unit
            ]
    decay = jnp.broadcast_to(jnp.exp(cumt[:, length - 1 : length]), (heads, LANES))
    high = decay.astype(BF16).astype(F32)
    low = decay - high
    for b in range(n_tm):
        owners = [(b * block + u * unit) // size for u in range(block // unit)]
        parts = [high[h : h + 1] for h in owners] + [low[h : h + 1] for h in owners]
        parts.append(jnp.zeros((EXTRA - len(parts), LANES), F32))
        g_ref[b, block : block + EXTRA, :] = jnp.concatenate(parts, axis=0).astype(BF16)


def scan_kernel(unit, parts_ref, out_ref):
    n_tm, block, states = out_ref.shape
    units = block // unit
    carry = [jnp.zeros((unit, states), F32)] * units
    for k in reversed(range(n_tm)):
        for u in range(units):
            span = slice(u * unit, (u + 1) * unit)
            out_ref[k, span, :] = carry[u].astype(BF16)
            if k:
                decay = parts_ref[k, block : block + EXTRA, :].astype(F32)
                decay = decay[u : u + 1] + decay[units + u : units + u + 1]
                carry[u] = parts_ref[k, span, :].astype(F32) + decay * carry[u]


def intra_kernel(
    x_ref, dy_ref, bc_ref, ld_ref, ldt_ref, step_ref, h_ref,
    dx_ref, xs_ref, db_ref, dc_ref, dec_ref, dst_ref, rowm_ref,
):
    length, width = x_ref.shape
    heads = ld_ref.shape[1]
    size = width // heads
    half = bc_ref.shape[1] // 2
    per = LANES // size
    b_rows = bc_ref[:, :half]
    c_rows = bc_ref[:, half:]
    cum = dot(triangle(length, lambda a, b: a >= b), ld_ref[...], 1, 0, HI)
    cumt = dot(ldt_ref[...], triangle(length, lambda a, b: a <= b), 1, 0, HI)
    step = step_ref[...]
    start = jnp.exp(cum)
    into_end = jnp.exp(cum[length - 1 : length] - cum) * step
    upper = iota((length, length), 0) <= iota((length, length), 1)
    scores = dot(b_rows, c_rows, 1, 1)
    lane = iota((1, LANES), 1)
    lane_bf = [jnp.where(lane // size == i, 1.0, 0.0).astype(BF16) for i in range(per)]
    mixed = jnp.zeros((length, length), F32)
    own = jnp.zeros((length, LANES), F32)
    carried = jnp.zeros((length, half), F32)
    reach = jnp.zeros((length, LANES), F32)
    for j in range(width // LANES):
        span = slice(j * LANES, (j + 1) * LANES)
        x_p = x_ref[:, span]
        dy_p = dy_ref[:, span]
        dy_f = dy_p.astype(F32)
        dy_h = jnp.concatenate([dy_p * m for m in lane_bf], axis=0)
        cross = dot(x_p, dy_h, 1, 1)
        kern = []
        for i in range(per):
            h = j * per + i
            diff = cumt[h : h + 1, :] - cum[:, h : h + 1]
            seg = jnp.exp(jnp.where(upper, diff, -1e30))
            kern.append((seg * scores).astype(BF16))
            scaled = seg * cross[:, i * length : (i + 1) * length] * step[:, h : h + 1]
            mixed = mixed + scaled
            full = scaled * scores
            rowm_ref[h : h + 1, :] = jnp.sum(full, axis=0, keepdims=True)
            own = jnp.where(lane == h, jnp.sum(full, axis=1, keepdims=True), own)
        back = dot(jnp.concatenate(kern, axis=1), dy_h, 1, 0)
        dx_ref[:, span] = back * spread(step, j, size)
        xs_ref[:, span] = (x_p.astype(F32) * spread(into_end, j, size)).astype(BF16)
        h_tile = h_ref[span, :]
        scaled = (dy_f * spread(start, j, size)).astype(BF16)
        carried = carried + dot(scaled, h_tile, 1, 0)
        seen = dy_f * dot(c_rows, h_tile, 1, 1)
        reach = reach + dot(halves(seen), by_head(j, size, 2), 1, 0)
    mixed = mixed.astype(BF16)
    db_ref[...] = dot(mixed, c_rows, 1, 0)
    dc_ref[...] = (dot(mixed, b_rows, 0, 0) + carried).astype(BF16)
    later = triangle(length, lambda a, b: a <= b)
    own = own[:, :heads]
    dec_ref[...] = dot(later, rowm_ref[...], 1, 1, HI) + dot(
        later, start * reach[:, :heads] - own, 1, 0, HI
    )
    dst_ref[...] = own / step


def db_kernel(xs_ref, r_ref, db_ref, dc_ref, out_ref):
    half = db_ref.shape[1]
    out_ref[:, :half] = (db_ref[...] + dot(xs_ref[...], r_ref[...], 1, 0)).astype(BF16)
    out_ref[:, half:] = dc_ref[...]


def finish_kernel(
    x_ref, bc_ref, ld_ref, step_ref, h_ref, r_ref, w_ref, dx_ref, dbc_ref, dec_ref, dst_ref,
    in_ref, decay_ref, grad_ref, edge_ref,
):
    length, width = x_ref.shape
    heads = ld_ref.shape[1]
    size = width // heads
    half = bc_ref.shape[1] // 2
    b_rows = bc_ref[:, :half]
    cum = dot(triangle(length, lambda a, b: a >= b), ld_ref[...], 1, 0, HI)
    total = cum[length - 1 : length]
    to_end = jnp.exp(total - cum)
    into_end = to_end * step_ref[...]
    seen = jnp.zeros((length, LANES), F32)
    for j in range(width // LANES):
        span = slice(j * LANES, (j + 1) * LANES)
        r_tile = r_ref[span, :]
        reach = dot(b_rows, r_tile, 1, 1)
        d_in = dx_ref[:, span] + spread(into_end, j, size) * reach
        d_in = d_in + dot(dbc_ref[...], w_ref[span, :], 1, 1)
        in_ref[:, span] = d_in.astype(BF16)
        product = x_ref[:, span].astype(F32) * reach
        seen = seen + dot(halves(product), by_head(j, size, 2), 1, 0)
        edge = r_tile.astype(F32) * h_ref[span, :].astype(F32)
        for i in range(LANES // size):
            h = j * (LANES // size) + i
            edge_ref[h : h + 1, :] = jnp.sum(
                edge[i * size : (i + 1) * size], axis=0, keepdims=True
            )
    seen = seen[:, :heads]
    grad_ref[...] = dst_ref[...] + to_end * seen
    edge = dot(jnp.ones((8, half), F32), edge_ref[...], 1, 1, HI)[:1]
    earlier = triangle(length, lambda a, b: a > b)
    decay_ref[...] = (
        dec_ref[...] + dot(earlier, into_end * seen, 1, 0, HI) + jnp.exp(total) * edge
    )


def term_kernel(n_tm, *refs):
    xt_ref, pieces, out_ref = refs[0], refs[1 : 1 + n_tm], refs[1 + n_tm]
    place = lax.axis_index("tm")
    total = None
    for i in range(n_tm):
        source = lax.rem(place + n_tm - i, n_tm)
        part = dot(xt_ref[source], pieces[i][...], 1, 0)
        total = part if total is None else total + part
    n_dp, share, _ = out_ref.shape
    for i in range(n_dp):
        out_ref[i] = total[i * share : (i + 1) * share].astype(BF16)


def shifted(array, axis, shift):
    count = lax.axis_size(axis)
    return lax.ppermute(array, axis, [(i, (i + shift) % count) for i in range(count)])


def from_all(array, axis):
    return [array] + [shifted(array, axis, s) for s in range(1, lax.axis_size(axis))]


def dealt(array, axis):
    count = lax.axis_size(axis)
    place = lax.axis_index(axis)
    own = lax.dynamic_index_in_dim(array, place, 0, False)
    pieces = [own]
    for s in range(1, count):
        block = lax.dynamic_index_in_dim(array, lax.rem(place + s, count), 0, False)
        pieces.append(shifted(block, axis, s))
    return pieces


def per_device(
    layer_in,
    out_grad,
    w_bc,
    log_decay,
    step,
    saved_states,
    w_gate,
    w_up,
    slot_rows,
    slot_counts,
    slot_gates,
):
    n_tm = lax.axis_size("tm")
    n_dp = lax.axis_size("dp")
    core = lax.rem(lax.axis_index("tm"), 2)
    x = layer_in[0]
    dy = out_grad[0]
    length, width = x.shape
    heads = log_decay.shape[2]
    size = width // heads
    columns = w_bc.shape[1]
    half = columns // 2
    ld = log_decay[0]
    ldt = ld.T
    steps = step[0]
    h_in = saved_states[0, 0].reshape(width, half)
    capacity = slot_rows.shape[2]
    piece = width // n_dp
    block = width // n_tm
    unit = min(size, block & -block)

    w_half = lax.dynamic_slice_in_dim(w_bc, core * half, half, 1)
    mine = from_all(w_half, "dp")[1:]
    swap = [(i, i ^ 1) for i in range(n_tm)]
    other = [lax.ppermute(m, "tm", swap) for m in mine]

    rows_in, rows_grad, x_cols = call(
        pick_kernel,
        [
            shape((capacity, width), BF16),
            shape((n_dp, capacity, piece), BF16),
            shape((width, length), BF16),
        ],
        4e8,
    )(x, dy, slot_rows[0], slot_counts, slot_gates[0])
    x_cols = lax.all_to_all(
        x_cols.reshape(n_tm, block, length), "tm", split_axis=0, concat_axis=0
    )
    rows_grad = jnp.concatenate(dealt(rows_grad, "dp"), axis=1)
    rows = from_all(jnp.concatenate([rows_in, rows_grad], axis=0), "tm")
    rows = jnp.stack(rows)
    rows_in = rows[:, :capacity].reshape(n_tm * capacity, width)
    rows_grad = rows[:, capacity:].reshape(n_tm * capacity, width)
    gate_h = jnp.dot(rows_in, w_gate[0], preferred_element_type=F32)
    up_h = jnp.dot(rows_in, w_up[0], preferred_element_type=F32)
    weighted = (jax.nn.silu(gate_h) * up_h).astype(BF16)
    weighted = jnp.concatenate(from_all(weighted, "dp"), axis=0)
    rows_grad = jnp.concatenate(
        [rows_grad[:, i * piece : (i + 1) * piece] for i in range(n_dp)], axis=0
    )
    w_down_grad = dot(weighted, rows_grad, 0, 0).astype(BF16)

    w_whole, bc, g_local = call(
        lambda *refs: project_kernel(n_dp, unit, *refs),
        [
            shape((width, columns), BF16),
            shape((length, columns), BF16),
            shape((n_tm, block + EXTRA, half), BF16),
        ],
        1e9,
    )(x, dy, ld, ldt, w_bc, *mine, *other)
    parts = lax.all_to_all(g_local, "tm", split_axis=0, concat_axis=0)
    dx, xs, db, dc, dec, dst = call(
        intra_kernel,
        [
            shape((length, width), F32),
            shape((length, width), BF16),
            shape((length, half), F32),
            shape((length, half), BF16),
            shape((length, heads), F32),
            shape((length, heads), F32),
        ],
        4e9,
        [pltpu.VMEM((heads, length), F32)],
    )(x, dy, bc, ld, ldt, steps, h_in)
    carried = call(
        lambda *refs: scan_kernel(unit, *refs), [shape((n_tm, block, half), BF16)], 1e8
    )(parts)[0]
    r_grad = lax.all_to_all(carried, "tm", split_axis=0, concat_axis=0).reshape(width, half)
    d_bc = call(db_kernel, [shape((length, columns), BF16)], 1e8)(xs, r_grad, db, dc)[0]
    d_bcs = from_all(d_bc, "tm")
    d_in, d_decay, d_step = call(
        finish_kernel,
        [
            shape((length, width), BF16),
            shape((length, heads), F32),
            shape((length, heads), F32),
        ],
        2e9,
        [pltpu.VMEM((heads, half), F32)],
    )(x, bc, ld, steps, h_in, r_grad, w_whole, dx, d_bc, dec, dst)
    term = call(
        lambda *refs: term_kernel(n_tm, *refs),
        [shape((n_dp, block // n_dp, columns), BF16)],
        2e8,
    )(x_cols, *d_bcs)[0]
    w_bc_grad = sum(p.astype(F32) for p in dealt(term, "dp"))
    return (d_in[None], d_decay[None], d_step[None], w_bc_grad, w_down_grad[None])


def solution(mesh):
    in_specs = (
        P("dp", "tm", None),
        P("dp", "tm", None),
        P("dp", None),
        P("dp", "tm", None),
        P("dp", "tm", None),
        P("dp", "tm", None, None, None),
        P(None, None, "tm"),
        P(None, None, "tm"),
        P("dp", None, "tm"),
        P("dp", "tm"),
        P("dp", None, "tm"),
    )
    out_specs = (
        P("dp", "tm", None),
        P("dp", "tm", None),
        P("dp", "tm", None),
        P(("tm", "dp"), None),
        P(None, "tm", "dp"),
    )
    return jax.shard_map(
        per_device, mesh=mesh, in_specs=in_specs, out_specs=out_specs, check_vma=False
    )
```

```python
import jax
import jax.numpy as jnp
from jax import lax
from jax.experimental import pallas as pl
from jax.experimental.pallas import tpu as pltpu
from jax.sharding import PartitionSpec as P

HI = lax.Precision.HIGHEST
F32 = jnp.float32
BF16 = jnp.bfloat16
LANES = 128


def dot(a, b, ca, cb, precision=None):
    return lax.dot_general(
        a, b, (((ca,), (cb,)), ((), ())), precision=precision, preferred_element_type=F32
    )


def iota(dims, axis):
    return lax.broadcasted_iota(jnp.int32, dims, axis)


def where_one(mask):
    return jnp.where(mask, 1.0, 0.0)


def triangle(n, keep):
    return where_one(keep(iota((n, n), 0), iota((n, n), 1))).astype(F32)


def halves(values, axis=1):
    high = values.astype(BF16)
    low = (values - high.astype(F32)).astype(BF16)
    return jnp.concatenate([high, low], axis=axis)


def to_lanes(j, size):
    dims = (LANES, LANES)
    one = where_one(iota(dims, 0) == iota(dims, 1) // size + j * (LANES // size)).astype(BF16)
    return jnp.concatenate([one, one], axis=0)


def to_heads(j, heads, size):
    dims = (heads, LANES)
    one = where_one(iota(dims, 0) == iota(dims, 1) // size + j * (LANES // size)).astype(BF16)
    return jnp.concatenate([one, one], axis=1)


def up16(n):
    return -(-n // 16) * 16


def call(kernel, outs, cost, args, after=(), scratch=(), limit=14):
    n_in, n_after = len(args), len(after)

    def body(*refs):
        kernel(*refs[:n_in], *refs[n_in + n_after :])

    return pl.pallas_call(
        body,
        out_shape=outs,
        in_specs=[pl.BlockSpec(memory_space=pltpu.VMEM)] * n_in
        + [pl.BlockSpec(memory_space=pl.ANY)] * n_after,
        out_specs=[pl.BlockSpec(memory_space=pltpu.VMEM)] * len(outs),
        scratch_shapes=list(scratch),
        cost_estimate=pl.CostEstimate(
            flops=int(cost * 1e9), bytes_accessed=1000, transcendentals=0
        ),
        compiler_params=pltpu.CompilerParams(vmem_limit_bytes=limit * 1024 * 1024),
    )(*args, *after)


def shape(dims, kind):
    return jax.ShapeDtypeStruct(dims, kind)


def core_and_chip():
    place = lax.axis_index("tm")
    return lax.rem(place, 2), lax.div(place, 2), lax.axis_size("tm") // 2


def ahead(index, shift, count):
    return lax.rem(index + shift, count)


def rows_at(index, size, align=16):
    return pl.ds(pl.multiple_of(index * size, align), size)


def prep_kernel(
    x_ref, dy_ref, ldt_ref, stept_ref, h_ref,
    cumt_ref, cum_ref, step_ref, dyt_ref, xt_ref, xs_ref, carried_ref,
):
    length, width = x_ref.shape
    heads = ldt_ref.shape[0]
    size = width // heads
    pad = jnp.zeros((LANES - heads, length), F32)
    cumt = dot(ldt_ref[...], triangle(length, lambda a, b: a <= b), 1, 0, HI)
    cumt_ref[...] = cumt
    cum = jnp.concatenate([cumt, pad], axis=0).T
    step = jnp.concatenate([stept_ref[...], pad], axis=0).T
    cum_ref[...] = cum
    step_ref[...] = step
    start = jnp.exp(cum)
    into_end = jnp.exp(cum[length - 1 : length] - cum) * step
    table = jnp.concatenate([halves(start), halves(into_end)], axis=0)
    carried = jnp.zeros(carried_ref.shape, F32)
    for j in range(width // LANES):
        span = slice(j * LANES, (j + 1) * LANES)
        scale = dot(table, to_lanes(j, size), 1, 0)
        x_f = x_ref[:, span].astype(F32)
        xt_ref[span, :] = x_f.T.astype(BF16)
        xs_ref[:, span] = (x_f * scale[length:]).astype(BF16)
        dys = dy_ref[:, span].astype(F32) * scale[:length]
        dyt_ref[span, :] = dys.T.astype(BF16)
        carried = carried + dot(dys.astype(BF16), h_ref[span, :], 1, 0)
    carried_ref[...] = carried


def pick_kernel(x_ref, dy_ref, rows_ref, count_ref, gate_ref, in_ref, grad_ref):
    length = x_ref.shape[0]
    slots = rows_ref.shape[1]
    hit = iota((length, slots), 0) == rows_ref[...]
    live = iota((1, slots), 1) < count_ref[...]
    weight = jnp.where(live, gate_ref[...].astype(F32), 0.0)
    pick = where_one(hit).astype(BF16)
    scaled = jnp.where(hit, weight, 0.0).astype(BF16)
    in_ref[...] = dot(pick, x_ref[...], 0, 0).astype(BF16)
    grads = dot(scaled, dy_ref[...], 0, 0).astype(BF16)
    piece = grad_ref.shape[2]
    for i in range(grad_ref.shape[0]):
        grad_ref[i] = grads[:, i * piece : (i + 1) * piece]


def assemble(w_ref, own_ref, mine_refs, other_ref):
    core, _, _ = core_and_chip()
    place, n_dp = lax.axis_index("dp"), lax.axis_size("dp")
    share = own_ref.shape[0]
    half = share // 2
    w_ref[rows_at(place, share), :] = own_ref[...]
    for i, mine in enumerate(mine_refs):
        source = ahead(place, n_dp - 1 - i, n_dp)
        w_ref[rows_at(source * 2 + core, half), :] = mine[...]
        w_ref[rows_at(source * 2 + 1 - core, half), :] = other_ref[i]


def project_kernel(n_mine, *refs):
    x_ref, dyt_ref, cumt_ref, own_ref = refs[:4]
    mine, other = refs[4 : 4 + n_mine], refs[4 + n_mine]
    w_ref, c_ref, keep_ref, send_ref = refs[5 + n_mine :]
    core, _, _ = core_and_chip()
    assemble(w_ref, own_ref, mine, other)
    c_rows = dot(x_ref[...], w_ref[...], 1, 0).astype(BF16)
    c_ref[...] = c_rows
    heads, length = cumt_ref.shape
    width = dyt_ref.shape[0]
    part, many = width // 2, heads // 2
    decay = jnp.broadcast_to(jnp.exp(cumt_ref[:, length - 1 : length]), (heads, LANES))
    for ref, index in ((keep_ref, core), (send_ref, 1 - core)):
        ref[:part, :] = dot(dyt_ref[rows_at(index, part), :], c_rows, 1, 0).astype(BF16)
        mine_decay = jnp.where(index == 0, decay[:many], decay[many:])
        high = mine_decay.astype(BF16).astype(F32)
        fill = jnp.zeros((ref.shape[0] - part - 2 * many, LANES), F32)
        extra = jnp.concatenate([high, mine_decay - high, fill], axis=0)
        ref[part:, :] = extra.astype(BF16)


def pair(keep_ref, recv_ref, many, size, head):
    core, _, _ = core_and_chip()
    part = many * size
    both = []
    for ref in (keep_ref, recv_ref):
        extra = ref[part:, :].astype(F32)
        decay = extra[head : head + 1] + extra[many + head : many + head + 1]
        both.append((ref[head * size : (head + 1) * size, :].astype(F32), decay))
    first = jax.tree.map(lambda a, b: jnp.where(core == 0, a, b), both[0], both[1])
    second = jax.tree.map(lambda a, b: jnp.where(core == 0, b, a), both[0], both[1])
    return first, second


def combine_kernel(many, size, unit, *refs):
    keep_ref, recv_ref = refs[:2]
    outs, held = refs[2:-1], refs[-1]
    _, chip, n_chip = core_and_chip()
    block = many * size // n_chip
    units = block // unit
    decays = []
    for head in range(many):
        (g0, a0), (g1, a1) = pair(keep_ref, recv_ref, many, size, head)
        state = (g0 + a0 * g1).astype(BF16)
        for i in range(size // unit):
            row = head * size + i * unit
            held[row // block, row % block : row % block + unit, :] = state[
                i * unit : (i + 1) * unit
            ]
            decays.append(a0 * a1)
    for b in range(n_chip):
        mine = jnp.concatenate(decays[b * units : (b + 1) * units], axis=0)
        high = mine.astype(BF16).astype(F32)
        fill = jnp.zeros((held.shape[1] - block - 2 * units, LANES), F32)
        extra = jnp.concatenate([high, mine - high, fill], axis=0)
        held[b, block:, :] = extra.astype(BF16)
    for s, out in enumerate(outs):
        out[...] = held[ahead(chip, s, n_chip)]


def scan_kernel(unit, *refs):
    _, chip, n_chip = core_and_chip()
    pieces, outs = refs[:n_chip], refs[n_chip : 2 * n_chip]
    held, result = refs[2 * n_chip :]
    block, states = outs[0].shape
    units = block // unit
    for s, ref in enumerate(pieces):
        held[ahead(chip, n_chip - s, n_chip)] = ref[...]
    carry = [jnp.zeros((unit, states), F32)] * units
    for k in reversed(range(n_chip)):
        extra = held[k, block:, :].astype(F32)
        for u in range(units):
            span = slice(u * unit, (u + 1) * unit)
            result[k, span, :] = carry[u].astype(BF16)
            if k:
                decay = extra[u : u + 1] + extra[units + u : units + u + 1]
                carry[u] = held[k, span, :].astype(F32) + decay * carry[u]
    for s, out in enumerate(outs):
        out[...] = result[ahead(chip, s, n_chip)]


def carry_kernel(many, size, *refs):
    core, chip, n_chip = core_and_chip()
    pieces = refs[:n_chip]
    keep_ref, recv_ref, own_ref, send_ref, held = refs[n_chip:]
    block = pieces[0].shape[0]
    for s, ref in enumerate(pieces):
        held[rows_at(ahead(chip, n_chip - s, n_chip), block), :] = ref[...]
    for head in range(many):
        span = slice(head * size, (head + 1) * size)
        _, (g1, a1) = pair(keep_ref, recv_ref, many, size, head)
        second = held[span, :].astype(F32)
        first = g1 + a1 * second
        own_ref[span, :] = jnp.where(core == 0, first, second).astype(BF16)
        send_ref[span, :] = jnp.where(core == 0, second, first).astype(BF16)


def b_kernel(n_mine, *refs):
    x_ref, own_ref = refs[:2]
    mine, other = refs[2 : 2 + n_mine], refs[2 + n_mine]
    w_ref, b_ref = refs[3 + n_mine :]
    assemble(w_ref, own_ref, mine, other)
    b_ref[...] = dot(x_ref[...], w_ref[...], 1, 0).astype(BF16)


def intra_kernel(
    first, many, x_ref, dy_ref, b_ref, c_ref, cumt_ref, cum_ref, step_ref, h_ref, before_ref,
    dx_ref, mixed_ref, ex_ref, own_ref, rowm_ref,
):
    length, width = x_ref.shape
    heads = cumt_ref.shape[0]
    size = width // heads
    per = LANES // size
    upper = iota((length, length), 0) <= iota((length, length), 1)
    b_rows, c_rows = b_ref[...], c_ref[...]
    scores = dot(b_rows, c_rows, 1, 1)
    lane = iota((1, LANES), 1)
    lane_bf = [where_one(lane // size == i).astype(BF16) for i in range(per)]
    mixed = before_ref[...]
    own = jnp.zeros((length, LANES), F32)
    reach = jnp.zeros((heads, length), F32)
    for j in range(first, first + many):
        span = slice(j * LANES, (j + 1) * LANES)
        out_span = slice((j - first) * LANES, (j - first + 1) * LANES)
        x_p = x_ref[:, span]
        dy_p = dy_ref[:, span]
        dy_h = jnp.concatenate([dy_p * m for m in lane_bf], axis=0)
        cross = dot(x_p, dy_h, 1, 1)
        kern = []
        wide = None
        for i in range(per):
            h = j * per + i
            diff = cumt_ref[h : h + 1, :] - cum_ref[:, h : h + 1]
            seg = jnp.exp(jnp.where(upper, diff, -1e30))
            kern.append((seg * scores).astype(BF16))
            step = jnp.broadcast_to(step_ref[:, h : h + 1], (length, LANES))
            wide = step if i == 0 else jnp.where(lane < i * size, wide, step)
            scaled = seg * cross[:, i * length : (i + 1) * length] * step
            mixed = mixed + scaled
            full = scaled * scores
            rowm_ref[h : h + 1, :] = jnp.sum(full, axis=0, keepdims=True)
            own = jnp.where(lane == h, jnp.sum(full, axis=1, keepdims=True), own)
        back = dot(jnp.concatenate(kern, axis=1), dy_h, 1, 0)
        dx_ref[:, out_span] = back * wide
        seen = dy_p.astype(F32) * dot(c_rows, h_ref[span, :], 1, 1)
        reach = reach + dot(to_heads(j, heads, size), halves(seen), 1, 1)
    mixed_ref[...] = mixed
    rows = slice(first * per, (first + many) * per)
    own = own.T[rows]
    own_ref[...] = own
    ex_ref[...] = rowm_ref[rows, :] + jnp.exp(cumt_ref[rows, :]) * reach[rows] - own


def close_kernel(mixed_ref, b_ref, c_ref, carried_ref, db_ref, dc_ref):
    mixed = mixed_ref[...].astype(BF16)
    db_ref[...] = dot(mixed, c_ref[...], 1, 0)
    dc_ref[...] = (dot(mixed, b_ref[...], 0, 0) + carried_ref[...]).astype(BF16)


def db_kernel(xs_ref, own_ref, recv_ref, db_ref, dc_ref, out_ref):
    core, _, _ = core_and_chip()
    half = db_ref.shape[1]
    part = own_ref.shape[0]
    total = db_ref[...]
    for ref, index in ((own_ref, core), (recv_ref, 1 - core)):
        total = total + dot(xs_ref[:, rows_at(index, part, LANES)], ref[...], 1, 0)
    out_ref[:, :half] = total.astype(BF16)
    out_ref[:, half:] = dc_ref[...]


def finish_kernel(parts, *refs):
    (x_ref, b_ref, cumt_ref, stept_ref, cum_ref, step_ref, h_ref, own_ref, recv_ref,
     wb_ref, wc_ref, dbc_ref) = refs[:12]
    dx_refs, ex_refs, st_refs = (refs[12 + i * parts : 12 + (i + 1) * parts] for i in range(3))
    in_ref, decay_ref, grad_ref, r_ref, edge_ref = refs[12 + 3 * parts :]
    core, _, _ = core_and_chip()
    length, width = x_ref.shape
    heads = cumt_ref.shape[0]
    size = width // heads
    half = b_ref.shape[1]
    part = width // 2
    r_ref[rows_at(core, part), :] = own_ref[...]
    r_ref[rows_at(1 - core, part), :] = recv_ref[...]
    cum = cum_ref[...]
    table = halves(jnp.exp(cum[length - 1 : length] - cum) * step_ref[...])
    seen = jnp.zeros((heads, length), F32)
    b_rows = b_ref[...]
    d_b, d_c = dbc_ref[:, :half], dbc_ref[:, half:]
    for j in range(width // LANES):
        span = slice(j * LANES, (j + 1) * LANES)
        local = dx_refs[j * LANES // (width // parts)]
        start = j * LANES % (width // parts)
        r_tile = r_ref[span, :]
        reach = dot(b_rows, r_tile, 1, 1)
        d_in = local[:, start : start + LANES] + dot(table, to_lanes(j, size), 1, 0) * reach
        d_in = d_in + dot(d_b, wb_ref[span, :], 1, 1) + dot(d_c, wc_ref[span, :], 1, 1)
        in_ref[:, span] = d_in.astype(BF16)
        product = x_ref[:, span].astype(F32) * reach
        seen = seen + dot(to_heads(j, heads, size), halves(product), 1, 1)
        edge = r_tile.astype(F32) * h_ref[span, :].astype(F32)
        for i in range(LANES // size):
            h = j * (LANES // size) + i
            edge_ref[h : h + 1, :] = jnp.sum(
                edge[i * size : (i + 1) * size], axis=0, keepdims=True
            )
    cumt = cumt_ref[...]
    total = cumt[:, length - 1 : length]
    to_end = jnp.exp(total - cumt)
    step = stept_ref[...]
    own = jnp.concatenate([r[...] for r in st_refs], axis=0)
    excess = jnp.concatenate([r[...] for r in ex_refs], axis=0)
    grad_ref[...] = own / step + to_end * seen
    edge = jnp.exp(total) * jnp.sum(edge_ref[...], axis=1, keepdims=True)
    decay_ref[...] = (
        dot(excess, triangle(length, lambda a, b: a >= b), 1, 0, HI)
        + dot(to_end * step * seen, triangle(length, lambda a, b: a < b), 1, 0, HI)
        + edge
    )


def term_kernel(n_chip, *refs):
    columns, pieces = refs[:n_chip], refs[n_chip : 2 * n_chip]
    keep_ref, send_ref = refs[2 * n_chip : 2 * n_chip + 2]
    held = refs[-1]
    core, _, _ = core_and_chip()
    total = None
    for a, b in zip(columns, pieces):
        part = dot(a[...], b[...], 1, 0)
        total = part if total is None else total + part
    block = keep_ref.shape[0]
    held[0] = total[:block]
    held[1] = total[block:]
    keep_ref[...] = held[core]
    send_ref[...] = held[1 - core].astype(BF16)


def deal_kernel(keep_ref, recv_ref, own_ref, *refs):
    outs, held = refs[:-1], refs[-1]
    place, n_dp = lax.axis_index("dp"), lax.axis_size("dp")
    total = keep_ref[...] + recv_ref[...].astype(F32)
    share = own_ref.shape[0]
    for i in range(n_dp):
        held[i] = total[i * share : (i + 1) * share]
    own_ref[...] = held[place]
    for s, out in enumerate(outs):
        out[...] = held[ahead(place, s + 1, n_dp)].astype(BF16)


def expert_kernel(flip, a_ref, b_ref, gate_ref, up_ref, out_ref, rows_ref, gate_acc, up_acc):
    step = pl.program_id(0)
    n_chip, double, _ = a_ref.shape
    slots = double // 2

    @pl.when(step == 0)
    def _():
        for i in range(n_chip):
            rows_ref[i * slots : (i + 1) * slots, :] = a_ref[i, :slots, :]
            rows_ref[(n_chip + i) * slots : (n_chip + i + 1) * slots, :] = b_ref[i, :slots, :]
        gate_acc[...] = jnp.zeros_like(gate_acc)
        up_acc[...] = jnp.zeros_like(up_acc)

    depth = gate_ref.shape[0]
    rows = rows_ref[:, rows_at(step, depth, LANES)]
    gate_acc[...] += dot(rows, gate_ref[...], 1, 0)
    up_acc[...] += dot(rows, up_ref[...], 1, 0)

    @pl.when(step == pl.num_programs(0) - 1)
    def _():
        weighted = jax.nn.silu(gate_acc[...]) * up_acc[...]
        out_ref[...] = (weighted.T if flip else weighted).astype(BF16)


def expert(a, b, w_gate, w_up, flip):
    n_chip, double, width = a.shape
    slots = n_chip * double
    hidden = w_gate.shape[1]
    depth = 512
    whole = pl.BlockSpec((n_chip, double, width), lambda i: (0, 0, 0))
    block = pl.BlockSpec((depth, hidden), lambda i: (i, 0))
    out = (hidden, slots) if flip else (slots, hidden)
    return pl.pallas_call(
        lambda *refs: expert_kernel(flip, *refs),
        out_shape=shape(out, BF16),
        grid=(width // depth,),
        in_specs=[whole, whole, block, block],
        out_specs=pl.BlockSpec(out, lambda i: (0, 0)),
        scratch_shapes=[
            pltpu.VMEM((slots, width), BF16),
            pltpu.VMEM((slots, hidden), F32),
            pltpu.VMEM((slots, hidden), F32),
        ],
        cost_estimate=pl.CostEstimate(
            flops=4 * slots * width * hidden,
            bytes_accessed=4 * width * hidden,
            transcendentals=0,
        ),
        compiler_params=pltpu.CompilerParams(vmem_limit_bytes=20 * 1024 * 1024),
    )(a, b, w_gate, w_up)


def down_kernel(n_dp, flip, *refs):
    pieces = refs[:n_dp]
    a_ref, b_ref, out_ref = refs[n_dp:]
    n_chip, double, _ = a_ref.shape
    slots = double // 2
    piece = out_ref.shape[1]
    total = None
    for s in range(n_dp):
        span = slice(s * piece, (s + 1) * piece)
        grads = jnp.concatenate(
            [r[i, slots:, span] for r in (a_ref, b_ref) for i in range(n_chip)], axis=0
        )
        part = dot(pieces[s][...], grads, 1 if flip else 0, 0)
        total = part if total is None else total + part
    out_ref[...] = total.astype(BF16)


def shifted(array, axis, shift, stride=1):
    count = lax.axis_size(axis)
    return lax.ppermute(array, axis, [(i, (i + shift * stride) % count) for i in range(count)])


def swapped(array):
    return lax.ppermute(array, "tm", [(i, i ^ 1) for i in range(lax.axis_size("tm"))])


def chips(arrays):
    return [arrays[0]] + [shifted(a, "tm", s + 1, 2) for s, a in enumerate(arrays[1:])]


def dealt(array, axis):
    count = lax.axis_size(axis)
    place = lax.axis_index(axis)
    pieces = [lax.dynamic_index_in_dim(array, place, 0, False)]
    for s in range(1, count):
        block = lax.dynamic_index_in_dim(array, lax.rem(place + s, count), 0, False)
        pieces.append(shifted(block, axis, s))
    return pieces


def per_device(
    layer_in,
    out_grad,
    w_bc,
    log_decay,
    step,
    saved_states,
    w_gate,
    w_up,
    slot_rows,
    slot_counts,
    slot_gates,
):
    n_dp = lax.axis_size("dp")
    core, chip, n_chip = core_and_chip()
    x = layer_in[0]
    dy = out_grad[0]
    length, width = x.shape
    heads = log_decay.shape[2]
    size = width // heads
    share, columns = w_bc.shape
    half = columns // 2
    ldt = log_decay[0].T
    stept = step[0].T
    h_in = saved_states[0, 0].reshape(width, half)
    capacity = slot_rows.shape[2]
    piece = width // n_dp
    part = width // 2
    many = heads // 2
    block = part // n_chip
    unit = min(size, block & -block)
    flip = w_gate.shape[2] % LANES == 0

    def gathered(start):
        own = w_bc[:, start : start + half]
        mine = lax.dynamic_slice(w_bc, (core * (share // 2), start), (share // 2, half))
        mine = [shifted(mine, "dp", s) for s in range(1, n_dp)]
        return [own, *mine, swapped(jnp.stack(mine))]

    w_c = gathered(half)

    cumt, cum, steps, dyt, xt, xs, carried = call(
        prep_kernel,
        [
            shape((heads, length), F32),
            shape((length, LANES), F32),
            shape((length, LANES), F32),
            shape((width, length), BF16),
            shape((width, length), BF16),
            shape((length, width), BF16),
            shape((length, half), F32),
        ],
        2.0,
        (x, dy, ldt, stept, h_in),
    )
    rows_in, rows_grad = call(
        pick_kernel,
        [shape((capacity, width), BF16), shape((n_dp, capacity, piece), BF16)],
        0.5,
        (x, dy, slot_rows[0], slot_counts, slot_gates[0]),
        after=(cumt,),
    )
    wc_whole, c_rows, keep, send = call(
        lambda *refs: project_kernel(n_dp - 1, *refs),
        [
            shape((width, half), BF16),
            shape((length, half), BF16),
            shape((part + up16(2 * many), half), BF16),
            shape((part + up16(2 * many), half), BF16),
        ],
        1.0,
        (x, dyt, cumt, *w_c),
    )
    recv = swapped(send)
    w_b = gathered(0)
    extra = up16(2 * (block // unit))
    pieces = call(
        lambda *refs: combine_kernel(many, size, unit, *refs),
        [shape((block + extra, half), BF16)] * n_chip,
        0.5,
        (keep, recv),
        scratch=[pltpu.VMEM((n_chip, block + extra, half), BF16)],
    )
    pieces = chips(pieces)

    rows_grad = jnp.concatenate(dealt(rows_grad, "dp"), axis=1)
    rows = jnp.concatenate([rows_in, rows_grad], axis=0)
    rows_a = jnp.stack(chips([rows] * n_chip))
    rows_b = swapped(rows_a)
    weighted = expert(rows_a, rows_b, w_gate[0], w_up[0], flip)

    wb_whole, b_rows = call(
        lambda *refs: b_kernel(n_dp - 1, *refs),
        [shape((width, half), BF16), shape((length, half), BF16)],
        0.5,
        (x, *w_b),
    )
    parts = 2
    tiles = width // LANES // parts
    dxs, exs, owns = [], [], []
    mixed = jnp.zeros((length, length), F32)
    for i in range(parts):
        dx, mixed, ex, own = call(
            lambda *refs, i=i: intra_kernel(i * tiles, tiles, *refs),
            [
                shape((length, width // parts), F32),
                shape((length, length), F32),
                shape((heads // parts, length), F32),
                shape((heads // parts, length), F32),
            ],
            3.0,
            (x, dy, b_rows, c_rows, cumt, cum, steps, h_in, mixed),
            scratch=[pltpu.VMEM((heads, length), F32)],
        )
        dxs.append(dx)
        exs.append(ex)
        owns.append(own)
    db, dc = call(
        close_kernel,
        [shape((length, half), F32), shape((length, half), BF16)],
        0.3,
        (mixed, b_rows, c_rows, carried),
    )

    returned = call(
        lambda *refs: scan_kernel(unit, *refs),
        [shape((block, half), BF16)] * n_chip,
        0.5,
        tuple(pieces),
        scratch=[
            pltpu.VMEM((n_chip, block + extra, half), BF16),
            pltpu.VMEM((n_chip, block, half), BF16),
        ],
    )
    returned = chips(returned)
    r_own, r_send = call(
        lambda *refs: carry_kernel(many, size, *refs),
        [shape((part, half), BF16)] * 2,
        0.5,
        (*returned, keep, recv),
        scratch=[pltpu.VMEM((part, half), BF16)],
    )
    r_recv = swapped(r_send)
    columns_in = chips(
        [
            lax.dynamic_index_in_dim(
                xt.reshape(n_chip, width // n_chip, length), ahead(chip, s, n_chip), 0, False
            )
            for s in range(n_chip)
        ]
    )
    d_bc = call(db_kernel, [shape((length, columns), BF16)], 0.3, (xs, r_own, r_recv, db, dc))[0]
    d_bcs = chips([d_bc] * n_chip)
    d_in, d_decay, d_step = call(
        lambda *refs: finish_kernel(parts, *refs),
        [
            shape((length, width), BF16),
            shape((heads, length), F32),
            shape((heads, length), F32),
        ],
        3.0,
        (x, b_rows, cumt, stept, cum, steps, h_in, r_own, r_recv, wb_whole, wc_whole, d_bc,
         *dxs, *exs, *owns),
        scratch=[pltpu.VMEM((width, half), BF16), pltpu.VMEM((heads, half), F32)],
    )
    w_rows = width // (2 * n_chip)
    term, term_send = call(
        lambda *refs: term_kernel(n_chip, *refs),
        [shape((w_rows, columns), F32), shape((w_rows, columns), BF16)],
        0.5,
        (*columns_in, *d_bcs),
        scratch=[pltpu.VMEM((2, w_rows, columns), F32)],
    )
    final = call(
        deal_kernel,
        [shape((w_rows // n_dp, columns), F32)]
        + [shape((w_rows // n_dp, columns), BF16)] * (n_dp - 1),
        0.3,
        (term, swapped(term_send)),
        scratch=[pltpu.VMEM((n_dp, w_rows // n_dp, columns), F32)],
    )
    w_bc_grad = final[0]
    for s in range(1, n_dp):
        w_bc_grad = w_bc_grad + shifted(final[s], "dp", s).astype(F32)

    spread = [weighted] + [shifted(weighted, "dp", s) for s in range(1, n_dp)]
    w_down_grad = call(
        lambda *refs: down_kernel(n_dp, flip, *refs),
        [shape((w_gate.shape[2], piece), BF16)],
        1.0,
        (*spread, rows_a, rows_b),
    )[0]
    return (d_in[None], d_decay.T[None], d_step.T[None], w_bc_grad, w_down_grad[None])


def solution(mesh):
    in_specs = (
        P("dp", "tm", None),
        P("dp", "tm", None),
        P("dp", None),
        P("dp", "tm", None),
        P("dp", "tm", None),
        P("dp", "tm", None, None, None),
        P(None, None, "tm"),
        P(None, None, "tm"),
        P("dp", None, "tm"),
        P("dp", "tm"),
        P("dp", None, "tm"),
    )
    out_specs = (
        P("dp", "tm", None),
        P("dp", "tm", None),
        P("dp", "tm", None),
        P(("tm", "dp"), None),
        P(None, "tm", "dp"),
    )
    return jax.shard_map(
        per_device, mesh=mesh, in_specs=in_specs, out_specs=out_specs, check_vma=False
    )
```

```python
import jax
import jax.numpy as jnp
from jax import lax
from jax.experimental import pallas as pl
from jax.experimental.pallas import tpu as pltpu
from jax.sharding import PartitionSpec as P

HI = lax.Precision.HIGHEST
F32 = jnp.float32
BF16 = jnp.bfloat16
LANES = 128


def dot(a, b, ca, cb, precision=None):
    return lax.dot_general(
        a, b, (((ca,), (cb,)), ((), ())), precision=precision, preferred_element_type=F32
    )


def iota(dims, axis):
    return lax.broadcasted_iota(jnp.int32, dims, axis)


def where_one(mask):
    return jnp.where(mask, 1.0, 0.0)


def triangle(n, keep):
    return where_one(keep(iota((n, n), 0), iota((n, n), 1))).astype(F32)


def halves(values, axis=1):
    high = values.astype(BF16)
    low = (values - high.astype(F32)).astype(BF16)
    return jnp.concatenate([high, low], axis=axis)


def to_lanes(j, size):
    dims = (LANES, LANES)
    one = where_one(iota(dims, 0) == iota(dims, 1) // size + j * (LANES // size)).astype(BF16)
    return jnp.concatenate([one, one], axis=0)


def to_heads(j, heads, size):
    dims = (heads, LANES)
    one = where_one(iota(dims, 0) == iota(dims, 1) // size + j * (LANES // size)).astype(BF16)
    return jnp.concatenate([one, one], axis=1)


def up16(n):
    return -(-n // 16) * 16


def call(kernel, outs, cost, args, after=(), scratch=(), limit=14, fetch=()):
    n_in, n_after, n_out = len(args), len(after), len(outs)
    fetch = tuple(fetch)

    def body(*refs):
        ins = list(refs[:n_in])
        rest = refs[n_in + n_after :]
        if fetch:
            sems = rest[-1]
            held = rest[len(rest) - 1 - len(fetch) : -1]
            rest = rest[: len(rest) - 1 - len(fetch)]
            copies = []
            for i, (index, ref) in enumerate(zip(fetch, held)):
                copies.append(pltpu.make_async_copy(ins[index], ref, sems.at[i]))
                ins[index] = ref
            for copy in copies:
                copy.start()
            for copy in copies:
                copy.wait()
        kernel(*ins, *rest)

    specs = [
        pl.BlockSpec(memory_space=pltpu.HBM if i in fetch else pltpu.VMEM) for i in range(n_in)
    ]
    held = [pltpu.VMEM(args[i].shape, args[i].dtype) for i in fetch]
    if fetch:
        held.append(pltpu.SemaphoreType.DMA((len(fetch),)))
    return pl.pallas_call(
        body,
        out_shape=outs,
        in_specs=specs + [pl.BlockSpec(memory_space=pl.ANY)] * n_after,
        out_specs=[pl.BlockSpec(memory_space=pltpu.VMEM)] * n_out,
        scratch_shapes=list(scratch) + held,
        cost_estimate=pl.CostEstimate(
            flops=int(cost * 1e9), bytes_accessed=1000, transcendentals=0
        ),
        compiler_params=pltpu.CompilerParams(vmem_limit_bytes=limit * 1024 * 1024),
    )(*args, *after)


def shape(dims, kind):
    return jax.ShapeDtypeStruct(dims, kind)


def core_and_chip():
    place = lax.axis_index("tm")
    return lax.rem(place, 2), lax.div(place, 2), lax.axis_size("tm") // 2


def ahead(index, shift, count):
    return lax.rem(index + shift, count)


def rows_at(index, size, align=16):
    return pl.ds(pl.multiple_of(index * size, align), size)


def prep_kernel(
    x_ref, dy_ref, ldt_ref, stept_ref, h_ref,
    cumt_ref, cum_ref, step_ref, dyt_ref, xs_ref, carried_ref, *rest,
):
    outs, xt_ref = rest[:-1], rest[-1]
    length, width = x_ref.shape
    heads = ldt_ref.shape[0]
    size = width // heads
    pad = jnp.zeros((LANES - heads, length), F32)
    cumt = dot(ldt_ref[...], triangle(length, lambda a, b: a <= b), 1, 0, HI)
    cumt_ref[...] = cumt
    cum = jnp.concatenate([cumt, pad], axis=0).T
    step = jnp.concatenate([stept_ref[...], pad], axis=0).T
    cum_ref[...] = cum
    step_ref[...] = step
    start = jnp.exp(cum)
    into_end = jnp.exp(cum[length - 1 : length] - cum) * step
    table = jnp.concatenate([halves(start), halves(into_end)], axis=0)
    carried = jnp.zeros(carried_ref.shape, F32)
    for j in range(width // LANES):
        span = slice(j * LANES, (j + 1) * LANES)
        scale = dot(table, to_lanes(j, size), 1, 0)
        x_f = x_ref[:, span].astype(F32)
        xt_ref[span, :] = x_f.T.astype(BF16)
        xs_ref[:, span] = (x_f * scale[length:]).astype(BF16)
        dys = dy_ref[:, span].astype(F32) * scale[:length]
        dyt_ref[span, :] = dys.T.astype(BF16)
        carried = carried + dot(dys.astype(BF16), h_ref[span, :], 1, 0)
    carried_ref[...] = carried
    _, chip, n_chip = core_and_chip()
    for s, out in enumerate(outs):
        out[...] = xt_ref[rows_at(ahead(chip, s, n_chip), width // n_chip), :]


def first_kernel(start, x_ref, dy_ref, pick_ref, w_ref, in_ref, own_ref, *rest):
    outs, held = rest[:-1], rest[-1]
    slots = pick_ref.shape[0] // 2
    width = x_ref.shape[1]
    rows = dot(pick_ref[:slots], x_ref[...], 1, 0).astype(BF16)
    for t in range(width // LANES):
        in_ref[t * slots : (t + 1) * slots, :] = rows[:, t * LANES : (t + 1) * LANES]
    grads = dot(pick_ref[slots:], dy_ref[...], 1, 0).astype(BF16)
    n_dp = held.shape[0]
    piece = width // n_dp
    held[...] = jnp.zeros_like(held)
    for i in range(n_dp):
        for t in range(held.shape[1] // slots):
            low, high = i * piece + t * LANES, min((i + 1) * piece, i * piece + (t + 1) * LANES)
            held[i, t * slots : (t + 1) * slots, : high - low] = grads[:, low:high]
    place = lax.axis_index("dp")
    core, _, _ = core_and_chip()
    own_ref[...] = held[place]
    half = w_ref.shape[0] // 2
    for s, out in enumerate(outs):
        out[:half, :] = w_ref[rows_at(core, half), start : start + LANES]
        out[half:, :] = held[ahead(place, s + 1, n_dp)]


def assemble(start, w_ref, own_ref, mine_refs, other_ref):
    core, _, _ = core_and_chip()
    place, n_dp = lax.axis_index("dp"), lax.axis_size("dp")
    share = own_ref.shape[0]
    half = share // 2
    w_ref[rows_at(place, share), :] = own_ref[:, start : start + LANES]
    for i, mine in enumerate(mine_refs):
        source = ahead(place, n_dp - 1 - i, n_dp)
        w_ref[rows_at(source * 2 + core, half), :] = mine[:half, :]
        w_ref[rows_at(source * 2 + 1 - core, half), :] = other_ref[i]


def project_kernel(n_mine, *refs):
    x_ref, dyt_ref, cumt_ref, own_ref = refs[:4]
    mine, other = refs[4 : 4 + n_mine], refs[4 + n_mine]
    w_ref, c_ref, keep_ref, send_ref, b_ref = refs[5 + n_mine :]
    core, _, _ = core_and_chip()
    assemble(LANES, w_ref, own_ref, mine, other)
    b_ref[...] = own_ref[rows_at(core, b_ref.shape[0]), :LANES]
    c_rows = dot(x_ref[...], w_ref[...], 1, 0).astype(BF16)
    c_ref[...] = c_rows
    heads, length = cumt_ref.shape
    width = dyt_ref.shape[0]
    part, many = width // 2, heads // 2
    decay = jnp.broadcast_to(jnp.exp(cumt_ref[:, length - 1 : length]), (heads, LANES))
    for ref, index in ((keep_ref, core), (send_ref, 1 - core)):
        ref[:part, :] = dot(dyt_ref[rows_at(index, part), :], c_rows, 1, 0).astype(BF16)
        mine_decay = jnp.where(index == 0, decay[:many], decay[many:])
        high = mine_decay.astype(BF16).astype(F32)
        fill = jnp.zeros((ref.shape[0] - part - 2 * many, LANES), F32)
        extra = jnp.concatenate([high, mine_decay - high, fill], axis=0)
        ref[part:, :] = extra.astype(BF16)


def pair(keep_ref, recv_ref, many, size, head):
    core, _, _ = core_and_chip()
    part = many * size
    both = []
    for ref in (keep_ref, recv_ref):
        extra = ref[part:, :].astype(F32)
        decay = extra[head : head + 1] + extra[many + head : many + head + 1]
        both.append((ref[head * size : (head + 1) * size, :].astype(F32), decay))
    first = jax.tree.map(lambda a, b: jnp.where(core == 0, a, b), both[0], both[1])
    second = jax.tree.map(lambda a, b: jnp.where(core == 0, b, a), both[0], both[1])
    return first, second


def payload(ref, many, states, decays):
    size = states[0].shape[0]
    for head, state in enumerate(states):
        ref[head * size : (head + 1) * size, :] = state.astype(BF16)
    decay = jnp.concatenate(decays, axis=0)
    high = decay.astype(BF16).astype(F32)
    fill = jnp.zeros((ref.shape[0] - many * size - 2 * many, LANES), F32)
    extra = jnp.concatenate([high, decay - high, fill], axis=0)
    ref[many * size :, :] = extra.astype(BF16)


def loaded(ref, many, size, head):
    extra = ref[many * size :, :].astype(F32)
    decay = extra[head : head + 1] + extra[many + head : many + head + 1]
    return ref[head * size : (head + 1) * size, :].astype(F32), decay


def combine_kernel(many, size, keep_ref, recv_ref, out_ref):
    states, decays = [], []
    for head in range(many):
        (g0, a0), (g1, a1) = pair(keep_ref, recv_ref, many, size, head)
        states.append(g0 + a0 * g1)
        decays.append(a0 * a1)
    payload(out_ref, many, states, decays)


def pick_side(upper, mine, theirs):
    return jnp.where(upper, theirs, mine), jnp.where(upper, mine, theirs)


def climb_kernel(many, size, bit, mine_ref, recv_ref, out_ref):
    _, chip, _ = core_and_chip()
    upper = lax.rem(lax.div(chip, bit), 2) == 1
    states, decays = [], []
    for head in range(many):
        t_mine, a_mine = loaded(mine_ref, many, size, head)
        t_recv, a_recv = loaded(recv_ref, many, size, head)
        t_low, t_high = pick_side(upper, t_mine, t_recv)
        a_low, a_high = pick_side(upper, a_mine, a_recv)
        states.append(t_low + a_low * t_high)
        decays.append(a_low * a_high)
    payload(out_ref, many, states, decays)


def carry_kernel(many, size, levels, *refs):
    core, chip, _ = core_and_chip()
    recvs = refs[:levels]
    keep_ref, recv_ref, own_ref, send_ref = refs[levels:]
    for head in range(many):
        span = slice(head * size, (head + 1) * size)
        carry, reach = None, None
        for level, ref in enumerate(recvs):
            state, decay = loaded(ref, many, size, head)
            lower = lax.rem(lax.div(chip, 2**level), 2) == 0
            state = jnp.where(lower, state, 0.0)
            decay = jnp.where(lower, decay, 1.0)
            carry = state if carry is None else carry + reach * state
            reach = decay if reach is None else reach * decay
        _, (g1, a1) = pair(keep_ref, recv_ref, many, size, head)
        second = carry
        first = g1 + a1 * second
        own_ref[span, :] = jnp.where(core == 0, first, second).astype(BF16)
        send_ref[span, :] = jnp.where(core == 0, second, first).astype(BF16)


def b_kernel(n_mine, *refs):
    x_ref, own_ref = refs[:2]
    mine, other = refs[2 : 2 + n_mine], refs[2 + n_mine]
    w_ref, b_ref = refs[3 + n_mine :]
    assemble(0, w_ref, own_ref, mine, other)
    b_ref[...] = dot(x_ref[...], w_ref[...], 1, 0).astype(BF16)


def intra_kernel(
    first, many, x_ref, dy_ref, b_ref, c_ref, cumt_ref, cum_ref, step_ref, h_ref, before_ref,
    dx_ref, mixed_ref, ex_ref, own_ref, rowm_ref,
):
    length, width = x_ref.shape
    heads = cumt_ref.shape[0]
    size = width // heads
    per = LANES // size
    upper = iota((length, length), 0) <= iota((length, length), 1)
    b_rows, c_rows = b_ref[...], c_ref[...]
    scores = dot(b_rows, c_rows, 1, 1)
    lane = iota((1, LANES), 1)
    lane_bf = [where_one(lane // size == i).astype(BF16) for i in range(per)]
    mixed = before_ref[...]
    own = jnp.zeros((length, LANES), F32)
    reach = jnp.zeros((heads, length), F32)
    for j in range(first, first + many):
        span = slice(j * LANES, (j + 1) * LANES)
        out_span = slice((j - first) * LANES, (j - first + 1) * LANES)
        x_p = x_ref[:, span]
        dy_p = dy_ref[:, span]
        dy_h = jnp.concatenate([dy_p * m for m in lane_bf], axis=0)
        cross = dot(x_p, dy_h, 1, 1)
        kern = []
        wide = None
        for i in range(per):
            h = j * per + i
            diff = cumt_ref[h : h + 1, :] - cum_ref[:, h : h + 1]
            seg = jnp.exp(jnp.where(upper, diff, -1e30))
            kern.append((seg * scores).astype(BF16))
            step = jnp.broadcast_to(step_ref[:, h : h + 1], (length, LANES))
            wide = step if i == 0 else jnp.where(lane < i * size, wide, step)
            scaled = seg * cross[:, i * length : (i + 1) * length] * step
            mixed = mixed + scaled
            full = scaled * scores
            rowm_ref[h : h + 1, :] = jnp.sum(full, axis=0, keepdims=True)
            own = jnp.where(lane == h, jnp.sum(full, axis=1, keepdims=True), own)
        back = dot(jnp.concatenate(kern, axis=1), dy_h, 1, 0)
        dx_ref[:, out_span] = back * wide
        seen = dy_p.astype(F32) * dot(c_rows, h_ref[span, :], 1, 1)
        reach = reach + dot(to_heads(j, heads, size), halves(seen), 1, 1)
    mixed_ref[...] = mixed
    rows = slice(first * per, (first + many) * per)
    own = own.T[rows]
    own_ref[...] = own
    ex_ref[...] = rowm_ref[rows, :] + jnp.exp(cumt_ref[rows, :]) * reach[rows] - own


def close_kernel(mixed_ref, b_ref, c_ref, carried_ref, db_ref, dc_ref):
    mixed = mixed_ref[...].astype(BF16)
    db_ref[...] = dot(mixed, c_ref[...], 1, 0)
    dc_ref[...] = (dot(mixed, b_ref[...], 0, 0) + carried_ref[...]).astype(BF16)


def db_kernel(xs_ref, own_ref, recv_ref, db_ref, dc_ref, out_ref):
    core, _, _ = core_and_chip()
    half = db_ref.shape[1]
    part = own_ref.shape[0]
    total = db_ref[...]
    for ref, index in ((own_ref, core), (recv_ref, 1 - core)):
        total = total + dot(xs_ref[:, rows_at(index, part, LANES)], ref[...], 1, 0)
    out_ref[:, :half] = total.astype(BF16)
    out_ref[:, half:] = dc_ref[...]


def finish_kernel(parts, *refs):
    (x_ref, b_ref, cumt_ref, stept_ref, cum_ref, step_ref, h_ref, own_ref, recv_ref,
     wb_ref, wc_ref, dbc_ref) = refs[:12]
    dx_refs, ex_refs, st_refs = (refs[12 + i * parts : 12 + (i + 1) * parts] for i in range(3))
    in_ref, decay_ref, grad_ref, r_ref, edge_ref = refs[12 + 3 * parts :]
    core, _, _ = core_and_chip()
    length, width = x_ref.shape
    heads = cumt_ref.shape[0]
    size = width // heads
    half = b_ref.shape[1]
    part = width // 2
    r_ref[rows_at(core, part), :] = own_ref[...]
    r_ref[rows_at(1 - core, part), :] = recv_ref[...]
    cum = cum_ref[...]
    table = halves(jnp.exp(cum[length - 1 : length] - cum) * step_ref[...])
    seen = jnp.zeros((heads, length), F32)
    b_rows = b_ref[...]
    d_b, d_c = dbc_ref[:, :half], dbc_ref[:, half:]
    for j in range(width // LANES):
        span = slice(j * LANES, (j + 1) * LANES)
        local = dx_refs[j * LANES // (width // parts)]
        start = j * LANES % (width // parts)
        r_tile = r_ref[span, :]
        reach = dot(b_rows, r_tile, 1, 1)
        d_in = local[:, start : start + LANES] + dot(table, to_lanes(j, size), 1, 0) * reach
        d_in = d_in + dot(d_b, wb_ref[span, :], 1, 1) + dot(d_c, wc_ref[span, :], 1, 1)
        in_ref[:, span] = d_in.astype(BF16)
        product = x_ref[:, span].astype(F32) * reach
        seen = seen + dot(to_heads(j, heads, size), halves(product), 1, 1)
        edge = r_tile.astype(F32) * h_ref[span, :].astype(F32)
        for i in range(LANES // size):
            h = j * (LANES // size) + i
            edge_ref[h : h + 1, :] = jnp.sum(
                edge[i * size : (i + 1) * size], axis=0, keepdims=True
            )
    cumt = cumt_ref[...]
    total = cumt[:, length - 1 : length]
    to_end = jnp.exp(total - cumt)
    step = stept_ref[...]
    own = jnp.concatenate([r[...] for r in st_refs], axis=0)
    excess = jnp.concatenate([r[...] for r in ex_refs], axis=0)
    grad_ref[...] = own / step + to_end * seen
    edge = jnp.exp(total) * jnp.sum(edge_ref[...], axis=1, keepdims=True)
    decay_ref[...] = (
        dot(excess, triangle(length, lambda a, b: a >= b), 1, 0, HI)
        + dot(to_end * step * seen, triangle(length, lambda a, b: a < b), 1, 0, HI)
        + edge
    )


def term_kernel(n_chip, *refs):
    columns, pieces = refs[:n_chip], refs[n_chip : 2 * n_chip]
    keep_ref, send_ref = refs[2 * n_chip : 2 * n_chip + 2]
    held = refs[-1]
    core, _, _ = core_and_chip()
    total = None
    for a, b in zip(columns, pieces):
        part = dot(a[...], b[...], 1, 0)
        total = part if total is None else total + part
    block = keep_ref.shape[0]
    held[0] = total[:block]
    held[1] = total[block:]
    keep_ref[...] = held[core]
    send_ref[...] = held[1 - core].astype(BF16)


def deal_kernel(keep_ref, recv_ref, own_ref, *refs):
    outs, held = refs[:-1], refs[-1]
    place, n_dp = lax.axis_index("dp"), lax.axis_size("dp")
    total = keep_ref[...] + recv_ref[...].astype(F32)
    share = own_ref.shape[0]
    for i in range(n_dp):
        held[i] = total[i * share : (i + 1) * share]
    own_ref[...] = held[place]
    for s, out in enumerate(outs):
        out[...] = held[ahead(place, s + 1, n_dp)].astype(BF16)


def expert_kernel(flip, slots, a_ref, gate_ref, up_ref, out_ref, rows_ref, gate_acc, up_acc):
    step = pl.program_id(0)
    n_tm = a_ref.shape[0]

    @pl.when(step == 0)
    def _():
        for i in range(n_tm):
            for t in range(rows_ref.shape[1] // LANES):
                rows_ref[i * slots : (i + 1) * slots, t * LANES : (t + 1) * LANES] = a_ref[
                    i, t * slots : (t + 1) * slots, :
                ]
        gate_acc[...] = jnp.zeros_like(gate_acc)
        up_acc[...] = jnp.zeros_like(up_acc)

    depth = gate_ref.shape[0]
    rows = rows_ref[:, rows_at(step, depth, LANES)]
    gate_acc[...] += dot(rows, gate_ref[...], 1, 0)
    up_acc[...] += dot(rows, up_ref[...], 1, 0)

    @pl.when(step == pl.num_programs(0) - 1)
    def _():
        weighted = jax.nn.silu(gate_acc[...]) * up_acc[...]
        out_ref[...] = (weighted.T if flip else weighted).astype(BF16)


def expert(a, w_gate, w_up, slots, flip):
    total = a.shape[0] * slots
    width, hidden = w_gate.shape
    depth = 512
    whole = pl.BlockSpec(a.shape, lambda i: (0, 0, 0))
    block = pl.BlockSpec((depth, hidden), lambda i: (i, 0))
    out = (hidden, total) if flip else (total, hidden)
    return pl.pallas_call(
        lambda *refs: expert_kernel(flip, slots, *refs),
        out_shape=shape(out, BF16),
        grid=(width // depth,),
        in_specs=[whole, block, block],
        out_specs=pl.BlockSpec(out, lambda i: (0, 0)),
        scratch_shapes=[
            pltpu.VMEM((total, width), BF16),
            pltpu.VMEM((total, hidden), F32),
            pltpu.VMEM((total, hidden), F32),
        ],
        cost_estimate=pl.CostEstimate(
            flops=4 * total * width * hidden,
            bytes_accessed=4 * width * hidden,
            transcendentals=0,
        ),
        compiler_params=pltpu.CompilerParams(vmem_limit_bytes=20 * 1024 * 1024),
    )(a, w_gate, w_up)


def down_kernel(n_dp, flip, slots, *refs):
    pieces = refs[:n_dp]
    a_ref, out_ref = refs[n_dp:]
    n_tm = a_ref.shape[0]
    piece = out_ref.shape[1]
    tiles = -(-piece // LANES)
    base = piece * n_dp // LANES * slots
    total = None
    for s in range(n_dp):
        columns = []
        for t in range(tiles):
            row = base + (s * tiles + t) * slots
            columns.append(
                jnp.concatenate([a_ref[i, row : row + slots, :] for i in range(n_tm)], axis=0)
            )
        grads = jnp.concatenate(columns, axis=1)[:, :piece]
        part = dot(pieces[s][...], grads, 1 if flip else 0, 0)
        total = part if total is None else total + part
    out_ref[...] = total.astype(BF16)


def shifted(array, axis, shift, stride=1):
    count = lax.axis_size(axis)
    return lax.ppermute(array, axis, [(i, (i + shift * stride) % count) for i in range(count)])


def swapped(array):
    return lax.ppermute(array, "tm", [(i, i ^ 1) for i in range(lax.axis_size("tm"))])


def chips(arrays):
    return [arrays[0]] + [shifted(a, "tm", s + 1, 2) for s, a in enumerate(arrays[1:])]


def per_device(
    layer_in,
    out_grad,
    w_bc,
    log_decay,
    step,
    saved_states,
    w_gate,
    w_up,
    slot_rows,
    slot_counts,
    slot_gates,
):
    n_dp = lax.axis_size("dp")
    core, chip, n_chip = core_and_chip()
    x = layer_in[0]
    dy = out_grad[0]
    length, width = x.shape
    heads = log_decay.shape[2]
    size = width // heads
    share, columns = w_bc.shape
    half = columns // 2
    ldt = log_decay[0].T
    stept = step[0].T
    h_in = saved_states[0, 0].reshape(width, half)
    capacity = slot_rows.shape[2]
    piece = width // n_dp
    part = width // 2
    many = heads // 2
    flip = w_gate.shape[2] % LANES == 0

    frames = jnp.arange(length)[None, :]
    live = jnp.arange(capacity) < slot_counts[0, 0]
    weights = jnp.where(live, slot_gates[0, 0], jnp.zeros_like(slot_gates[0, 0]))
    scale = jnp.concatenate([jnp.ones_like(weights), weights])
    chosen = jnp.concatenate([slot_rows[0, 0], slot_rows[0, 0]])
    pick = jnp.where(chosen[:, None] == frames, scale[:, None], jnp.zeros_like(scale)[:, None])
    grad_rows = -(-piece // LANES) * capacity
    rows_in, rows_own, *sends = call(
        lambda *refs: first_kernel(half, *refs),
        [shape((width // LANES * capacity, LANES), BF16), shape((grad_rows, LANES), BF16)]
        + [shape((share // 2 + grad_rows, LANES), BF16)] * (n_dp - 1),
        0.5,
        (x, dy, pick, w_bc),
        scratch=[pltpu.VMEM((n_dp, grad_rows, LANES), BF16)],
        fetch=(0, 1, 3),
    )
    mine = [shifted(a, "dp", s + 1) for s, a in enumerate(sends)]
    other = swapped(jnp.stack([m[: share // 2] for m in mine]))

    cumt, cum, steps, dyt, xs, carried, *xt = call(
        prep_kernel,
        [
            shape((heads, length), F32),
            shape((length, LANES), F32),
            shape((length, LANES), F32),
            shape((width, length), BF16),
            shape((length, width), BF16),
            shape((length, half), F32),
        ]
        + [shape((width // n_chip, length), BF16)] * n_chip,
        2.0,
        (x, dy, ldt, stept, h_in),
        after=(rows_own,),
        scratch=[pltpu.VMEM((width, length), BF16)],
        fetch=(0, 1, 2, 3, 4),
    )
    columns_in = chips(xt)
    wc_whole, c_rows, keep, send, wb_half = call(
        lambda *refs: project_kernel(n_dp - 1, *refs),
        [
            shape((width, half), BF16),
            shape((length, half), BF16),
            shape((part + up16(2 * many), half), BF16),
            shape((part + up16(2 * many), half), BF16),
            shape((share // 2, half), BF16),
        ],
        1.0,
        (x, dyt, cumt, w_bc, *mine, other),
    )
    recv = swapped(send)
    mine_b = [shifted(wb_half, "dp", s) for s in range(1, n_dp)]
    other_b = swapped(jnp.stack(mine_b))
    climbs = [
        call(
            lambda *refs: combine_kernel(many, size, *refs),
            [shape((part + up16(2 * many), half), BF16)],
            0.5,
            (keep, recv),
        )[0]
    ]
    arrived = []
    bit = 1
    while bit < n_chip:
        last = bit * 2 == n_chip
        moves = [
            (k, k ^ (2 * bit)) for k in range(2 * n_chip) if not last or k & (2 * bit)
        ]
        arrived.append(lax.ppermute(climbs[-1], "tm", moves))
        if not last:
            climbs.append(
                call(
                    lambda *refs, bit=bit: climb_kernel(many, size, bit, *refs),
                    [shape((part + up16(2 * many), half), BF16)],
                    0.5,
                    (climbs[-1], arrived[-1]),
                )[0]
            )
        bit *= 2

    rows = jnp.concatenate([rows_in, rows_own] + [m[share // 2 :] for m in mine], axis=0)
    rows = lax.all_gather(rows, "tm")
    weighted = expert(rows, w_gate[0], w_up[0], capacity, flip)

    wb_whole, b_rows = call(
        lambda *refs: b_kernel(n_dp - 1, *refs),
        [shape((width, half), BF16), shape((length, half), BF16)],
        0.5,
        (x, w_bc, *mine_b, other_b),
    )
    parts = 2
    tiles = width // LANES // parts
    dxs, exs, owns = [], [], []
    mixed = jnp.zeros((length, length), F32)
    for i in range(parts):
        dx, mixed, ex, own = call(
            lambda *refs, i=i: intra_kernel(i * tiles, tiles, *refs),
            [
                shape((length, width // parts), F32),
                shape((length, length), F32),
                shape((heads // parts, length), F32),
                shape((heads // parts, length), F32),
            ],
            3.0,
            (x, dy, b_rows, c_rows, cumt, cum, steps, h_in, mixed),
            scratch=[pltpu.VMEM((heads, length), F32)],
        )
        dxs.append(dx)
        exs.append(ex)
        owns.append(own)
    db, dc = call(
        close_kernel,
        [shape((length, half), F32), shape((length, half), BF16)],
        0.3,
        (mixed, b_rows, c_rows, carried),
    )

    r_own, r_send = call(
        lambda *refs: carry_kernel(many, size, len(arrived), *refs),
        [shape((part, half), BF16)] * 2,
        0.5,
        (*arrived, keep, recv),
    )
    r_recv = swapped(r_send)
    d_bc = call(db_kernel, [shape((length, columns), BF16)], 0.3, (xs, r_own, r_recv, db, dc))[0]
    d_bcs = chips([d_bc] * n_chip)
    d_in, d_decay, d_step = call(
        lambda *refs: finish_kernel(parts, *refs),
        [
            shape((length, width), BF16),
            shape((heads, length), F32),
            shape((heads, length), F32),
        ],
        3.0,
        (x, b_rows, cumt, stept, cum, steps, h_in, r_own, r_recv, wb_whole, wc_whole, d_bc,
         *dxs, *exs, *owns),
        scratch=[pltpu.VMEM((width, half), BF16), pltpu.VMEM((heads, half), F32)],
    )
    w_rows = width // (2 * n_chip)
    term, term_send = call(
        lambda *refs: term_kernel(n_chip, *refs),
        [shape((w_rows, columns), F32), shape((w_rows, columns), BF16)],
        0.5,
        (*columns_in, *d_bcs),
        scratch=[pltpu.VMEM((2, w_rows, columns), F32)],
    )
    final = call(
        deal_kernel,
        [shape((w_rows // n_dp, columns), F32)]
        + [shape((w_rows // n_dp, columns), BF16)] * (n_dp - 1),
        0.3,
        (term, swapped(term_send)),
        scratch=[pltpu.VMEM((n_dp, w_rows // n_dp, columns), F32)],
    )
    w_bc_grad = final[0]
    for s in range(1, n_dp):
        w_bc_grad = w_bc_grad + shifted(final[s], "dp", s).astype(F32)

    spread = [weighted] + [shifted(weighted, "dp", s) for s in range(1, n_dp)]
    w_down_grad = call(
        lambda *refs: down_kernel(n_dp, flip, capacity, *refs),
        [shape((w_gate.shape[2], piece), BF16)],
        1.0,
        (*spread, rows),
        after=(final[0],),
    )[0]
    return (d_in[None], d_decay.T[None], d_step.T[None], w_bc_grad, w_down_grad[None])


def solution(mesh):
    in_specs = (
        P("dp", "tm", None),
        P("dp", "tm", None),
        P("dp", None),
        P("dp", "tm", None),
        P("dp", "tm", None),
        P("dp", "tm", None, None, None),
        P(None, None, "tm"),
        P(None, None, "tm"),
        P("dp", None, "tm"),
        P("dp", "tm"),
        P("dp", None, "tm"),
    )
    out_specs = (
        P("dp", "tm", None),
        P("dp", "tm", None),
        P("dp", "tm", None),
        P(("tm", "dp"), None),
        P(None, "tm", "dp"),
    )
    return jax.shard_map(
        per_device, mesh=mesh, in_specs=in_specs, out_specs=out_specs, check_vma=False
    )
```

```python
import jax
import jax.numpy as jnp
from jax import lax
from jax.experimental import pallas as pl
from jax.experimental.pallas import tpu as pltpu
from jax.sharding import PartitionSpec as P

HI = lax.Precision.HIGHEST
F32 = jnp.float32
BF16 = jnp.bfloat16
LANES = 128


def dot(a, b, ca, cb, precision=None):
    return lax.dot_general(
        a, b, (((ca,), (cb,)), ((), ())), precision=precision, preferred_element_type=F32
    )


def iota(dims, axis):
    return lax.broadcasted_iota(jnp.int32, dims, axis)


def where_one(mask):
    return jnp.where(mask, 1.0, 0.0)


def triangle(n, keep):
    return where_one(keep(iota((n, n), 0), iota((n, n), 1))).astype(F32)


def halves(values, axis=1):
    high = values.astype(BF16)
    low = (values - high.astype(F32)).astype(BF16)
    return jnp.concatenate([high, low], axis=axis)


def to_lanes(j, size):
    dims = (LANES, LANES)
    one = where_one(iota(dims, 0) == iota(dims, 1) // size + j * (LANES // size)).astype(BF16)
    return jnp.concatenate([one, one], axis=0)


def to_heads(j, heads, size):
    dims = (heads, LANES)
    one = where_one(iota(dims, 0) == iota(dims, 1) // size + j * (LANES // size)).astype(BF16)
    return jnp.concatenate([one, one], axis=1)


def up16(n):
    return -(-n // 16) * 16


def call(kernel, outs, cost, args, after=(), scratch=(), limit=14, fetch=()):
    n_in, n_after, n_out = len(args), len(after), len(outs)
    fetch = tuple(fetch)

    def body(*refs):
        ins = list(refs[:n_in])
        rest = refs[n_in + n_after :]
        if fetch:
            sems = rest[-1]
            held = rest[len(rest) - 1 - len(fetch) : -1]
            rest = rest[: len(rest) - 1 - len(fetch)]
            copies = []
            for i, (index, ref) in enumerate(zip(fetch, held)):
                copies.append(pltpu.make_async_copy(ins[index], ref, sems.at[i]))
                ins[index] = ref
            for copy in copies:
                copy.start()
            for copy in copies:
                copy.wait()
        kernel(*ins, *rest)

    specs = [
        pl.BlockSpec(memory_space=pltpu.HBM if i in fetch else pltpu.VMEM) for i in range(n_in)
    ]
    held = [pltpu.VMEM(args[i].shape, args[i].dtype) for i in fetch]
    if fetch:
        held.append(pltpu.SemaphoreType.DMA((len(fetch),)))
    return pl.pallas_call(
        body,
        out_shape=outs,
        in_specs=specs + [pl.BlockSpec(memory_space=pl.ANY)] * n_after,
        out_specs=[pl.BlockSpec(memory_space=pltpu.VMEM)] * n_out,
        scratch_shapes=list(scratch) + held,
        cost_estimate=pl.CostEstimate(
            flops=int(cost * 1e9), bytes_accessed=1000, transcendentals=0
        ),
        compiler_params=pltpu.CompilerParams(vmem_limit_bytes=limit * 1024 * 1024),
    )(*args, *after)


def shape(dims, kind):
    return jax.ShapeDtypeStruct(dims, kind)


def core_and_chip():
    place = lax.axis_index("tm")
    return lax.rem(place, 2), lax.div(place, 2), lax.axis_size("tm") // 2


def ahead(index, shift, count):
    return lax.rem(index + shift, count)


def rows_at(index, size, align=16):
    return pl.ds(pl.multiple_of(index * size, align), size)


def prep_kernel(
    x_ref, dy_ref, ldt_ref, stept_ref, h_ref,
    cumt_ref, cum_ref, step_ref, dyt_ref, xs_ref, carried_ref, *rest,
):
    outs, xt_ref = rest[:-1], rest[-1]
    length, width = x_ref.shape
    heads = ldt_ref.shape[0]
    size = width // heads
    pad = jnp.zeros((LANES - heads, length), F32)
    cumt = dot(ldt_ref[...], triangle(length, lambda a, b: a <= b), 1, 0, HI)
    cumt_ref[...] = cumt
    cum = jnp.concatenate([cumt, pad], axis=0).T
    step = jnp.concatenate([stept_ref[...], pad], axis=0).T
    cum_ref[...] = cum
    step_ref[...] = step
    start = jnp.exp(cum)
    into_end = jnp.exp(cum[length - 1 : length] - cum) * step
    table = jnp.concatenate([halves(start), halves(into_end)], axis=0)
    carried = jnp.zeros(carried_ref.shape, F32)
    for j in range(width // LANES):
        span = slice(j * LANES, (j + 1) * LANES)
        scale = dot(table, to_lanes(j, size), 1, 0)
        x_f = x_ref[:, span].astype(F32)
        xt_ref[span, :] = x_f.T.astype(BF16)
        xs_ref[:, span] = (x_f * scale[length:]).astype(BF16)
        dys = dy_ref[:, span].astype(F32) * scale[:length]
        dyt_ref[span, :] = dys.T.astype(BF16)
        carried = carried + dot(dys.astype(BF16), h_ref[span, :], 1, 0)
    carried_ref[...] = carried
    _, chip, n_chip = core_and_chip()
    for s, out in enumerate(outs):
        out[...] = xt_ref[rows_at(ahead(chip, s, n_chip), width // n_chip), :]


def pick_kernel(n_dp, x_ref, dy_ref, slot_ref, count_ref, gate_ref, out_ref):
    length, width = x_ref.shape
    slots = slot_ref.shape[1]
    hit = iota((length, slots), 0) == slot_ref[...]
    live = iota((1, slots), 1) < count_ref[...]
    weight = jnp.where(live, gate_ref[...].astype(F32), 0.0)
    rows = dot(where_one(hit).astype(BF16), x_ref[...], 0, 0).astype(BF16)
    base = width // LANES * slots
    for t in range(width // LANES):
        out_ref[t * slots : (t + 1) * slots, :] = rows[:, t * LANES : (t + 1) * LANES]
    grads = dot(jnp.where(hit, weight, 0.0).astype(BF16), dy_ref[...], 0, 0).astype(BF16)
    piece = width // n_dp
    tiles = -(-piece // LANES)
    if piece % LANES:
        out_ref[base:, :] = jnp.zeros((out_ref.shape[0] - base, LANES), BF16)
    for i in range(n_dp):
        for t in range(tiles):
            low, high = i * piece + t * LANES, min((i + 1) * piece, i * piece + (t + 1) * LANES)
            row = base + (i * tiles + t) * slots
            out_ref[row : row + slots, : high - low] = grads[:, low:high]


def stack_kernel(*refs):
    for i, ref in enumerate(refs[:-1]):
        refs[-1][i] = ref[...]


def stacked(arrays, after=()):
    return call(
        stack_kernel,
        [shape((len(arrays), *arrays[0].shape), arrays[0].dtype)],
        0.2,
        tuple(arrays),
        after=after,
    )[0]


def project_kernel(n_mine, *refs):
    x_ref, dyt_ref, cumt_ref, own_ref = refs[:4]
    mine, other = refs[4 : 4 + n_mine], refs[4 + n_mine]
    w_ref, bc_ref, keep_ref, send_ref = refs[5 + n_mine :]
    core, _, _ = core_and_chip()
    place, n_dp = lax.axis_index("dp"), lax.axis_size("dp")
    share = own_ref.shape[0]
    half = share // 2
    w_ref[rows_at(place, share), :] = own_ref[...]
    for i in range(n_mine):
        source = ahead(place, n_dp - 1 - i, n_dp)
        w_ref[rows_at(source * 2 + core, half), :] = mine[i][...]
        w_ref[rows_at(source * 2 + 1 - core, half), :] = other[i]
    bc = dot(x_ref[...], w_ref[...], 1, 0).astype(BF16)
    bc_ref[...] = bc
    c_rows = bc[:, LANES:]
    heads, length = cumt_ref.shape
    width = dyt_ref.shape[0]
    part, many = width // 2, heads // 2
    decay = jnp.broadcast_to(jnp.exp(cumt_ref[:, length - 1 : length]), (heads, LANES))
    for ref, index in ((keep_ref, core), (send_ref, 1 - core)):
        ref[:part, :] = dot(dyt_ref[rows_at(index, part), :], c_rows, 1, 0).astype(BF16)
        mine_decay = jnp.where(index == 0, decay[:many], decay[many:])
        high = mine_decay.astype(BF16).astype(F32)
        fill = jnp.zeros((ref.shape[0] - part - 2 * many, LANES), F32)
        extra = jnp.concatenate([high, mine_decay - high, fill], axis=0)
        ref[part:, :] = extra.astype(BF16)


def pair(keep_ref, recv_ref, many, size, head):
    core, _, _ = core_and_chip()
    part = many * size
    both = []
    for ref in (keep_ref, recv_ref):
        extra = ref[part:, :].astype(F32)
        decay = extra[head : head + 1] + extra[many + head : many + head + 1]
        both.append((ref[head * size : (head + 1) * size, :].astype(F32), decay))
    first = jax.tree.map(lambda a, b: jnp.where(core == 0, a, b), both[0], both[1])
    second = jax.tree.map(lambda a, b: jnp.where(core == 0, b, a), both[0], both[1])
    return first, second


def payload(ref, many, states, decays):
    size = states[0].shape[0]
    for head, state in enumerate(states):
        ref[head * size : (head + 1) * size, :] = state.astype(BF16)
    decay = jnp.concatenate(decays, axis=0)
    high = decay.astype(BF16).astype(F32)
    fill = jnp.zeros((ref.shape[0] - many * size - 2 * many, LANES), F32)
    extra = jnp.concatenate([high, decay - high, fill], axis=0)
    ref[many * size :, :] = extra.astype(BF16)


def loaded(ref, many, size, head):
    extra = ref[many * size :, :].astype(F32)
    decay = extra[head : head + 1] + extra[many + head : many + head + 1]
    return ref[head * size : (head + 1) * size, :].astype(F32), decay


def combine_kernel(many, size, keep_ref, recv_ref, out_ref):
    states, decays = [], []
    for head in range(many):
        (g0, a0), (g1, a1) = pair(keep_ref, recv_ref, many, size, head)
        states.append(g0 + a0 * g1)
        decays.append(a0 * a1)
    payload(out_ref, many, states, decays)


def pick_side(upper, mine, theirs):
    return jnp.where(upper, theirs, mine), jnp.where(upper, mine, theirs)


def climb_kernel(many, size, bit, mine_ref, recv_ref, out_ref):
    _, chip, _ = core_and_chip()
    upper = lax.rem(lax.div(chip, bit), 2) == 1
    states, decays = [], []
    for head in range(many):
        t_mine, a_mine = loaded(mine_ref, many, size, head)
        t_recv, a_recv = loaded(recv_ref, many, size, head)
        t_low, t_high = pick_side(upper, t_mine, t_recv)
        a_low, a_high = pick_side(upper, a_mine, a_recv)
        states.append(t_low + a_low * t_high)
        decays.append(a_low * a_high)
    payload(out_ref, many, states, decays)


def carry_kernel(many, size, levels, *refs):
    core, chip, _ = core_and_chip()
    recvs = refs[:levels]
    keep_ref, recv_ref, own_ref, send_ref = refs[levels:]
    for head in range(many):
        span = slice(head * size, (head + 1) * size)
        carry, reach = None, None
        for level, ref in enumerate(recvs):
            state, decay = loaded(ref, many, size, head)
            lower = lax.rem(lax.div(chip, 2**level), 2) == 0
            state = jnp.where(lower, state, 0.0)
            decay = jnp.where(lower, decay, 1.0)
            carry = state if carry is None else carry + reach * state
            reach = decay if reach is None else reach * decay
        _, (g1, a1) = pair(keep_ref, recv_ref, many, size, head)
        second = carry
        first = g1 + a1 * second
        own_ref[span, :] = jnp.where(core == 0, first, second).astype(BF16)
        send_ref[span, :] = jnp.where(core == 0, second, first).astype(BF16)


def intra_kernel(
    first, many, x_ref, dy_ref, bc_ref, cumt_ref, cum_ref, step_ref, h_ref, before_ref,
    dx_ref, mixed_ref, ex_ref, own_ref, rowm_ref,
):
    length, width = x_ref.shape
    heads = cumt_ref.shape[0]
    size = width // heads
    per = LANES // size
    upper = iota((length, length), 0) <= iota((length, length), 1)
    b_rows, c_rows = bc_ref[:, :LANES], bc_ref[:, LANES:]
    scores = dot(b_rows, c_rows, 1, 1)
    lane = iota((1, LANES), 1)
    lane_bf = [where_one(lane // size == i).astype(BF16) for i in range(per)]
    mixed = before_ref[...]
    own = jnp.zeros((length, LANES), F32)
    reach = jnp.zeros((heads, length), F32)
    for j in range(first, first + many):
        span = slice(j * LANES, (j + 1) * LANES)
        out_span = slice((j - first) * LANES, (j - first + 1) * LANES)
        x_p = x_ref[:, span]
        dy_p = dy_ref[:, span]
        dy_h = jnp.concatenate([dy_p * m for m in lane_bf], axis=0)
        cross = dot(x_p, dy_h, 1, 1)
        kern = []
        wide = None
        for i in range(per):
            h = j * per + i
            diff = cumt_ref[h : h + 1, :] - cum_ref[:, h : h + 1]
            seg = jnp.exp(jnp.where(upper, diff, -1e30))
            kern.append((seg * scores).astype(BF16))
            step = jnp.broadcast_to(step_ref[:, h : h + 1], (length, LANES))
            wide = step if i == 0 else jnp.where(lane < i * size, wide, step)
            scaled = seg * cross[:, i * length : (i + 1) * length] * step
            mixed = mixed + scaled
            full = scaled * scores
            rowm_ref[h : h + 1, :] = jnp.sum(full, axis=0, keepdims=True)
            own = jnp.where(lane == h, jnp.sum(full, axis=1, keepdims=True), own)
        back = dot(jnp.concatenate(kern, axis=1), dy_h, 1, 0)
        dx_ref[:, out_span] = back * wide
        seen = dy_p.astype(F32) * dot(c_rows, h_ref[span, :], 1, 1)
        reach = reach + dot(to_heads(j, heads, size), halves(seen), 1, 1)
    mixed_ref[...] = mixed
    rows = slice(first * per, (first + many) * per)
    own = own.T[rows]
    own_ref[...] = own
    ex_ref[...] = rowm_ref[rows, :] + jnp.exp(cumt_ref[rows, :]) * reach[rows] - own


def close_kernel(mixed_ref, bc_ref, carried_ref, db_ref, dc_ref):
    mixed = mixed_ref[...].astype(BF16)
    db_ref[...] = dot(mixed, bc_ref[:, LANES:], 1, 0)
    dc_ref[...] = (dot(mixed, bc_ref[:, :LANES], 0, 0) + carried_ref[...]).astype(BF16)


def db_kernel(xs_ref, own_ref, recv_ref, db_ref, dc_ref, out_ref):
    core, _, _ = core_and_chip()
    half = db_ref.shape[1]
    part = own_ref.shape[0]
    total = db_ref[...]
    for ref, index in ((own_ref, core), (recv_ref, 1 - core)):
        total = total + dot(xs_ref[:, rows_at(index, part, LANES)], ref[...], 1, 0)
    out_ref[:, :half] = total.astype(BF16)
    out_ref[:, half:] = dc_ref[...]


def finish_kernel(parts, *refs):
    (x_ref, bc_ref, cumt_ref, stept_ref, cum_ref, step_ref, h_ref, own_ref, recv_ref,
     w_ref, dbc_ref) = refs[:11]
    dx_refs, ex_refs, st_refs = (refs[11 + i * parts : 11 + (i + 1) * parts] for i in range(3))
    in_ref, decay_ref, grad_ref, r_ref, edge_ref = refs[11 + 3 * parts :]
    core, _, _ = core_and_chip()
    length, width = x_ref.shape
    heads = cumt_ref.shape[0]
    size = width // heads
    part = width // 2
    r_ref[rows_at(core, part), :] = own_ref[...]
    r_ref[rows_at(1 - core, part), :] = recv_ref[...]
    cum = cum_ref[...]
    table = halves(jnp.exp(cum[length - 1 : length] - cum) * step_ref[...])
    seen = jnp.zeros((heads, length), F32)
    b_rows = bc_ref[:, :LANES]
    d_bc = dbc_ref[...]
    for j in range(width // LANES):
        span = slice(j * LANES, (j + 1) * LANES)
        local = dx_refs[j * LANES // (width // parts)]
        start = j * LANES % (width // parts)
        r_tile = r_ref[span, :]
        reach = dot(b_rows, r_tile, 1, 1)
        d_in = local[:, start : start + LANES] + dot(table, to_lanes(j, size), 1, 0) * reach
        d_in = d_in + dot(d_bc, w_ref[span, :], 1, 1)
        in_ref[:, span] = d_in.astype(BF16)
        product = x_ref[:, span].astype(F32) * reach
        seen = seen + dot(to_heads(j, heads, size), halves(product), 1, 1)
        edge = r_tile.astype(F32) * h_ref[span, :].astype(F32)
        for i in range(LANES // size):
            h = j * (LANES // size) + i
            edge_ref[h : h + 1, :] = jnp.sum(
                edge[i * size : (i + 1) * size], axis=0, keepdims=True
            )
    cumt = cumt_ref[...]
    total = cumt[:, length - 1 : length]
    to_end = jnp.exp(total - cumt)
    step = stept_ref[...]
    own = jnp.concatenate([r[...] for r in st_refs], axis=0)
    excess = jnp.concatenate([r[...] for r in ex_refs], axis=0)
    grad_ref[...] = own / step + to_end * seen
    edge = jnp.exp(total) * jnp.sum(edge_ref[...], axis=1, keepdims=True)
    decay_ref[...] = (
        dot(excess, triangle(length, lambda a, b: a >= b), 1, 0, HI)
        + dot(to_end * step * seen, triangle(length, lambda a, b: a < b), 1, 0, HI)
        + edge
    )


def term_kernel(n_chip, *refs):
    columns, pieces = refs[:n_chip], refs[n_chip : 2 * n_chip]
    keep_ref, send_ref = refs[2 * n_chip : 2 * n_chip + 2]
    held = refs[-1]
    core, _, _ = core_and_chip()
    total = None
    for a, b in zip(columns, pieces):
        part = dot(a[...], b[...], 1, 0)
        total = part if total is None else total + part
    block = keep_ref.shape[0]
    held[0] = total[:block]
    held[1] = total[block:]
    keep_ref[...] = held[core]
    send_ref[...] = held[1 - core].astype(BF16)


def deal_kernel(keep_ref, recv_ref, own_ref, *refs):
    outs, held = refs[:-1], refs[-1]
    place, n_dp = lax.axis_index("dp"), lax.axis_size("dp")
    total = keep_ref[...] + recv_ref[...].astype(F32)
    share = own_ref.shape[0]
    for i in range(n_dp):
        held[i] = total[i * share : (i + 1) * share]
    own_ref[...] = held[place]
    for s, out in enumerate(outs):
        out[...] = held[ahead(place, s + 1, n_dp)].astype(BF16)


def expert_kernel(flip, merge, slots, grad_rows, a_ref, b_ref, gate_ref, up_ref, *refs):
    outs, (rows_ref, gate_acc, up_acc) = refs[:-3], refs[-3:]
    step = pl.program_id(0)
    n_chip = a_ref.shape[0]
    width = rows_ref.shape[1]

    @pl.when(step == 0)
    def _():
        for half, ref in enumerate((a_ref, b_ref)):
            for i in range(n_chip):
                row = (half * n_chip + i) * slots
                for t in range(width // LANES):
                    rows_ref[row : row + slots, t * LANES : (t + 1) * LANES] = ref[
                        i, t * slots : (t + 1) * slots, :
                    ]
        gate_acc[...] = jnp.zeros_like(gate_acc)
        up_acc[...] = jnp.zeros_like(up_acc)

    depth = gate_ref.shape[0]
    rows = rows_ref[:, rows_at(step, depth, LANES)]
    gate_acc[...] += dot(rows, gate_ref[...], 1, 0)
    up_acc[...] += dot(rows, up_ref[...], 1, 0)

    @pl.when(step == pl.num_programs(0) - 1)
    def _():
        weighted = jax.nn.silu(gate_acc[...]) * up_acc[...]
        weighted = (weighted.T if flip else weighted).astype(BF16)
        place, n_dp = lax.axis_index("dp"), lax.axis_size("dp")
        base = width // LANES * slots
        hidden = gate_acc.shape[1]
        for s in range(n_dp):
            rows = [
                a_ref[i, pl.ds(pl.multiple_of(base + ahead(place, s, n_dp) * grad_rows, 16), grad_rows), :]
                for i in range(n_chip)
            ]
            grads = outs[s] if merge else outs[n_dp + s]
            for i in range(n_chip):
                row = (hidden if merge else 0) + i * grad_rows
                grads[row : row + grad_rows, :] = rows[i]
            if merge:
                outs[s][:hidden, :] = weighted
            elif s == 0:
                for out in outs[:n_dp]:
                    out[...] = weighted


def expert(a, b, w_gate, w_up, slots, grad_rows, n_dp, flip, merge):
    n_chip = a.shape[0]
    total = 2 * n_chip * slots
    width, hidden = w_gate.shape
    depth = 512
    whole = pl.BlockSpec(a.shape, lambda i: (0, 0, 0))
    block = pl.BlockSpec((depth, hidden), lambda i: (i, 0))
    grads = n_chip * grad_rows
    if merge:
        outs = [(hidden + grads, LANES)] * n_dp
    else:
        outs = [(hidden, total) if flip else (total, hidden)] * n_dp + [(grads, LANES)] * n_dp
    return pl.pallas_call(
        lambda *refs: expert_kernel(flip, merge, slots, grad_rows, *refs),
        out_shape=[shape(o, BF16) for o in outs],
        grid=(width // depth,),
        in_specs=[whole, whole, block, block],
        out_specs=[pl.BlockSpec(o, lambda i: (0, 0)) for o in outs],
        scratch_shapes=[
            pltpu.VMEM((total, width), BF16),
            pltpu.VMEM((total, hidden), F32),
            pltpu.VMEM((total, hidden), F32),
        ],
        cost_estimate=pl.CostEstimate(
            flops=4 * total * width * hidden,
            bytes_accessed=4 * width * hidden,
            transcendentals=0,
        ),
        compiler_params=pltpu.CompilerParams(vmem_limit_bytes=50 * 1024 * 1024),
    )(a, b, w_gate, w_up)


def down_kernel(n_dp, flip, merge, slots, grad_rows, *refs):
    weighted = refs[:n_dp]
    near = weighted if merge else refs[n_dp : 2 * n_dp]
    b_ref, far_ref, out_ref = refs[-3:]
    hidden, piece = out_ref.shape
    n_chip = b_ref.shape[0]
    tiles = grad_rows // slots
    place = lax.axis_index("dp")
    total = None
    for s in range(n_dp):
        base = hidden if merge else 0
        blocks = [
            near[s][base + i * grad_rows : base + (i + 1) * grad_rows, :] for i in range(n_chip)
        ]
        if s == 0:
            row = b_ref.shape[1] - n_dp * grad_rows + place * grad_rows
            rows = pl.ds(pl.multiple_of(row, 16), grad_rows)
            blocks += [b_ref[i, rows, :] for i in range(n_chip)]
        else:
            blocks += [far_ref[s - 1, i * grad_rows : (i + 1) * grad_rows, :] for i in range(n_chip)]
        columns = [
            jnp.concatenate([b[t * slots : (t + 1) * slots] for b in blocks], axis=0)
            for t in range(tiles)
        ]
        grads = jnp.concatenate(columns, axis=1)[:, :piece]
        part = dot(weighted[s][:hidden, :] if merge else weighted[s][...], grads, 1 if flip else 0, 0)
        total = part if total is None else total + part
    out_ref[...] = total.astype(BF16)


def shifted(array, axis, shift, stride=1):
    count = lax.axis_size(axis)
    return lax.ppermute(array, axis, [(i, (i + shift * stride) % count) for i in range(count)])


def swapped(array):
    return lax.ppermute(array, "tm", [(i, i ^ 1) for i in range(lax.axis_size("tm"))])


def chips(arrays):
    return [arrays[0]] + [shifted(a, "tm", s + 1, 2) for s, a in enumerate(arrays[1:])]


def per_device(
    layer_in,
    out_grad,
    w_bc,
    log_decay,
    step,
    saved_states,
    w_gate,
    w_up,
    slot_rows,
    slot_counts,
    slot_gates,
):
    n_dp = lax.axis_size("dp")
    core, chip, n_chip = core_and_chip()
    x = layer_in[0]
    dy = out_grad[0]
    length, width = x.shape
    heads = log_decay.shape[2]
    size = width // heads
    share, columns = w_bc.shape
    half = columns // 2
    ldt = log_decay[0].T
    stept = step[0].T
    h_in = saved_states[0, 0].reshape(width, half)
    capacity = slot_rows.shape[2]
    piece = width // n_dp
    part = width // 2
    many = heads // 2
    flip = w_gate.shape[2] % LANES == 0
    merge = flip and 2 * n_chip * capacity == LANES

    grad_rows = -(-piece // LANES) * capacity
    w_half = lax.dynamic_slice_in_dim(w_bc, core * (share // 2), share // 2, 0)
    mine = [shifted(w_half, "dp", s) for s in range(1, n_dp)]

    rows = call(
        lambda *refs: pick_kernel(n_dp, *refs),
        [shape((width // LANES * capacity + n_dp * grad_rows, LANES), BF16)],
        0.5,
        (x, dy, slot_rows[0], slot_counts, slot_gates[0]),
        fetch=(0, 1),
        limit=60,
    )[0]
    rows_a = jnp.stack(chips([rows] * n_chip))
    rows_b = swapped(rows_a)

    cumt, cum, steps, dyt, xs, carried, *xt = call(
        prep_kernel,
        [
            shape((heads, length), F32),
            shape((length, LANES), F32),
            shape((length, LANES), F32),
            shape((width, length), BF16),
            shape((length, width), BF16),
            shape((length, half), F32),
        ]
        + [shape((width // n_chip, length), BF16)] * n_chip,
        2.0,
        (x, dy, ldt, stept, h_in),
        after=(rows,),
        scratch=[pltpu.VMEM((width, length), BF16)],
        fetch=(0, 1, 2, 3, 4),
        limit=60,
    )
    columns_in = chips(xt)
    other = swapped(stacked(mine, after=(cumt,)))
    w_whole, bc, keep, send = call(
        lambda *refs: project_kernel(n_dp - 1, *refs),
        [
            shape((width, columns), BF16),
            shape((length, columns), BF16),
            shape((part + up16(2 * many), half), BF16),
            shape((part + up16(2 * many), half), BF16),
        ],
        1.0,
        (x, dyt, cumt, w_bc, *mine, other),
    )
    recv = swapped(send)
    climbs = [
        call(
            lambda *refs: combine_kernel(many, size, *refs),
            [shape((part + up16(2 * many), half), BF16)],
            0.5,
            (keep, recv),
            after=tuple(columns_in[1:]),
        )[0]
    ]
    arrived = []
    bit = 1
    while bit < n_chip:
        last = bit * 2 == n_chip
        moves = [
            (k, k ^ (2 * bit)) for k in range(2 * n_chip) if not last or k & (2 * bit)
        ]
        arrived.append(lax.ppermute(climbs[-1], "tm", moves))
        if not last:
            climbs.append(
                call(
                    lambda *refs, bit=bit: climb_kernel(many, size, bit, *refs),
                    [shape((part + up16(2 * many), half), BF16)],
                    0.5,
                    (climbs[-1], arrived[-1]),
                )[0]
            )
        bit *= 2

    outs = expert(rows_a, rows_b, w_gate[0], w_up[0], capacity, grad_rows, n_dp, flip, merge)
    outs = list(outs)
    spread = outs[:1] + [shifted(o, "dp", s + 1) for s, o in enumerate(outs[1:n_dp])]
    near = outs[n_dp : n_dp + 1]
    near += [shifted(o, "dp", s + 1) for s, o in enumerate(outs[n_dp + 1 :])]
    moved = [o[w_gate.shape[2] :] for o in spread[1:]] if merge else near[1:]
    far = swapped(jnp.stack(moved))

    parts = 2
    tiles = width // LANES // parts
    dxs, exs, owns = [], [], []
    mixed = jnp.zeros((length, length), F32)
    for i in range(parts):
        dx, mixed, ex, own = call(
            lambda *refs, i=i: intra_kernel(i * tiles, tiles, *refs),
            [
                shape((length, width // parts), F32),
                shape((length, length), F32),
                shape((heads // parts, length), F32),
                shape((heads // parts, length), F32),
            ],
            3.0,
            (x, dy, bc, cumt, cum, steps, h_in, mixed),
            scratch=[pltpu.VMEM((heads, length), F32)],
        )
        dxs.append(dx)
        exs.append(ex)
        owns.append(own)
    db, dc = call(
        close_kernel,
        [shape((length, half), F32), shape((length, half), BF16)],
        0.3,
        (mixed, bc, carried),
    )

    r_own, r_send = call(
        lambda *refs: carry_kernel(many, size, len(arrived), *refs),
        [shape((part, half), BF16)] * 2,
        0.5,
        (*arrived, keep, recv),
    )
    r_recv = swapped(r_send)
    d_bc = call(db_kernel, [shape((length, columns), BF16)], 0.3, (xs, r_own, r_recv, db, dc))[0]
    d_bcs = chips([d_bc] * n_chip)
    d_in, d_decay, d_step = call(
        lambda *refs: finish_kernel(parts, *refs),
        [
            shape((length, width), BF16),
            shape((heads, length), F32),
            shape((heads, length), F32),
        ],
        3.0,
        (x, bc, cumt, stept, cum, steps, h_in, r_own, r_recv, w_whole, d_bc,
         *dxs, *exs, *owns),
        scratch=[pltpu.VMEM((width, half), BF16), pltpu.VMEM((heads, half), F32)],
    )
    w_rows = width // (2 * n_chip)
    term, term_send = call(
        lambda *refs: term_kernel(n_chip, *refs),
        [shape((w_rows, columns), F32), shape((w_rows, columns), BF16)],
        0.5,
        (*columns_in, *d_bcs),
        scratch=[pltpu.VMEM((2, w_rows, columns), F32)],
    )
    final = call(
        deal_kernel,
        [shape((w_rows // n_dp, columns), F32)]
        + [shape((w_rows // n_dp, columns), BF16)] * (n_dp - 1),
        0.3,
        (term, swapped(term_send)),
        scratch=[pltpu.VMEM((n_dp, w_rows // n_dp, columns), F32)],
    )
    w_bc_grad = final[0]
    for s in range(1, n_dp):
        w_bc_grad = w_bc_grad + shifted(final[s], "dp", s).astype(F32)

    w_down_grad = call(
        lambda *refs: down_kernel(n_dp, flip, merge, capacity, grad_rows, *refs),
        [shape((w_gate.shape[2], piece), BF16)],
        1.0,
        (*spread, *near, rows_b, far),
        after=(final[0],),
    )[0]
    return (d_in[None], d_decay.T[None], d_step.T[None], w_bc_grad, w_down_grad[None])


def solution(mesh):
    in_specs = (
        P("dp", "tm", None),
        P("dp", "tm", None),
        P("dp", None),
        P("dp", "tm", None),
        P("dp", "tm", None),
        P("dp", "tm", None, None, None),
        P(None, None, "tm"),
        P(None, None, "tm"),
        P("dp", None, "tm"),
        P("dp", "tm"),
        P("dp", None, "tm"),
    )
    out_specs = (
        P("dp", "tm", None),
        P("dp", "tm", None),
        P("dp", "tm", None),
        P(("tm", "dp"), None),
        P(None, "tm", "dp"),
    )
    return jax.shard_map(
        per_device, mesh=mesh, in_specs=in_specs, out_specs=out_specs, check_vma=False
    )
```

```python
import jax
import jax.numpy as jnp
from jax import lax
from jax.experimental import pallas as pl
from jax.experimental.pallas import tpu as pltpu
from jax.sharding import PartitionSpec as P

HI = lax.Precision.HIGHEST
F32 = jnp.float32
BF16 = jnp.bfloat16
LANES = 128


def dot(a, b, ca, cb, precision=None):
    return lax.dot_general(
        a, b, (((ca,), (cb,)), ((), ())), precision=precision, preferred_element_type=F32
    )


def iota(dims, axis):
    return lax.broadcasted_iota(jnp.int32, dims, axis)


def where_one(mask):
    return jnp.where(mask, 1.0, 0.0)


def triangle(n, keep):
    return where_one(keep(iota((n, n), 0), iota((n, n), 1))).astype(F32)


def halves(values, axis=1):
    high = values.astype(BF16)
    low = (values - high.astype(F32)).astype(BF16)
    return jnp.concatenate([high, low], axis=axis)


def to_lanes(j, size):
    dims = (LANES, LANES)
    one = where_one(iota(dims, 0) == iota(dims, 1) // size + j * (LANES // size)).astype(BF16)
    return jnp.concatenate([one, one], axis=0)


def to_heads(j, heads, size):
    dims = (heads, LANES)
    one = where_one(iota(dims, 0) == iota(dims, 1) // size + j * (LANES // size)).astype(BF16)
    return jnp.concatenate([one, one], axis=1)


def up16(n):
    return -(-n // 16) * 16


def call(kernel, outs, cost, args, after=(), scratch=(), limit=14, fetch=()):
    n_in, n_after, n_out = len(args), len(after), len(outs)
    fetch = tuple(fetch)

    def body(*refs):
        ins = list(refs[:n_in])
        rest = refs[n_in + n_after :]
        if fetch:
            sems = rest[-1]
            held = rest[len(rest) - 1 - len(fetch) : -1]
            rest = rest[: len(rest) - 1 - len(fetch)]
            copies = []
            for i, (index, ref) in enumerate(zip(fetch, held)):
                copies.append(pltpu.make_async_copy(ins[index], ref, sems.at[i]))
                ins[index] = ref
            for copy in copies:
                copy.start()
            for copy in copies:
                copy.wait()
        kernel(*ins, *rest)

    specs = [
        pl.BlockSpec(memory_space=pltpu.HBM if i in fetch else pltpu.VMEM) for i in range(n_in)
    ]
    held = [pltpu.VMEM(args[i].shape, args[i].dtype) for i in fetch]
    if fetch:
        held.append(pltpu.SemaphoreType.DMA((len(fetch),)))
    return pl.pallas_call(
        body,
        out_shape=outs,
        in_specs=specs + [pl.BlockSpec(memory_space=pl.ANY)] * n_after,
        out_specs=[pl.BlockSpec(memory_space=pltpu.VMEM)] * n_out,
        scratch_shapes=list(scratch) + held,
        cost_estimate=pl.CostEstimate(
            flops=int(cost * 1e5), bytes_accessed=1000, transcendentals=0
        ),
        compiler_params=pltpu.CompilerParams(vmem_limit_bytes=limit * 1024 * 1024),
    )(*args, *after)


def shape(dims, kind):
    return jax.ShapeDtypeStruct(dims, kind)


def core_and_chip():
    place = lax.axis_index("tm")
    return lax.rem(place, 2), lax.div(place, 2), lax.axis_size("tm") // 2


def rows_at(index, size, align=16):
    return pl.ds(pl.multiple_of(index * size, align), size)


def picked(n_dp, x_ref, dy_ref, slot_ref, count_ref, gate_ref, out_refs):
    length, width = x_ref.shape
    slots = slot_ref.shape[1]
    hit = iota((length, slots), 0) == slot_ref[...]
    live = iota((1, slots), 1) < count_ref[...]
    weight = jnp.where(live, gate_ref[...].astype(F32), 0.0)
    rows = dot(where_one(hit).astype(BF16), x_ref[...], 0, 0).astype(BF16)
    grads = dot(jnp.where(hit, weight, 0.0).astype(BF16), dy_ref[...], 0, 0).astype(BF16)
    blocks = [rows[:, t * LANES : (t + 1) * LANES] for t in range(width // LANES)]
    piece = width // n_dp
    for i in range(n_dp):
        for low in range(i * piece, (i + 1) * piece, LANES):
            block = grads[:, low : min(low + LANES, (i + 1) * piece)]
            if block.shape[1] < LANES:
                fill = jnp.zeros((slots, LANES - block.shape[1]), BF16)
                block = jnp.concatenate([block, fill], axis=1)
            blocks.append(block)
    for i, block in enumerate(blocks):
        for out in out_refs:
            out[i * slots : (i + 1) * slots, :] = block


def high_low(values):
    high = values.astype(BF16).astype(F32)
    return [high, values - high]


def prep_kernel(
    n_dp, x_ref, dy_ref, ldt_ref, stept_ref, h_ref, slot_ref, count_ref, gate_ref,
    cumt_ref, cum_ref, step_ref, dyt_ref, xs_ref, carried_ref, *rest,
):
    outs, xt_ref = rest[:-1], rest[-1]
    length, width = x_ref.shape
    heads = ldt_ref.shape[0]
    size = width // heads
    _, chip, n_chip = core_and_chip()
    picked(n_dp, x_ref, dy_ref, slot_ref, count_ref, gate_ref, outs)
    pad = jnp.zeros((LANES - heads, length), F32)
    cumt = dot(ldt_ref[...], triangle(length, lambda a, b: a <= b), 1, 0, HI)
    cumt_ref[...] = cumt
    cum = jnp.concatenate([cumt, pad], axis=0).T
    step = jnp.concatenate([stept_ref[...], pad], axis=0).T
    cum_ref[...] = cum
    step_ref[...] = step
    start = jnp.exp(cum)
    into_end = jnp.exp(cum[length - 1 : length] - cum) * step
    table = jnp.concatenate([halves(start), halves(into_end)], axis=0)
    carried = jnp.zeros(carried_ref.shape, F32)
    for j in range(width // LANES):
        span = slice(j * LANES, (j + 1) * LANES)
        scale = dot(table, to_lanes(j, size), 1, 0)
        x_f = x_ref[:, span].astype(F32)
        xt_ref[span, :] = x_f.T.astype(BF16)
        xs_ref[:, span] = (x_f * scale[length:]).astype(BF16)
        dys = dy_ref[:, span].astype(F32) * scale[:length]
        dyt_ref[span, :] = dys.T.astype(BF16)
        carried = carried + dot(dys.astype(BF16), h_ref[span, :], 1, 0)
    carried_ref[...] = carried
    decay = jnp.broadcast_to(jnp.exp(cumt[:, length - 1 : length]), (heads, LANES))
    dyt_ref[width : width + 2 * heads, :] = jnp.concatenate(high_low(decay), axis=0).astype(BF16)
    block = width // n_chip
    for s, out in enumerate(outs):
        out[out.shape[0] - block :, :] = xt_ref[rows_at(chip ^ s, block), :]


def stack_kernel(starts, *refs):
    rows = refs[-1].shape[1]
    for i, start in enumerate(starts):
        refs[-1][i] = refs[i][start : start + rows, :]


def stacked(arrays, after=(), rows=None, starts=None):
    rows = rows or arrays[0].shape[0]
    starts = starts or [0] * len(arrays)
    return call(
        lambda *refs: stack_kernel(starts, *refs),
        [shape((len(arrays), rows, arrays[0].shape[1]), arrays[0].dtype)],
        0.2,
        tuple(arrays),
        after=after,
    )[0]


def join_kernel(*refs):
    start = 0
    for ref in refs[:-1]:
        refs[-1][start : start + ref.shape[0]] = ref[...]
        start += ref.shape[0]


def joined(arrays):
    dims = (sum(a.shape[0] for a in arrays), *arrays[0].shape[1:])
    return call(join_kernel, [shape(dims, arrays[0].dtype)], 0.2, tuple(arrays))[0]


def project_kernel(n_mine, many, *refs):
    x_ref, dyt_ref, own_ref = refs[:3]
    mine, other = refs[3 : 3 + n_mine], refs[3 + n_mine]
    w_ref, bc_ref, keep_ref, send_ref = refs[4 + n_mine :]
    core, _, _ = core_and_chip()
    place, n_dp = lax.axis_index("dp"), lax.axis_size("dp")
    share = own_ref.shape[0]
    half = share // 2
    w_ref[rows_at(place, share), :] = own_ref[...]
    for i in range(n_mine):
        source = place ^ (i + 1)
        w_ref[rows_at(source * 2 + core, half), :] = mine[i][...]
        w_ref[rows_at(source * 2 + 1 - core, half), :] = other[i]
    bc = dot(x_ref[...], w_ref[...], 1, 0).astype(BF16)
    bc_ref[...] = bc
    c_rows = bc[:, LANES:]
    width = x_ref.shape[1]
    part = width // 2
    for ref, index in ((keep_ref, core), (send_ref, 1 - core)):
        ref[:part, :] = dot(dyt_ref[rows_at(index, part), :], c_rows, 1, 0).astype(BF16)
        table = dyt_ref[width : width + 4 * many, :].astype(F32)
        quarter = [table[i * many : (i + 1) * many] for i in range(4)]
        high = jnp.where(index == 0, quarter[0], quarter[1])
        low = jnp.where(index == 0, quarter[2], quarter[3])
        fill = jnp.zeros((ref.shape[0] - part - 2 * many, LANES), F32)
        ref[part:, :] = jnp.concatenate([high, low, fill], axis=0).astype(BF16)


def pair(keep_ref, recv_ref, many, size, head):
    core, _, _ = core_and_chip()
    part = many * size
    both = []
    for ref in (keep_ref, recv_ref):
        extra = ref[part:, :].astype(F32)
        decay = extra[head : head + 1] + extra[many + head : many + head + 1]
        both.append((ref[head * size : (head + 1) * size, :].astype(F32), decay))
    first = jax.tree.map(lambda a, b: jnp.where(core == 0, a, b), both[0], both[1])
    second = jax.tree.map(lambda a, b: jnp.where(core == 0, b, a), both[0], both[1])
    return first, second


def payload(ref, many, states, decays):
    size = states[0].shape[0]
    for head, state in enumerate(states):
        ref[head * size : (head + 1) * size, :] = state.astype(BF16)
    decay = jnp.concatenate(decays, axis=0)
    high = decay.astype(BF16).astype(F32)
    fill = jnp.zeros((ref.shape[0] - many * size - 2 * many, LANES), F32)
    extra = jnp.concatenate([high, decay - high, fill], axis=0)
    ref[many * size :, :] = extra.astype(BF16)


def loaded(ref, many, size, head):
    extra = ref[many * size :, :].astype(F32)
    decay = extra[head : head + 1] + extra[many + head : many + head + 1]
    return ref[head * size : (head + 1) * size, :].astype(F32), decay


def combine_kernel(many, size, keep_ref, recv_ref, out_ref):
    states, decays = [], []
    for head in range(many):
        (g0, a0), (g1, a1) = pair(keep_ref, recv_ref, many, size, head)
        states.append(g0 + a0 * g1)
        decays.append(a0 * a1)
    payload(out_ref, many, states, decays)


def pick_side(upper, mine, theirs):
    return jnp.where(upper, theirs, mine), jnp.where(upper, mine, theirs)


def climb_kernel(many, size, bit, mine_ref, recv_ref, out_ref):
    _, chip, _ = core_and_chip()
    upper = lax.rem(lax.div(chip, bit), 2) == 1
    states, decays = [], []
    for head in range(many):
        t_mine, a_mine = loaded(mine_ref, many, size, head)
        t_recv, a_recv = loaded(recv_ref, many, size, head)
        t_low, t_high = pick_side(upper, t_mine, t_recv)
        a_low, a_high = pick_side(upper, a_mine, a_recv)
        states.append(t_low + a_low * t_high)
        decays.append(a_low * a_high)
    payload(out_ref, many, states, decays)


def carry_kernel(many, size, levels, *refs):
    core, chip, _ = core_and_chip()
    recvs = refs[:levels]
    keep_ref, recv_ref, own_ref, send_ref = refs[levels:]
    for head in range(many):
        span = slice(head * size, (head + 1) * size)
        carry, reach = None, None
        for level, ref in enumerate(recvs):
            state, decay = loaded(ref, many, size, head)
            lower = lax.rem(lax.div(chip, 2**level), 2) == 0
            state = jnp.where(lower, state, 0.0)
            decay = jnp.where(lower, decay, 1.0)
            carry = state if carry is None else carry + reach * state
            reach = decay if reach is None else reach * decay
        _, (g1, a1) = pair(keep_ref, recv_ref, many, size, head)
        second = carry
        first = g1 + a1 * second
        own_ref[span, :] = jnp.where(core == 0, first, second).astype(BF16)
        send_ref[span, :] = jnp.where(core == 0, second, first).astype(BF16)


def intra_kernel(
    first, many, x_ref, dy_ref, bc_ref, cumt_ref, cum_ref, step_ref, h_ref, before_ref,
    dx_ref, mixed_ref, ex_ref, own_ref, rowm_ref,
):
    length, width = x_ref.shape
    heads = cumt_ref.shape[0]
    size = width // heads
    per = LANES // size
    upper = iota((length, length), 0) <= iota((length, length), 1)
    b_rows, c_rows = bc_ref[:, :LANES], bc_ref[:, LANES:]
    scores = dot(b_rows, c_rows, 1, 1)
    lane = iota((1, LANES), 1)
    lane_bf = [where_one(lane // size == i).astype(BF16) for i in range(per)]
    mixed = before_ref[...]
    own = jnp.zeros((length, LANES), F32)
    reach = jnp.zeros((heads, length), F32)
    for j in range(first, first + many):
        span = slice(j * LANES, (j + 1) * LANES)
        out_span = slice((j - first) * LANES, (j - first + 1) * LANES)
        x_p = x_ref[:, span]
        dy_p = dy_ref[:, span]
        dy_h = jnp.concatenate([dy_p * m for m in lane_bf], axis=0)
        cross = dot(x_p, dy_h, 1, 1)
        kern = []
        wide = None
        for i in range(per):
            h = j * per + i
            diff = cumt_ref[h : h + 1, :] - cum_ref[:, h : h + 1]
            seg = jnp.exp(jnp.where(upper, diff, -1e30))
            kern.append((seg * scores).astype(BF16))
            step = jnp.broadcast_to(step_ref[:, h : h + 1], (length, LANES))
            wide = step if i == 0 else jnp.where(lane < i * size, wide, step)
            scaled = seg * cross[:, i * length : (i + 1) * length] * step
            mixed = mixed + scaled
            full = scaled * scores
            rowm_ref[h : h + 1, :] = jnp.sum(full, axis=0, keepdims=True)
            own = jnp.where(lane == h, jnp.sum(full, axis=1, keepdims=True), own)
        back = dot(jnp.concatenate(kern, axis=1), dy_h, 1, 0)
        dx_ref[:, out_span] = back * wide
        seen = dy_p.astype(F32) * dot(c_rows, h_ref[span, :], 1, 1)
        reach = reach + dot(to_heads(j, heads, size), halves(seen), 1, 1)
    mixed_ref[...] = mixed
    rows = slice(first * per, (first + many) * per)
    own = own.T[rows]
    own_ref[...] = own
    ex_ref[...] = rowm_ref[rows, :] + jnp.exp(cumt_ref[rows, :]) * reach[rows] - own


def close_kernel(mixed_ref, bc_ref, carried_ref, db_ref, dc_ref):
    mixed = mixed_ref[...].astype(BF16)
    db_ref[...] = dot(mixed, bc_ref[:, LANES:], 1, 0)
    dc_ref[...] = (dot(mixed, bc_ref[:, :LANES], 0, 0) + carried_ref[...]).astype(BF16)


def db_kernel(xs_ref, own_ref, recv_ref, db_ref, dc_ref, out_ref):
    core, _, _ = core_and_chip()
    half = db_ref.shape[1]
    part = own_ref.shape[0]
    total = db_ref[...]
    for ref, index in ((own_ref, core), (recv_ref, 1 - core)):
        total = total + dot(xs_ref[:, rows_at(index, part, LANES)], ref[...], 1, 0)
    out_ref[:, :half] = total.astype(BF16)
    out_ref[:, half:] = dc_ref[...]


def finish_kernel(parts, *refs):
    (x_ref, bc_ref, cumt_ref, stept_ref, cum_ref, step_ref, h_ref, own_ref, recv_ref,
     w_ref, dbc_ref) = refs[:11]
    dx_refs, ex_refs, st_refs = (refs[11 + i * parts : 11 + (i + 1) * parts] for i in range(3))
    in_ref, decay_ref, grad_ref, r_ref, edge_ref = refs[11 + 3 * parts :]
    core, _, _ = core_and_chip()
    length, width = x_ref.shape
    heads = cumt_ref.shape[0]
    size = width // heads
    part = width // 2
    r_ref[rows_at(core, part), :] = own_ref[...]
    r_ref[rows_at(1 - core, part), :] = recv_ref[...]
    cum = cum_ref[...]
    table = halves(jnp.exp(cum[length - 1 : length] - cum) * step_ref[...])
    seen = jnp.zeros((heads, length), F32)
    b_rows = bc_ref[:, :LANES]
    d_bc = dbc_ref[...]
    for j in range(width // LANES):
        span = slice(j * LANES, (j + 1) * LANES)
        local = dx_refs[j * LANES // (width // parts)]
        start = j * LANES % (width // parts)
        r_tile = r_ref[span, :]
        reach = dot(b_rows, r_tile, 1, 1)
        d_in = local[:, start : start + LANES] + dot(table, to_lanes(j, size), 1, 0) * reach
        d_in = d_in + dot(d_bc, w_ref[span, :], 1, 1)
        in_ref[:, span] = d_in.astype(BF16)
        product = x_ref[:, span].astype(F32) * reach
        seen = seen + dot(to_heads(j, heads, size), halves(product), 1, 1)
        edge = r_tile.astype(F32) * h_ref[span, :].astype(F32)
        for i in range(LANES // size):
            h = j * (LANES // size) + i
            edge_ref[h : h + 1, :] = jnp.sum(
                edge[i * size : (i + 1) * size], axis=0, keepdims=True
            )
    cumt = cumt_ref[...]
    total = cumt[:, length - 1 : length]
    to_end = jnp.exp(total - cumt)
    step = stept_ref[...]
    own = jnp.concatenate([r[...] for r in st_refs], axis=0)
    excess = jnp.concatenate([r[...] for r in ex_refs], axis=0)
    grad_ref[...] = own / step + to_end * seen
    edge = jnp.exp(total) * jnp.sum(edge_ref[...], axis=1, keepdims=True)
    decay_ref[...] = (
        dot(excess, triangle(length, lambda a, b: a >= b), 1, 0, HI)
        + dot(to_end * step * seen, triangle(length, lambda a, b: a < b), 1, 0, HI)
        + edge
    )


def term_kernel(n_chip, *refs):
    columns, pieces = refs[:n_chip], refs[n_chip:-3]
    keep_ref, send_ref, held = refs[-3:]
    pieces = [(p, i) for p in pieces for i in range(p.shape[0])]
    core, _, _ = core_and_chip()
    total = None
    for a, (b, i) in zip(columns, pieces):
        part = dot(a[a.shape[0] - 2 * keep_ref.shape[0] :, :], b[i], 1, 0)
        total = part if total is None else total + part
    block = keep_ref.shape[0]
    held[0] = total[:block]
    held[1] = total[block:]
    keep_ref[...] = held[core]
    send_ref[...] = held[1 - core].astype(BF16)


def deal_kernel(keep_ref, recv_ref, own_ref, *refs):
    outs, held = refs[:-1], refs[-1]
    place, n_dp = lax.axis_index("dp"), lax.axis_size("dp")
    total = keep_ref[...] + recv_ref[...].astype(F32)
    share = own_ref.shape[0]
    for i in range(n_dp):
        held[i] = total[i * share : (i + 1) * share]
    own_ref[...] = held[place]
    for s, out in enumerate(outs):
        out[...] = held[place ^ (s + 1)].astype(BF16)


def expert_kernel(flip, merge, slots, grad_rows, a_ref, b_ref, gate_ref, up_ref, *refs):
    outs, (rows_ref, gate_acc, up_acc) = refs[:-3], refs[-3:]
    step = pl.program_id(0)
    n_chip = a_ref.shape[0]
    width = rows_ref.shape[1]

    @pl.when(step == 0)
    def _():
        for half, ref in enumerate((a_ref, b_ref)):
            for i in range(n_chip):
                row = (half * n_chip + i) * slots
                for t in range(width // LANES):
                    rows_ref[row : row + slots, t * LANES : (t + 1) * LANES] = ref[
                        i, t * slots : (t + 1) * slots, :
                    ]
        gate_acc[...] = jnp.zeros_like(gate_acc)
        up_acc[...] = jnp.zeros_like(up_acc)

    depth = gate_ref.shape[0]
    rows = rows_ref[:, rows_at(step, depth, LANES)]
    gate_acc[...] += dot(rows, gate_ref[...], 1, 0)
    up_acc[...] += dot(rows, up_ref[...], 1, 0)

    @pl.when(step == pl.num_programs(0) - 1)
    def _():
        weighted = jax.nn.silu(gate_acc[...]) * up_acc[...]
        weighted = (weighted.T if flip else weighted).astype(BF16)
        place, n_dp = lax.axis_index("dp"), lax.axis_size("dp")
        base = width // LANES * slots
        hidden = gate_acc.shape[1]

        def put(out, start, target):
            for i in range(n_chip):
                row = pl.multiple_of(base + target * grad_rows, 16)
                to = start + i * grad_rows
                out[to : to + grad_rows, :] = a_ref[i, pl.ds(row, grad_rows), :]

        if merge:
            grads = n_chip * grad_rows
            for s, out in enumerate(outs):
                out[grads : grads + hidden, :] = weighted
                put(out, 0, place ^ s)
            put(outs[2], grads + hidden, place ^ 3)
        else:
            outs[0][...] = weighted
            for s in range(n_dp):
                put(outs[1 + s], 0, place ^ s)


def expert(a, b, w_gate, w_up, slots, grad_rows, n_dp, flip, merge):
    n_chip = a.shape[0]
    total = 2 * n_chip * slots
    width, hidden = w_gate.shape
    depth = 512
    whole = pl.BlockSpec(a.shape, lambda i: (0, 0, 0))
    block = pl.BlockSpec((depth, hidden), lambda i: (i, 0))
    grads = n_chip * grad_rows
    if merge:
        outs = [(grads + hidden, LANES)] * 2 + [(2 * grads + hidden, LANES)]
    else:
        outs = [(hidden, total) if flip else (total, hidden)] + [(grads, LANES)] * n_dp
    return pl.pallas_call(
        lambda *refs: expert_kernel(flip, merge, slots, grad_rows, *refs),
        out_shape=[shape(o, BF16) for o in outs],
        grid=(width // depth,),
        in_specs=[whole, whole, block, block],
        out_specs=[pl.BlockSpec(o, lambda i: (0, 0)) for o in outs],
        scratch_shapes=[
            pltpu.VMEM((total, width), BF16),
            pltpu.VMEM((total, hidden), F32),
            pltpu.VMEM((total, hidden), F32),
        ],
        cost_estimate=pl.CostEstimate(
            flops=int(3e10),
            bytes_accessed=1000,
            transcendentals=0,
        ),
        compiler_params=pltpu.CompilerParams(vmem_limit_bytes=20 * 1024 * 1024),
    )(a, b, w_gate, w_up)


def down_kernel(n_dp, flip, merge, slots, grad_rows, *refs):
    weighted = refs[:n_dp]
    near = weighted if merge else refs[n_dp : 2 * n_dp]
    b_ref, far_ref, out_ref = refs[-3:]
    hidden, piece = out_ref.shape
    n_chip = b_ref.shape[0]
    tiles = grad_rows // slots
    count = n_chip * grad_rows
    place = lax.axis_index("dp")
    total = None
    for s in range(n_dp):
        first = merge and s < 3
        base = hidden if merge and not first else 0
        blocks = [
            near[s][base + i * grad_rows : base + (i + 1) * grad_rows, :] for i in range(n_chip)
        ]
        if s == 0:
            row = b_ref.shape[1] - n_dp * grad_rows + place * grad_rows
            rows = pl.ds(pl.multiple_of(row, 16), grad_rows)
            blocks += [b_ref[i, rows, :] for i in range(n_chip)]
        else:
            blocks += [far_ref[s - 1, i * grad_rows : (i + 1) * grad_rows, :] for i in range(n_chip)]
        columns = [
            jnp.concatenate([b[t * slots : (t + 1) * slots] for b in blocks], axis=0)
            for t in range(tiles)
        ]
        grads = jnp.concatenate(columns, axis=1)[:, :piece]
        low = count if first else 0
        left = weighted[s][low : low + hidden, :] if merge else weighted[s][...]
        part = dot(left, grads, 1 if flip else 0, 0)
        total = part if total is None else total + part
    out_ref[...] = total.astype(BF16)


def xored(array, axis, mask):
    count = lax.axis_size(axis)
    return lax.ppermute(array, axis, [(i, i ^ mask) for i in range(count)])


def swapped(array):
    return xored(array, "tm", 1)


def chips(arrays):
    return [arrays[0]] + [xored(a, "tm", 2 * s) for s, a in enumerate(arrays) if s]


def gathered(array, axis, count):
    if count == 1:
        return [array]
    far = xored(array, axis, count // 2)
    return gathered(array, axis, count // 2) + gathered(far, axis, count // 2)


def per_device(
    layer_in,
    out_grad,
    w_bc,
    log_decay,
    step,
    saved_states,
    w_gate,
    w_up,
    slot_rows,
    slot_counts,
    slot_gates,
):
    n_dp = lax.axis_size("dp")
    core, chip, n_chip = core_and_chip()
    x = layer_in[0]
    dy = out_grad[0]
    length, width = x.shape
    heads = log_decay.shape[2]
    size = width // heads
    share, columns = w_bc.shape
    half = columns // 2
    ldt = log_decay[0].T
    stept = step[0].T
    h_in = saved_states[0, 0].reshape(width, half)
    capacity = slot_rows.shape[2]
    piece = width // n_dp
    part = width // 2
    many = heads // 2
    flip = w_gate.shape[2] % LANES == 0
    merge = flip and 2 * n_chip * capacity == LANES and n_dp == 4

    grad_rows = -(-piece // LANES) * capacity
    w_half = lax.dynamic_slice_in_dim(w_bc, core * (share // 2), share // 2, 0)
    mine = gathered(w_half, "dp", n_dp)[1:]

    n_rows = width // LANES * capacity + n_dp * grad_rows
    cumt, cum, steps, dyt, xs, carried, *sends = call(
        lambda *refs: prep_kernel(n_dp, *refs),
        [
            shape((heads, length), F32),
            shape((length, LANES), F32),
            shape((length, LANES), F32),
            shape((width + up16(2 * heads), length), BF16),
            shape((length, width), BF16),
            shape((length, half), F32),
        ]
        + [shape((n_rows + width // n_chip, length), BF16)] * n_chip,
        2.0,
        (x, dy, ldt, stept, h_in, slot_rows[0], slot_counts, slot_gates[0]),
        scratch=[pltpu.VMEM((width, length), BF16)],
        fetch=(0, 1, 2, 3, 4),
        limit=60,
    )
    arrivals = chips(sends)
    other = swapped(stacked(mine, after=(cumt,)))
    rows_a = stacked(arrivals, rows=n_rows)
    rows_b = swapped(rows_a)
    w_whole, bc, keep, send = call(
        lambda *refs: project_kernel(n_dp - 1, many, *refs),
        [
            shape((width, columns), BF16),
            shape((length, columns), BF16),
            shape((part + up16(2 * many), half), BF16),
            shape((part + up16(2 * many), half), BF16),
        ],
        1.0,
        (x, dyt, w_bc, *mine, other),
    )
    recv = swapped(send)
    climbs = [
        call(
            lambda *refs: combine_kernel(many, size, *refs),
            [shape((part + up16(2 * many), half), BF16)],
            0.5,
            (keep, recv),
            after=tuple(arrivals[1:]),
        )[0]
    ]
    outs = expert(rows_a, rows_b, w_gate[0], w_up[0], capacity, grad_rows, n_dp, flip, merge)
    outs = list(outs)
    arrived = []
    bit = 1
    while bit < n_chip:
        last = bit * 2 == n_chip
        moves = [
            (k, k ^ (2 * bit)) for k in range(2 * n_chip) if not last or k & (2 * bit)
        ]
        arrived.append(lax.ppermute(climbs[-1], "tm", moves))
        if not last:
            climbs.append(
                call(
                    lambda *refs, bit=bit: climb_kernel(many, size, bit, *refs),
                    [shape((part + up16(2 * many), half), BF16)],
                    0.5,
                    (climbs[-1], arrived[-1]),
                    after=(outs[0],),
                )[0]
            )
        bit *= 2

    if merge:
        near_rows = n_chip * grad_rows
        arrived_2 = xored(outs[2], "dp", 2)
        spread = [outs[0], xored(outs[1], "dp", 1), arrived_2]
        spread.append(xored(arrived_2[near_rows:], "dp", 1))
        near = spread
    else:
        spread = gathered(outs[0], "dp", n_dp)
        near = outs[1:2] + [xored(o, "dp", s + 1) for s, o in enumerate(outs[2:])]

    parts = 2
    tiles = width // LANES // parts
    dxs, exs, owns = [], [], []
    mixed = jnp.zeros((length, length), F32)
    for i in range(parts):
        dx, mixed, ex, own = call(
            lambda *refs, i=i: intra_kernel(i * tiles, tiles, *refs),
            [
                shape((length, width // parts), F32),
                shape((length, length), F32),
                shape((heads // parts, length), F32),
                shape((heads // parts, length), F32),
            ],
            3.0,
            (x, dy, bc, cumt, cum, steps, h_in, mixed),
            scratch=[pltpu.VMEM((heads, length), F32)],
        )
        dxs.append(dx)
        exs.append(ex)
        owns.append(own)
    db, dc = call(
        close_kernel,
        [shape((length, half), F32), shape((length, half), BF16)],
        0.3,
        (mixed, bc, carried),
    )

    r_own, r_send = call(
        lambda *refs: carry_kernel(many, size, len(arrived), *refs),
        [shape((part, half), BF16)] * 2,
        0.5,
        (*arrived, keep, recv),
        after=(dc,),
    )
    r_recv = swapped(r_send)
    d_bc = call(db_kernel, [shape((length, columns), BF16)], 0.3, (xs, r_own, r_recv, db, dc))[0]
    d_bcs = [d_bc.reshape(1, length, columns)]
    while 2 ** (len(d_bcs) - 1) < n_chip:
        level = 2 ** (len(d_bcs) - 1)
        sent = d_bcs[0] if level == 1 else joined(d_bcs)
        d_bcs.append(xored(sent, "tm", 2 * level))
    d_in, d_decay, d_step = call(
        lambda *refs: finish_kernel(parts, *refs),
        [
            shape((length, width), BF16),
            shape((heads, length), F32),
            shape((heads, length), F32),
        ],
        3.0,
        (x, bc, cumt, stept, cum, steps, h_in, r_own, r_recv, w_whole, d_bc,
         *dxs, *exs, *owns),
        scratch=[pltpu.VMEM((width, half), BF16), pltpu.VMEM((heads, half), F32)],
    )
    w_rows = width // (2 * n_chip)
    term, term_send = call(
        lambda *refs: term_kernel(n_chip, *refs),
        [shape((w_rows, columns), F32), shape((w_rows, columns), BF16)],
        0.5,
        (*arrivals, *d_bcs),
        after=(d_in,),
        scratch=[pltpu.VMEM((2, w_rows, columns), F32)],
    )
    final = call(
        deal_kernel,
        [shape((w_rows // n_dp, columns), F32)]
        + [shape((w_rows // n_dp, columns), BF16)] * (n_dp - 1),
        0.3,
        (term, swapped(term_send)),
        scratch=[pltpu.VMEM((n_dp, w_rows // n_dp, columns), F32)],
    )
    w_bc_grad = final[0]
    for s in range(1, n_dp):
        w_bc_grad = w_bc_grad + xored(final[s], "dp", s).astype(F32)

    starts = [0, 0, w_gate.shape[2]] if merge else None
    far = swapped(stacked(near[1:], after=(term,), rows=n_chip * grad_rows, starts=starts))
    w_down_grad = call(
        lambda *refs: down_kernel(n_dp, flip, merge, capacity, grad_rows, *refs),
        [shape((w_gate.shape[2], piece), BF16)],
        1.0,
        (*spread, *([] if merge else near), rows_b, far),
        after=(final[0],),
    )[0]
    return (d_in[None], d_decay.T[None], d_step.T[None], w_bc_grad, w_down_grad[None])


def solution(mesh):
    in_specs = (
        P("dp", "tm", None),
        P("dp", "tm", None),
        P("dp", None),
        P("dp", "tm", None),
        P("dp", "tm", None),
        P("dp", "tm", None, None, None),
        P(None, None, "tm"),
        P(None, None, "tm"),
        P("dp", None, "tm"),
        P("dp", "tm"),
        P("dp", None, "tm"),
    )
    out_specs = (
        P("dp", "tm", None),
        P("dp", "tm", None),
        P("dp", "tm", None),
        P(("tm", "dp"), None),
        P(None, "tm", "dp"),
    )
    return jax.shard_map(
        per_device, mesh=mesh, in_specs=in_specs, out_specs=out_specs, check_vma=False
    )
```

```python
import jax
import jax.numpy as jnp
from jax import lax
from jax.experimental import pallas as pl
from jax.experimental.pallas import tpu as pltpu
from jax.sharding import PartitionSpec as P

HI = lax.Precision.HIGHEST
F32 = jnp.float32
BF16 = jnp.bfloat16
LANES = 128


def dot(a, b, ca, cb, precision=None):
    return lax.dot_general(
        a, b, (((ca,), (cb,)), ((), ())), precision=precision, preferred_element_type=F32
    )


def iota(dims, axis):
    return lax.broadcasted_iota(jnp.int32, dims, axis)


def where_one(mask):
    return jnp.where(mask, 1.0, 0.0)


def triangle(n, keep):
    return where_one(keep(iota((n, n), 0), iota((n, n), 1))).astype(F32)


def halves(values, axis=1):
    high = values.astype(BF16)
    low = (values - high.astype(F32)).astype(BF16)
    return jnp.concatenate([high, low], axis=axis)


def to_lanes(j, size):
    dims = (LANES, LANES)
    one = where_one(iota(dims, 0) == iota(dims, 1) // size + j * (LANES // size)).astype(BF16)
    return jnp.concatenate([one, one], axis=0)


def to_heads(j, heads, size):
    dims = (heads, LANES)
    one = where_one(iota(dims, 0) == iota(dims, 1) // size + j * (LANES // size)).astype(BF16)
    return jnp.concatenate([one, one], axis=1)


def up16(n):
    return -(-n // 16) * 16


def call(kernel, outs, cost, args, after=(), scratch=(), limit=14, fetch=()):
    n_in, n_after, n_out = len(args), len(after), len(outs)
    fetch = tuple(fetch)

    def body(*refs):
        ins = list(refs[:n_in])
        rest = refs[n_in + n_after :]
        if fetch:
            sems = rest[-1]
            held = rest[len(rest) - 1 - len(fetch) : -1]
            rest = rest[: len(rest) - 1 - len(fetch)]
            copies = []
            for i, (index, ref) in enumerate(zip(fetch, held)):
                copies.append(pltpu.make_async_copy(ins[index], ref, sems.at[i]))
                ins[index] = ref
            for copy in copies:
                copy.start()
            for copy in copies:
                copy.wait()
        kernel(*ins, *rest)

    specs = [
        pl.BlockSpec(memory_space=pltpu.HBM if i in fetch else pltpu.VMEM) for i in range(n_in)
    ]
    held = [pltpu.VMEM(args[i].shape, args[i].dtype) for i in fetch]
    if fetch:
        held.append(pltpu.SemaphoreType.DMA((len(fetch),)))
    return pl.pallas_call(
        body,
        out_shape=outs,
        in_specs=specs + [pl.BlockSpec(memory_space=pl.ANY)] * n_after,
        out_specs=[pl.BlockSpec(memory_space=pltpu.VMEM)] * n_out,
        scratch_shapes=list(scratch) + held,
        cost_estimate=pl.CostEstimate(
            flops=int(cost * 1e5), bytes_accessed=1000, transcendentals=0
        ),
        compiler_params=pltpu.CompilerParams(vmem_limit_bytes=limit * 1024 * 1024),
    )(*args, *after)


def shape(dims, kind):
    return jax.ShapeDtypeStruct(dims, kind)


def core_and_chip():
    place = lax.axis_index("tm")
    return lax.rem(place, 2), lax.div(place, 2), lax.axis_size("tm") // 2


def rows_at(index, size, align=16):
    return pl.ds(pl.multiple_of(index * size, align), size)


def picked(n_dp, x_ref, dy_ref, slot_ref, count_ref, gate_ref, out_ref):
    length, width = x_ref.shape
    slots = slot_ref.shape[1]
    hit = iota((length, slots), 0) == slot_ref[...]
    live = iota((1, slots), 1) < count_ref[...]
    weight = jnp.where(live, gate_ref[...].astype(F32), 0.0)
    rows = dot(where_one(hit).astype(BF16), x_ref[...], 0, 0).astype(BF16)
    grads = dot(jnp.where(hit, weight, 0.0).astype(BF16), dy_ref[...], 0, 0).astype(BF16)
    blocks = [rows[:, t * LANES : (t + 1) * LANES] for t in range(width // LANES)]
    piece = width // n_dp
    for i in range(n_dp):
        for low in range(i * piece, (i + 1) * piece, LANES):
            block = grads[:, low : min(low + LANES, (i + 1) * piece)]
            if block.shape[1] < LANES:
                fill = jnp.zeros((slots, LANES - block.shape[1]), BF16)
                block = jnp.concatenate([block, fill], axis=1)
            blocks.append(block)
    for i, block in enumerate(blocks):
        out_ref[i * slots : (i + 1) * slots, :] = block


def high_low(values):
    high = values.astype(BF16).astype(F32)
    return [high, values - high]


def prep_kernel(
    n_dp, x_ref, dy_ref, ldt_ref, stept_ref, h_ref, slot_ref, count_ref, gate_ref,
    cumt_ref, cum_ref, step_ref, dyt_ref, xs_ref, carried_ref, rows_ref, *rest,
):
    outs, xt_ref = rest[:-1], rest[-1]
    length, width = x_ref.shape
    heads = ldt_ref.shape[0]
    size = width // heads
    _, chip, n_chip = core_and_chip()
    picked(n_dp, x_ref, dy_ref, slot_ref, count_ref, gate_ref, rows_ref)
    pad = jnp.zeros((LANES - heads, length), F32)
    cumt = dot(ldt_ref[...], triangle(length, lambda a, b: a <= b), 1, 0, HI)
    cumt_ref[...] = cumt
    cum = jnp.concatenate([cumt, pad], axis=0).T
    step = jnp.concatenate([stept_ref[...], pad], axis=0).T
    cum_ref[...] = cum
    step_ref[...] = step
    start = jnp.exp(cum)
    into_end = jnp.exp(cum[length - 1 : length] - cum) * step
    table = jnp.concatenate([halves(start), halves(into_end)], axis=0)
    carried = jnp.zeros(carried_ref.shape, F32)
    for j in range(width // LANES):
        span = slice(j * LANES, (j + 1) * LANES)
        scale = dot(table, to_lanes(j, size), 1, 0)
        x_f = x_ref[:, span].astype(F32)
        xt_ref[span, :] = x_f.T.astype(BF16)
        xs_ref[:, span] = (x_f * scale[length:]).astype(BF16)
        dys = dy_ref[:, span].astype(F32) * scale[:length]
        dyt_ref[span, :] = dys.T.astype(BF16)
        carried = carried + dot(dys.astype(BF16), h_ref[span, :], 1, 0)
    carried_ref[...] = carried
    decay = jnp.broadcast_to(jnp.exp(cumt[:, length - 1 : length]), (heads, LANES))
    dyt_ref[width : width + 2 * heads, :] = jnp.concatenate(high_low(decay), axis=0).astype(BF16)
    block = width // n_chip
    s = 0
    for out in outs:
        for start in range(0, out.shape[0], block):
            out[start : start + block, :] = xt_ref[rows_at(chip ^ s, block), :]
            s += 1


def join_kernel(ranges, *refs):
    out, at = refs[-1], 0
    for ref, (start, stop) in zip(refs, ranges):
        out[at : at + stop - start] = ref[start:stop]
        at += stop - start


def joined(arrays, after=(), ranges=None):
    ranges = ranges or [(0, a.shape[0]) for a in arrays]
    dims = (sum(stop - start for start, stop in ranges), *arrays[0].shape[1:])
    return call(
        lambda *refs: join_kernel(ranges, *refs),
        [shape(dims, arrays[0].dtype)],
        0.2,
        tuple(arrays),
        after=after,
    )[0]


def stacked(arrays, after=(), ranges=None):
    count = len(arrays)
    out = joined(arrays, after, ranges)
    return out.reshape(count, out.shape[0] // count, *out.shape[1:])


def project_kernel(n_mine, many, *refs):
    x_ref, dyt_ref, own_ref = refs[:3]
    mine, other = refs[3 : 3 + n_mine], refs[3 + n_mine]
    w_ref, bc_ref, keep_ref, send_ref = refs[4 + n_mine :]
    core, _, _ = core_and_chip()
    place, n_dp = lax.axis_index("dp"), lax.axis_size("dp")
    share = own_ref.shape[0]
    half = share // 2
    w_ref[rows_at(place, share), :] = own_ref[...]
    for i in range(n_mine):
        source = place ^ (i + 1)
        w_ref[rows_at(source * 2 + core, half), :] = mine[i][...]
        w_ref[rows_at(source * 2 + 1 - core, half), :] = other[i]
    bc = dot(x_ref[...], w_ref[...], 1, 0).astype(BF16)
    bc_ref[...] = bc
    c_rows = bc[:, LANES:]
    width = x_ref.shape[1]
    part = width // 2
    for ref, index in ((keep_ref, core), (send_ref, 1 - core)):
        ref[:part, :] = dot(dyt_ref[rows_at(index, part), :], c_rows, 1, 0).astype(BF16)
        table = dyt_ref[width : width + 4 * many, :].astype(F32)
        quarter = [table[i * many : (i + 1) * many] for i in range(4)]
        high = jnp.where(index == 0, quarter[0], quarter[1])
        low = jnp.where(index == 0, quarter[2], quarter[3])
        fill = jnp.zeros((ref.shape[0] - part - 2 * many, LANES), F32)
        ref[part:, :] = jnp.concatenate([high, low, fill], axis=0).astype(BF16)


def pair(keep_ref, recv_ref, many, size, head):
    core, _, _ = core_and_chip()
    part = many * size
    both = []
    for ref in (keep_ref, recv_ref):
        extra = ref[part:, :].astype(F32)
        decay = extra[head : head + 1] + extra[many + head : many + head + 1]
        both.append((ref[head * size : (head + 1) * size, :].astype(F32), decay))
    first = jax.tree.map(lambda a, b: jnp.where(core == 0, a, b), both[0], both[1])
    second = jax.tree.map(lambda a, b: jnp.where(core == 0, b, a), both[0], both[1])
    return first, second


def payload(ref, many, states, decays):
    size = states[0].shape[0]
    for head, state in enumerate(states):
        ref[head * size : (head + 1) * size, :] = state.astype(BF16)
    decay = jnp.concatenate(decays, axis=0)
    high = decay.astype(BF16).astype(F32)
    fill = jnp.zeros((ref.shape[0] - many * size - 2 * many, LANES), F32)
    extra = jnp.concatenate([high, decay - high, fill], axis=0)
    ref[many * size :, :] = extra.astype(BF16)


def loaded(ref, many, size, head):
    extra = ref[many * size :, :].astype(F32)
    decay = extra[head : head + 1] + extra[many + head : many + head + 1]
    return ref[head * size : (head + 1) * size, :].astype(F32), decay


def combine_kernel(many, size, keep_ref, recv_ref, out_ref):
    states, decays = [], []
    for head in range(many):
        (g0, a0), (g1, a1) = pair(keep_ref, recv_ref, many, size, head)
        states.append(g0 + a0 * g1)
        decays.append(a0 * a1)
    payload(out_ref, many, states, decays)


def pick_side(upper, mine, theirs):
    return jnp.where(upper, theirs, mine), jnp.where(upper, mine, theirs)


def climb_kernel(many, size, bit, mine_ref, recv_ref, out_ref):
    _, chip, _ = core_and_chip()
    upper = lax.rem(lax.div(chip, bit), 2) == 1
    states, decays = [], []
    for head in range(many):
        t_mine, a_mine = loaded(mine_ref, many, size, head)
        t_recv, a_recv = loaded(recv_ref, many, size, head)
        t_low, t_high = pick_side(upper, t_mine, t_recv)
        a_low, a_high = pick_side(upper, a_mine, a_recv)
        states.append(t_low + a_low * t_high)
        decays.append(a_low * a_high)
    payload(out_ref, many, states, decays)


def carry_kernel(many, size, levels, *refs):
    core, chip, _ = core_and_chip()
    recvs = refs[:levels]
    keep_ref, recv_ref, own_ref, send_ref = refs[levels:]
    for head in range(many):
        span = slice(head * size, (head + 1) * size)
        carry, reach = None, None
        for level, ref in enumerate(recvs):
            state, decay = loaded(ref, many, size, head)
            lower = lax.rem(lax.div(chip, 2**level), 2) == 0
            state = jnp.where(lower, state, 0.0)
            decay = jnp.where(lower, decay, 1.0)
            carry = state if carry is None else carry + reach * state
            reach = decay if reach is None else reach * decay
        _, (g1, a1) = pair(keep_ref, recv_ref, many, size, head)
        second = carry
        first = g1 + a1 * second
        own_ref[span, :] = jnp.where(core == 0, first, second).astype(BF16)
        send_ref[span, :] = jnp.where(core == 0, second, first).astype(BF16)


def intra_kernel(
    first, many, x_ref, dy_ref, bc_ref, cumt_ref, cum_ref, step_ref, h_ref, before_ref,
    dx_ref, mixed_ref, ex_ref, own_ref, rowm_ref,
):
    length, width = x_ref.shape
    heads = cumt_ref.shape[0]
    size = width // heads
    per = LANES // size
    upper = iota((length, length), 0) <= iota((length, length), 1)
    b_rows, c_rows = bc_ref[:, :LANES], bc_ref[:, LANES:]
    scores = dot(b_rows, c_rows, 1, 1)
    lane = iota((1, LANES), 1)
    lane_bf = [where_one(lane // size == i).astype(BF16) for i in range(per)]
    mixed = before_ref[...]
    own = jnp.zeros((length, LANES), F32)
    reach = jnp.zeros((heads, length), F32)
    for j in range(first, first + many):
        span = slice(j * LANES, (j + 1) * LANES)
        out_span = slice((j - first) * LANES, (j - first + 1) * LANES)
        x_p = x_ref[:, span]
        dy_p = dy_ref[:, span]
        dy_h = jnp.concatenate([dy_p * m for m in lane_bf], axis=0)
        cross = dot(x_p, dy_h, 1, 1)
        kern = []
        wide = None
        for i in range(per):
            h = j * per + i
            diff = cumt_ref[h : h + 1, :] - cum_ref[:, h : h + 1]
            seg = jnp.exp(jnp.where(upper, diff, -1e30))
            kern.append((seg * scores).astype(BF16))
            step = jnp.broadcast_to(step_ref[:, h : h + 1], (length, LANES))
            wide = step if i == 0 else jnp.where(lane < i * size, wide, step)
            scaled = seg * cross[:, i * length : (i + 1) * length] * step
            mixed = mixed + scaled
            full = scaled * scores
            rowm_ref[h : h + 1, :] = jnp.sum(full, axis=0, keepdims=True)
            own = jnp.where(lane == h, jnp.sum(full, axis=1, keepdims=True), own)
        back = dot(jnp.concatenate(kern, axis=1), dy_h, 1, 0)
        dx_ref[:, out_span] = back * wide
        seen = dy_p.astype(F32) * dot(c_rows, h_ref[span, :], 1, 1)
        reach = reach + dot(to_heads(j, heads, size), halves(seen), 1, 1)
    mixed_ref[...] = mixed
    rows = slice(first * per, (first + many) * per)
    own = own.T[rows]
    own_ref[...] = own
    ex_ref[...] = rowm_ref[rows, :] + jnp.exp(cumt_ref[rows, :]) * reach[rows] - own


def close_kernel(mixed_ref, bc_ref, carried_ref, db_ref, dc_ref):
    mixed = mixed_ref[...].astype(BF16)
    db_ref[...] = dot(mixed, bc_ref[:, LANES:], 1, 0)
    dc_ref[...] = (dot(mixed, bc_ref[:, :LANES], 0, 0) + carried_ref[...]).astype(BF16)


def db_kernel(xs_ref, own_ref, recv_ref, db_ref, dc_ref, out_ref):
    core, _, _ = core_and_chip()
    half = db_ref.shape[1]
    part = own_ref.shape[0]
    total = db_ref[...]
    for ref, index in ((own_ref, core), (recv_ref, 1 - core)):
        total = total + dot(xs_ref[:, rows_at(index, part, LANES)], ref[...], 1, 0)
    out_ref[:, :half] = total.astype(BF16)
    out_ref[:, half:] = dc_ref[...]


def finish_kernel(parts, *refs):
    (x_ref, bc_ref, cumt_ref, stept_ref, cum_ref, step_ref, h_ref, own_ref, recv_ref,
     w_ref, dbc_ref) = refs[:11]
    dx_refs, ex_refs, st_refs = (refs[11 + i * parts : 11 + (i + 1) * parts] for i in range(3))
    in_ref, decay_ref, grad_ref, r_ref, edge_ref = refs[11 + 3 * parts :]
    core, _, _ = core_and_chip()
    length, width = x_ref.shape
    heads = cumt_ref.shape[0]
    size = width // heads
    part = width // 2
    r_ref[rows_at(core, part), :] = own_ref[...]
    r_ref[rows_at(1 - core, part), :] = recv_ref[...]
    cum = cum_ref[...]
    table = halves(jnp.exp(cum[length - 1 : length] - cum) * step_ref[...])
    seen = jnp.zeros((heads, length), F32)
    b_rows = bc_ref[:, :LANES]
    d_bc = dbc_ref[...]
    for j in range(width // LANES):
        span = slice(j * LANES, (j + 1) * LANES)
        local = dx_refs[j * LANES // (width // parts)]
        start = j * LANES % (width // parts)
        r_tile = r_ref[span, :]
        reach = dot(b_rows, r_tile, 1, 1)
        d_in = local[:, start : start + LANES] + dot(table, to_lanes(j, size), 1, 0) * reach
        d_in = d_in + dot(d_bc, w_ref[span, :], 1, 1)
        in_ref[:, span] = d_in.astype(BF16)
        product = x_ref[:, span].astype(F32) * reach
        seen = seen + dot(to_heads(j, heads, size), halves(product), 1, 1)
        edge = r_tile.astype(F32) * h_ref[span, :].astype(F32)
        for i in range(LANES // size):
            h = j * (LANES // size) + i
            edge_ref[h : h + 1, :] = jnp.sum(
                edge[i * size : (i + 1) * size], axis=0, keepdims=True
            )
    cumt = cumt_ref[...]
    total = cumt[:, length - 1 : length]
    to_end = jnp.exp(total - cumt)
    step = stept_ref[...]
    own = jnp.concatenate([r[...] for r in st_refs], axis=0)
    excess = jnp.concatenate([r[...] for r in ex_refs], axis=0)
    grad_ref[...] = own / step + to_end * seen
    edge = jnp.exp(total) * jnp.sum(edge_ref[...], axis=1, keepdims=True)
    decay_ref[...] = (
        dot(excess, triangle(length, lambda a, b: a >= b), 1, 0, HI)
        + dot(to_end * step * seen, triangle(length, lambda a, b: a < b), 1, 0, HI)
        + edge
    )


def term_kernel(places, n_columns, *refs):
    columns, pieces = refs[:n_columns], refs[n_columns:-3]
    keep_ref, send_ref, held = refs[-3:]
    pieces = [(p, i) for p in pieces for i in range(p.shape[0])]
    rows = 2 * keep_ref.shape[0]
    core, _, _ = core_and_chip()
    total = None
    for (a, start), (b, i) in zip(places, pieces):
        part = dot(columns[a][start : start + rows, :], b[i], 1, 0)
        total = part if total is None else total + part
    block = keep_ref.shape[0]
    held[0] = total[:block]
    held[1] = total[block:]
    keep_ref[...] = held[core]
    send_ref[...] = held[1 - core].astype(BF16)


def deal_kernel(keep_ref, recv_ref, own_ref, *refs):
    outs, held = refs[:-1], refs[-1]
    place, n_dp = lax.axis_index("dp"), lax.axis_size("dp")
    total = keep_ref[...] + recv_ref[...].astype(F32)
    share = own_ref.shape[0]
    for i in range(n_dp):
        held[i] = total[i * share : (i + 1) * share]
    own_ref[...] = held[place]
    for s, out in enumerate(outs):
        out[...] = held[place ^ (s + 1)].astype(BF16)


def expert_kernel(flip, merge, slots, grad_rows, a_ref, b_ref, gate_ref, up_ref, *refs):
    outs, (rows_ref, gate_buf, up_buf, sems) = refs[:-4], refs[-4:]
    n_chip = a_ref.shape[0]
    blocks, depth, hidden = gate_buf.shape
    width = blocks * depth
    copies = []
    for i in range(blocks):
        pair = []
        for half, (ref, buf) in enumerate(((gate_ref, gate_buf), (up_ref, up_buf))):
            pair.append(
                pltpu.make_async_copy(
                    ref.at[pl.ds(i * depth, depth), :], buf.at[i], sems.at[half, i]
                )
            )
            pair[-1].start()
        copies.append(pair)
    for half, ref in enumerate((a_ref, b_ref)):
        for i in range(n_chip):
            row = (half * n_chip + i) * slots
            for t in range(width // LANES):
                rows_ref[row : row + slots, t * LANES : (t + 1) * LANES] = ref[
                    i, t * slots : (t + 1) * slots, :
                ]
    gate = up = None
    for i in range(blocks):
        rows = rows_ref[:, i * depth : (i + 1) * depth]
        copies[i][0].wait()
        part = dot(rows, gate_buf[i], 1, 0)
        gate = part if gate is None else gate + part
        copies[i][1].wait()
        part = dot(rows, up_buf[i], 1, 0)
        up = part if up is None else up + part
    weighted = jax.nn.silu(gate) * up
    weighted = (weighted.T if flip else weighted).astype(BF16)
    place, n_dp = lax.axis_index("dp"), lax.axis_size("dp")
    base = width // LANES * slots
    grads = n_chip * grad_rows

    def put(out, start, target):
        for i in range(n_chip):
            row = pl.multiple_of(base + target * grad_rows, 16)
            to = start + i * grad_rows
            out[to : to + grad_rows, :] = a_ref[i, pl.ds(row, grad_rows), :]

    if merge:
        own, near, low, high = outs
        middle = hidden // 2
        for s, out in enumerate((own, near)):
            out[grads:, :] = weighted
            put(out, 0, place ^ s)
        put(low, 0, place ^ 2)
        low[grads:, :] = weighted[:middle]
        high[:middle, :] = weighted[middle:]
        put(high, middle, place ^ 3)
    else:
        outs[0][...] = weighted
        for s in range(n_dp):
            put(outs[1 + s], 0, place ^ s)


def expert(a, b, w_gate, w_up, slots, grad_rows, n_dp, flip, merge, after):
    n_chip = a.shape[0]
    total = 2 * n_chip * slots
    width, hidden = w_gate.shape
    depth = 512
    grads = n_chip * grad_rows
    if merge:
        outs = [(grads + hidden, LANES)] * 2 + [(grads + hidden // 2, LANES)] * 2
    else:
        outs = [(hidden, total) if flip else (total, hidden)] + [(grads, LANES)] * n_dp

    def body(*refs):
        expert_kernel(flip, merge, slots, grad_rows, *refs[:4], *refs[4 + len(after) :])

    return pl.pallas_call(
        body,
        out_shape=[shape(o, BF16) for o in outs],
        in_specs=[pl.BlockSpec(memory_space=pltpu.VMEM)] * 2
        + [pl.BlockSpec(memory_space=pl.ANY)] * (2 + len(after)),
        out_specs=[pl.BlockSpec(memory_space=pltpu.VMEM)] * len(outs),
        scratch_shapes=[
            pltpu.VMEM((total, width), BF16),
            pltpu.VMEM((width // depth, depth, hidden), BF16),
            pltpu.VMEM((width // depth, depth, hidden), BF16),
            pltpu.SemaphoreType.DMA((2, width // depth)),
        ],
        cost_estimate=pl.CostEstimate(
            flops=int(2 * 1e5), bytes_accessed=1000, transcendentals=0
        ),
        compiler_params=pltpu.CompilerParams(vmem_limit_bytes=52 * 1024 * 1024),
    )(a, b, w_gate, w_up, *after)


def down_kernel(n_dp, flip, merge, slots, grad_rows, *refs):
    b_ref, far_ref, out_ref = refs[-3:]
    hidden, piece = out_ref.shape
    n_chip = b_ref.shape[0]
    tiles = grad_rows // slots
    count = n_chip * grad_rows
    place = lax.axis_index("dp")
    if merge:
        own, near, low, high, last = refs[:5]
        middle = hidden // 2
        left = [
            own[count:, :],
            near[count:, :],
            jnp.concatenate([low[count:, :], high[:middle, :]], axis=0),
            last[:hidden, :],
        ]
        grads = [own[:count, :], near[:count, :], low[:count, :], last[hidden:, :]]
    else:
        left = [r[...] for r in refs[:n_dp]]
        grads = [r[...] for r in refs[n_dp : 2 * n_dp]]
    total = None
    for s in range(n_dp):
        blocks = [grads[s][i * grad_rows : (i + 1) * grad_rows] for i in range(n_chip)]
        if s == 0:
            row = b_ref.shape[1] - n_dp * grad_rows + place * grad_rows
            rows = pl.ds(pl.multiple_of(row, 16), grad_rows)
            blocks += [b_ref[i, rows, :] for i in range(n_chip)]
        else:
            blocks += [far_ref[s - 1, i * grad_rows : (i + 1) * grad_rows, :] for i in range(n_chip)]
        columns = [
            jnp.concatenate([b[t * slots : (t + 1) * slots] for b in blocks], axis=0)
            for t in range(tiles)
        ]
        right = jnp.concatenate(columns, axis=1)[:, :piece]
        part = dot(left[s], right, 1 if flip else 0, 0)
        total = part if total is None else total + part
    out_ref[...] = total.astype(BF16)


def xored(array, axis, mask):
    count = lax.axis_size(axis)
    return lax.ppermute(array, axis, [(i, i ^ mask) for i in range(count)])


def swapped(array):
    return xored(array, "tm", 1)


def chips(arrays):
    return [arrays[0]] + [xored(a, "tm", 2 * s) for s, a in enumerate(arrays) if s]


def gathered(array, axis, count):
    if count == 1:
        return [array]
    far = xored(array, axis, count // 2)
    return gathered(array, axis, count // 2) + gathered(far, axis, count // 2)


def per_device(
    layer_in,
    out_grad,
    w_bc,
    log_decay,
    step,
    saved_states,
    w_gate,
    w_up,
    slot_rows,
    slot_counts,
    slot_gates,
):
    n_dp = lax.axis_size("dp")
    core, chip, n_chip = core_and_chip()
    x = layer_in[0]
    dy = out_grad[0]
    length, width = x.shape
    heads = log_decay.shape[2]
    size = width // heads
    share, columns = w_bc.shape
    half = columns // 2
    ldt = log_decay[0].T
    stept = step[0].T
    h_in = saved_states[0, 0].reshape(width, half)
    capacity = slot_rows.shape[2]
    piece = width // n_dp
    part = width // 2
    many = heads // 2
    flip = w_gate.shape[2] % LANES == 0
    merge = flip and 2 * n_chip * capacity == LANES and n_dp == 4

    grad_rows = -(-piece // LANES) * capacity
    w_half = lax.dynamic_slice_in_dim(w_bc, core * (share // 2), share // 2, 0)

    n_rows = width // LANES * capacity + n_dp * grad_rows
    blocks = [1, 1, 2] if n_chip == 4 else [1] * n_chip
    cumt, cum, steps, dyt, xs, carried, rows, *xt = call(
        lambda *refs: prep_kernel(n_dp, *refs),
        [
            shape((heads, length), F32),
            shape((length, LANES), F32),
            shape((length, LANES), F32),
            shape((width + up16(2 * heads), length), BF16),
            shape((length, width), BF16),
            shape((length, half), F32),
        ]
        + [shape((n_rows, LANES), BF16)]
        + [shape((k * width // n_chip, length), BF16) for k in blocks],
        2.0,
        (x, dy, ldt, stept, h_in, slot_rows[0], slot_counts, slot_gates[0]),
        scratch=[pltpu.VMEM((width, length), BF16)],
        fetch=(0, 1, 2, 3, 4),
        limit=60,
    )
    w_far = xored(w_half, "dp", n_dp // 2)
    mine = gathered(w_half, "dp", n_dp // 2)[1:]
    mine += gathered(joined([w_far], after=(cumt,)), "dp", n_dp // 2)
    rows_in = chips([rows] * n_chip)
    other = swapped(stacked(mine, after=tuple(rows_in[1:4])))
    rows_a = stacked(rows_in, after=(other,))
    rows_b = swapped(rows_a)
    w_whole, bc, keep, send = call(
        lambda *refs: project_kernel(n_dp - 1, many, *refs),
        [
            shape((width, columns), BF16),
            shape((length, columns), BF16),
            shape((part + up16(2 * many), half), BF16),
            shape((part + up16(2 * many), half), BF16),
        ],
        1.0,
        (x, dyt, w_bc, *mine, other),
    )
    recv = swapped(send)
    hidden = w_gate.shape[2]
    near_rows = n_chip * grad_rows
    outs = expert(
        rows_a, rows_b, w_gate[0], w_up[0], capacity, grad_rows, n_dp, flip, merge, (keep,)
    )
    climbs = [
        call(
            lambda *refs: combine_kernel(many, size, *refs),
            [shape((part + up16(2 * many), half), BF16)],
            0.5,
            (keep, recv),
            after=(outs[0],),
        )[0]
    ]
    if n_chip == 4:
        x_rows = width // n_chip
        over_y = xored(xt[2], "tm", 4)
    if merge:
        low = xored(outs[2], "dp", 2)

    parts = 2
    tiles = width // LANES // parts
    dxs, exs, owns = [], [], []
    later = ()
    mixed = jnp.zeros((length, length), F32)
    for i in range(parts):
        dx, mixed, ex, own = call(
            lambda *refs, i=i: intra_kernel(i * tiles, tiles, *refs),
            [
                shape((length, width // parts), F32),
                shape((length, length), F32),
                shape((heads // parts, length), F32),
                shape((heads // parts, length), F32),
            ],
            3.0,
            (x, dy, bc, cumt, cum, steps, h_in, mixed),
            after=later,
            scratch=[pltpu.VMEM((heads, length), F32)],
        )
        if i == 0:
            held = (dx, *((over_y,) if n_chip == 4 else ()), *((low,) if merge else ()))
            arrived = []
            bit = 1
            while bit < n_chip:
                last = bit * 2 == n_chip
                moves = [
                    (k, k ^ (2 * bit)) for k in range(2 * n_chip) if not last or k & (2 * bit)
                ]
                arrived.append(lax.ppermute(climbs[-1], "tm", moves))
                if not last:
                    climbs.append(
                        call(
                            lambda *refs, bit=bit: climb_kernel(many, size, bit, *refs),
                            [shape((part + up16(2 * many), half), BF16)],
                            0.5,
                            (climbs[-1], arrived[-1]),
                            after=held,
                        )[0]
                    )
                bit *= 2
            later = (climbs[-1],)
        dxs.append(dx)
        exs.append(ex)
        owns.append(own)
    db, dc = call(
        close_kernel,
        [shape((length, half), F32), shape((length, half), BF16)],
        0.3,
        (mixed, bc, carried),
    )

    held = (dc,)
    if n_chip == 4:
        over_x = xored(joined([xt[1], over_y], later, [(0, x_rows), (x_rows, 2 * x_rows)]), "tm", 2)
        columns_in = [xt[0], over_x, over_y]
        places = [(0, 0), (1, 0), (2, 0), (1, x_rows)]
        held += (over_x,)
    else:
        columns_in = chips(xt)
        places = [(i, 0) for i in range(n_chip)]
    if merge:
        high = xored(joined([outs[3]], later), "dp", 2)
        near = xored(outs[1], "dp", 1)
        held += (high, near)
    r_own, r_send = call(
        lambda *refs: carry_kernel(many, size, len(arrived), *refs),
        [shape((part, half), BF16)] * 2,
        0.5,
        (*arrived, keep, recv),
        after=held,
    )
    r_recv = swapped(r_send)
    d_bc = call(db_kernel, [shape((length, columns), BF16)], 0.3, (xs, r_own, r_recv, db, dc))[0]
    d_bcs = [d_bc.reshape(1, length, columns)]
    while 2 ** (len(d_bcs) - 1) < n_chip:
        level = 2 ** (len(d_bcs) - 1)
        sent = d_bcs[0] if level == 1 else joined(d_bcs)
        d_bcs.append(xored(sent, "tm", 2 * level))
    d_in, d_decay, d_step = call(
        lambda *refs: finish_kernel(parts, *refs),
        [
            shape((length, width), BF16),
            shape((heads, length), F32),
            shape((heads, length), F32),
        ],
        3.0,
        (x, bc, cumt, stept, cum, steps, h_in, r_own, r_recv, w_whole, d_bc,
         *dxs, *exs, *owns),
        scratch=[pltpu.VMEM((width, half), BF16), pltpu.VMEM((heads, half), F32)],
    )
    w_rows = width // (2 * n_chip)
    term, term_send = call(
        lambda *refs: term_kernel(places, len(columns_in), *refs),
        [shape((w_rows, columns), F32), shape((w_rows, columns), BF16)],
        0.5,
        (*columns_in, *d_bcs),
        after=(d_in,),
        scratch=[pltpu.VMEM((2, w_rows, columns), F32)],
    )
    final = call(
        deal_kernel,
        [shape((w_rows // n_dp, columns), F32)]
        + [shape((w_rows // n_dp, columns), BF16)] * (n_dp - 1),
        0.3,
        (term, swapped(term_send)),
        scratch=[pltpu.VMEM((n_dp, w_rows // n_dp, columns), F32)],
    )
    w_bc_grad = final[0]
    for s in range(1, n_dp):
        w_bc_grad = w_bc_grad + xored(final[s], "dp", s).astype(F32)

    if merge:
        ranges = [(near_rows, low.shape[0]), (0, high.shape[0])]
        last = xored(joined([low, high], (r_own,), ranges), "dp", 1)
        pieces = [outs[0], near, low, high, last]
        sent = [near, low, last]
        ranges = [(0, near_rows), (0, near_rows), (hidden, hidden + near_rows)]
    else:
        sent = [xored(o, "dp", s + 1) for s, o in enumerate(outs[2:])]
        pieces = [*gathered(outs[0], "dp", n_dp), outs[1], *sent]
        ranges = None
    far = swapped(stacked(sent, (term,), ranges))
    w_down_grad = call(
        lambda *refs: down_kernel(n_dp, flip, merge, capacity, grad_rows, *refs),
        [shape((hidden, piece), BF16)],
        1.0,
        (*pieces, rows_b, far),
        after=(final[0],),
    )[0]
    return (d_in[None], d_decay.T[None], d_step.T[None], w_bc_grad, w_down_grad[None])


def solution(mesh):
    in_specs = (
        P("dp", "tm", None),
        P("dp", "tm", None),
        P("dp", None),
        P("dp", "tm", None),
        P("dp", "tm", None),
        P("dp", "tm", None, None, None),
        P(None, None, "tm"),
        P(None, None, "tm"),
        P("dp", None, "tm"),
        P("dp", "tm"),
        P("dp", None, "tm"),
    )
    out_specs = (
        P("dp", "tm", None),
        P("dp", "tm", None),
        P("dp", "tm", None),
        P(("tm", "dp"), None),
        P(None, "tm", "dp"),
    )
    return jax.shard_map(
        per_device, mesh=mesh, in_specs=in_specs, out_specs=out_specs, check_vma=False
    )
```

```python
import jax
import jax.numpy as jnp
from jax import lax
from jax.experimental import pallas as pl
from jax.experimental.pallas import tpu as pltpu
from jax.sharding import PartitionSpec as P

HI = lax.Precision.HIGHEST
F32 = jnp.float32
BF16 = jnp.bfloat16
LANES = 128


def dot(a, b, ca, cb, precision=None):
    return lax.dot_general(
        a, b, (((ca,), (cb,)), ((), ())), precision=precision, preferred_element_type=F32
    )


def iota(dims, axis):
    return lax.broadcasted_iota(jnp.int32, dims, axis)


def where_one(mask):
    return jnp.where(mask, 1.0, 0.0)


def triangle(n, keep):
    return where_one(keep(iota((n, n), 0), iota((n, n), 1))).astype(F32)


def halves(values, axis=1):
    high = values.astype(BF16)
    low = (values - high.astype(F32)).astype(BF16)
    return jnp.concatenate([high, low], axis=axis)


def to_lanes(j, size):
    dims = (LANES, LANES)
    one = where_one(iota(dims, 0) == iota(dims, 1) // size + j * (LANES // size)).astype(BF16)
    return jnp.concatenate([one, one], axis=0)


def to_heads(j, heads, size):
    dims = (heads, LANES)
    one = where_one(iota(dims, 0) == iota(dims, 1) // size + j * (LANES // size)).astype(BF16)
    return jnp.concatenate([one, one], axis=1)


def up16(n):
    return -(-n // 16) * 16


def call(kernel, outs, cost, args, after=(), scratch=(), limit=14, fetch=()):
    n_in, n_after, n_out = len(args), len(after), len(outs)
    fetch = tuple(fetch)

    def body(*refs):
        ins = list(refs[:n_in])
        rest = refs[n_in + n_after :]
        if fetch:
            sems = rest[-1]
            held = rest[len(rest) - 1 - len(fetch) : -1]
            rest = rest[: len(rest) - 1 - len(fetch)]
            copies = []
            for i, (index, ref) in enumerate(zip(fetch, held)):
                copies.append(pltpu.make_async_copy(ins[index], ref, sems.at[i]))
                ins[index] = ref
            for copy in copies:
                copy.start()
            for copy in copies:
                copy.wait()
        kernel(*ins, *rest)

    specs = [
        pl.BlockSpec(memory_space=pltpu.HBM if i in fetch else pltpu.VMEM) for i in range(n_in)
    ]
    held = [pltpu.VMEM(args[i].shape, args[i].dtype) for i in fetch]
    if fetch:
        held.append(pltpu.SemaphoreType.DMA((len(fetch),)))
    return pl.pallas_call(
        body,
        out_shape=outs,
        in_specs=specs + [pl.BlockSpec(memory_space=pl.ANY)] * n_after,
        out_specs=[pl.BlockSpec(memory_space=pltpu.VMEM)] * n_out,
        scratch_shapes=list(scratch) + held,
        cost_estimate=pl.CostEstimate(
            flops=int(cost * 3e9), bytes_accessed=1000, transcendentals=0
        ),
        compiler_params=pltpu.CompilerParams(vmem_limit_bytes=limit * 1024 * 1024),
    )(*args, *after)


def shape(dims, kind):
    return jax.ShapeDtypeStruct(dims, kind)


def core_and_chip():
    place = lax.axis_index("tm")
    return lax.rem(place, 2), lax.div(place, 2), lax.axis_size("tm") // 2


def rows_at(index, size, align=16):
    return pl.ds(pl.multiple_of(index * size, align), size)


def picked(x_ref, dy_ref, slot_ref, count_ref, gate_ref, rows_ref, out_refs):
    length, width = x_ref.shape
    slots = slot_ref.shape[1]
    hit = iota((length, slots), 0) == slot_ref[...]
    live = iota((1, slots), 1) < count_ref[...]
    weight = jnp.where(live, gate_ref[...].astype(F32), 0.0)
    rows = dot(where_one(hit).astype(BF16), x_ref[...], 0, 0).astype(BF16)
    for t in range(width // LANES):
        rows_ref[t * slots : (t + 1) * slots, :] = rows[:, t * LANES : (t + 1) * LANES]
    grads = dot(jnp.where(hit, weight, 0.0).astype(BF16), dy_ref[...], 0, 0).astype(BF16)
    n_dp = len(out_refs) - 1
    held = out_refs[-1]
    piece = width // n_dp
    for i in range(n_dp):
        for t, low in enumerate(range(i * piece, (i + 1) * piece, LANES)):
            block = grads[:, low : min(low + LANES, (i + 1) * piece)]
            if block.shape[1] < LANES:
                fill = jnp.zeros((slots, LANES - block.shape[1]), BF16)
                block = jnp.concatenate([block, fill], axis=1)
            held[i, t * slots : (t + 1) * slots, :] = block
    place = lax.axis_index("dp")
    for s, out in enumerate(out_refs[:-1]):
        out[...] = held[place ^ s]


def high_low(values):
    high = values.astype(BF16).astype(F32)
    return [high, values - high]


def prep_kernel(
    n_dp, x_ref, dy_ref, ldt_ref, stept_ref, h_ref, slot_ref, count_ref, gate_ref,
    cumt_ref, cum_ref, step_ref, dyt_ref, xs_ref, carried_ref, rows_ref, *rest,
):
    outs, xt_ref, held_ref = rest[n_dp:-2], rest[-2], rest[-1]
    length, width = x_ref.shape
    heads = ldt_ref.shape[0]
    size = width // heads
    _, chip, n_chip = core_and_chip()
    picked(x_ref, dy_ref, slot_ref, count_ref, gate_ref, rows_ref, (*rest[:n_dp], held_ref))
    pad = jnp.zeros((LANES - heads, length), F32)
    cumt = dot(ldt_ref[...], triangle(length, lambda a, b: a <= b), 1, 0, HI)
    cumt_ref[...] = cumt
    cum = jnp.concatenate([cumt, pad], axis=0).T
    step = jnp.concatenate([stept_ref[...], pad], axis=0).T
    cum_ref[...] = cum
    step_ref[...] = step
    start = jnp.exp(cum)
    into_end = jnp.exp(cum[length - 1 : length] - cum) * step
    table = jnp.concatenate([halves(start), halves(into_end)], axis=0)
    carried = jnp.zeros(carried_ref.shape, F32)
    for j in range(width // LANES):
        span = slice(j * LANES, (j + 1) * LANES)
        scale = dot(table, to_lanes(j, size), 1, 0)
        x_f = x_ref[:, span].astype(F32)
        xt_ref[span, :] = x_f.T.astype(BF16)
        xs_ref[:, span] = (x_f * scale[length:]).astype(BF16)
        dys = dy_ref[:, span].astype(F32) * scale[:length]
        dyt_ref[span, :] = dys.T.astype(BF16)
        carried = carried + dot(dys.astype(BF16), h_ref[span, :], 1, 0)
    carried_ref[...] = carried
    decay = jnp.broadcast_to(jnp.exp(cumt[:, length - 1 : length]), (heads, LANES))
    dyt_ref[width : width + 2 * heads, :] = jnp.concatenate(high_low(decay), axis=0).astype(BF16)
    block = width // n_chip
    s = 0
    for out in outs:
        for start in range(0, out.shape[0], block):
            out[start : start + block, :] = xt_ref[rows_at(chip ^ s, block), :]
            s += 1


def join_kernel(ranges, *refs):
    out, at = refs[-1], 0
    for ref, (start, stop) in zip(refs, ranges):
        out[at : at + stop - start] = ref[start:stop]
        at += stop - start


def joined(arrays, after=(), ranges=None):
    ranges = ranges or [(0, a.shape[0]) for a in arrays]
    dims = (sum(stop - start for start, stop in ranges), *arrays[0].shape[1:])
    return call(
        lambda *refs: join_kernel(ranges, *refs),
        [shape(dims, arrays[0].dtype)],
        0.2,
        tuple(arrays),
        after=after,
    )[0]


def stacked(arrays, after=(), ranges=None):
    count = len(arrays)
    out = joined(arrays, after, ranges)
    return out.reshape(count, out.shape[0] // count, *out.shape[1:])


def project_kernel(n_mine, many, *refs):
    x_ref, dyt_ref, own_ref = refs[:3]
    mine, other = refs[3 : 3 + n_mine], refs[3 + n_mine]
    w_ref, bc_ref, keep_ref, send_ref = refs[4 + n_mine :]
    core, _, _ = core_and_chip()
    place, n_dp = lax.axis_index("dp"), lax.axis_size("dp")
    share = own_ref.shape[0]
    half = share // 2
    w_ref[rows_at(place, share), :] = own_ref[...]
    for i in range(n_mine):
        source = place ^ (i + 1)
        w_ref[rows_at(source * 2 + core, half), :] = mine[i][...]
        w_ref[rows_at(source * 2 + 1 - core, half), :] = other[i]
    bc = dot(x_ref[...], w_ref[...], 1, 0).astype(BF16)
    bc_ref[...] = bc
    c_rows = bc[:, LANES:]
    width = x_ref.shape[1]
    part = width // 2
    for ref, index in ((keep_ref, core), (send_ref, 1 - core)):
        ref[:part, :] = dot(dyt_ref[rows_at(index, part), :], c_rows, 1, 0).astype(BF16)
        table = dyt_ref[width : width + 4 * many, :].astype(F32)
        quarter = [table[i * many : (i + 1) * many] for i in range(4)]
        high = jnp.where(index == 0, quarter[0], quarter[1])
        low = jnp.where(index == 0, quarter[2], quarter[3])
        fill = jnp.zeros((ref.shape[0] - part - 2 * many, LANES), F32)
        ref[part:, :] = jnp.concatenate([high, low, fill], axis=0).astype(BF16)


def pair(keep_ref, recv_ref, many, size, head):
    core, _, _ = core_and_chip()
    part = many * size
    both = []
    for ref in (keep_ref, recv_ref):
        extra = ref[part:, :].astype(F32)
        decay = extra[head : head + 1] + extra[many + head : many + head + 1]
        both.append((ref[head * size : (head + 1) * size, :].astype(F32), decay))
    first = jax.tree.map(lambda a, b: jnp.where(core == 0, a, b), both[0], both[1])
    second = jax.tree.map(lambda a, b: jnp.where(core == 0, b, a), both[0], both[1])
    return first, second


def payload(ref, many, states, decays):
    size = states[0].shape[0]
    for head, state in enumerate(states):
        ref[head * size : (head + 1) * size, :] = state.astype(BF16)
    decay = jnp.concatenate(decays, axis=0)
    high = decay.astype(BF16).astype(F32)
    fill = jnp.zeros((ref.shape[0] - many * size - 2 * many, LANES), F32)
    extra = jnp.concatenate([high, decay - high, fill], axis=0)
    ref[many * size :, :] = extra.astype(BF16)


def loaded(ref, many, size, head):
    extra = ref[many * size :, :].astype(F32)
    decay = extra[head : head + 1] + extra[many + head : many + head + 1]
    return ref[head * size : (head + 1) * size, :].astype(F32), decay


def combine_kernel(many, size, keep_ref, recv_ref, out_ref):
    states, decays = [], []
    for head in range(many):
        (g0, a0), (g1, a1) = pair(keep_ref, recv_ref, many, size, head)
        states.append(g0 + a0 * g1)
        decays.append(a0 * a1)
    payload(out_ref, many, states, decays)


def pick_side(upper, mine, theirs):
    return jnp.where(upper, theirs, mine), jnp.where(upper, mine, theirs)


def climb_kernel(many, size, bit, mine_ref, recv_ref, out_ref):
    _, chip, _ = core_and_chip()
    upper = lax.rem(lax.div(chip, bit), 2) == 1
    states, decays = [], []
    for head in range(many):
        t_mine, a_mine = loaded(mine_ref, many, size, head)
        t_recv, a_recv = loaded(recv_ref, many, size, head)
        t_low, t_high = pick_side(upper, t_mine, t_recv)
        a_low, a_high = pick_side(upper, a_mine, a_recv)
        states.append(t_low + a_low * t_high)
        decays.append(a_low * a_high)
    payload(out_ref, many, states, decays)


def carry_kernel(many, size, levels, *refs):
    core, chip, _ = core_and_chip()
    recvs = refs[:levels]
    keep_ref, recv_ref, own_ref, send_ref = refs[levels:]
    for head in range(many):
        span = slice(head * size, (head + 1) * size)
        carry, reach = None, None
        for level, ref in enumerate(recvs):
            state, decay = loaded(ref, many, size, head)
            lower = lax.rem(lax.div(chip, 2**level), 2) == 0
            state = jnp.where(lower, state, 0.0)
            decay = jnp.where(lower, decay, 1.0)
            carry = state if carry is None else carry + reach * state
            reach = decay if reach is None else reach * decay
        _, (g1, a1) = pair(keep_ref, recv_ref, many, size, head)
        second = carry
        first = g1 + a1 * second
        own_ref[span, :] = jnp.where(core == 0, first, second).astype(BF16)
        send_ref[span, :] = jnp.where(core == 0, second, first).astype(BF16)


def intra_kernel(
    first, many, x_ref, dy_ref, bc_ref, cumt_ref, cum_ref, step_ref, h_ref, before_ref,
    dx_ref, mixed_ref, ex_ref, own_ref, rowm_ref,
):
    length, width = x_ref.shape
    heads = cumt_ref.shape[0]
    size = width // heads
    per = LANES // size
    upper = iota((length, length), 0) <= iota((length, length), 1)
    b_rows, c_rows = bc_ref[:, :LANES], bc_ref[:, LANES:]
    scores = dot(b_rows, c_rows, 1, 1)
    lane = iota((1, LANES), 1)
    lane_bf = [where_one(lane // size == i).astype(BF16) for i in range(per)]
    mixed = before_ref[...]
    own = jnp.zeros((length, LANES), F32)
    reach = jnp.zeros((heads, length), F32)
    for j in range(first, first + many):
        span = slice(j * LANES, (j + 1) * LANES)
        out_span = slice((j - first) * LANES, (j - first + 1) * LANES)
        x_p = x_ref[:, span]
        dy_p = dy_ref[:, span]
        dy_h = jnp.concatenate([dy_p * m for m in lane_bf], axis=0)
        cross = dot(x_p, dy_h, 1, 1)
        kern = []
        wide = None
        for i in range(per):
            h = j * per + i
            diff = cumt_ref[h : h + 1, :] - cum_ref[:, h : h + 1]
            seg = jnp.exp(jnp.where(upper, diff, -1e30))
            kern.append((seg * scores).astype(BF16))
            step = jnp.broadcast_to(step_ref[:, h : h + 1], (length, LANES))
            wide = step if i == 0 else jnp.where(lane < i * size, wide, step)
            scaled = seg * cross[:, i * length : (i + 1) * length] * step
            mixed = mixed + scaled
            full = scaled * scores
            rowm_ref[h : h + 1, :] = jnp.sum(full, axis=0, keepdims=True)
            own = jnp.where(lane == h, jnp.sum(full, axis=1, keepdims=True), own)
        back = dot(jnp.concatenate(kern, axis=1), dy_h, 1, 0)
        dx_ref[:, out_span] = back * wide
        seen = dy_p.astype(F32) * dot(c_rows, h_ref[span, :], 1, 1)
        reach = reach + dot(to_heads(j, heads, size), halves(seen), 1, 1)
    mixed_ref[...] = mixed
    rows = slice(first * per, (first + many) * per)
    own = own.T[rows]
    own_ref[...] = own
    ex_ref[...] = rowm_ref[rows, :] + jnp.exp(cumt_ref[rows, :]) * reach[rows] - own


def close_kernel(mixed_ref, bc_ref, carried_ref, db_ref, dc_ref):
    mixed = mixed_ref[...].astype(BF16)
    db_ref[...] = dot(mixed, bc_ref[:, LANES:], 1, 0)
    dc_ref[...] = (dot(mixed, bc_ref[:, :LANES], 0, 0) + carried_ref[...]).astype(BF16)


def db_kernel(xs_ref, own_ref, recv_ref, db_ref, dc_ref, out_ref):
    core, _, _ = core_and_chip()
    half = db_ref.shape[1]
    part = own_ref.shape[0]
    total = db_ref[...]
    for ref, index in ((own_ref, core), (recv_ref, 1 - core)):
        total = total + dot(xs_ref[:, rows_at(index, part, LANES)], ref[...], 1, 0)
    out_ref[:, :half] = total.astype(BF16)
    out_ref[:, half:] = dc_ref[...]


def finish_kernel(parts, *refs):
    (x_ref, bc_ref, cumt_ref, stept_ref, cum_ref, step_ref, h_ref, own_ref, recv_ref,
     w_ref, dbc_ref) = refs[:11]
    dx_refs, ex_refs, st_refs = (refs[11 + i * parts : 11 + (i + 1) * parts] for i in range(3))
    in_ref, decay_ref, grad_ref, r_ref, edge_ref = refs[11 + 3 * parts :]
    core, _, _ = core_and_chip()
    length, width = x_ref.shape
    heads = cumt_ref.shape[0]
    size = width // heads
    part = width // 2
    r_ref[rows_at(core, part), :] = own_ref[...]
    r_ref[rows_at(1 - core, part), :] = recv_ref[...]
    cum = cum_ref[...]
    table = halves(jnp.exp(cum[length - 1 : length] - cum) * step_ref[...])
    seen = jnp.zeros((heads, length), F32)
    b_rows = bc_ref[:, :LANES]
    d_bc = dbc_ref[...]
    for j in range(width // LANES):
        span = slice(j * LANES, (j + 1) * LANES)
        local = dx_refs[j * LANES // (width // parts)]
        start = j * LANES % (width // parts)
        r_tile = r_ref[span, :]
        reach = dot(b_rows, r_tile, 1, 1)
        d_in = local[:, start : start + LANES] + dot(table, to_lanes(j, size), 1, 0) * reach
        d_in = d_in + dot(d_bc, w_ref[span, :], 1, 1)
        in_ref[:, span] = d_in.astype(BF16)
        product = x_ref[:, span].astype(F32) * reach
        seen = seen + dot(to_heads(j, heads, size), halves(product), 1, 1)
        edge = r_tile.astype(F32) * h_ref[span, :].astype(F32)
        for i in range(LANES // size):
            h = j * (LANES // size) + i
            edge_ref[h : h + 1, :] = jnp.sum(
                edge[i * size : (i + 1) * size], axis=0, keepdims=True
            )
    cumt = cumt_ref[...]
    total = cumt[:, length - 1 : length]
    to_end = jnp.exp(total - cumt)
    step = stept_ref[...]
    own = jnp.concatenate([r[...] for r in st_refs], axis=0)
    excess = jnp.concatenate([r[...] for r in ex_refs], axis=0)
    grad_ref[...] = own / step + to_end * seen
    edge = jnp.exp(total) * jnp.sum(edge_ref[...], axis=1, keepdims=True)
    decay_ref[...] = (
        dot(excess, triangle(length, lambda a, b: a >= b), 1, 0, HI)
        + dot(to_end * step * seen, triangle(length, lambda a, b: a < b), 1, 0, HI)
        + edge
    )


def term_kernel(places, n_columns, *refs):
    columns, pieces = refs[:n_columns], refs[n_columns:-3]
    keep_ref, send_ref, held = refs[-3:]
    pieces = [(p, i) for p in pieces for i in range(p.shape[0])]
    rows = 2 * keep_ref.shape[0]
    core, _, _ = core_and_chip()
    total = None
    for (a, start), (b, i) in zip(places, pieces):
        part = dot(columns[a][start : start + rows, :], b[i], 1, 0)
        total = part if total is None else total + part
    block = keep_ref.shape[0]
    held[0] = total[:block]
    held[1] = total[block:]
    keep_ref[...] = held[core]
    send_ref[...] = held[1 - core].astype(BF16)


def deal_kernel(keep_ref, recv_ref, own_ref, *refs):
    outs, held = refs[:-1], refs[-1]
    place, n_dp = lax.axis_index("dp"), lax.axis_size("dp")
    total = keep_ref[...] + recv_ref[...].astype(F32)
    share = own_ref.shape[0]
    for i in range(n_dp):
        held[i] = total[i * share : (i + 1) * share]
    own_ref[...] = held[place]
    for s, out in enumerate(outs):
        out[...] = held[place ^ (s + 1)].astype(BF16)


def expert_kernel(flip, slots, a_ref, b_ref, gate_ref, up_ref, out_ref, *scratch):
    rows_ref, gate_acc, up_acc = scratch
    step = pl.program_id(0)
    n_chip = a_ref.shape[0]

    @pl.when(step == 0)
    def _():
        for half, ref in enumerate((a_ref, b_ref)):
            for i in range(n_chip):
                row = (half * n_chip + i) * slots
                for t in range(rows_ref.shape[1] // LANES):
                    rows_ref[row : row + slots, t * LANES : (t + 1) * LANES] = ref[
                        i, t * slots : (t + 1) * slots, :
                    ]
        gate_acc[...] = jnp.zeros_like(gate_acc)
        up_acc[...] = jnp.zeros_like(up_acc)

    depth = gate_ref.shape[0]
    rows = rows_ref[:, rows_at(step, depth, LANES)]
    gate_acc[...] += dot(rows, gate_ref[...], 1, 0)
    up_acc[...] += dot(rows, up_ref[...], 1, 0)

    @pl.when(step == pl.num_programs(0) - 1)
    def _():
        weighted = jax.nn.silu(gate_acc[...]) * up_acc[...]
        out_ref[...] = (weighted.T if flip else weighted).astype(BF16)


def expert(a, b, w_gate, w_up, slots, flip, after):
    n_chip = a.shape[0]
    total = 2 * n_chip * slots
    width, hidden = w_gate.shape
    depth = 512
    out = (hidden, total) if flip else (total, hidden)

    def body(*refs):
        expert_kernel(flip, slots, *refs[:4], *refs[4 + len(after) :])

    whole = pl.BlockSpec(a.shape, lambda i: (0, 0, 0))
    block = pl.BlockSpec((depth, hidden), lambda i: (i, 0))
    return pl.pallas_call(
        body,
        out_shape=shape(out, BF16),
        grid=(width // depth,),
        in_specs=[whole, whole, block, block]
        + [pl.BlockSpec(memory_space=pl.ANY)] * len(after),
        out_specs=pl.BlockSpec(out, lambda i: (0, 0)),
        scratch_shapes=[
            pltpu.VMEM((total, width), BF16),
            pltpu.VMEM((total, hidden), F32),
            pltpu.VMEM((total, hidden), F32),
        ],
        cost_estimate=pl.CostEstimate(
            flops=int(3e9), bytes_accessed=1000, transcendentals=0
        ),
        compiler_params=pltpu.CompilerParams(vmem_limit_bytes=20 * 1024 * 1024),
    )(a, b, w_gate, w_up, *after)


def down_kernel(n_dp, flip, slots, grad_rows, *refs):
    pieces = refs[:n_dp]
    a_ref, b_ref, out_ref = refs[n_dp:]
    n_chip = a_ref.shape[0]
    piece = out_ref.shape[1]
    base = a_ref.shape[1] - n_dp * grad_rows
    total = None
    for s in range(n_dp):
        columns = []
        for t in range(grad_rows // slots):
            row = base + s * grad_rows + t * slots
            blocks = [r[i, row : row + slots, :] for r in (a_ref, b_ref) for i in range(n_chip)]
            columns.append(jnp.concatenate(blocks, axis=0))
        right = jnp.concatenate(columns, axis=1)[:, :piece]
        part = dot(pieces[s][...], right, 1 if flip else 0, 0)
        total = part if total is None else total + part
    out_ref[...] = total.astype(BF16)


def xored(array, axis, mask):
    count = lax.axis_size(axis)
    return lax.ppermute(array, axis, [(i, i ^ mask) for i in range(count)])


def swapped(array):
    return xored(array, "tm", 1)


def chips(arrays):
    return [arrays[0]] + [xored(a, "tm", 2 * s) for s, a in enumerate(arrays) if s]


def gathered(array, axis, count):
    if count == 1:
        return [array]
    far = xored(array, axis, count // 2)
    return gathered(array, axis, count // 2) + gathered(far, axis, count // 2)


def per_device(
    layer_in,
    out_grad,
    w_bc,
    log_decay,
    step,
    saved_states,
    w_gate,
    w_up,
    slot_rows,
    slot_counts,
    slot_gates,
):
    n_dp = lax.axis_size("dp")
    core, chip, n_chip = core_and_chip()
    x = layer_in[0]
    dy = out_grad[0]
    length, width = x.shape
    heads = log_decay.shape[2]
    size = width // heads
    share, columns = w_bc.shape
    half = columns // 2
    ldt = log_decay[0].T
    stept = step[0].T
    h_in = saved_states[0, 0].reshape(width, half)
    capacity = slot_rows.shape[2]
    piece = width // n_dp
    part = width // 2
    many = heads // 2
    flip = w_gate.shape[2] % LANES == 0

    grad_rows = -(-piece // LANES) * capacity
    w_half = lax.dynamic_slice_in_dim(w_bc, core * (share // 2), share // 2, 0)

    in_rows = width // LANES * capacity
    blocks = [1, 1, 2] if n_chip == 4 else [1] * n_chip
    cumt, cum, steps, dyt, xs, carried, rows, *xt = call(
        lambda *refs: prep_kernel(n_dp, *refs),
        [
            shape((heads, length), F32),
            shape((length, LANES), F32),
            shape((length, LANES), F32),
            shape((width + up16(2 * heads), length), BF16),
            shape((length, width), BF16),
            shape((length, half), F32),
        ]
        + [shape((in_rows, LANES), BF16)]
        + [shape((grad_rows, LANES), BF16)] * n_dp
        + [shape((k * width // n_chip, length), BF16) for k in blocks],
        2.0,
        (x, dy, ldt, stept, h_in, slot_rows[0], slot_counts, slot_gates[0]),
        scratch=[
            pltpu.VMEM((width, length), BF16),
            pltpu.VMEM((n_dp, grad_rows, LANES), BF16),
        ],
        fetch=(0, 1, 2, 3, 4),
        limit=60,
    )
    w_far = xored(w_half, "dp", n_dp // 2)
    mine = gathered(w_half, "dp", n_dp // 2)[1:]
    mine += gathered(joined([w_far], after=(cumt,)), "dp", n_dp // 2)
    deals, xt = xt[:n_dp], xt[n_dp:]
    deals = deals[:1] + [xored(d, "dp", s + 1) for s, d in enumerate(deals[1:])]
    payload = joined([rows, *deals])
    rows_in = chips([payload] * n_chip)
    other = swapped(stacked(mine, after=(payload,)))
    w_whole, bc, keep, send = call(
        lambda *refs: project_kernel(n_dp - 1, many, *refs),
        [
            shape((width, columns), BF16),
            shape((length, columns), BF16),
            shape((part + up16(2 * many), half), BF16),
            shape((part + up16(2 * many), half), BF16),
        ],
        1.0,
        (x, dyt, w_bc, *mine, other),
    )
    recv = swapped(send)
    hidden = w_gate.shape[2]
    climbs = [
        call(
            lambda *refs: combine_kernel(many, size, *refs),
            [shape((part + up16(2 * many), half), BF16)],
            0.5,
            (keep, recv),
        )[0]
    ]
    rows_a = stacked(rows_in, after=(climbs[0],))
    rows_b = swapped(rows_a)
    weighted = expert(rows_a, rows_b, w_gate[0], w_up[0], capacity, flip, (climbs[0],))
    if n_chip == 4:
        x_rows = width // n_chip
        over_y = xored(xt[2], "tm", 4)

    parts = 2
    tiles = width // LANES // parts
    dxs, exs, owns = [], [], []
    later = ()
    mixed = jnp.zeros((length, length), F32)
    for i in range(parts):
        dx, mixed, ex, own = call(
            lambda *refs, i=i: intra_kernel(i * tiles, tiles, *refs),
            [
                shape((length, width // parts), F32),
                shape((length, length), F32),
                shape((heads // parts, length), F32),
                shape((heads // parts, length), F32),
            ],
            3.0,
            (x, dy, bc, cumt, cum, steps, h_in, mixed),
            after=later,
            scratch=[pltpu.VMEM((heads, length), F32)],
        )
        if i == 0:
            held = (dx, weighted, *((over_y,) if n_chip == 4 else ()))
            arrived = []
            bit = 1
            while bit < n_chip:
                last = bit * 2 == n_chip
                moves = [
                    (k, k ^ (2 * bit)) for k in range(2 * n_chip) if not last or k & (2 * bit)
                ]
                arrived.append(lax.ppermute(climbs[-1], "tm", moves))
                if not last:
                    climbs.append(
                        call(
                            lambda *refs, bit=bit: climb_kernel(many, size, bit, *refs),
                            [shape((part + up16(2 * many), half), BF16)],
                            0.5,
                            (climbs[-1], arrived[-1]),
                            after=held,
                        )[0]
                    )
                bit *= 2
            later = (climbs[-1],)
        dxs.append(dx)
        exs.append(ex)
        owns.append(own)
    db, dc = call(
        close_kernel,
        [shape((length, half), F32), shape((length, half), BF16)],
        0.3,
        (mixed, bc, carried),
    )

    held = (dc,)
    if n_chip == 4:
        over_x = xored(joined([xt[1], over_y], later, [(0, x_rows), (x_rows, 2 * x_rows)]), "tm", 2)
        columns_in = [xt[0], over_x, over_y]
        places = [(0, 0), (1, 0), (2, 0), (1, x_rows)]
        held += (over_x,)
    else:
        columns_in = chips(xt)
        places = [(i, 0) for i in range(n_chip)]
    far = xored(weighted, "dp", n_dp // 2)
    near = gathered(weighted, "dp", n_dp // 2)
    held += (far, *near[1:])
    r_own, r_send = call(
        lambda *refs: carry_kernel(many, size, len(arrived), *refs),
        [shape((part, half), BF16)] * 2,
        0.5,
        (*arrived, keep, recv),
        after=held,
    )
    r_recv = swapped(r_send)
    fars = gathered(joined([far], (r_own,)), "dp", n_dp // 2)
    d_bc = call(db_kernel, [shape((length, columns), BF16)], 0.3, (xs, r_own, r_recv, db, dc))[0]
    d_bcs = [d_bc.reshape(1, length, columns)]
    while 2 ** (len(d_bcs) - 1) < n_chip:
        level = 2 ** (len(d_bcs) - 1)
        sent = d_bcs[0] if level == 1 else joined(d_bcs)
        d_bcs.append(xored(sent, "tm", 2 * level))
    d_in, d_decay, d_step = call(
        lambda *refs: finish_kernel(parts, *refs),
        [
            shape((length, width), BF16),
            shape((heads, length), F32),
            shape((heads, length), F32),
        ],
        3.0,
        (x, bc, cumt, stept, cum, steps, h_in, r_own, r_recv, w_whole, d_bc,
         *dxs, *exs, *owns),
        scratch=[pltpu.VMEM((width, half), BF16), pltpu.VMEM((heads, half), F32)],
    )
    w_rows = width // (2 * n_chip)
    term, term_send = call(
        lambda *refs: term_kernel(places, len(columns_in), *refs),
        [shape((w_rows, columns), F32), shape((w_rows, columns), BF16)],
        0.5,
        (*columns_in, *d_bcs),
        after=(d_in, *fars[1:]),
        scratch=[pltpu.VMEM((2, w_rows, columns), F32)],
    )
    final = call(
        deal_kernel,
        [shape((w_rows // n_dp, columns), F32)]
        + [shape((w_rows // n_dp, columns), BF16)] * (n_dp - 1),
        0.3,
        (term, swapped(term_send)),
        scratch=[pltpu.VMEM((n_dp, w_rows // n_dp, columns), F32)],
    )
    w_bc_grad = final[0]
    for s in range(1, n_dp):
        w_bc_grad = w_bc_grad + xored(final[s], "dp", s).astype(F32)

    w_down_grad = call(
        lambda *refs: down_kernel(n_dp, flip, capacity, grad_rows, *refs),
        [shape((hidden, piece), BF16)],
        1.0,
        (*near, *fars, rows_a, rows_b),
        after=(final[0],),
    )[0]
    return (d_in[None], d_decay.T[None], d_step.T[None], w_bc_grad, w_down_grad[None])


def solution(mesh):
    in_specs = (
        P("dp", "tm", None),
        P("dp", "tm", None),
        P("dp", None),
        P("dp", "tm", None),
        P("dp", "tm", None),
        P("dp", "tm", None, None, None),
        P(None, None, "tm"),
        P(None, None, "tm"),
        P("dp", None, "tm"),
        P("dp", "tm"),
        P("dp", None, "tm"),
    )
    out_specs = (
        P("dp", "tm", None),
        P("dp", "tm", None),
        P("dp", "tm", None),
        P(("tm", "dp"), None),
        P(None, "tm", "dp"),
    )
    return jax.shard_map(
        per_device, mesh=mesh, in_specs=in_specs, out_specs=out_specs, check_vma=False
    )
```

```python
import jax
import jax.numpy as jnp
from jax import lax
from jax.experimental import pallas as pl
from jax.experimental.pallas import tpu as pltpu
from jax.sharding import PartitionSpec as P

HI = lax.Precision.HIGHEST
F32 = jnp.float32
BF16 = jnp.bfloat16
LANES = 128


def dot(a, b, ca, cb, precision=None):
    return lax.dot_general(
        a, b, (((ca,), (cb,)), ((), ())), precision=precision, preferred_element_type=F32
    )


def iota(dims, axis):
    return lax.broadcasted_iota(jnp.int32, dims, axis)


def where_one(mask):
    return jnp.where(mask, 1.0, 0.0)


def triangle(n, keep):
    return where_one(keep(iota((n, n), 0), iota((n, n), 1))).astype(F32)


def halves(values, axis=1):
    high = values.astype(BF16)
    low = (values - high.astype(F32)).astype(BF16)
    return jnp.concatenate([high, low], axis=axis)


def to_lanes(j, size):
    dims = (LANES, LANES)
    one = where_one(iota(dims, 0) == iota(dims, 1) // size + j * (LANES // size)).astype(BF16)
    return jnp.concatenate([one, one], axis=0)


def to_heads(j, heads, size):
    dims = (heads, LANES)
    one = where_one(iota(dims, 0) == iota(dims, 1) // size + j * (LANES // size)).astype(BF16)
    return jnp.concatenate([one, one], axis=1)


def up16(n):
    return -(-n // 16) * 16


def call(kernel, outs, cost, args, after=(), scratch=(), limit=14, fetch=()):
    n_in, n_after, n_out = len(args), len(after), len(outs)
    fetch = tuple(fetch)

    def body(*refs):
        ins = list(refs[:n_in])
        rest = refs[n_in + n_after :]
        if fetch:
            sems = rest[-1]
            held = rest[len(rest) - 1 - len(fetch) : -1]
            rest = rest[: len(rest) - 1 - len(fetch)]
            copies = []
            for i, (index, ref) in enumerate(zip(fetch, held)):
                copies.append(pltpu.make_async_copy(ins[index], ref, sems.at[i]))
                ins[index] = ref
            for copy in copies:
                copy.start()
            for copy in copies:
                copy.wait()
        kernel(*ins, *rest)

    specs = [
        pl.BlockSpec(memory_space=pltpu.HBM if i in fetch else pltpu.VMEM) for i in range(n_in)
    ]
    held = [pltpu.VMEM(args[i].shape, args[i].dtype) for i in fetch]
    if fetch:
        held.append(pltpu.SemaphoreType.DMA((len(fetch),)))
    return pl.pallas_call(
        body,
        out_shape=outs,
        in_specs=specs + [pl.BlockSpec(memory_space=pl.ANY)] * n_after,
        out_specs=[pl.BlockSpec(memory_space=pltpu.VMEM)] * n_out,
        scratch_shapes=list(scratch) + held,
        cost_estimate=pl.CostEstimate(
            flops=int(cost * 3e9), bytes_accessed=1000, transcendentals=0
        ),
        compiler_params=pltpu.CompilerParams(vmem_limit_bytes=limit * 1024 * 1024),
    )(*args, *after)


def shape(dims, kind):
    return jax.ShapeDtypeStruct(dims, kind)


def core_and_chip():
    place = lax.axis_index("tm")
    return lax.rem(place, 2), lax.div(place, 2), lax.axis_size("tm") // 2


def rows_at(index, size, align=16):
    return pl.ds(pl.multiple_of(index * size, align), size)


def picked(x_ref, dy_ref, slot_ref, count_ref, gate_ref, rows_ref, out_refs):
    length, width = x_ref.shape
    slots = slot_ref.shape[1]
    hit = iota((length, slots), 0) == slot_ref[...]
    live = iota((1, slots), 1) < count_ref[...]
    weight = jnp.where(live, gate_ref[...].astype(F32), 0.0)
    rows = dot(where_one(hit).astype(BF16), x_ref[...], 0, 0).astype(BF16)
    for t in range(width // LANES):
        rows_ref[t * slots : (t + 1) * slots, :] = rows[:, t * LANES : (t + 1) * LANES]
    grads = dot(jnp.where(hit, weight, 0.0).astype(BF16), dy_ref[...], 0, 0).astype(BF16)
    held = out_refs[-1]
    n_dp = held.shape[0]
    piece = width // n_dp
    for i in range(n_dp):
        for t, low in enumerate(range(i * piece, (i + 1) * piece, LANES)):
            block = grads[:, low : min(low + LANES, (i + 1) * piece)]
            if block.shape[1] < LANES:
                fill = jnp.zeros((slots, LANES - block.shape[1]), BF16)
                block = jnp.concatenate([block, fill], axis=1)
            held[i, t * slots : (t + 1) * slots, :] = block
    place = lax.axis_index("dp")
    s = 0
    for start in range(width // LANES * slots, rows_ref.shape[0], held.shape[1]):
        rows_ref[start : start + held.shape[1], :] = held[place ^ s]
        s += 1
    for out in out_refs[:-1]:
        for start in range(0, out.shape[0], held.shape[1]):
            out[start : start + held.shape[1], :] = held[place ^ s]
            s += 1


def high_low(values):
    high = values.astype(BF16).astype(F32)
    return [high, values - high]


def prep_kernel(
    n_deals, x_ref, dy_ref, ldt_ref, stept_ref, h_ref, slot_ref, count_ref, gate_ref,
    cumt_ref, cum_ref, step_ref, dyt_ref, xs_ref, carried_ref, rows_ref, *rest,
):
    outs, xt_ref, held_ref = rest[n_deals:-2], rest[-2], rest[-1]
    length, width = x_ref.shape
    heads = ldt_ref.shape[0]
    size = width // heads
    _, chip, n_chip = core_and_chip()
    picked(x_ref, dy_ref, slot_ref, count_ref, gate_ref, rows_ref, (*rest[:n_deals], held_ref))
    pad = jnp.zeros((LANES - heads, length), F32)
    cumt = dot(ldt_ref[...], triangle(length, lambda a, b: a <= b), 1, 0, HI)
    cumt_ref[...] = cumt
    cum = jnp.concatenate([cumt, pad], axis=0).T
    step = jnp.concatenate([stept_ref[...], pad], axis=0).T
    cum_ref[...] = cum
    step_ref[...] = step
    start = jnp.exp(cum)
    into_end = jnp.exp(cum[length - 1 : length] - cum) * step
    table = jnp.concatenate([halves(start), halves(into_end)], axis=0)
    carried = jnp.zeros(carried_ref.shape, F32)
    for j in range(width // LANES):
        span = slice(j * LANES, (j + 1) * LANES)
        scale = dot(table, to_lanes(j, size), 1, 0)
        x_f = x_ref[:, span].astype(F32)
        xt_ref[span, :] = x_f.T.astype(BF16)
        xs_ref[:, span] = (x_f * scale[length:]).astype(BF16)
        dys = dy_ref[:, span].astype(F32) * scale[:length]
        dyt_ref[span, :] = dys.T.astype(BF16)
        carried = carried + dot(dys.astype(BF16), h_ref[span, :], 1, 0)
    carried_ref[...] = carried
    decay = jnp.broadcast_to(jnp.exp(cumt[:, length - 1 : length]), (heads, LANES))
    dyt_ref[width : width + 2 * heads, :] = jnp.concatenate(high_low(decay), axis=0).astype(BF16)
    block = width // n_chip
    s = 0
    for out in outs:
        for start in range(0, out.shape[0], block):
            out[start : start + block, :] = xt_ref[rows_at(chip ^ s, block), :]
            s += 1


def join_kernel(ranges, *refs):
    out, at = refs[-1], 0
    for ref, (start, stop) in zip(refs, ranges):
        out[at : at + stop - start] = ref[start:stop]
        at += stop - start


def joined(arrays, after=(), ranges=None):
    ranges = ranges or [(0, a.shape[0]) for a in arrays]
    dims = (sum(stop - start for start, stop in ranges), *arrays[0].shape[1:])
    return call(
        lambda *refs: join_kernel(ranges, *refs),
        [shape(dims, arrays[0].dtype)],
        0.2,
        tuple(arrays),
        after=after,
    )[0]


def stacked(arrays, after=(), ranges=None):
    count = len(arrays)
    out = joined(arrays, after, ranges)
    return out.reshape(count, out.shape[0] // count, *out.shape[1:])


def pack_kernel(w_ref, one_ref, two_ref, out_ref):
    w_rows, rows = w_ref.shape[0], two_ref.shape[0] // 2
    for i in range(2):
        out_ref[i * w_rows : (i + 1) * w_rows, :] = w_ref[:, i * LANES : (i + 1) * LANES]
    out_ref[2 * w_rows : 2 * w_rows + rows, :] = one_ref[one_ref.shape[0] - rows :, :]
    out_ref[2 * w_rows + rows :, :] = two_ref[rows:, :]


def packed(arrays, rows, after):
    total = 2 * arrays[0].shape[0] + 2 * rows
    return call(pack_kernel, [shape((total, LANES), BF16)], 0.2, tuple(arrays), after)[0]


def stack_w_kernel(*refs):
    out = refs[-1]
    rows = out.shape[1]
    for i, ref in enumerate(refs[:-1]):
        wide = ref.shape[1] == out.shape[2]
        out[i] = ref[...] if wide else unpacked(ref, rows)


def unpacked(ref, rows):
    return jnp.concatenate([ref[:rows, :], ref[rows : 2 * rows, :]], axis=1)


def stack_w(arrays, rows):
    return call(
        stack_w_kernel, [shape((len(arrays), rows, 2 * LANES), BF16)], 0.2, tuple(arrays)
    )[0]


def project_kernel(n_mine, many, *refs):
    x_ref, dyt_ref, own_ref = refs[:3]
    mine, other = refs[3 : 3 + n_mine], refs[3 + n_mine]
    w_ref, bc_ref, keep_ref, send_ref = refs[4 + n_mine :]
    core, _, _ = core_and_chip()
    place, n_dp = lax.axis_index("dp"), lax.axis_size("dp")
    share = own_ref.shape[0]
    half = share // 2
    w_ref[rows_at(place, share), :] = own_ref[...]
    for i in range(n_mine):
        source = place ^ (i + 1)
        wide = mine[i].shape[1] == w_ref.shape[1]
        w_ref[rows_at(source * 2 + core, half), :] = mine[i][...] if wide else unpacked(mine[i], half)
        w_ref[rows_at(source * 2 + 1 - core, half), :] = other[i]
    bc = dot(x_ref[...], w_ref[...], 1, 0).astype(BF16)
    bc_ref[...] = bc
    c_rows = bc[:, LANES:]
    width = x_ref.shape[1]
    part = width // 2
    for ref, index in ((keep_ref, core), (send_ref, 1 - core)):
        ref[:part, :] = dot(dyt_ref[rows_at(index, part), :], c_rows, 1, 0).astype(BF16)
        table = dyt_ref[width : width + 4 * many, :].astype(F32)
        quarter = [table[i * many : (i + 1) * many] for i in range(4)]
        high = jnp.where(index == 0, quarter[0], quarter[1])
        low = jnp.where(index == 0, quarter[2], quarter[3])
        fill = jnp.zeros((ref.shape[0] - part - 2 * many, LANES), F32)
        ref[part:, :] = jnp.concatenate([high, low, fill], axis=0).astype(BF16)


def pair(keep_ref, recv_ref, many, size, head):
    core, _, _ = core_and_chip()
    part = many * size
    both = []
    for ref in (keep_ref, recv_ref):
        extra = ref[part:, :].astype(F32)
        decay = extra[head : head + 1] + extra[many + head : many + head + 1]
        both.append((ref[head * size : (head + 1) * size, :].astype(F32), decay))
    first = jax.tree.map(lambda a, b: jnp.where(core == 0, a, b), both[0], both[1])
    second = jax.tree.map(lambda a, b: jnp.where(core == 0, b, a), both[0], both[1])
    return first, second


def payload(ref, many, states, decays):
    size = states[0].shape[0]
    for head, state in enumerate(states):
        ref[head * size : (head + 1) * size, :] = state.astype(BF16)
    decay = jnp.concatenate(decays, axis=0)
    high = decay.astype(BF16).astype(F32)
    fill = jnp.zeros((ref.shape[0] - many * size - 2 * many, LANES), F32)
    extra = jnp.concatenate([high, decay - high, fill], axis=0)
    ref[many * size :, :] = extra.astype(BF16)


def loaded(ref, many, size, head):
    extra = ref[many * size :, :].astype(F32)
    decay = extra[head : head + 1] + extra[many + head : many + head + 1]
    return ref[head * size : (head + 1) * size, :].astype(F32), decay


def combine_kernel(many, size, keep_ref, recv_ref, out_ref):
    states, decays = [], []
    for head in range(many):
        (g0, a0), (g1, a1) = pair(keep_ref, recv_ref, many, size, head)
        states.append(g0 + a0 * g1)
        decays.append(a0 * a1)
    payload(out_ref, many, states, decays)


def pick_side(upper, mine, theirs):
    return jnp.where(upper, theirs, mine), jnp.where(upper, mine, theirs)


def climb_kernel(many, size, bit, mine_ref, recv_ref, out_ref):
    _, chip, _ = core_and_chip()
    upper = lax.rem(lax.div(chip, bit), 2) == 1
    states, decays = [], []
    for head in range(many):
        t_mine, a_mine = loaded(mine_ref, many, size, head)
        t_recv, a_recv = loaded(recv_ref, many, size, head)
        t_low, t_high = pick_side(upper, t_mine, t_recv)
        a_low, a_high = pick_side(upper, a_mine, a_recv)
        states.append(t_low + a_low * t_high)
        decays.append(a_low * a_high)
    payload(out_ref, many, states, decays)


def carry_kernel(many, size, levels, *refs):
    core, chip, _ = core_and_chip()
    recvs = refs[:levels]
    keep_ref, recv_ref, own_ref, send_ref = refs[levels:]
    for head in range(many):
        span = slice(head * size, (head + 1) * size)
        carry, reach = None, None
        for level, ref in enumerate(recvs):
            state, decay = loaded(ref, many, size, head)
            lower = lax.rem(lax.div(chip, 2**level), 2) == 0
            state = jnp.where(lower, state, 0.0)
            decay = jnp.where(lower, decay, 1.0)
            carry = state if carry is None else carry + reach * state
            reach = decay if reach is None else reach * decay
        _, (g1, a1) = pair(keep_ref, recv_ref, many, size, head)
        second = carry
        first = g1 + a1 * second
        own_ref[span, :] = jnp.where(core == 0, first, second).astype(BF16)
        send_ref[span, :] = jnp.where(core == 0, second, first).astype(BF16)


def intra_kernel(
    first, many, x_ref, dy_ref, bc_ref, cumt_ref, cum_ref, step_ref, h_ref, before_ref,
    dx_ref, mixed_ref, ex_ref, own_ref, rowm_ref,
):
    length, width = x_ref.shape
    heads = cumt_ref.shape[0]
    size = width // heads
    per = LANES // size
    upper = iota((length, length), 0) <= iota((length, length), 1)
    b_rows, c_rows = bc_ref[:, :LANES], bc_ref[:, LANES:]
    scores = dot(b_rows, c_rows, 1, 1)
    lane = iota((1, LANES), 1)
    lane_bf = [where_one(lane // size == i).astype(BF16) for i in range(per)]
    mixed = before_ref[...]
    own = jnp.zeros((length, LANES), F32)
    reach = jnp.zeros((heads, length), F32)
    for j in range(first, first + many):
        span = slice(j * LANES, (j + 1) * LANES)
        out_span = slice((j - first) * LANES, (j - first + 1) * LANES)
        x_p = x_ref[:, span]
        dy_p = dy_ref[:, span]
        dy_h = jnp.concatenate([dy_p * m for m in lane_bf], axis=0)
        cross = dot(x_p, dy_h, 1, 1)
        kern = []
        wide = None
        for i in range(per):
            h = j * per + i
            diff = cumt_ref[h : h + 1, :] - cum_ref[:, h : h + 1]
            seg = jnp.exp(jnp.where(upper, diff, -1e30))
            kern.append((seg * scores).astype(BF16))
            step = jnp.broadcast_to(step_ref[:, h : h + 1], (length, LANES))
            wide = step if i == 0 else jnp.where(lane < i * size, wide, step)
            scaled = seg * cross[:, i * length : (i + 1) * length] * step
            mixed = mixed + scaled
            full = scaled * scores
            rowm_ref[h : h + 1, :] = jnp.sum(full, axis=0, keepdims=True)
            own = jnp.where(lane == h, jnp.sum(full, axis=1, keepdims=True), own)
        back = dot(jnp.concatenate(kern, axis=1), dy_h, 1, 0)
        dx_ref[:, out_span] = back * wide
        seen = dy_p.astype(F32) * dot(c_rows, h_ref[span, :], 1, 1)
        reach = reach + dot(to_heads(j, heads, size), halves(seen), 1, 1)
    mixed_ref[...] = mixed
    rows = slice(first * per, (first + many) * per)
    own = own.T[rows]
    own_ref[...] = own
    ex_ref[...] = rowm_ref[rows, :] + jnp.exp(cumt_ref[rows, :]) * reach[rows] - own


def close_kernel(mixed_ref, bc_ref, carried_ref, db_ref, dc_ref):
    mixed = mixed_ref[...].astype(BF16)
    db_ref[...] = dot(mixed, bc_ref[:, LANES:], 1, 0)
    dc_ref[...] = (dot(mixed, bc_ref[:, :LANES], 0, 0) + carried_ref[...]).astype(BF16)


def db_kernel(xs_ref, own_ref, recv_ref, db_ref, dc_ref, out_ref):
    core, _, _ = core_and_chip()
    half = db_ref.shape[1]
    part = own_ref.shape[0]
    total = db_ref[...]
    for ref, index in ((own_ref, core), (recv_ref, 1 - core)):
        total = total + dot(xs_ref[:, rows_at(index, part, LANES)], ref[...], 1, 0)
    out_ref[:, :half] = total.astype(BF16)
    out_ref[:, half:] = dc_ref[...]


def finish_kernel(parts, *refs):
    (x_ref, bc_ref, cumt_ref, stept_ref, cum_ref, step_ref, h_ref, own_ref, recv_ref,
     w_ref, dbc_ref) = refs[:11]
    dx_refs, ex_refs, st_refs = (refs[11 + i * parts : 11 + (i + 1) * parts] for i in range(3))
    in_ref, decay_ref, grad_ref, token_ref, r_ref, edge_ref = refs[11 + 3 * parts :]
    token_ref[...] = jnp.zeros_like(token_ref)
    core, _, _ = core_and_chip()
    length, width = x_ref.shape
    heads = cumt_ref.shape[0]
    size = width // heads
    part = width // 2
    r_ref[rows_at(core, part), :] = own_ref[...]
    r_ref[rows_at(1 - core, part), :] = recv_ref[...]
    cum = cum_ref[...]
    table = halves(jnp.exp(cum[length - 1 : length] - cum) * step_ref[...])
    seen = jnp.zeros((heads, length), F32)
    b_rows = bc_ref[:, :LANES]
    d_bc = dbc_ref[...]
    for j in range(width // LANES):
        span = slice(j * LANES, (j + 1) * LANES)
        local = dx_refs[j * LANES // (width // parts)]
        start = j * LANES % (width // parts)
        r_tile = r_ref[span, :]
        reach = dot(b_rows, r_tile, 1, 1)
        d_in = local[:, start : start + LANES] + dot(table, to_lanes(j, size), 1, 0) * reach
        d_in = d_in + dot(d_bc, w_ref[span, :], 1, 1)
        in_ref[:, span] = d_in.astype(BF16)
        product = x_ref[:, span].astype(F32) * reach
        seen = seen + dot(to_heads(j, heads, size), halves(product), 1, 1)
        edge = r_tile.astype(F32) * h_ref[span, :].astype(F32)
        for i in range(LANES // size):
            h = j * (LANES // size) + i
            edge_ref[h : h + 1, :] = jnp.sum(
                edge[i * size : (i + 1) * size], axis=0, keepdims=True
            )
    cumt = cumt_ref[...]
    total = cumt[:, length - 1 : length]
    to_end = jnp.exp(total - cumt)
    step = stept_ref[...]
    own = jnp.concatenate([r[...] for r in st_refs], axis=0)
    excess = jnp.concatenate([r[...] for r in ex_refs], axis=0)
    grad_ref[...] = own / step + to_end * seen
    edge = jnp.exp(total) * jnp.sum(edge_ref[...], axis=1, keepdims=True)
    decay_ref[...] = (
        dot(excess, triangle(length, lambda a, b: a >= b), 1, 0, HI)
        + dot(to_end * step * seen, triangle(length, lambda a, b: a < b), 1, 0, HI)
        + edge
    )


def term_kernel(places, n_columns, *refs):
    columns, pieces = refs[:n_columns], refs[n_columns:-3]
    keep_ref, send_ref, held = refs[-3:]
    pieces = [(p, i) for p in pieces for i in range(p.shape[0])]
    rows = 2 * keep_ref.shape[0]
    core, _, _ = core_and_chip()
    total = None
    for (a, start), (b, i) in zip(places, pieces):
        part = dot(columns[a][start : start + rows, :], b[i], 1, 0)
        total = part if total is None else total + part
    block = keep_ref.shape[0]
    held[0] = total[:block]
    held[1] = total[block:]
    keep_ref[...] = held[core]
    send_ref[...] = held[1 - core].astype(BF16)


def deal_kernel(keep_ref, recv_ref, own_ref, *refs):
    outs, held = refs[:-1], refs[-1]
    place, n_dp = lax.axis_index("dp"), lax.axis_size("dp")
    total = keep_ref[...] + recv_ref[...].astype(F32)
    share = own_ref.shape[0]
    for i in range(n_dp):
        held[i] = total[i * share : (i + 1) * share]
    own_ref[...] = held[place]
    for s, out in enumerate(outs):
        out[...] = held[place ^ (s + 1)].astype(BF16)


def expert_kernel(flip, slots, a_ref, b_ref, gate_ref, up_ref, *refs):
    outs, (rows_ref, gate_acc, up_acc) = refs[:-3], refs[-3:]
    step = pl.program_id(0)
    n_chip = a_ref.shape[0]

    @pl.when(step == 0)
    def _():
        for half, ref in enumerate((a_ref, b_ref)):
            for i in range(n_chip):
                row = (half * n_chip + i) * slots
                for t in range(rows_ref.shape[1] // LANES):
                    rows_ref[row : row + slots, t * LANES : (t + 1) * LANES] = ref[
                        i, t * slots : (t + 1) * slots, :
                    ]
        gate_acc[...] = jnp.zeros_like(gate_acc)
        up_acc[...] = jnp.zeros_like(up_acc)

    depth = gate_ref.shape[0]
    rows = rows_ref[:, rows_at(step, depth, LANES)]
    gate_acc[...] += dot(rows, gate_ref[...], 1, 0)
    up_acc[...] += dot(rows, up_ref[...], 1, 0)

    @pl.when(step == pl.num_programs(0) - 1)
    def _():
        weighted = jax.nn.silu(gate_acc[...]) * up_acc[...]
        weighted = (weighted.T if flip else weighted).astype(BF16)
        outs[0][...] = weighted
        at = 0
        for out in outs[1:]:
            out[...] = weighted[at : at + out.shape[0]]
            at += out.shape[0]


def expert(a, b, w_gate, w_up, slots, flip, after):
    n_chip = a.shape[0]
    total = 2 * n_chip * slots
    width, hidden = w_gate.shape
    depth = 512
    rows, lanes = (hidden, total) if flip else (total, hidden)
    outs = [(rows, lanes), (rows // 2, lanes), (rows // 2, lanes)]

    def body(*refs):
        expert_kernel(flip, slots, *refs[:4], *refs[4 + len(after) :])

    whole = pl.BlockSpec(a.shape, lambda i: (0, 0, 0))
    block = pl.BlockSpec((depth, hidden), lambda i: (i, 0))
    return pl.pallas_call(
        body,
        out_shape=[shape(o, BF16) for o in outs],
        grid=(width // depth,),
        in_specs=[whole, whole, block, block]
        + [pl.BlockSpec(memory_space=pl.ANY)] * len(after),
        out_specs=[pl.BlockSpec(o, lambda i: (0, 0)) for o in outs],
        scratch_shapes=[
            pltpu.VMEM((total, width), BF16),
            pltpu.VMEM((total, hidden), F32),
            pltpu.VMEM((total, hidden), F32),
        ],
        cost_estimate=pl.CostEstimate(
            flops=int(3e9), bytes_accessed=1000, transcendentals=0
        ),
        compiler_params=pltpu.CompilerParams(vmem_limit_bytes=20 * 1024 * 1024),
    )(a, b, w_gate, w_up, *after)


def down_kernel(n_dp, flip, slots, grad_rows, *refs):
    pieces = refs[:n_dp]
    a_ref, b_ref, out_ref = refs[n_dp:]
    n_chip = a_ref.shape[0]
    piece = out_ref.shape[1]
    base = a_ref.shape[1] - n_dp * grad_rows
    total = None
    for s in range(n_dp):
        columns = []
        for t in range(grad_rows // slots):
            row = base + s * grad_rows + t * slots
            blocks = [r[i, row : row + slots, :] for r in (a_ref, b_ref) for i in range(n_chip)]
            columns.append(jnp.concatenate(blocks, axis=0))
        right = jnp.concatenate(columns, axis=1)[:, :piece]
        part = dot(pieces[s][...], right, 1 if flip else 0, 0)
        total = part if total is None else total + part
    out_ref[...] = total.astype(BF16)


def xored(array, axis, mask):
    count = lax.axis_size(axis)
    return lax.ppermute(array, axis, [(i, i ^ mask) for i in range(count)])


def swapped(array):
    return xored(array, "tm", 1)


def chips(arrays):
    return [arrays[0]] + [xored(a, "tm", 2 * s) for s, a in enumerate(arrays) if s]


def gathered(array, axis, count):
    if count == 1:
        return [array]
    far = xored(array, axis, count // 2)
    return gathered(array, axis, count // 2) + gathered(far, axis, count // 2)


def per_device(
    layer_in,
    out_grad,
    w_bc,
    log_decay,
    step,
    saved_states,
    w_gate,
    w_up,
    slot_rows,
    slot_counts,
    slot_gates,
):
    n_dp = lax.axis_size("dp")
    core, chip, n_chip = core_and_chip()
    x = layer_in[0]
    dy = out_grad[0]
    length, width = x.shape
    heads = log_decay.shape[2]
    size = width // heads
    share, columns = w_bc.shape
    half = columns // 2
    ldt = log_decay[0].T
    stept = step[0].T
    h_in = saved_states[0, 0].reshape(width, half)
    capacity = slot_rows.shape[2]
    piece = width // n_dp
    part = width // 2
    many = heads // 2
    flip = w_gate.shape[2] % LANES == 0

    grad_rows = -(-piece // LANES) * capacity
    w_rows = share // 2
    w_half = lax.dynamic_slice_in_dim(w_bc, core * w_rows, w_rows, 0)

    in_rows = width // LANES * capacity
    blocks = [1, 1, 2] if n_chip == 4 else [1] * n_chip
    base, groups = (2, [2]) if n_dp == 4 else (0, [1] * n_dp)
    cumt, cum, steps, dyt, xs, carried, rows, *xt = call(
        lambda *refs: prep_kernel(len(groups), *refs),
        [
            shape((heads, length), F32),
            shape((length, LANES), F32),
            shape((length, LANES), F32),
            shape((width + up16(2 * heads), length), BF16),
            shape((length, width), BF16),
            shape((length, half), F32),
        ]
        + [shape((in_rows + base * grad_rows, LANES), BF16)]
        + [shape((k * grad_rows, LANES), BF16) for k in groups]
        + [shape((k * width // n_chip, length), BF16) for k in blocks],
        2.0,
        (x, dy, ldt, stept, h_in, slot_rows[0], slot_counts, slot_gates[0]),
        scratch=[
            pltpu.VMEM((width, length), BF16),
            pltpu.VMEM((n_dp, grad_rows, LANES), BF16),
        ],
        fetch=(0, 1, 2, 3, 4),
        limit=60,
    )
    deals, xt = xt[: len(groups)], xt[len(groups) :]
    if n_dp == 4:
        w_far, w_near = xored(w_half, "dp", 2), xored(w_half, "dp", 1)
        deal_2 = xored(deals[0], "dp", 2)
        ride = packed([w_far, rows, deal_2], grad_rows, (w_near,))
        ride = xored(ride, "dp", 1)
        mine = [w_near, w_far, ride]
        payload = joined(
            [rows, ride, deal_2, ride],
            ranges=[
                (0, in_rows + grad_rows),
                (2 * w_rows, 2 * w_rows + grad_rows),
                (0, grad_rows),
                (2 * w_rows + grad_rows, 2 * w_rows + 2 * grad_rows),
            ],
        )
    else:
        mine = gathered(w_half, "dp", n_dp)[1:]
        deals = deals[:1] + [xored(d, "dp", s + 1) for s, d in enumerate(deals[1:])]
        payload = joined([rows, *deals])
    rows_in = chips([payload] * n_chip)
    other = swapped(stack_w(mine, w_rows))
    w_whole, bc, keep, send = call(
        lambda *refs: project_kernel(n_dp - 1, many, *refs),
        [
            shape((width, columns), BF16),
            shape((length, columns), BF16),
            shape((part + up16(2 * many), half), BF16),
            shape((part + up16(2 * many), half), BF16),
        ],
        1.0,
        (x, dyt, w_bc, *mine, other),
    )
    recv = swapped(send)
    hidden = w_gate.shape[2]
    climbs = [
        call(
            lambda *refs: combine_kernel(many, size, *refs),
            [shape((part + up16(2 * many), half), BF16)],
            0.5,
            (keep, recv),
        )[0]
    ]
    if n_chip == 4:
        x_rows = width // n_chip
        over_y = xored(xt[2], "tm", 4)

    parts = 2
    tiles = width // LANES // parts
    dxs, exs, owns = [], [], []
    later = (climbs[0],)
    mixed = jnp.zeros((length, length), F32)
    for i in range(parts):
        dx, mixed, ex, own = call(
            lambda *refs, i=i: intra_kernel(i * tiles, tiles, *refs),
            [
                shape((length, width // parts), F32),
                shape((length, length), F32),
                shape((heads // parts, length), F32),
                shape((heads // parts, length), F32),
            ],
            3.0,
            (x, dy, bc, cumt, cum, steps, h_in, mixed),
            after=later,
            scratch=[pltpu.VMEM((heads, length), F32)],
        )
        if i == 0:
            held = (over_y, dx) if n_chip == 4 else (dx,)
            arrived = []
            bit = 1
            while bit < n_chip:
                last = bit * 2 == n_chip
                moves = [
                    (k, k ^ (2 * bit)) for k in range(2 * n_chip) if not last or k & (2 * bit)
                ]
                arrived.append(lax.ppermute(climbs[-1], "tm", moves))
                if not last:
                    climbs.append(
                        call(
                            lambda *refs, bit=bit: climb_kernel(many, size, bit, *refs),
                            [shape((part + up16(2 * many), half), BF16)],
                            0.5,
                            (climbs[-1], arrived[-1]),
                            after=held,
                        )[0]
                    )
                bit *= 2
            later = (climbs[-1],)
            rows_a = stacked(rows_in, after=later)
            rows_b = swapped(rows_a)
            weighted, low, high = expert(
                rows_a, rows_b, w_gate[0], w_up[0], capacity, flip, later
            )
        dxs.append(dx)
        exs.append(ex)
        owns.append(own)
    db, dc = call(
        close_kernel,
        [shape((length, half), F32), shape((length, half), BF16)],
        0.3,
        (mixed, bc, carried),
    )

    held = (dc,)
    if n_chip == 4:
        over_x = xored(joined([xt[1], over_y], later, [(0, x_rows), (x_rows, 2 * x_rows)]), "tm", 2)
        columns_in = [xt[0], over_x, over_y]
        places = [(0, 0), (1, 0), (2, 0), (1, x_rows)]
        held += (over_x,)
    else:
        columns_in = chips(xt)
        places = [(i, 0) for i in range(n_chip)]
    low = xored(low, "dp", n_dp // 2)
    high = xored(high, "dp", n_dp // 2)
    near = gathered(weighted, "dp", n_dp // 2)
    held += (low, weighted)
    r_own, r_send = call(
        lambda *refs: carry_kernel(many, size, len(arrived), *refs),
        [shape((part, half), BF16)] * 2,
        0.5,
        (*arrived, keep, recv),
        after=held,
    )
    r_recv = swapped(r_send)
    fars = gathered(joined([low, high]), "dp", n_dp // 2)
    d_bc = call(db_kernel, [shape((length, columns), BF16)], 0.3, (xs, r_own, r_recv, db, dc))[0]
    d_bcs = [d_bc.reshape(1, length, columns)]
    while 2 ** (len(d_bcs) - 1) < n_chip:
        level = 2 ** (len(d_bcs) - 1)
        sent = d_bcs[0] if level == 1 else joined(d_bcs, (high,))
        d_bcs.append(xored(sent, "tm", 2 * level))
    d_in, d_decay, d_step, token = call(
        lambda *refs: finish_kernel(parts, *refs),
        [
            shape((length, width), BF16),
            shape((heads, length), F32),
            shape((heads, length), F32),
            shape((8, LANES), F32),
        ],
        3.0,
        (x, bc, cumt, stept, cum, steps, h_in, r_own, r_recv, w_whole, d_bc,
         *dxs, *exs, *owns),
        scratch=[pltpu.VMEM((width, half), BF16), pltpu.VMEM((heads, half), F32)],
    )
    out_rows = width // (2 * n_chip)
    term, term_send = call(
        lambda *refs: term_kernel(places, len(columns_in), *refs),
        [shape((out_rows, columns), F32), shape((out_rows, columns), BF16)],
        0.5,
        (*columns_in, *d_bcs),
        after=(token, *fars[1:], *near[1:]),
        scratch=[pltpu.VMEM((2, out_rows, columns), F32)],
    )
    final = call(
        deal_kernel,
        [shape((out_rows // n_dp, columns), F32)]
        + [shape((out_rows // n_dp, columns), BF16)] * (n_dp - 1),
        0.3,
        (term, swapped(term_send)),
        scratch=[pltpu.VMEM((n_dp, out_rows // n_dp, columns), F32)],
    )
    w_bc_grad = final[0]
    for s in range(1, n_dp):
        w_bc_grad = w_bc_grad + xored(final[s], "dp", s).astype(F32)

    w_down_grad = call(
        lambda *refs: down_kernel(n_dp, flip, capacity, grad_rows, *refs),
        [shape((hidden, piece), BF16)],
        1.0,
        (*near, *fars, rows_a, rows_b),
        after=(final[0],),
    )[0]
    return (d_in[None], d_decay.T[None], d_step.T[None], w_bc_grad, w_down_grad[None])


def solution(mesh):
    in_specs = (
        P("dp", "tm", None),
        P("dp", "tm", None),
        P("dp", None),
        P("dp", "tm", None),
        P("dp", "tm", None),
        P("dp", "tm", None, None, None),
        P(None, None, "tm"),
        P(None, None, "tm"),
        P("dp", None, "tm"),
        P("dp", "tm"),
        P("dp", None, "tm"),
    )
    out_specs = (
        P("dp", "tm", None),
        P("dp", "tm", None),
        P("dp", "tm", None),
        P(("tm", "dp"), None),
        P(None, "tm", "dp"),
    )
    return jax.shard_map(
        per_device, mesh=mesh, in_specs=in_specs, out_specs=out_specs, check_vma=False
    )
```

```python
import jax
import jax.numpy as jnp
from jax import lax
from jax.experimental import pallas as pl
from jax.experimental.pallas import tpu as pltpu
from jax.sharding import PartitionSpec as P

HI = lax.Precision.HIGHEST
F32 = jnp.float32
BF16 = jnp.bfloat16
LANES = 128


def dot(a, b, ca, cb, precision=None):
    return lax.dot_general(
        a, b, (((ca,), (cb,)), ((), ())), precision=precision, preferred_element_type=F32
    )


def iota(dims, axis):
    return lax.broadcasted_iota(jnp.int32, dims, axis)


def where_one(mask):
    return jnp.where(mask, 1.0, 0.0)


def triangle(n, keep):
    return where_one(keep(iota((n, n), 0), iota((n, n), 1))).astype(F32)


def halves(values, axis=1):
    high = values.astype(BF16)
    low = (values - high.astype(F32)).astype(BF16)
    return jnp.concatenate([high, low], axis=axis)


def to_lanes(j, size):
    dims = (LANES, LANES)
    one = where_one(iota(dims, 0) == iota(dims, 1) // size + j * (LANES // size)).astype(BF16)
    return jnp.concatenate([one, one], axis=0)


def to_heads(j, heads, size):
    dims = (heads, LANES)
    one = where_one(iota(dims, 0) == iota(dims, 1) // size + j * (LANES // size)).astype(BF16)
    return jnp.concatenate([one, one], axis=1)


def up16(n):
    return -(-n // 16) * 16


def call(kernel, outs, cost, args, after=(), scratch=(), limit=14, fetch=()):
    n_in, n_after, n_out = len(args), len(after), len(outs)
    fetch = tuple(fetch)

    def body(*refs):
        ins = list(refs[:n_in])
        rest = refs[n_in + n_after :]
        if fetch:
            sems = rest[-1]
            held = rest[len(rest) - 1 - len(fetch) : -1]
            rest = rest[: len(rest) - 1 - len(fetch)]
            copies = []
            for i, (index, ref) in enumerate(zip(fetch, held)):
                copies.append(pltpu.make_async_copy(ins[index], ref, sems.at[i]))
                ins[index] = ref
            for copy in copies:
                copy.start()
            for copy in copies:
                copy.wait()
        kernel(*ins, *rest)

    specs = [
        pl.BlockSpec(memory_space=pltpu.HBM if i in fetch else pltpu.VMEM) for i in range(n_in)
    ]
    held = [pltpu.VMEM(args[i].shape, args[i].dtype) for i in fetch]
    if fetch:
        held.append(pltpu.SemaphoreType.DMA((len(fetch),)))
    return pl.pallas_call(
        body,
        out_shape=outs,
        in_specs=specs + [pl.BlockSpec(memory_space=pl.ANY)] * n_after,
        out_specs=[pl.BlockSpec(memory_space=pltpu.VMEM)] * n_out,
        scratch_shapes=list(scratch) + held,
        cost_estimate=pl.CostEstimate(
            flops=int(cost * 3e9), bytes_accessed=1000, transcendentals=0
        ),
        compiler_params=pltpu.CompilerParams(vmem_limit_bytes=limit * 1024 * 1024),
    )(*args, *after)


def shape(dims, kind):
    return jax.ShapeDtypeStruct(dims, kind)


def core_and_chip():
    place = lax.axis_index("tm")
    return lax.rem(place, 2), lax.div(place, 2), lax.axis_size("tm") // 2


def rows_at(index, size, align=16):
    return pl.ds(pl.multiple_of(index * size, align), size)


def picked(x_ref, dy_ref, slot_ref, count_ref, gate_ref, rows_ref, out_refs):
    length, width = x_ref.shape
    slots = slot_ref.shape[1]
    hit = iota((length, slots), 0) == slot_ref[...]
    live = iota((1, slots), 1) < count_ref[...]
    weight = jnp.where(live, gate_ref[...].astype(F32), 0.0)
    rows = dot(where_one(hit).astype(BF16), x_ref[...], 0, 0).astype(BF16)
    for t in range(width // LANES):
        rows_ref[t * slots : (t + 1) * slots, :] = rows[:, t * LANES : (t + 1) * LANES]
    grads = dot(jnp.where(hit, weight, 0.0).astype(BF16), dy_ref[...], 0, 0).astype(BF16)
    held = out_refs[-1]
    n_dp = held.shape[0]
    piece = width // n_dp
    for i in range(n_dp):
        for t, low in enumerate(range(i * piece, (i + 1) * piece, LANES)):
            block = grads[:, low : min(low + LANES, (i + 1) * piece)]
            if block.shape[1] < LANES:
                fill = jnp.zeros((slots, LANES - block.shape[1]), BF16)
                block = jnp.concatenate([block, fill], axis=1)
            held[i, t * slots : (t + 1) * slots, :] = block
    place = lax.axis_index("dp")
    s = 0
    for out in out_refs[:-1]:
        for start in range(0, out.shape[0], held.shape[1]):
            out[start : start + held.shape[1], :] = held[place ^ s]
            s += 1


def high_low(values):
    high = values.astype(BF16).astype(F32)
    return [high, values - high]


def prep_kernel(
    n_deals, x_ref, dy_ref, ldt_ref, stept_ref, h_ref, slot_ref, count_ref, gate_ref,
    cumt_ref, cum_ref, step_ref, dyt_ref, xs_ref, carried_ref, rows_ref, *rest,
):
    outs, xt_ref, held_ref = rest[n_deals:-2], rest[-2], rest[-1]
    length, width = x_ref.shape
    heads = ldt_ref.shape[0]
    size = width // heads
    _, chip, n_chip = core_and_chip()
    picked(x_ref, dy_ref, slot_ref, count_ref, gate_ref, rows_ref, (*rest[:n_deals], held_ref))
    pad = jnp.zeros((LANES - heads, length), F32)
    cumt = dot(ldt_ref[...], triangle(length, lambda a, b: a <= b), 1, 0, HI)
    cumt_ref[...] = cumt
    cum = jnp.concatenate([cumt, pad], axis=0).T
    step = jnp.concatenate([stept_ref[...], pad], axis=0).T
    cum_ref[...] = cum
    step_ref[...] = step
    start = jnp.exp(cum)
    into_end = jnp.exp(cum[length - 1 : length] - cum) * step
    table = jnp.concatenate([halves(start), halves(into_end)], axis=0)
    carried = jnp.zeros(carried_ref.shape, F32)
    for j in range(width // LANES):
        span = slice(j * LANES, (j + 1) * LANES)
        scale = dot(table, to_lanes(j, size), 1, 0)
        x_f = x_ref[:, span].astype(F32)
        xt_ref[span, :] = x_f.T.astype(BF16)
        xs_ref[:, span] = (x_f * scale[length:]).astype(BF16)
        dys = dy_ref[:, span].astype(F32) * scale[:length]
        dyt_ref[span, :] = dys.T.astype(BF16)
        carried = carried + dot(dys.astype(BF16), h_ref[span, :], 1, 0)
    carried_ref[...] = carried
    decay = jnp.broadcast_to(jnp.exp(cumt[:, length - 1 : length]), (heads, LANES))
    dyt_ref[width : width + 2 * heads, :] = jnp.concatenate(high_low(decay), axis=0).astype(BF16)
    block = width // n_chip
    s = 0
    for out in outs:
        for start in range(0, out.shape[0], block):
            out[start : start + block, :] = xt_ref[rows_at(chip ^ s, block), :]
            s += 1


def join_kernel(ranges, *refs):
    out, at = refs[-1], 0
    for ref, (start, stop) in zip(refs, ranges):
        out[at : at + stop - start] = ref[start:stop]
        at += stop - start


def joined(arrays, after=(), ranges=None):
    ranges = ranges or [(0, a.shape[0]) for a in arrays]
    dims = (sum(stop - start for start, stop in ranges), *arrays[0].shape[1:])
    return call(
        lambda *refs: join_kernel(ranges, *refs),
        [shape(dims, arrays[0].dtype)],
        0.2,
        tuple(arrays),
        after=after,
    )[0]


def stacked(arrays, after=(), ranges=None):
    count = len(arrays)
    out = joined(arrays, after, ranges)
    return out.reshape(count, out.shape[0] // count, *out.shape[1:])


def project_kernel(n_mine, many, *refs):
    x_ref, dyt_ref, own_ref = refs[:3]
    mine, other = refs[3 : 3 + n_mine], refs[3 + n_mine]
    w_ref, bc_ref, keep_ref, send_ref = refs[4 + n_mine :]
    core, _, _ = core_and_chip()
    place, n_dp = lax.axis_index("dp"), lax.axis_size("dp")
    share = own_ref.shape[0]
    half = share // 2
    w_ref[rows_at(place, share), :] = own_ref[...]
    for i in range(n_mine):
        source = place ^ (i + 1)
        w_ref[rows_at(source * 2 + core, half), :] = mine[i][...]
        w_ref[rows_at(source * 2 + 1 - core, half), :] = other[i]
    bc = dot(x_ref[...], w_ref[...], 1, 0).astype(BF16)
    bc_ref[...] = bc
    c_rows = bc[:, LANES:]
    width = x_ref.shape[1]
    part = width // 2
    for ref, index in ((keep_ref, core), (send_ref, 1 - core)):
        ref[:part, :] = dot(dyt_ref[rows_at(index, part), :], c_rows, 1, 0).astype(BF16)
        table = dyt_ref[width : width + 4 * many, :].astype(F32)
        quarter = [table[i * many : (i + 1) * many] for i in range(4)]
        high = jnp.where(index == 0, quarter[0], quarter[1])
        low = jnp.where(index == 0, quarter[2], quarter[3])
        fill = jnp.zeros((ref.shape[0] - part - 2 * many, LANES), F32)
        ref[part:, :] = jnp.concatenate([high, low, fill], axis=0).astype(BF16)


def pair(keep_ref, recv_ref, many, size, head):
    core, _, _ = core_and_chip()
    part = many * size
    both = []
    for ref in (keep_ref, recv_ref):
        extra = ref[part:, :].astype(F32)
        decay = extra[head : head + 1] + extra[many + head : many + head + 1]
        both.append((ref[head * size : (head + 1) * size, :].astype(F32), decay))
    first = jax.tree.map(lambda a, b: jnp.where(core == 0, a, b), both[0], both[1])
    second = jax.tree.map(lambda a, b: jnp.where(core == 0, b, a), both[0], both[1])
    return first, second


def payload(ref, many, states, decays):
    size = states[0].shape[0]
    for head, state in enumerate(states):
        ref[head * size : (head + 1) * size, :] = state.astype(BF16)
    decay = jnp.concatenate(decays, axis=0)
    high = decay.astype(BF16).astype(F32)
    fill = jnp.zeros((ref.shape[0] - many * size - 2 * many, LANES), F32)
    extra = jnp.concatenate([high, decay - high, fill], axis=0)
    ref[many * size :, :] = extra.astype(BF16)


def loaded(ref, many, size, head):
    extra = ref[many * size :, :].astype(F32)
    decay = extra[head : head + 1] + extra[many + head : many + head + 1]
    return ref[head * size : (head + 1) * size, :].astype(F32), decay


def combine_kernel(many, size, keep_ref, recv_ref, out_ref):
    states, decays = [], []
    for head in range(many):
        (g0, a0), (g1, a1) = pair(keep_ref, recv_ref, many, size, head)
        states.append(g0 + a0 * g1)
        decays.append(a0 * a1)
    payload(out_ref, many, states, decays)


def pick_side(upper, mine, theirs):
    return jnp.where(upper, theirs, mine), jnp.where(upper, mine, theirs)


def climb_kernel(many, size, bit, mine_ref, recv_ref, out_ref):
    _, chip, _ = core_and_chip()
    upper = lax.rem(lax.div(chip, bit), 2) == 1
    states, decays = [], []
    for head in range(many):
        t_mine, a_mine = loaded(mine_ref, many, size, head)
        t_recv, a_recv = loaded(recv_ref, many, size, head)
        t_low, t_high = pick_side(upper, t_mine, t_recv)
        a_low, a_high = pick_side(upper, a_mine, a_recv)
        states.append(t_low + a_low * t_high)
        decays.append(a_low * a_high)
    payload(out_ref, many, states, decays)


def carry_kernel(many, size, levels, *refs):
    core, chip, _ = core_and_chip()
    recvs = refs[:levels]
    keep_ref, recv_ref, own_ref, send_ref = refs[levels:]
    for head in range(many):
        span = slice(head * size, (head + 1) * size)
        carry, reach = None, None
        for level, ref in enumerate(recvs):
            state, decay = loaded(ref, many, size, head)
            lower = lax.rem(lax.div(chip, 2**level), 2) == 0
            state = jnp.where(lower, state, 0.0)
            decay = jnp.where(lower, decay, 1.0)
            carry = state if carry is None else carry + reach * state
            reach = decay if reach is None else reach * decay
        _, (g1, a1) = pair(keep_ref, recv_ref, many, size, head)
        second = carry
        first = g1 + a1 * second
        own_ref[span, :] = jnp.where(core == 0, first, second).astype(BF16)
        send_ref[span, :] = jnp.where(core == 0, second, first).astype(BF16)


def intra_kernel(
    first, many, x_ref, dy_ref, bc_ref, cumt_ref, cum_ref, step_ref, h_ref, before_ref,
    dx_ref, mixed_ref, ex_ref, own_ref, rowm_ref,
):
    length, width = x_ref.shape
    heads = cumt_ref.shape[0]
    size = width // heads
    per = LANES // size
    upper = iota((length, length), 0) <= iota((length, length), 1)
    b_rows, c_rows = bc_ref[:, :LANES], bc_ref[:, LANES:]
    scores = dot(b_rows, c_rows, 1, 1)
    lane = iota((1, LANES), 1)
    lane_bf = [where_one(lane // size == i).astype(BF16) for i in range(per)]
    mixed = before_ref[...]
    own = jnp.zeros((length, LANES), F32)
    reach = jnp.zeros((heads, length), F32)
    for j in range(first, first + many):
        span = slice(j * LANES, (j + 1) * LANES)
        out_span = slice((j - first) * LANES, (j - first + 1) * LANES)
        x_p = x_ref[:, span]
        dy_p = dy_ref[:, span]
        dy_h = jnp.concatenate([dy_p * m for m in lane_bf], axis=0)
        cross = dot(x_p, dy_h, 1, 1)
        kern = []
        wide = None
        for i in range(per):
            h = j * per + i
            diff = cumt_ref[h : h + 1, :] - cum_ref[:, h : h + 1]
            seg = jnp.exp(jnp.where(upper, diff, -1e30))
            kern.append((seg * scores).astype(BF16))
            step = jnp.broadcast_to(step_ref[:, h : h + 1], (length, LANES))
            wide = step if i == 0 else jnp.where(lane < i * size, wide, step)
            scaled = seg * cross[:, i * length : (i + 1) * length] * step
            mixed = mixed + scaled
            full = scaled * scores
            rowm_ref[h : h + 1, :] = jnp.sum(full, axis=0, keepdims=True)
            own = jnp.where(lane == h, jnp.sum(full, axis=1, keepdims=True), own)
        back = dot(jnp.concatenate(kern, axis=1), dy_h, 1, 0)
        dx_ref[:, out_span] = back * wide
        seen = dy_p.astype(F32) * dot(c_rows, h_ref[span, :], 1, 1)
        reach = reach + dot(to_heads(j, heads, size), halves(seen), 1, 1)
    mixed_ref[...] = mixed
    rows = slice(first * per, (first + many) * per)
    own = own.T[rows]
    own_ref[...] = own
    ex_ref[...] = rowm_ref[rows, :] + jnp.exp(cumt_ref[rows, :]) * reach[rows] - own


def close_kernel(mixed_ref, bc_ref, carried_ref, db_ref, dc_ref):
    mixed = mixed_ref[...].astype(BF16)
    db_ref[...] = dot(mixed, bc_ref[:, LANES:], 1, 0)
    dc_ref[...] = (dot(mixed, bc_ref[:, :LANES], 0, 0) + carried_ref[...]).astype(BF16)


def db_kernel(xs_ref, own_ref, recv_ref, db_ref, dc_ref, out_ref):
    core, _, _ = core_and_chip()
    half = db_ref.shape[1]
    part = own_ref.shape[0]
    total = db_ref[...]
    for ref, index in ((own_ref, core), (recv_ref, 1 - core)):
        total = total + dot(xs_ref[:, rows_at(index, part, LANES)], ref[...], 1, 0)
    out_ref[:, :half] = total.astype(BF16)
    out_ref[:, half:] = dc_ref[...]


def finish_kernel(parts, *refs):
    (x_ref, bc_ref, cumt_ref, stept_ref, cum_ref, step_ref, h_ref, own_ref, recv_ref,
     w_ref, dbc_ref) = refs[:11]
    dx_refs, ex_refs, st_refs = (refs[11 + i * parts : 11 + (i + 1) * parts] for i in range(3))
    in_ref, decay_ref, grad_ref, token_ref, r_ref, edge_ref = refs[11 + 3 * parts :]
    token_ref[...] = jnp.zeros_like(token_ref)
    core, _, _ = core_and_chip()
    length, width = x_ref.shape
    heads = cumt_ref.shape[0]
    size = width // heads
    part = width // 2
    r_ref[rows_at(core, part), :] = own_ref[...]
    r_ref[rows_at(1 - core, part), :] = recv_ref[...]
    cum = cum_ref[...]
    table = halves(jnp.exp(cum[length - 1 : length] - cum) * step_ref[...])
    seen = jnp.zeros((heads, length), F32)
    b_rows = bc_ref[:, :LANES]
    d_bc = dbc_ref[...]
    for j in range(width // LANES):
        span = slice(j * LANES, (j + 1) * LANES)
        local = dx_refs[j * LANES // (width // parts)]
        start = j * LANES % (width // parts)
        r_tile = r_ref[span, :]
        reach = dot(b_rows, r_tile, 1, 1)
        d_in = local[:, start : start + LANES] + dot(table, to_lanes(j, size), 1, 0) * reach
        d_in = d_in + dot(d_bc, w_ref[span, :], 1, 1)
        in_ref[:, span] = d_in.astype(BF16)
        product = x_ref[:, span].astype(F32) * reach
        seen = seen + dot(to_heads(j, heads, size), halves(product), 1, 1)
        edge = r_tile.astype(F32) * h_ref[span, :].astype(F32)
        for i in range(LANES // size):
            h = j * (LANES // size) + i
            edge_ref[h : h + 1, :] = jnp.sum(
                edge[i * size : (i + 1) * size], axis=0, keepdims=True
            )
    cumt = cumt_ref[...]
    total = cumt[:, length - 1 : length]
    to_end = jnp.exp(total - cumt)
    step = stept_ref[...]
    own = jnp.concatenate([r[...] for r in st_refs], axis=0)
    excess = jnp.concatenate([r[...] for r in ex_refs], axis=0)
    grad_ref[...] = own / step + to_end * seen
    edge = jnp.exp(total) * jnp.sum(edge_ref[...], axis=1, keepdims=True)
    decay_ref[...] = (
        dot(excess, triangle(length, lambda a, b: a >= b), 1, 0, HI)
        + dot(to_end * step * seen, triangle(length, lambda a, b: a < b), 1, 0, HI)
        + edge
    )


def term_kernel(places, n_columns, *refs):
    columns, pieces = refs[:n_columns], refs[n_columns:-3]
    keep_ref, send_ref, held = refs[-3:]
    pieces = [(p, i) for p in pieces for i in range(p.shape[0])]
    rows = 2 * keep_ref.shape[0]
    core, _, _ = core_and_chip()
    total = None
    for (a, start), (b, i) in zip(places, pieces):
        part = dot(columns[a][start : start + rows, :], b[i], 1, 0)
        total = part if total is None else total + part
    block = keep_ref.shape[0]
    held[0] = total[:block]
    held[1] = total[block:]
    keep_ref[...] = held[core]
    send_ref[...] = held[1 - core].astype(BF16)


def deal_kernel(keep_ref, recv_ref, own_ref, *refs):
    outs, held = refs[:-1], refs[-1]
    place, n_dp = lax.axis_index("dp"), lax.axis_size("dp")
    total = keep_ref[...] + recv_ref[...].astype(F32)
    share = own_ref.shape[0]
    for i in range(n_dp):
        held[i] = total[i * share : (i + 1) * share]
    own_ref[...] = held[place]
    for s, out in enumerate(outs):
        out[...] = held[place ^ (s + 1)].astype(BF16)


def expert_kernel(flip, slots, a_ref, b_ref, gate_ref, up_ref, out_ref, *scratch):
    rows_ref, gate_acc, up_acc = scratch
    step = pl.program_id(0)
    n_chip = a_ref.shape[0]

    @pl.when(step == 0)
    def _():
        for half, ref in enumerate((a_ref, b_ref)):
            for i in range(n_chip):
                row = (half * n_chip + i) * slots
                for t in range(rows_ref.shape[1] // LANES):
                    rows_ref[row : row + slots, t * LANES : (t + 1) * LANES] = ref[
                        i, t * slots : (t + 1) * slots, :
                    ]
        gate_acc[...] = jnp.zeros_like(gate_acc)
        up_acc[...] = jnp.zeros_like(up_acc)

    depth = gate_ref.shape[0]
    rows = rows_ref[:, rows_at(step, depth, LANES)]
    gate_acc[...] += dot(rows, gate_ref[...], 1, 0)
    up_acc[...] += dot(rows, up_ref[...], 1, 0)

    @pl.when(step == pl.num_programs(0) - 1)
    def _():
        weighted = jax.nn.silu(gate_acc[...]) * up_acc[...]
        out_ref[...] = (weighted.T if flip else weighted).astype(BF16)


def expert(a, b, w_gate, w_up, slots, flip, after):
    n_chip = a.shape[0]
    total = 2 * n_chip * slots
    width, hidden = w_gate.shape
    depth = 512
    out = (hidden, total) if flip else (total, hidden)

    def body(*refs):
        expert_kernel(flip, slots, *refs[:4], *refs[4 + len(after) :])

    whole = pl.BlockSpec(a.shape, lambda i: (0, 0, 0))
    block = pl.BlockSpec((depth, hidden), lambda i: (i, 0))
    return pl.pallas_call(
        body,
        out_shape=shape(out, BF16),
        grid=(width // depth,),
        in_specs=[whole, whole, block, block]
        + [pl.BlockSpec(memory_space=pl.ANY)] * len(after),
        out_specs=pl.BlockSpec(out, lambda i: (0, 0)),
        scratch_shapes=[
            pltpu.VMEM((total, width), BF16),
            pltpu.VMEM((total, hidden), F32),
            pltpu.VMEM((total, hidden), F32),
        ],
        cost_estimate=pl.CostEstimate(
            flops=int(3e9), bytes_accessed=1000, transcendentals=0
        ),
        compiler_params=pltpu.CompilerParams(vmem_limit_bytes=20 * 1024 * 1024),
    )(a, b, w_gate, w_up, *after)


def down_kernel(n_dp, flip, slots, grad_rows, *refs):
    pieces = refs[:n_dp]
    a_ref, b_ref, out_ref = refs[n_dp:]
    n_chip = a_ref.shape[0]
    piece = out_ref.shape[1]
    base = a_ref.shape[1] - n_dp * grad_rows
    total = None
    for s in range(n_dp):
        columns = []
        for t in range(grad_rows // slots):
            row = base + s * grad_rows + t * slots
            blocks = [r[i, row : row + slots, :] for r in (a_ref, b_ref) for i in range(n_chip)]
            columns.append(jnp.concatenate(blocks, axis=0))
        right = jnp.concatenate(columns, axis=1)[:, :piece]
        part = dot(pieces[s][...], right, 1 if flip else 0, 0)
        total = part if total is None else total + part
    out_ref[...] = total.astype(BF16)


def xored(array, axis, mask):
    count = lax.axis_size(axis)
    return lax.ppermute(array, axis, [(i, i ^ mask) for i in range(count)])


def swapped(array):
    return xored(array, "tm", 1)


def chips(arrays):
    return [arrays[0]] + [xored(a, "tm", 2 * s) for s, a in enumerate(arrays) if s]


def gathered(array, axis, count):
    if count == 1:
        return [array]
    far = xored(array, axis, count // 2)
    return gathered(array, axis, count // 2) + gathered(far, axis, count // 2)


def per_device(
    layer_in,
    out_grad,
    w_bc,
    log_decay,
    step,
    saved_states,
    w_gate,
    w_up,
    slot_rows,
    slot_counts,
    slot_gates,
):
    n_dp = lax.axis_size("dp")
    core, chip, n_chip = core_and_chip()
    x = layer_in[0]
    dy = out_grad[0]
    length, width = x.shape
    heads = log_decay.shape[2]
    size = width // heads
    share, columns = w_bc.shape
    half = columns // 2
    ldt = log_decay[0].T
    stept = step[0].T
    h_in = saved_states[0, 0].reshape(width, half)
    capacity = slot_rows.shape[2]
    piece = width // n_dp
    part = width // 2
    many = heads // 2
    flip = w_gate.shape[2] % LANES == 0

    grad_rows = -(-piece // LANES) * capacity
    w_half = lax.dynamic_slice_in_dim(w_bc, core * (share // 2), share // 2, 0)

    in_rows = width // LANES * capacity
    blocks = [1, 1, 2] if n_chip == 4 else [1] * n_chip
    groups = [2, 2] if n_dp == 4 else [1] * n_dp
    cumt, cum, steps, dyt, xs, carried, rows, *xt = call(
        lambda *refs: prep_kernel(len(groups), *refs),
        [
            shape((heads, length), F32),
            shape((length, LANES), F32),
            shape((length, LANES), F32),
            shape((width + up16(2 * heads), length), BF16),
            shape((length, width), BF16),
            shape((length, half), F32),
        ]
        + [shape((in_rows, LANES), BF16)]
        + [shape((k * grad_rows, LANES), BF16) for k in groups]
        + [shape((k * width // n_chip, length), BF16) for k in blocks],
        2.0,
        (x, dy, ldt, stept, h_in, slot_rows[0], slot_counts, slot_gates[0]),
        scratch=[
            pltpu.VMEM((width, length), BF16),
            pltpu.VMEM((n_dp, grad_rows, LANES), BF16),
        ],
        fetch=(0, 1, 2, 3, 4),
        limit=60,
    )
    rows_in = chips([rows] * n_chip)
    deals, xt = xt[: len(groups)], xt[len(groups) :]
    if n_dp == 4:
        one = (0, grad_rows), (grad_rows, 2 * grad_rows)
        over_2 = xored(deals[1], "dp", 2)
        over_1 = xored(joined([deals[0], over_2], ranges=[one[1], one[1]]), "dp", 1)
        dealt = joined([deals[0], over_1, over_2, over_1], (), [one[0], one[0], one[0], one[1]])
        first_hop, second_hop = (over_2,), (over_1,)
    else:
        first_hop = second_hop = ()
        dealt = joined(deals[:1] + [xored(d, "dp", s + 1) for s, d in enumerate(deals[1:])])
    w_far = xored(w_half, "dp", n_dp // 2)
    mine = gathered(w_half, "dp", n_dp // 2)[1:]
    mine += gathered(joined([w_far], after=(rows,)), "dp", n_dp // 2)
    other = swapped(stacked(mine, after=tuple(rows_in[1:])))
    rows_a = stacked(rows_in, after=(other,))
    rows_b = swapped(rows_a)
    w_whole, bc, keep, send = call(
        lambda *refs: project_kernel(n_dp - 1, many, *refs),
        [
            shape((width, columns), BF16),
            shape((length, columns), BF16),
            shape((part + up16(2 * many), half), BF16),
            shape((part + up16(2 * many), half), BF16),
        ],
        1.0,
        (x, dyt, w_bc, *mine, other),
        after=first_hop,
    )
    recv = swapped(send)
    hidden = w_gate.shape[2]
    climbs = [
        call(
            lambda *refs: combine_kernel(many, size, *refs),
            [shape((part + up16(2 * many), half), BF16)],
            0.5,
            (keep, recv),
            after=second_hop,
        )[0]
    ]
    weighted = expert(rows_a, rows_b, w_gate[0], w_up[0], capacity, flip, (climbs[0],))
    if n_chip == 4:
        x_rows = width // n_chip
        over_y = xored(joined([xt[2], dealt], (climbs[0],)), "tm", 4)

    parts = 2
    tiles = width // LANES // parts
    dxs, exs, owns = [], [], []
    later = (weighted,)
    mixed = jnp.zeros((length, length), F32)
    for i in range(parts):
        dx, mixed, ex, own = call(
            lambda *refs, i=i: intra_kernel(i * tiles, tiles, *refs),
            [
                shape((length, width // parts), F32),
                shape((length, length), F32),
                shape((heads // parts, length), F32),
                shape((heads // parts, length), F32),
            ],
            1.0,
            (x, dy, bc, cumt, cum, steps, h_in, mixed),
            after=later,
            scratch=[pltpu.VMEM((heads, length), F32)],
        )
        if i == 0:
            held = (dx, weighted, *((over_y,) if n_chip == 4 else ()))
            arrived = []
            bit = 1
            while bit < n_chip:
                last = bit * 2 == n_chip
                moves = [
                    (k, k ^ (2 * bit)) for k in range(2 * n_chip) if not last or k & (2 * bit)
                ]
                arrived.append(lax.ppermute(climbs[-1], "tm", moves))
                if not last:
                    climbs.append(
                        call(
                            lambda *refs, bit=bit: climb_kernel(many, size, bit, *refs),
                            [shape((part + up16(2 * many), half), BF16)],
                            0.5,
                            (climbs[-1], arrived[-1]),
                            after=held,
                        )[0]
                    )
                bit *= 2
            later = (climbs[-1],)
        dxs.append(dx)
        exs.append(ex)
        owns.append(own)
    db, dc = call(
        close_kernel,
        [shape((length, half), F32), shape((length, half), BF16)],
        0.3,
        (mixed, bc, carried),
    )

    held = (dc,)
    if n_chip == 4:
        over_x = xored(joined([xt[1], over_y], later, [(0, x_rows), (x_rows, 2 * x_rows)]), "tm", 2)
        columns_in = [xt[0], over_x, over_y]
        places = [(0, 0), (1, 0), (2, 0), (1, x_rows)]
        from_y = (2 * x_rows, over_y.shape[0])
        grads = joined([dealt, over_y], (later[0],), [(0, dealt.shape[0]), from_y])
        grads = [dealt, xored(grads, "tm", 2), over_y]
        spans = [(0, dealt.shape[0]), (0, dealt.shape[0]), from_y, (dealt.shape[0], 2 * dealt.shape[0])]
        grads = joined([grads[0], grads[1], grads[2], grads[1]], (), spans)
        held += (over_x,)
    else:
        columns_in = chips(xt)
        grads = joined(chips([dealt] * n_chip))
        places = [(i, 0) for i in range(n_chip)]
    far = xored(weighted, "dp", n_dp // 2)
    near = gathered(weighted, "dp", n_dp // 2)
    held += (far, *near[1:])
    r_own, r_send = call(
        lambda *refs: carry_kernel(many, size, len(arrived), *refs),
        [shape((part, half), BF16)] * 2,
        0.5,
        (*arrived, keep, recv),
        after=held,
    )
    grads_a = grads.reshape(n_chip, grads.shape[0] // n_chip, LANES)
    grads_b = swapped(grads_a)
    r_recv = swapped(r_send)
    fars = gathered(joined([far], (r_own,)), "dp", n_dp // 2)
    d_bc = call(db_kernel, [shape((length, columns), BF16)], 0.3, (xs, r_own, r_recv, db, dc))[0]
    d_bcs = [d_bc.reshape(1, length, columns)]
    while 2 ** (len(d_bcs) - 1) < n_chip:
        level = 2 ** (len(d_bcs) - 1)
        sent = d_bcs[0] if level == 1 else joined(d_bcs)
        d_bcs.append(xored(sent, "tm", 2 * level))
    d_in, d_decay, d_step, token = call(
        lambda *refs: finish_kernel(parts, *refs),
        [
            shape((length, width), BF16),
            shape((heads, length), F32),
            shape((heads, length), F32),
            shape((8, LANES), F32),
        ],
        3.0,
        (x, bc, cumt, stept, cum, steps, h_in, r_own, r_recv, w_whole, d_bc,
         *dxs, *exs, *owns),
        scratch=[pltpu.VMEM((width, half), BF16), pltpu.VMEM((heads, half), F32)],
    )
    w_rows = width // (2 * n_chip)
    term, term_send = call(
        lambda *refs: term_kernel(places, len(columns_in), *refs),
        [shape((w_rows, columns), F32), shape((w_rows, columns), BF16)],
        0.5,
        (*columns_in, *d_bcs),
        after=(token, *fars[1:]),
        scratch=[pltpu.VMEM((2, w_rows, columns), F32)],
    )
    final = call(
        deal_kernel,
        [shape((w_rows // n_dp, columns), F32)]
        + [shape((w_rows // n_dp, columns), BF16)] * (n_dp - 1),
        0.3,
        (term, swapped(term_send)),
        scratch=[pltpu.VMEM((n_dp, w_rows // n_dp, columns), F32)],
    )
    w_bc_grad = final[0]
    for s in range(1, n_dp):
        w_bc_grad = w_bc_grad + xored(final[s], "dp", s).astype(F32)

    w_down_grad = call(
        lambda *refs: down_kernel(n_dp, flip, capacity, grad_rows, *refs),
        [shape((hidden, piece), BF16)],
        1.0,
        (*near, *fars, grads_a, grads_b),
        after=(final[0],),
    )[0]
    return (d_in[None], d_decay.T[None], d_step.T[None], w_bc_grad, w_down_grad[None])


def solution(mesh):
    in_specs = (
        P("dp", "tm", None),
        P("dp", "tm", None),
        P("dp", None),
        P("dp", "tm", None),
        P("dp", "tm", None),
        P("dp", "tm", None, None, None),
        P(None, None, "tm"),
        P(None, None, "tm"),
        P("dp", None, "tm"),
        P("dp", "tm"),
        P("dp", None, "tm"),
    )
    out_specs = (
        P("dp", "tm", None),
        P("dp", "tm", None),
        P("dp", "tm", None),
        P(("tm", "dp"), None),
        P(None, "tm", "dp"),
    )
    return jax.shard_map(
        per_device, mesh=mesh, in_specs=in_specs, out_specs=out_specs, check_vma=False
    )
```

```python
import jax
import jax.numpy as jnp
from jax import lax
from jax.experimental import pallas as pl
from jax.experimental.pallas import tpu as pltpu
from jax.sharding import PartitionSpec as P

HI = lax.Precision.HIGHEST
F32 = jnp.float32
BF16 = jnp.bfloat16
LANES = 128


def dot(a, b, ca, cb, precision=None):
    return lax.dot_general(
        a, b, (((ca,), (cb,)), ((), ())), precision=precision, preferred_element_type=F32
    )


def iota(dims, axis):
    return lax.broadcasted_iota(jnp.int32, dims, axis)


def where_one(mask):
    return jnp.where(mask, 1.0, 0.0)


def triangle(n, keep):
    return where_one(keep(iota((n, n), 0), iota((n, n), 1))).astype(F32)


def halves(values, axis=1):
    high = values.astype(BF16)
    low = (values - high.astype(F32)).astype(BF16)
    return jnp.concatenate([high, low], axis=axis)


def to_lanes(j, size):
    dims = (LANES, LANES)
    one = where_one(iota(dims, 0) == iota(dims, 1) // size + j * (LANES // size)).astype(BF16)
    return jnp.concatenate([one, one], axis=0)


def to_heads(j, heads, size):
    dims = (heads, LANES)
    one = where_one(iota(dims, 0) == iota(dims, 1) // size + j * (LANES // size)).astype(BF16)
    return jnp.concatenate([one, one], axis=1)


def up16(n):
    return -(-n // 16) * 16


def call(kernel, outs, cost, args, after=(), scratch=(), limit=14, fetch=()):
    n_in, n_after, n_out = len(args), len(after), len(outs)
    fetch = tuple(fetch)

    def body(*refs):
        ins = list(refs[:n_in])
        rest = refs[n_in + n_after :]
        if fetch:
            sems = rest[-1]
            held = rest[len(rest) - 1 - len(fetch) : -1]
            rest = rest[: len(rest) - 1 - len(fetch)]
            copies = []
            for i, (index, ref) in enumerate(zip(fetch, held)):
                copies.append(pltpu.make_async_copy(ins[index], ref, sems.at[i]))
                ins[index] = ref
            for copy in copies:
                copy.start()
            for copy in copies:
                copy.wait()
        kernel(*ins, *rest)

    specs = [
        pl.BlockSpec(memory_space=pltpu.HBM if i in fetch else pltpu.VMEM) for i in range(n_in)
    ]
    held = [pltpu.VMEM(args[i].shape, args[i].dtype) for i in fetch]
    if fetch:
        held.append(pltpu.SemaphoreType.DMA((len(fetch),)))
    return pl.pallas_call(
        body,
        out_shape=outs,
        in_specs=specs + [pl.BlockSpec(memory_space=pl.ANY)] * n_after,
        out_specs=[pl.BlockSpec(memory_space=pltpu.VMEM)] * n_out,
        scratch_shapes=list(scratch) + held,
        cost_estimate=pl.CostEstimate(
            flops=int(cost * 3e9), bytes_accessed=1000, transcendentals=0
        ),
        compiler_params=pltpu.CompilerParams(vmem_limit_bytes=limit * 1024 * 1024),
    )(*args, *after)


def shape(dims, kind):
    return jax.ShapeDtypeStruct(dims, kind)


def core_and_chip():
    place = lax.axis_index("tm")
    return lax.rem(place, 2), lax.div(place, 2), lax.axis_size("tm") // 2


def rows_at(index, size, align=16):
    return pl.ds(pl.multiple_of(index * size, align), size)


def picked(x_ref, dy_ref, slot_ref, count_ref, gate_ref, rows_ref, out_refs):
    length, width = x_ref.shape
    slots = slot_ref.shape[1]
    hit = iota((length, slots), 0) == slot_ref[...]
    live = iota((1, slots), 1) < count_ref[...]
    weight = jnp.where(live, gate_ref[...].astype(F32), 0.0)
    rows = dot(where_one(hit).astype(BF16), x_ref[...], 0, 0).astype(BF16)
    for t in range(width // LANES):
        rows_ref[t * slots : (t + 1) * slots, :] = rows[:, t * LANES : (t + 1) * LANES]
    grads = dot(jnp.where(hit, weight, 0.0).astype(BF16), dy_ref[...], 0, 0).astype(BF16)
    held = out_refs[-1]
    n_dp = held.shape[0]
    piece = width // n_dp
    for i in range(n_dp):
        for t, low in enumerate(range(i * piece, (i + 1) * piece, LANES)):
            block = grads[:, low : min(low + LANES, (i + 1) * piece)]
            if block.shape[1] < LANES:
                fill = jnp.zeros((slots, LANES - block.shape[1]), BF16)
                block = jnp.concatenate([block, fill], axis=1)
            held[i, t * slots : (t + 1) * slots, :] = block
    place = lax.axis_index("dp")
    s = 0
    for out in out_refs[:-1]:
        for start in range(0, out.shape[0], held.shape[1]):
            out[start : start + held.shape[1], :] = held[place ^ s]
            s += 1


def high_low(values):
    high = values.astype(BF16).astype(F32)
    return [high, values - high]


def prep_kernel(
    n_deals, x_ref, dy_ref, ldt_ref, stept_ref, h_ref, slot_ref, count_ref, gate_ref,
    cumt_ref, cum_ref, step_ref, dyt_ref, xs_ref, carried_ref, rows_ref, *rest,
):
    outs, xt_ref, held_ref = rest[n_deals:-2], rest[-2], rest[-1]
    length, width = x_ref.shape
    heads = ldt_ref.shape[0]
    size = width // heads
    _, chip, n_chip = core_and_chip()
    picked(x_ref, dy_ref, slot_ref, count_ref, gate_ref, rows_ref, (*rest[:n_deals], held_ref))
    pad = jnp.zeros((LANES - heads, length), F32)
    cumt = dot(ldt_ref[...], triangle(length, lambda a, b: a <= b), 1, 0, HI)
    cumt_ref[...] = cumt
    cum = jnp.concatenate([cumt, pad], axis=0).T
    step = jnp.concatenate([stept_ref[...], pad], axis=0).T
    cum_ref[...] = cum
    step_ref[...] = step
    start = jnp.exp(cum)
    into_end = jnp.exp(cum[length - 1 : length] - cum) * step
    table = jnp.concatenate([halves(start), halves(into_end)], axis=0)
    carried = jnp.zeros(carried_ref.shape, F32)
    for j in range(width // LANES):
        span = slice(j * LANES, (j + 1) * LANES)
        scale = dot(table, to_lanes(j, size), 1, 0)
        x_f = x_ref[:, span].astype(F32)
        xt_ref[span, :] = x_f.T.astype(BF16)
        xs_ref[:, span] = (x_f * scale[length:]).astype(BF16)
        dys = dy_ref[:, span].astype(F32) * scale[:length]
        dyt_ref[span, :] = dys.T.astype(BF16)
        carried = carried + dot(dys.astype(BF16), h_ref[span, :], 1, 0)
    carried_ref[...] = carried
    decay = jnp.broadcast_to(jnp.exp(cumt[:, length - 1 : length]), (heads, LANES))
    dyt_ref[width : width + 2 * heads, :] = jnp.concatenate(high_low(decay), axis=0).astype(BF16)
    block = width // n_chip
    s = 0
    for out in outs:
        for start in range(0, out.shape[0], block):
            out[start : start + block, :] = xt_ref[rows_at(chip ^ s, block), :]
            s += 1


def join_kernel(ranges, *refs):
    out, at = refs[-1], 0
    for ref, (start, stop) in zip(refs, ranges):
        out[at : at + stop - start] = ref[start:stop]
        at += stop - start


def joined(arrays, after=(), ranges=None, cost=0.2):
    ranges = ranges or [(0, a.shape[0]) for a in arrays]
    dims = (sum(stop - start for start, stop in ranges), *arrays[0].shape[1:])
    return call(
        lambda *refs: join_kernel(ranges, *refs),
        [shape(dims, arrays[0].dtype)],
        cost,
        tuple(arrays),
        after=after,
    )[0]


def stacked(arrays, after=(), ranges=None, cost=0.2):
    count = len(arrays)
    out = joined(arrays, after, ranges, cost)
    return out.reshape(count, out.shape[0] // count, *out.shape[1:])


def project_kernel(n_mine, many, *refs):
    x_ref, dyt_ref, own_ref = refs[:3]
    mine, other = refs[3 : 3 + n_mine], refs[3 + n_mine]
    w_ref, bc_ref, keep_ref, send_ref = refs[4 + n_mine :]
    core, _, _ = core_and_chip()
    place, n_dp = lax.axis_index("dp"), lax.axis_size("dp")
    share = own_ref.shape[0]
    half = share // 2
    w_ref[rows_at(place, share), :] = own_ref[...]
    for i in range(n_mine):
        source = place ^ (i + 1)
        w_ref[rows_at(source * 2 + core, half), :] = mine[i][...]
        w_ref[rows_at(source * 2 + 1 - core, half), :] = other[i]
    bc = dot(x_ref[...], w_ref[...], 1, 0).astype(BF16)
    bc_ref[...] = bc
    c_rows = bc[:, LANES:]
    width = x_ref.shape[1]
    part = width // 2
    for ref, index in ((keep_ref, core), (send_ref, 1 - core)):
        ref[:part, :] = dot(dyt_ref[rows_at(index, part), :], c_rows, 1, 0).astype(BF16)
        table = dyt_ref[width : width + 4 * many, :].astype(F32)
        quarter = [table[i * many : (i + 1) * many] for i in range(4)]
        high = jnp.where(index == 0, quarter[0], quarter[1])
        low = jnp.where(index == 0, quarter[2], quarter[3])
        fill = jnp.zeros((ref.shape[0] - part - 2 * many, LANES), F32)
        ref[part:, :] = jnp.concatenate([high, low, fill], axis=0).astype(BF16)


def pair(keep_ref, recv_ref, many, size, head):
    core, _, _ = core_and_chip()
    part = many * size
    both = []
    for ref in (keep_ref, recv_ref):
        extra = ref[part:, :].astype(F32)
        decay = extra[head : head + 1] + extra[many + head : many + head + 1]
        both.append((ref[head * size : (head + 1) * size, :].astype(F32), decay))
    first = jax.tree.map(lambda a, b: jnp.where(core == 0, a, b), both[0], both[1])
    second = jax.tree.map(lambda a, b: jnp.where(core == 0, b, a), both[0], both[1])
    return first, second


def payload(ref, many, states, decays):
    size = states[0].shape[0]
    for head, state in enumerate(states):
        ref[head * size : (head + 1) * size, :] = state.astype(BF16)
    decay = jnp.concatenate(decays, axis=0)
    high = decay.astype(BF16).astype(F32)
    fill = jnp.zeros((ref.shape[0] - many * size - 2 * many, LANES), F32)
    extra = jnp.concatenate([high, decay - high, fill], axis=0)
    ref[many * size :, :] = extra.astype(BF16)


def loaded(ref, many, size, head):
    extra = ref[many * size :, :].astype(F32)
    decay = extra[head : head + 1] + extra[many + head : many + head + 1]
    return ref[head * size : (head + 1) * size, :].astype(F32), decay


def combine_kernel(many, size, keep_ref, recv_ref, out_ref):
    states, decays = [], []
    for head in range(many):
        (g0, a0), (g1, a1) = pair(keep_ref, recv_ref, many, size, head)
        states.append(g0 + a0 * g1)
        decays.append(a0 * a1)
    payload(out_ref, many, states, decays)


def pick_side(upper, mine, theirs):
    return jnp.where(upper, theirs, mine), jnp.where(upper, mine, theirs)


def climb_kernel(many, size, bit, mine_ref, recv_ref, out_ref):
    _, chip, _ = core_and_chip()
    upper = lax.rem(lax.div(chip, bit), 2) == 1
    states, decays = [], []
    for head in range(many):
        t_mine, a_mine = loaded(mine_ref, many, size, head)
        t_recv, a_recv = loaded(recv_ref, many, size, head)
        t_low, t_high = pick_side(upper, t_mine, t_recv)
        a_low, a_high = pick_side(upper, a_mine, a_recv)
        states.append(t_low + a_low * t_high)
        decays.append(a_low * a_high)
    payload(out_ref, many, states, decays)


def carry_kernel(many, size, levels, *refs):
    core, chip, _ = core_and_chip()
    recvs = refs[:levels]
    keep_ref, recv_ref, own_ref, send_ref = refs[levels:]
    for head in range(many):
        span = slice(head * size, (head + 1) * size)
        carry, reach = None, None
        for level, ref in enumerate(recvs):
            state, decay = loaded(ref, many, size, head)
            lower = lax.rem(lax.div(chip, 2**level), 2) == 0
            state = jnp.where(lower, state, 0.0)
            decay = jnp.where(lower, decay, 1.0)
            carry = state if carry is None else carry + reach * state
            reach = decay if reach is None else reach * decay
        _, (g1, a1) = pair(keep_ref, recv_ref, many, size, head)
        second = carry
        first = g1 + a1 * second
        own_ref[span, :] = jnp.where(core == 0, first, second).astype(BF16)
        send_ref[span, :] = jnp.where(core == 0, second, first).astype(BF16)


def intra_kernel(
    first, many, x_ref, dy_ref, bc_ref, cumt_ref, cum_ref, step_ref, h_ref, before_ref,
    dx_ref, mixed_ref, ex_ref, own_ref, rowm_ref,
):
    length, width = x_ref.shape
    heads = cumt_ref.shape[0]
    size = width // heads
    per = LANES // size
    upper = iota((length, length), 0) <= iota((length, length), 1)
    b_rows, c_rows = bc_ref[:, :LANES], bc_ref[:, LANES:]
    scores = dot(b_rows, c_rows, 1, 1)
    lane = iota((1, LANES), 1)
    lane_bf = [where_one(lane // size == i).astype(BF16) for i in range(per)]
    mixed = before_ref[...]
    own = jnp.zeros((length, LANES), F32)
    reach = jnp.zeros((heads, length), F32)
    for j in range(first, first + many):
        span = slice(j * LANES, (j + 1) * LANES)
        out_span = slice((j - first) * LANES, (j - first + 1) * LANES)
        x_p = x_ref[:, span]
        dy_p = dy_ref[:, span]
        dy_h = jnp.concatenate([dy_p * m for m in lane_bf], axis=0)
        cross = dot(x_p, dy_h, 1, 1)
        kern = []
        wide = None
        for i in range(per):
            h = j * per + i
            diff = cumt_ref[h : h + 1, :] - cum_ref[:, h : h + 1]
            seg = jnp.exp(jnp.where(upper, diff, -1e30))
            kern.append((seg * scores).astype(BF16))
            step = jnp.broadcast_to(step_ref[:, h : h + 1], (length, LANES))
            wide = step if i == 0 else jnp.where(lane < i * size, wide, step)
            scaled = seg * cross[:, i * length : (i + 1) * length] * step
            mixed = mixed + scaled
            full = scaled * scores
            rowm_ref[h : h + 1, :] = jnp.sum(full, axis=0, keepdims=True)
            own = jnp.where(lane == h, jnp.sum(full, axis=1, keepdims=True), own)
        back = dot(jnp.concatenate(kern, axis=1), dy_h, 1, 0)
        dx_ref[:, out_span] = back * wide
        seen = dy_p.astype(F32) * dot(c_rows, h_ref[span, :], 1, 1)
        reach = reach + dot(to_heads(j, heads, size), halves(seen), 1, 1)
    mixed_ref[...] = mixed
    rows = slice(first * per, (first + many) * per)
    own = own.T[rows]
    own_ref[...] = own
    ex_ref[...] = rowm_ref[rows, :] + jnp.exp(cumt_ref[rows, :]) * reach[rows] - own


def close_kernel(mixed_ref, bc_ref, carried_ref, db_ref, dc_ref):
    mixed = mixed_ref[...].astype(BF16)
    db_ref[...] = dot(mixed, bc_ref[:, LANES:], 1, 0)
    dc_ref[...] = (dot(mixed, bc_ref[:, :LANES], 0, 0) + carried_ref[...]).astype(BF16)


def db_kernel(xs_ref, own_ref, recv_ref, db_ref, dc_ref, out_ref):
    core, _, _ = core_and_chip()
    half = db_ref.shape[1]
    part = own_ref.shape[0]
    total = db_ref[...]
    for ref, index in ((own_ref, core), (recv_ref, 1 - core)):
        total = total + dot(xs_ref[:, rows_at(index, part, LANES)], ref[...], 1, 0)
    out_ref[:, :half] = total.astype(BF16)
    out_ref[:, half:] = dc_ref[...]


def finish_kernel(parts, *refs):
    (x_ref, bc_ref, cumt_ref, stept_ref, cum_ref, step_ref, h_ref, own_ref, recv_ref,
     w_ref, dbc_ref) = refs[:11]
    dx_refs, ex_refs, st_refs = (refs[11 + i * parts : 11 + (i + 1) * parts] for i in range(3))
    in_ref, decay_ref, grad_ref, token_ref, r_ref, edge_ref = refs[11 + 3 * parts :]
    token_ref[...] = jnp.zeros_like(token_ref)
    core, _, _ = core_and_chip()
    length, width = x_ref.shape
    heads = cumt_ref.shape[0]
    size = width // heads
    part = width // 2
    r_ref[rows_at(core, part), :] = own_ref[...]
    r_ref[rows_at(1 - core, part), :] = recv_ref[...]
    cum = cum_ref[...]
    table = halves(jnp.exp(cum[length - 1 : length] - cum) * step_ref[...])
    seen = jnp.zeros((heads, length), F32)
    b_rows = bc_ref[:, :LANES]
    d_bc = dbc_ref[...]
    for j in range(width // LANES):
        span = slice(j * LANES, (j + 1) * LANES)
        local = dx_refs[j * LANES // (width // parts)]
        start = j * LANES % (width // parts)
        r_tile = r_ref[span, :]
        reach = dot(b_rows, r_tile, 1, 1)
        d_in = local[:, start : start + LANES] + dot(table, to_lanes(j, size), 1, 0) * reach
        d_in = d_in + dot(d_bc, w_ref[span, :], 1, 1)
        in_ref[:, span] = d_in.astype(BF16)
        product = x_ref[:, span].astype(F32) * reach
        seen = seen + dot(to_heads(j, heads, size), halves(product), 1, 1)
        edge = r_tile.astype(F32) * h_ref[span, :].astype(F32)
        for i in range(LANES // size):
            h = j * (LANES // size) + i
            edge_ref[h : h + 1, :] = jnp.sum(
                edge[i * size : (i + 1) * size], axis=0, keepdims=True
            )
    cumt = cumt_ref[...]
    total = cumt[:, length - 1 : length]
    to_end = jnp.exp(total - cumt)
    step = stept_ref[...]
    own = jnp.concatenate([r[...] for r in st_refs], axis=0)
    excess = jnp.concatenate([r[...] for r in ex_refs], axis=0)
    grad_ref[...] = own / step + to_end * seen
    edge = jnp.exp(total) * jnp.sum(edge_ref[...], axis=1, keepdims=True)
    decay_ref[...] = (
        dot(excess, triangle(length, lambda a, b: a >= b), 1, 0, HI)
        + dot(to_end * step * seen, triangle(length, lambda a, b: a < b), 1, 0, HI)
        + edge
    )


def term_kernel(places, n_columns, *refs):
    columns, pieces = refs[:n_columns], refs[n_columns:-3]
    keep_ref, send_ref, held = refs[-3:]
    pieces = [(p, i) for p in pieces for i in range(p.shape[0])]
    rows = 2 * keep_ref.shape[0]
    core, _, _ = core_and_chip()
    total = None
    for (a, start), (b, i) in zip(places, pieces):
        part = dot(columns[a][start : start + rows, :], b[i], 1, 0)
        total = part if total is None else total + part
    block = keep_ref.shape[0]
    held[0] = total[:block]
    held[1] = total[block:]
    keep_ref[...] = held[core]
    send_ref[...] = held[1 - core].astype(BF16)


def deal_kernel(keep_ref, recv_ref, own_ref, *refs):
    outs, held = refs[:-1], refs[-1]
    place, n_dp = lax.axis_index("dp"), lax.axis_size("dp")
    total = keep_ref[...] + recv_ref[...].astype(F32)
    share = own_ref.shape[0]
    for i in range(n_dp):
        held[i] = total[i * share : (i + 1) * share]
    own_ref[...] = held[place]
    for s, out in enumerate(outs):
        out[...] = held[place ^ (s + 1)].astype(BF16)


def expert_kernel(flip, slots, a_ref, b_ref, gate_ref, up_ref, out_ref, *scratch):
    rows_ref, gate_acc, up_acc = scratch
    step = pl.program_id(0)
    n_chip = a_ref.shape[0]

    @pl.when(step == 0)
    def _():
        for half, ref in enumerate((a_ref, b_ref)):
            for i in range(n_chip):
                row = (half * n_chip + i) * slots
                for t in range(rows_ref.shape[1] // LANES):
                    rows_ref[row : row + slots, t * LANES : (t + 1) * LANES] = ref[
                        i, t * slots : (t + 1) * slots, :
                    ]
        gate_acc[...] = jnp.zeros_like(gate_acc)
        up_acc[...] = jnp.zeros_like(up_acc)

    depth = gate_ref.shape[0]
    rows = rows_ref[:, rows_at(step, depth, LANES)]
    gate_acc[...] += dot(rows, gate_ref[...], 1, 0)
    up_acc[...] += dot(rows, up_ref[...], 1, 0)

    @pl.when(step == pl.num_programs(0) - 1)
    def _():
        weighted = jax.nn.silu(gate_acc[...]) * up_acc[...]
        out_ref[...] = (weighted.T if flip else weighted).astype(BF16)


def expert(a, b, w_gate, w_up, slots, flip, after):
    n_chip = a.shape[0]
    total = 2 * n_chip * slots
    width, hidden = w_gate.shape
    depth = 512
    out = (hidden, total) if flip else (total, hidden)

    def body(*refs):
        expert_kernel(flip, slots, *refs[:4], *refs[4 + len(after) :])

    whole = pl.BlockSpec(a.shape, lambda i: (0, 0, 0))
    block = pl.BlockSpec((depth, hidden), lambda i: (i, 0))
    return pl.pallas_call(
        body,
        out_shape=shape(out, BF16),
        grid=(width // depth,),
        in_specs=[whole, whole, block, block]
        + [pl.BlockSpec(memory_space=pl.ANY)] * len(after),
        out_specs=pl.BlockSpec(out, lambda i: (0, 0)),
        scratch_shapes=[
            pltpu.VMEM((total, width), BF16),
            pltpu.VMEM((total, hidden), F32),
            pltpu.VMEM((total, hidden), F32),
        ],
        cost_estimate=pl.CostEstimate(
            flops=int(1e9), bytes_accessed=1000, transcendentals=0
        ),
        compiler_params=pltpu.CompilerParams(vmem_limit_bytes=20 * 1024 * 1024),
    )(a, b, w_gate, w_up, *after)


def down_kernel(n_dp, flip, slots, grad_rows, *refs):
    pieces = refs[:n_dp]
    a_ref, b_ref, out_ref = refs[n_dp:]
    n_chip = a_ref.shape[0]
    piece = out_ref.shape[1]
    base = a_ref.shape[1] - n_dp * grad_rows
    total = None
    for s in range(n_dp):
        columns = []
        for t in range(grad_rows // slots):
            row = base + s * grad_rows + t * slots
            blocks = [r[i, row : row + slots, :] for r in (a_ref, b_ref) for i in range(n_chip)]
            columns.append(jnp.concatenate(blocks, axis=0))
        right = jnp.concatenate(columns, axis=1)[:, :piece]
        part = dot(pieces[s][...], right, 1 if flip else 0, 0)
        total = part if total is None else total + part
    out_ref[...] = total.astype(BF16)


def xored(array, axis, mask):
    count = lax.axis_size(axis)
    return lax.ppermute(array, axis, [(i, i ^ mask) for i in range(count)])


def swapped(array):
    return xored(array, "tm", 1)


def chips(arrays):
    return [arrays[0]] + [xored(a, "tm", 2 * s) for s, a in enumerate(arrays) if s]


def gathered(array, axis, count):
    if count == 1:
        return [array]
    far = xored(array, axis, count // 2)
    return gathered(array, axis, count // 2) + gathered(far, axis, count // 2)


def per_device(
    layer_in,
    out_grad,
    w_bc,
    log_decay,
    step,
    saved_states,
    w_gate,
    w_up,
    slot_rows,
    slot_counts,
    slot_gates,
):
    n_dp = lax.axis_size("dp")
    core, chip, n_chip = core_and_chip()
    x = layer_in[0]
    dy = out_grad[0]
    length, width = x.shape
    heads = log_decay.shape[2]
    size = width // heads
    share, columns = w_bc.shape
    half = columns // 2
    ldt = log_decay[0].T
    stept = step[0].T
    h_in = saved_states[0, 0].reshape(width, half)
    capacity = slot_rows.shape[2]
    piece = width // n_dp
    part = width // 2
    many = heads // 2
    flip = w_gate.shape[2] % LANES == 0

    grad_rows = -(-piece // LANES) * capacity
    w_half = lax.dynamic_slice_in_dim(w_bc, core * (share // 2), share // 2, 0)

    in_rows = width // LANES * capacity
    blocks = [1, 1, 2] if n_chip == 4 else [1] * n_chip
    groups = [2, 2] if n_dp == 4 else [1] * n_dp
    cumt, cum, steps, dyt, xs, carried, rows, *xt = call(
        lambda *refs: prep_kernel(len(groups), *refs),
        [
            shape((heads, length), F32),
            shape((length, LANES), F32),
            shape((length, LANES), F32),
            shape((width + up16(2 * heads), length), BF16),
            shape((length, width), BF16),
            shape((length, half), F32),
        ]
        + [shape((in_rows, LANES), BF16)]
        + [shape((k * grad_rows, LANES), BF16) for k in groups]
        + [shape((k * width // n_chip, length), BF16) for k in blocks],
        2.0,
        (x, dy, ldt, stept, h_in, slot_rows[0], slot_counts, slot_gates[0]),
        scratch=[
            pltpu.VMEM((width, length), BF16),
            pltpu.VMEM((n_dp, grad_rows, LANES), BF16),
        ],
        fetch=(0, 1, 2, 3, 4),
        limit=60,
    )
    rows_in = chips([rows] * n_chip)
    deals, xt = xt[: len(groups)], xt[len(groups) :]
    if n_dp == 4:
        one = (0, grad_rows), (grad_rows, 2 * grad_rows)
        over_2 = xored(deals[1], "dp", 2)
        early = (over_2,)
    else:
        early = ()
        source, spans = deals[:1] + [xored(d, "dp", s + 1) for s, d in enumerate(deals[1:])], None
    w_far = xored(w_half, "dp", n_dp // 2)
    mine = gathered(w_half, "dp", n_dp // 2)[1:]
    mine += gathered(joined([w_far], after=(rows,)), "dp", n_dp // 2)
    other = swapped(stacked(mine, after=(*rows_in[1:3],), cost=1.0))
    w_whole, bc, keep, send = call(
        lambda *refs: project_kernel(n_dp - 1, many, *refs),
        [
            shape((width, columns), BF16),
            shape((length, columns), BF16),
            shape((part + up16(2 * many), half), BF16),
            shape((part + up16(2 * many), half), BF16),
        ],
        1.0,
        (x, dyt, w_bc, *mine, other),
    )
    recv = swapped(send)
    hidden = w_gate.shape[2]
    climbs = [
        call(
            lambda *refs: combine_kernel(many, size, *refs),
            [shape((part + up16(2 * many), half), BF16)],
            0.5,
            (keep, recv),
        )[0]
    ]
    rows_a = stacked(rows_in, after=(climbs[0],))
    rows_b = swapped(rows_a)
    weighted = expert(rows_a, rows_b, w_gate[0], w_up[0], capacity, flip, (climbs[0],))
    if n_chip == 4:
        x_rows = width // n_chip
        over_y = xored(xt[2], "tm", 4)

    parts = 2
    tiles = width // LANES // parts
    dxs, exs, owns = [], [], []
    later = (weighted,)
    mixed = jnp.zeros((length, length), F32)
    for i in range(parts):
        dx, mixed, ex, own = call(
            lambda *refs, i=i: intra_kernel(i * tiles, tiles, *refs),
            [
                shape((length, width // parts), F32),
                shape((length, length), F32),
                shape((heads // parts, length), F32),
                shape((heads // parts, length), F32),
            ],
            0.7,
            (x, dy, bc, cumt, cum, steps, h_in, mixed),
            after=later,
            scratch=[pltpu.VMEM((heads, length), F32)],
        )
        if i == 0:
            held = (dx, weighted, *early, *((over_y,) if n_chip == 4 else ()))
            arrived = []
            bit = 1
            while bit < n_chip:
                last = bit * 2 == n_chip
                moves = [
                    (k, k ^ (2 * bit)) for k in range(2 * n_chip) if not last or k & (2 * bit)
                ]
                arrived.append(lax.ppermute(climbs[-1], "tm", moves))
                if not last:
                    climbs.append(
                        call(
                            lambda *refs, bit=bit: climb_kernel(many, size, bit, *refs),
                            [shape((part + up16(2 * many), half), BF16)],
                            0.5,
                            (climbs[-1], arrived[-1]),
                            after=held,
                        )[0]
                    )
                bit *= 2
            later = (climbs[-1],)
        dxs.append(dx)
        exs.append(ex)
        owns.append(own)
    db, dc = call(
        close_kernel,
        [shape((length, half), F32), shape((length, half), BF16)],
        0.3,
        (mixed, bc, carried),
    )

    held = (dc,)
    if n_dp == 4:
        over_1 = xored(joined([deals[0], over_2], later, [one[1], one[1]]), "dp", 1)
        source, spans = [deals[0], over_1, over_2, over_1], [one[0], one[0], one[0], one[1]]
    dealt = joined(source, later, spans)
    held += (dealt,)
    if n_chip == 4:
        over_x = xored(joined([xt[1], over_y], later, [(0, x_rows), (x_rows, 2 * x_rows)]), "tm", 2)
        columns_in = [xt[0], over_x, over_y]
        places = [(0, 0), (1, 0), (2, 0), (1, x_rows)]
        held += (over_x,)
    else:
        columns_in = chips(xt)
        places = [(i, 0) for i in range(n_chip)]
    far = xored(weighted, "dp", n_dp // 2)
    near = gathered(weighted, "dp", n_dp // 2)
    held += (far, *near[1:])
    r_own, r_send = call(
        lambda *refs: carry_kernel(many, size, len(arrived), *refs),
        [shape((part, half), BF16)] * 2,
        0.5,
        (*arrived, keep, recv),
        after=held,
    )
    r_recv = swapped(r_send)
    if n_chip == 4:
        grads_y = xored(dealt, "tm", 4)
        grads_x = xored(joined([dealt, grads_y], (r_own,)), "tm", 2)
        rest = dealt.shape[0]
        grads = [dealt, grads_x, grads_y, grads_x]
        spans = [(0, rest), (0, rest), (0, rest), (rest, 2 * rest)]
    else:
        grads, spans = chips([dealt] * n_chip), None
    fars = gathered(joined([far], (r_own,)), "dp", n_dp // 2)
    d_bc = call(db_kernel, [shape((length, columns), BF16)], 0.3, (xs, r_own, r_recv, db, dc))[0]
    d_bcs = [d_bc.reshape(1, length, columns)]
    while 2 ** (len(d_bcs) - 1) < n_chip:
        level = 2 ** (len(d_bcs) - 1)
        sent = d_bcs[0] if level == 1 else joined(d_bcs, tuple(fars[1:]))
        d_bcs.append(xored(sent, "tm", 2 * level))
    d_in, d_decay, d_step, token = call(
        lambda *refs: finish_kernel(parts, *refs),
        [
            shape((length, width), BF16),
            shape((heads, length), F32),
            shape((heads, length), F32),
            shape((8, LANES), F32),
        ],
        3.0,
        (x, bc, cumt, stept, cum, steps, h_in, r_own, r_recv, w_whole, d_bc,
         *dxs, *exs, *owns),
        scratch=[pltpu.VMEM((width, half), BF16), pltpu.VMEM((heads, half), F32)],
    )
    w_rows = width // (2 * n_chip)
    term, term_send = call(
        lambda *refs: term_kernel(places, len(columns_in), *refs),
        [shape((w_rows, columns), F32), shape((w_rows, columns), BF16)],
        0.5,
        (*columns_in, *d_bcs),
        after=(token,),
        scratch=[pltpu.VMEM((2, w_rows, columns), F32)],
    )
    final = call(
        deal_kernel,
        [shape((w_rows // n_dp, columns), F32)]
        + [shape((w_rows // n_dp, columns), BF16)] * (n_dp - 1),
        0.3,
        (term, swapped(term_send)),
        scratch=[pltpu.VMEM((n_dp, w_rows // n_dp, columns), F32)],
    )
    w_bc_grad = final[0]
    for s in range(1, n_dp):
        w_bc_grad = w_bc_grad + xored(final[s], "dp", s).astype(F32)

    grads_a = stacked(grads, (token,), spans)
    grads_b = swapped(grads_a)
    w_down_grad = call(
        lambda *refs: down_kernel(n_dp, flip, capacity, grad_rows, *refs),
        [shape((hidden, piece), BF16)],
        1.0,
        (*near, *fars, grads_a, grads_b),
        after=(final[0],),
    )[0]
    return (d_in[None], d_decay.T[None], d_step.T[None], w_bc_grad, w_down_grad[None])


def solution(mesh):
    in_specs = (
        P("dp", "tm", None),
        P("dp", "tm", None),
        P("dp", None),
        P("dp", "tm", None),
        P("dp", "tm", None),
        P("dp", "tm", None, None, None),
        P(None, None, "tm"),
        P(None, None, "tm"),
        P("dp", None, "tm"),
        P("dp", "tm"),
        P("dp", None, "tm"),
    )
    out_specs = (
        P("dp", "tm", None),
        P("dp", "tm", None),
        P("dp", "tm", None),
        P(("tm", "dp"), None),
        P(None, "tm", "dp"),
    )
    return jax.shard_map(
        per_device, mesh=mesh, in_specs=in_specs, out_specs=out_specs, check_vma=False
    )
```

```python
import jax
import jax.numpy as jnp
from jax import lax
from jax.experimental import pallas as pl
from jax.experimental.pallas import tpu as pltpu
from jax.sharding import PartitionSpec as P

HI = lax.Precision.HIGHEST
F32 = jnp.float32
BF16 = jnp.bfloat16
LANES = 128


def dot(a, b, ca, cb, precision=None):
    return lax.dot_general(
        a, b, (((ca,), (cb,)), ((), ())), precision=precision, preferred_element_type=F32
    )


def iota(dims, axis):
    return lax.broadcasted_iota(jnp.int32, dims, axis)


def where_one(mask):
    return jnp.where(mask, 1.0, 0.0)


def triangle(n, keep):
    return where_one(keep(iota((n, n), 0), iota((n, n), 1))).astype(F32)


def halves(values, axis=1):
    high = values.astype(BF16)
    low = (values - high.astype(F32)).astype(BF16)
    return jnp.concatenate([high, low], axis=axis)


def to_lanes(j, size):
    dims = (LANES, LANES)
    one = where_one(iota(dims, 0) == iota(dims, 1) // size + j * (LANES // size)).astype(BF16)
    return jnp.concatenate([one, one], axis=0)


def to_heads(j, heads, size):
    dims = (heads, LANES)
    one = where_one(iota(dims, 0) == iota(dims, 1) // size + j * (LANES // size)).astype(BF16)
    return jnp.concatenate([one, one], axis=1)


def up16(n):
    return -(-n // 16) * 16


def call(kernel, outs, cost, args, after=(), scratch=(), limit=14, fetch=()):
    n_in, n_after, n_out = len(args), len(after), len(outs)
    fetch = tuple(fetch)

    def body(*refs):
        ins = list(refs[:n_in])
        rest = refs[n_in + n_after :]
        if fetch:
            sems = rest[-1]
            held = rest[len(rest) - 1 - len(fetch) : -1]
            rest = rest[: len(rest) - 1 - len(fetch)]
            copies = []
            for i, (index, ref) in enumerate(zip(fetch, held)):
                copies.append(pltpu.make_async_copy(ins[index], ref, sems.at[i]))
                ins[index] = ref
            for copy in copies:
                copy.start()
            for copy in copies:
                copy.wait()
        kernel(*ins, *rest)

    specs = [
        pl.BlockSpec(memory_space=pltpu.HBM if i in fetch else pltpu.VMEM) for i in range(n_in)
    ]
    held = [pltpu.VMEM(args[i].shape, args[i].dtype) for i in fetch]
    if fetch:
        held.append(pltpu.SemaphoreType.DMA((len(fetch),)))
    return pl.pallas_call(
        body,
        out_shape=outs,
        in_specs=specs + [pl.BlockSpec(memory_space=pl.ANY)] * n_after,
        out_specs=[pl.BlockSpec(memory_space=pltpu.VMEM)] * n_out,
        scratch_shapes=list(scratch) + held,
        cost_estimate=pl.CostEstimate(
            flops=int(cost * 3e9), bytes_accessed=1000, transcendentals=0
        ),
        compiler_params=pltpu.CompilerParams(vmem_limit_bytes=limit * 1024 * 1024),
    )(*args, *after)


def shape(dims, kind):
    return jax.ShapeDtypeStruct(dims, kind)


def core_and_chip():
    place = lax.axis_index("tm")
    return lax.rem(place, 2), lax.div(place, 2), lax.axis_size("tm") // 2


def rows_at(index, size, align=16):
    return pl.ds(pl.multiple_of(index * size, align), size)


def picked(x_ref, dy_ref, slot_ref, count_ref, gate_ref, rows_ref, out_refs):
    length, width = x_ref.shape
    slots = slot_ref.shape[1]
    hit = iota((length, slots), 0) == slot_ref[...]
    live = iota((1, slots), 1) < count_ref[...]
    weight = jnp.where(live, gate_ref[...].astype(F32), 0.0)
    rows = dot(where_one(hit).astype(BF16), x_ref[...], 0, 0).astype(BF16)
    for t in range(width // LANES):
        rows_ref[t * slots : (t + 1) * slots, :] = rows[:, t * LANES : (t + 1) * LANES]
    grads = dot(jnp.where(hit, weight, 0.0).astype(BF16), dy_ref[...], 0, 0).astype(BF16)
    held = out_refs[-1]
    n_dp = held.shape[0]
    piece = width // n_dp
    for i in range(n_dp):
        for t, low in enumerate(range(i * piece, (i + 1) * piece, LANES)):
            block = grads[:, low : min(low + LANES, (i + 1) * piece)]
            if block.shape[1] < LANES:
                fill = jnp.zeros((slots, LANES - block.shape[1]), BF16)
                block = jnp.concatenate([block, fill], axis=1)
            held[i, t * slots : (t + 1) * slots, :] = block
    place = lax.axis_index("dp")
    s = 0
    for out in out_refs[:-1]:
        for start in range(0, out.shape[0], held.shape[1]):
            out[start : start + held.shape[1], :] = held[place ^ s]
            s += 1


def high_low(values):
    high = values.astype(BF16).astype(F32)
    return [high, values - high]


def prep_kernel(
    n_deals, x_ref, dy_ref, ldt_ref, stept_ref, h_ref, slot_ref, count_ref, gate_ref,
    cumt_ref, cum_ref, step_ref, dyt_ref, xs_ref, carried_ref, rows_ref, *rest,
):
    outs, xt_ref, held_ref = rest[n_deals:-2], rest[-2], rest[-1]
    length, width = x_ref.shape
    heads = ldt_ref.shape[0]
    size = width // heads
    _, chip, n_chip = core_and_chip()
    picked(x_ref, dy_ref, slot_ref, count_ref, gate_ref, rows_ref, (*rest[:n_deals], held_ref))
    pad = jnp.zeros((LANES - heads, length), F32)
    cumt = dot(ldt_ref[...], triangle(length, lambda a, b: a <= b), 1, 0, HI)
    cumt_ref[...] = cumt
    cum = jnp.concatenate([cumt, pad], axis=0).T
    step = jnp.concatenate([stept_ref[...], pad], axis=0).T
    cum_ref[...] = cum
    step_ref[...] = step
    start = jnp.exp(cum)
    into_end = jnp.exp(cum[length - 1 : length] - cum) * step
    table = jnp.concatenate([halves(start), halves(into_end)], axis=0)
    carried = jnp.zeros(carried_ref.shape, F32)
    for j in range(width // LANES):
        span = slice(j * LANES, (j + 1) * LANES)
        scale = dot(table, to_lanes(j, size), 1, 0)
        x_f = x_ref[:, span].astype(F32)
        xt_ref[span, :] = x_f.T.astype(BF16)
        xs_ref[:, span] = (x_f * scale[length:]).astype(BF16)
        dys = dy_ref[:, span].astype(F32) * scale[:length]
        dyt_ref[span, :] = dys.T.astype(BF16)
        carried = carried + dot(dys.astype(BF16), h_ref[span, :], 1, 0)
    carried_ref[...] = carried
    decay = jnp.broadcast_to(jnp.exp(cumt[:, length - 1 : length]), (heads, LANES))
    dyt_ref[width : width + 2 * heads, :] = jnp.concatenate(high_low(decay), axis=0).astype(BF16)
    block = width // n_chip
    s = 0
    for out in outs:
        for start in range(0, out.shape[0], block):
            out[start : start + block, :] = xt_ref[rows_at(chip ^ s, block), :]
            s += 1


def join_kernel(ranges, *refs):
    out, at = refs[-1], 0
    for ref, (start, stop) in zip(refs, ranges):
        out[at : at + stop - start] = ref[start:stop]
        at += stop - start


def joined(arrays, after=(), ranges=None, cost=0.2):
    ranges = ranges or [(0, a.shape[0]) for a in arrays]
    dims = (sum(stop - start for start, stop in ranges), *arrays[0].shape[1:])
    return call(
        lambda *refs: join_kernel(ranges, *refs),
        [shape(dims, arrays[0].dtype)],
        cost,
        tuple(arrays),
        after=after,
    )[0]


def stacked(arrays, after=(), ranges=None, cost=0.2):
    count = len(arrays)
    out = joined(arrays, after, ranges, cost)
    return out.reshape(count, out.shape[0] // count, *out.shape[1:])


def project_kernel(n_mine, many, *refs):
    x_ref, dyt_ref, own_ref = refs[:3]
    mine, other = refs[3 : 3 + n_mine], refs[3 + n_mine]
    w_ref, bc_ref, keep_ref, send_ref = refs[4 + n_mine :]
    core, _, _ = core_and_chip()
    place, n_dp = lax.axis_index("dp"), lax.axis_size("dp")
    share = own_ref.shape[0]
    half = share // 2
    w_ref[rows_at(place, share), :] = own_ref[...]
    for i in range(n_mine):
        source = place ^ (i + 1)
        w_ref[rows_at(source * 2 + core, half), :] = mine[i][...]
        w_ref[rows_at(source * 2 + 1 - core, half), :] = other[i]
    bc = dot(x_ref[...], w_ref[...], 1, 0).astype(BF16)
    bc_ref[...] = bc
    c_rows = bc[:, LANES:]
    width = x_ref.shape[1]
    part = width // 2
    for ref, index in ((keep_ref, core), (send_ref, 1 - core)):
        ref[:part, :] = dot(dyt_ref[rows_at(index, part), :], c_rows, 1, 0).astype(BF16)
        table = dyt_ref[width : width + 4 * many, :].astype(F32)
        quarter = [table[i * many : (i + 1) * many] for i in range(4)]
        high = jnp.where(index == 0, quarter[0], quarter[1])
        low = jnp.where(index == 0, quarter[2], quarter[3])
        fill = jnp.zeros((ref.shape[0] - part - 2 * many, LANES), F32)
        ref[part:, :] = jnp.concatenate([high, low, fill], axis=0).astype(BF16)


def pair(keep_ref, recv_ref, many, size, head):
    core, _, _ = core_and_chip()
    part = many * size
    both = []
    for ref in (keep_ref, recv_ref):
        extra = ref[part:, :].astype(F32)
        decay = extra[head : head + 1] + extra[many + head : many + head + 1]
        both.append((ref[head * size : (head + 1) * size, :].astype(F32), decay))
    first = jax.tree.map(lambda a, b: jnp.where(core == 0, a, b), both[0], both[1])
    second = jax.tree.map(lambda a, b: jnp.where(core == 0, b, a), both[0], both[1])
    return first, second


def payload(ref, many, states, decays):
    size = states[0].shape[0]
    for head, state in enumerate(states):
        ref[head * size : (head + 1) * size, :] = state.astype(BF16)
    decay = jnp.concatenate(decays, axis=0)
    high = decay.astype(BF16).astype(F32)
    fill = jnp.zeros((ref.shape[0] - many * size - 2 * many, LANES), F32)
    extra = jnp.concatenate([high, decay - high, fill], axis=0)
    ref[many * size :, :] = extra.astype(BF16)


def loaded(ref, many, size, head):
    extra = ref[many * size :, :].astype(F32)
    decay = extra[head : head + 1] + extra[many + head : many + head + 1]
    return ref[head * size : (head + 1) * size, :].astype(F32), decay


def combine_kernel(many, size, keep_ref, recv_ref, out_ref):
    states, decays = [], []
    for head in range(many):
        (g0, a0), (g1, a1) = pair(keep_ref, recv_ref, many, size, head)
        states.append(g0 + a0 * g1)
        decays.append(a0 * a1)
    payload(out_ref, many, states, decays)


def pick_side(upper, mine, theirs):
    return jnp.where(upper, theirs, mine), jnp.where(upper, mine, theirs)


def climb_kernel(many, size, bit, mine_ref, recv_ref, out_ref):
    _, chip, _ = core_and_chip()
    upper = lax.rem(lax.div(chip, bit), 2) == 1
    states, decays = [], []
    for head in range(many):
        t_mine, a_mine = loaded(mine_ref, many, size, head)
        t_recv, a_recv = loaded(recv_ref, many, size, head)
        t_low, t_high = pick_side(upper, t_mine, t_recv)
        a_low, a_high = pick_side(upper, a_mine, a_recv)
        states.append(t_low + a_low * t_high)
        decays.append(a_low * a_high)
    payload(out_ref, many, states, decays)


def carry_kernel(many, size, levels, *refs):
    core, chip, _ = core_and_chip()
    recvs = refs[:levels]
    keep_ref, recv_ref, own_ref, send_ref = refs[levels:]
    for head in range(many):
        span = slice(head * size, (head + 1) * size)
        carry, reach = None, None
        for level, ref in enumerate(recvs):
            state, decay = loaded(ref, many, size, head)
            lower = lax.rem(lax.div(chip, 2**level), 2) == 0
            state = jnp.where(lower, state, 0.0)
            decay = jnp.where(lower, decay, 1.0)
            carry = state if carry is None else carry + reach * state
            reach = decay if reach is None else reach * decay
        _, (g1, a1) = pair(keep_ref, recv_ref, many, size, head)
        second = carry
        first = g1 + a1 * second
        own_ref[span, :] = jnp.where(core == 0, first, second).astype(BF16)
        send_ref[span, :] = jnp.where(core == 0, second, first).astype(BF16)


def intra_kernel(
    first, many, x_ref, dy_ref, bc_ref, cumt_ref, cum_ref, step_ref, h_ref, before_ref,
    dx_ref, mixed_ref, ex_ref, own_ref, rowm_ref,
):
    length, width = x_ref.shape
    heads = cumt_ref.shape[0]
    size = width // heads
    per = LANES // size
    upper = iota((length, length), 0) <= iota((length, length), 1)
    b_rows, c_rows = bc_ref[:, :LANES], bc_ref[:, LANES:]
    scores = dot(b_rows, c_rows, 1, 1)
    lane = iota((1, LANES), 1)
    lane_bf = [where_one(lane // size == i).astype(BF16) for i in range(per)]
    mixed = before_ref[...]
    own = jnp.zeros((length, LANES), F32)
    reach = jnp.zeros((heads, length), F32)
    for j in range(first, first + many):
        span = slice(j * LANES, (j + 1) * LANES)
        out_span = slice((j - first) * LANES, (j - first + 1) * LANES)
        x_p = x_ref[:, span]
        dy_p = dy_ref[:, span]
        dy_h = jnp.concatenate([dy_p * m for m in lane_bf], axis=0)
        cross = dot(x_p, dy_h, 1, 1)
        kern = []
        wide = None
        for i in range(per):
            h = j * per + i
            diff = cumt_ref[h : h + 1, :] - cum_ref[:, h : h + 1]
            seg = jnp.exp(jnp.where(upper, diff, -1e30))
            kern.append((seg * scores).astype(BF16))
            step = jnp.broadcast_to(step_ref[:, h : h + 1], (length, LANES))
            wide = step if i == 0 else jnp.where(lane < i * size, wide, step)
            scaled = seg * cross[:, i * length : (i + 1) * length] * step
            mixed = mixed + scaled
            full = scaled * scores
            rowm_ref[h : h + 1, :] = jnp.sum(full, axis=0, keepdims=True)
            own = jnp.where(lane == h, jnp.sum(full, axis=1, keepdims=True), own)
        back = dot(jnp.concatenate(kern, axis=1), dy_h, 1, 0)
        dx_ref[:, out_span] = back * wide
        seen = dy_p.astype(F32) * dot(c_rows, h_ref[span, :], 1, 1)
        reach = reach + dot(to_heads(j, heads, size), halves(seen), 1, 1)
    mixed_ref[...] = mixed
    rows = slice(first * per, (first + many) * per)
    own = own.T[rows]
    own_ref[...] = own
    ex_ref[...] = rowm_ref[rows, :] + jnp.exp(cumt_ref[rows, :]) * reach[rows] - own


def close_kernel(mixed_ref, bc_ref, carried_ref, db_ref, dc_ref):
    mixed = mixed_ref[...].astype(BF16)
    db_ref[...] = dot(mixed, bc_ref[:, LANES:], 1, 0)
    dc_ref[...] = (dot(mixed, bc_ref[:, :LANES], 0, 0) + carried_ref[...]).astype(BF16)


def db_kernel(xs_ref, own_ref, recv_ref, db_ref, dc_ref, out_ref):
    core, _, _ = core_and_chip()
    half = db_ref.shape[1]
    part = own_ref.shape[0]
    total = db_ref[...]
    for ref, index in ((own_ref, core), (recv_ref, 1 - core)):
        total = total + dot(xs_ref[:, rows_at(index, part, LANES)], ref[...], 1, 0)
    out_ref[:, :half] = total.astype(BF16)
    out_ref[:, half:] = dc_ref[...]


def finish_kernel(parts, *refs):
    (x_ref, bc_ref, cumt_ref, stept_ref, cum_ref, step_ref, h_ref, own_ref, recv_ref,
     w_ref, dbc_ref) = refs[:11]
    dx_refs, ex_refs, st_refs = (refs[11 + i * parts : 11 + (i + 1) * parts] for i in range(3))
    in_ref, decay_ref, grad_ref, token_ref, r_ref, edge_ref = refs[11 + 3 * parts :]
    token_ref[...] = jnp.zeros_like(token_ref)
    core, _, _ = core_and_chip()
    length, width = x_ref.shape
    heads = cumt_ref.shape[0]
    size = width // heads
    part = width // 2
    r_ref[rows_at(core, part), :] = own_ref[...]
    r_ref[rows_at(1 - core, part), :] = recv_ref[...]
    cum = cum_ref[...]
    table = halves(jnp.exp(cum[length - 1 : length] - cum) * step_ref[...])
    seen = jnp.zeros((heads, length), F32)
    b_rows = bc_ref[:, :LANES]
    d_bc = dbc_ref[...]
    for j in range(width // LANES):
        span = slice(j * LANES, (j + 1) * LANES)
        local = dx_refs[j * LANES // (width // parts)]
        start = j * LANES % (width // parts)
        r_tile = r_ref[span, :]
        reach = dot(b_rows, r_tile, 1, 1)
        d_in = local[:, start : start + LANES] + dot(table, to_lanes(j, size), 1, 0) * reach
        d_in = d_in + dot(d_bc, w_ref[span, :], 1, 1)
        in_ref[:, span] = d_in.astype(BF16)
        product = x_ref[:, span].astype(F32) * reach
        seen = seen + dot(to_heads(j, heads, size), halves(product), 1, 1)
        edge = r_tile.astype(F32) * h_ref[span, :].astype(F32)
        for i in range(LANES // size):
            h = j * (LANES // size) + i
            edge_ref[h : h + 1, :] = jnp.sum(
                edge[i * size : (i + 1) * size], axis=0, keepdims=True
            )
    cumt = cumt_ref[...]
    total = cumt[:, length - 1 : length]
    to_end = jnp.exp(total - cumt)
    step = stept_ref[...]
    own = jnp.concatenate([r[...] for r in st_refs], axis=0)
    excess = jnp.concatenate([r[...] for r in ex_refs], axis=0)
    grad_ref[...] = own / step + to_end * seen
    edge = jnp.exp(total) * jnp.sum(edge_ref[...], axis=1, keepdims=True)
    decay_ref[...] = (
        dot(excess, triangle(length, lambda a, b: a >= b), 1, 0, HI)
        + dot(to_end * step * seen, triangle(length, lambda a, b: a < b), 1, 0, HI)
        + edge
    )


def term_kernel(places, n_columns, *refs):
    columns, pieces = refs[:n_columns], refs[n_columns:-3]
    keep_ref, send_ref, held = refs[-3:]
    pieces = [(p, i) for p in pieces for i in range(p.shape[0])]
    rows = 2 * keep_ref.shape[0]
    core, _, _ = core_and_chip()
    total = None
    for (a, start), (b, i) in zip(places, pieces):
        part = dot(columns[a][start : start + rows, :], b[i], 1, 0)
        total = part if total is None else total + part
    block = keep_ref.shape[0]
    held[0] = total[:block]
    held[1] = total[block:]
    keep_ref[...] = held[core]
    send_ref[...] = held[1 - core].astype(BF16)


def deal_kernel(keep_ref, recv_ref, own_ref, *refs):
    outs, held = refs[:-1], refs[-1]
    place, n_dp = lax.axis_index("dp"), lax.axis_size("dp")
    total = keep_ref[...] + recv_ref[...].astype(F32)
    share = own_ref.shape[0]
    for i in range(n_dp):
        held[i] = total[i * share : (i + 1) * share]
    own_ref[...] = held[place]
    for s, out in enumerate(outs):
        out[...] = held[place ^ (s + 1)].astype(BF16)


def sum_kernel(*refs):
    total = refs[0][...]
    for ref in refs[1:-1]:
        total = total + ref[...].astype(F32)
    refs[-1][...] = total


def expert_kernel(flip, slots, a_ref, b_ref, gate_ref, up_ref, out_ref, *scratch):
    rows_ref, gate_acc, up_acc = scratch
    step = pl.program_id(0)
    n_chip = a_ref.shape[0]

    @pl.when(step == 0)
    def _():
        for half, ref in enumerate((a_ref, b_ref)):
            for i in range(n_chip):
                row = (half * n_chip + i) * slots
                for t in range(rows_ref.shape[1] // LANES):
                    rows_ref[row : row + slots, t * LANES : (t + 1) * LANES] = ref[
                        i, t * slots : (t + 1) * slots, :
                    ]
        gate_acc[...] = jnp.zeros_like(gate_acc)
        up_acc[...] = jnp.zeros_like(up_acc)

    depth = gate_ref.shape[0]
    rows = rows_ref[:, rows_at(step, depth, LANES)]
    gate_acc[...] += dot(rows, gate_ref[...], 1, 0)
    up_acc[...] += dot(rows, up_ref[...], 1, 0)

    @pl.when(step == pl.num_programs(0) - 1)
    def _():
        weighted = jax.nn.silu(gate_acc[...]) * up_acc[...]
        out_ref[...] = (weighted.T if flip else weighted).astype(BF16)


def expert(a, b, w_gate, w_up, slots, flip, after):
    n_chip = a.shape[0]
    total = 2 * n_chip * slots
    width, hidden = w_gate.shape
    depth = 512
    out = (hidden, total) if flip else (total, hidden)

    def body(*refs):
        expert_kernel(flip, slots, *refs[:4], *refs[4 + len(after) :])

    whole = pl.BlockSpec(a.shape, lambda i: (0, 0, 0))
    block = pl.BlockSpec((depth, hidden), lambda i: (i, 0))
    return pl.pallas_call(
        body,
        out_shape=shape(out, BF16),
        grid=(width // depth,),
        in_specs=[whole, whole, block, block]
        + [pl.BlockSpec(memory_space=pl.ANY)] * len(after),
        out_specs=pl.BlockSpec(out, lambda i: (0, 0)),
        scratch_shapes=[
            pltpu.VMEM((total, width), BF16),
            pltpu.VMEM((total, hidden), F32),
            pltpu.VMEM((total, hidden), F32),
        ],
        cost_estimate=pl.CostEstimate(
            flops=int(1e9), bytes_accessed=1000, transcendentals=0
        ),
        compiler_params=pltpu.CompilerParams(vmem_limit_bytes=20 * 1024 * 1024),
    )(a, b, w_gate, w_up, *after)


def down_kernel(n_dp, flip, slots, grad_rows, *refs):
    pieces = refs[:n_dp]
    a_ref, b_ref, out_ref, token_ref = refs[n_dp:]
    token_ref[...] = jnp.zeros_like(token_ref)
    n_chip = a_ref.shape[0]
    piece = out_ref.shape[1]
    base = a_ref.shape[1] - n_dp * grad_rows
    total = None
    for s in range(n_dp):
        columns = []
        for t in range(grad_rows // slots):
            row = base + s * grad_rows + t * slots
            blocks = [r[i, row : row + slots, :] for r in (a_ref, b_ref) for i in range(n_chip)]
            columns.append(jnp.concatenate(blocks, axis=0))
        right = jnp.concatenate(columns, axis=1)[:, :piece]
        part = dot(pieces[s][...], right, 1 if flip else 0, 0)
        total = part if total is None else total + part
    out_ref[...] = total.astype(BF16)


def xored(array, axis, mask):
    count = lax.axis_size(axis)
    return lax.ppermute(array, axis, [(i, i ^ mask) for i in range(count)])


def swapped(array):
    return xored(array, "tm", 1)


def chips(arrays):
    return [arrays[0]] + [xored(a, "tm", 2 * s) for s, a in enumerate(arrays) if s]


def gathered(array, axis, count):
    if count == 1:
        return [array]
    far = xored(array, axis, count // 2)
    return gathered(array, axis, count // 2) + gathered(far, axis, count // 2)


def per_device(
    layer_in,
    out_grad,
    w_bc,
    log_decay,
    step,
    saved_states,
    w_gate,
    w_up,
    slot_rows,
    slot_counts,
    slot_gates,
):
    n_dp = lax.axis_size("dp")
    core, chip, n_chip = core_and_chip()
    x = layer_in[0]
    dy = out_grad[0]
    length, width = x.shape
    heads = log_decay.shape[2]
    size = width // heads
    share, columns = w_bc.shape
    half = columns // 2
    ldt = log_decay[0].T
    stept = step[0].T
    h_in = saved_states[0, 0].reshape(width, half)
    capacity = slot_rows.shape[2]
    piece = width // n_dp
    part = width // 2
    many = heads // 2
    flip = w_gate.shape[2] % LANES == 0

    grad_rows = -(-piece // LANES) * capacity
    w_half = lax.dynamic_slice_in_dim(w_bc, core * (share // 2), share // 2, 0)

    in_rows = width // LANES * capacity
    blocks = [1, 1, 2] if n_chip == 4 else [1] * n_chip
    groups = [2, 2] if n_dp == 4 else [1] * n_dp
    cumt, cum, steps, dyt, xs, carried, rows, *xt = call(
        lambda *refs: prep_kernel(len(groups), *refs),
        [
            shape((heads, length), F32),
            shape((length, LANES), F32),
            shape((length, LANES), F32),
            shape((width + up16(2 * heads), length), BF16),
            shape((length, width), BF16),
            shape((length, half), F32),
        ]
        + [shape((in_rows, LANES), BF16)]
        + [shape((k * grad_rows, LANES), BF16) for k in groups]
        + [shape((k * width // n_chip, length), BF16) for k in blocks],
        2.0,
        (x, dy, ldt, stept, h_in, slot_rows[0], slot_counts, slot_gates[0]),
        scratch=[
            pltpu.VMEM((width, length), BF16),
            pltpu.VMEM((n_dp, grad_rows, LANES), BF16),
        ],
        fetch=(0, 1, 2, 3, 4),
        limit=60,
    )
    rows_in = chips([rows] * n_chip)
    deals, xt = xt[: len(groups)], xt[len(groups) :]
    if n_dp == 4:
        one = (0, grad_rows), (grad_rows, 2 * grad_rows)
        over_2 = xored(deals[1], "dp", 2)
        early = (over_2,)
    else:
        early = ()
        source, spans = deals[:1] + [xored(d, "dp", s + 1) for s, d in enumerate(deals[1:])], None
    w_far = xored(w_half, "dp", n_dp // 2)
    mine = gathered(w_half, "dp", n_dp // 2)[1:]
    mine += gathered(joined([w_far], after=(rows,)), "dp", n_dp // 2)
    other = swapped(stacked(mine, after=(*rows_in[1:4],), cost=1.0))
    w_whole, bc, keep, send = call(
        lambda *refs: project_kernel(n_dp - 1, many, *refs),
        [
            shape((width, columns), BF16),
            shape((length, columns), BF16),
            shape((part + up16(2 * many), half), BF16),
            shape((part + up16(2 * many), half), BF16),
        ],
        1.0,
        (x, dyt, w_bc, *mine, other),
    )
    recv = swapped(send)
    hidden = w_gate.shape[2]
    climbs = [
        call(
            lambda *refs: combine_kernel(many, size, *refs),
            [shape((part + up16(2 * many), half), BF16)],
            0.5,
            (keep, recv),
        )[0]
    ]
    rows_a = stacked(rows_in, after=(climbs[0],))
    rows_b = swapped(rows_a)
    weighted = expert(rows_a, rows_b, w_gate[0], w_up[0], capacity, flip, (climbs[0],))
    if n_chip == 4:
        x_rows = width // n_chip
        over_y = xored(xt[2], "tm", 4)

    parts = 2
    tiles = width // LANES // parts
    dxs, exs, owns = [], [], []
    held = (weighted, *early, *((over_y,) if n_chip == 4 else ()))
    arrived = []
    bit = 1
    while bit < n_chip:
        last = bit * 2 == n_chip
        moves = [(k, k ^ (2 * bit)) for k in range(2 * n_chip) if not last or k & (2 * bit)]
        arrived.append(lax.ppermute(climbs[-1], "tm", moves))
        if not last:
            climbs.append(
                call(
                    lambda *refs, bit=bit: climb_kernel(many, size, bit, *refs),
                    [shape((part + up16(2 * many), half), BF16)],
                    0.5,
                    (climbs[-1], arrived[-1]),
                    after=held,
                )[0]
            )
        bit *= 2
    later = (climbs[-1],)
    mixed = jnp.zeros((length, length), F32)
    for i in range(parts):
        dx, mixed, ex, own = call(
            lambda *refs, i=i: intra_kernel(i * tiles, tiles, *refs),
            [
                shape((length, width // parts), F32),
                shape((length, length), F32),
                shape((heads // parts, length), F32),
                shape((heads // parts, length), F32),
            ],
            0.7,
            (x, dy, bc, cumt, cum, steps, h_in, mixed),
            after=later,
            scratch=[pltpu.VMEM((heads, length), F32)],
        )
        dxs.append(dx)
        exs.append(ex)
        owns.append(own)
    db, dc = call(
        close_kernel,
        [shape((length, half), F32), shape((length, half), BF16)],
        0.3,
        (mixed, bc, carried),
    )

    held = (dc,)
    if n_dp == 4:
        over_1 = xored(joined([deals[0], over_2], later, [one[1], one[1]]), "dp", 1)
        source, spans = [deals[0], over_1, over_2, over_1], [one[0], one[0], one[0], one[1]]
    dealt = joined(source, later, spans)
    held += (dealt,)
    if n_chip == 4:
        over_x = xored(joined([xt[1], over_y], later, [(0, x_rows), (x_rows, 2 * x_rows)]), "tm", 2)
        columns_in = [xt[0], over_x, over_y]
        places = [(0, 0), (1, 0), (2, 0), (1, x_rows)]
        held += (over_x,)
    else:
        columns_in = chips(xt)
        places = [(i, 0) for i in range(n_chip)]
    far = xored(weighted, "dp", n_dp // 2)
    near = gathered(weighted, "dp", n_dp // 2)
    held += (far, *near[1:])
    r_own, r_send = call(
        lambda *refs: carry_kernel(many, size, len(arrived), *refs),
        [shape((part, half), BF16)] * 2,
        0.5,
        (*arrived, keep, recv),
        after=held,
    )
    r_recv = swapped(r_send)
    if n_chip == 4:
        grads_y = xored(dealt, "tm", 4)
        rest = dealt.shape[0]
        spans = [(0, rest), (0, rest), (0, rest), (rest, 2 * rest)]
    else:
        grads, spans = chips([dealt] * n_chip), None
    fars = gathered(joined([far], (r_own,)), "dp", n_dp // 2)
    d_bc = call(db_kernel, [shape((length, columns), BF16)], 0.3, (xs, r_own, r_recv, db, dc))[0]
    d_bcs = [d_bc.reshape(1, length, columns)]
    while 2 ** (len(d_bcs) - 1) < n_chip:
        level = 2 ** (len(d_bcs) - 1)
        sent = d_bcs[0] if level == 1 else joined(d_bcs)
        d_bcs.append(xored(sent, "tm", 2 * level))
    d_in, d_decay, d_step, token = call(
        lambda *refs: finish_kernel(parts, *refs),
        [
            shape((length, width), BF16),
            shape((heads, length), F32),
            shape((heads, length), F32),
            shape((8, LANES), F32),
        ],
        3.0,
        (x, bc, cumt, stept, cum, steps, h_in, r_own, r_recv, w_whole, d_bc,
         *dxs, *exs, *owns),
        after=tuple(fars[1:]),
        scratch=[pltpu.VMEM((width, half), BF16), pltpu.VMEM((heads, half), F32)],
    )
    w_rows = width // (2 * n_chip)
    term, term_send = call(
        lambda *refs: term_kernel(places, len(columns_in), *refs),
        [shape((w_rows, columns), F32), shape((w_rows, columns), BF16)],
        0.5,
        (*columns_in, *d_bcs),
        after=(token,),
        scratch=[pltpu.VMEM((2, w_rows, columns), F32)],
    )
    final = call(
        deal_kernel,
        [shape((w_rows // n_dp, columns), F32)]
        + [shape((w_rows // n_dp, columns), BF16)] * (n_dp - 1),
        0.3,
        (term, swapped(term_send)),
        scratch=[pltpu.VMEM((n_dp, w_rows // n_dp, columns), F32)],
    )
    final = list(final[:1]) + [xored(f, "dp", s + 1) for s, f in enumerate(final[1:])]

    if n_chip == 4:
        grads_x = xored(joined([dealt, grads_y], (sent,)), "tm", 2)
        grads = [dealt, grads_x, grads_y, grads_x]
    grads_a = stacked(grads, (token,), spans)
    grads_b = swapped(grads_a)
    w_down_grad, done = call(
        lambda *refs: down_kernel(n_dp, flip, capacity, grad_rows, *refs),
        [shape((hidden, piece), BF16), shape((8, LANES), F32)],
        1.0,
        (*near, *fars, grads_a, grads_b),
        after=(final[0],),
    )
    w_bc_grad = call(sum_kernel, [shape(final[0].shape, F32)], 0.1, final, (done,))[0]
    return (d_in[None], d_decay.T[None], d_step.T[None], w_bc_grad, w_down_grad[None])


def solution(mesh):
    in_specs = (
        P("dp", "tm", None),
        P("dp", "tm", None),
        P("dp", None),
        P("dp", "tm", None),
        P("dp", "tm", None),
        P("dp", "tm", None, None, None),
        P(None, None, "tm"),
        P(None, None, "tm"),
        P("dp", None, "tm"),
        P("dp", "tm"),
        P("dp", None, "tm"),
    )
    out_specs = (
        P("dp", "tm", None),
        P("dp", "tm", None),
        P("dp", "tm", None),
        P(("tm", "dp"), None),
        P(None, "tm", "dp"),
    )
    return jax.shard_map(
        per_device, mesh=mesh, in_specs=in_specs, out_specs=out_specs, check_vma=False
    )
```

```python
import jax
import jax.numpy as jnp
from jax import lax
from jax.experimental import pallas as pl
from jax.experimental.pallas import tpu as pltpu
from jax.sharding import PartitionSpec as P

HI = lax.Precision.HIGHEST
F32 = jnp.float32
BF16 = jnp.bfloat16
LANES = 128


def dot(a, b, ca, cb, precision=None):
    return lax.dot_general(
        a, b, (((ca,), (cb,)), ((), ())), precision=precision, preferred_element_type=F32
    )


def iota(dims, axis):
    return lax.broadcasted_iota(jnp.int32, dims, axis)


def where_one(mask):
    return jnp.where(mask, 1.0, 0.0)


def triangle(n, keep):
    return where_one(keep(iota((n, n), 0), iota((n, n), 1))).astype(F32)


def halves(values, axis=1):
    high = values.astype(BF16)
    low = (values - high.astype(F32)).astype(BF16)
    return jnp.concatenate([high, low], axis=axis)


def to_lanes(j, size):
    dims = (LANES, LANES)
    one = where_one(iota(dims, 0) == iota(dims, 1) // size + j * (LANES // size)).astype(BF16)
    return jnp.concatenate([one, one], axis=0)


def to_heads(j, heads, size):
    dims = (heads, LANES)
    one = where_one(iota(dims, 0) == iota(dims, 1) // size + j * (LANES // size)).astype(BF16)
    return jnp.concatenate([one, one], axis=1)


def up16(n):
    return -(-n // 16) * 16


def call(kernel, outs, cost, args, after=(), scratch=(), limit=14, fetch=()):
    n_in, n_after, n_out = len(args), len(after), len(outs)
    fetch = tuple(fetch)

    def body(*refs):
        ins = list(refs[:n_in])
        rest = refs[n_in + n_after :]
        if fetch:
            sems = rest[-1]
            held = rest[len(rest) - 1 - len(fetch) : -1]
            rest = rest[: len(rest) - 1 - len(fetch)]
            copies = []
            for i, (index, ref) in enumerate(zip(fetch, held)):
                copies.append(pltpu.make_async_copy(ins[index], ref, sems.at[i]))
                ins[index] = ref
            for copy in copies:
                copy.start()
            for copy in copies:
                copy.wait()
        kernel(*ins, *rest)

    specs = [
        pl.BlockSpec(memory_space=pltpu.HBM if i in fetch else pltpu.VMEM) for i in range(n_in)
    ]
    held = [pltpu.VMEM(args[i].shape, args[i].dtype) for i in fetch]
    if fetch:
        held.append(pltpu.SemaphoreType.DMA((len(fetch),)))
    return pl.pallas_call(
        body,
        out_shape=outs,
        in_specs=specs + [pl.BlockSpec(memory_space=pl.ANY)] * n_after,
        out_specs=[pl.BlockSpec(memory_space=pltpu.VMEM)] * n_out,
        scratch_shapes=list(scratch) + held,
        cost_estimate=pl.CostEstimate(
            flops=int(cost * 3e9), bytes_accessed=1000, transcendentals=0
        ),
        compiler_params=pltpu.CompilerParams(vmem_limit_bytes=limit * 1024 * 1024),
    )(*args, *after)


def shape(dims, kind):
    return jax.ShapeDtypeStruct(dims, kind)


def core_and_chip():
    place = lax.axis_index("tm")
    return lax.rem(place, 2), lax.div(place, 2), lax.axis_size("tm") // 2


def rows_at(index, size, align=16):
    return pl.ds(pl.multiple_of(index * size, align), size)


def picked(x_ref, dy_ref, slot_ref, count_ref, gate_ref, rows_ref, out_refs):
    length, width = x_ref.shape
    slots = slot_ref.shape[1]
    hit = iota((length, slots), 0) == slot_ref[...]
    live = iota((1, slots), 1) < count_ref[...]
    weight = jnp.where(live, gate_ref[...].astype(F32), 0.0)
    rows = dot(where_one(hit).astype(BF16), x_ref[...], 0, 0).astype(BF16)
    for t in range(width // LANES):
        rows_ref[t * slots : (t + 1) * slots, :] = rows[:, t * LANES : (t + 1) * LANES]
    grads = dot(jnp.where(hit, weight, 0.0).astype(BF16), dy_ref[...], 0, 0).astype(BF16)
    held = out_refs[-1]
    n_dp = held.shape[0]
    piece = width // n_dp
    for i in range(n_dp):
        for t, low in enumerate(range(i * piece, (i + 1) * piece, LANES)):
            block = grads[:, low : min(low + LANES, (i + 1) * piece)]
            if block.shape[1] < LANES:
                fill = jnp.zeros((slots, LANES - block.shape[1]), BF16)
                block = jnp.concatenate([block, fill], axis=1)
            held[i, t * slots : (t + 1) * slots, :] = block
    place = lax.axis_index("dp")
    s = 0
    for out in out_refs[:-1]:
        for start in range(0, out.shape[0], held.shape[1]):
            out[start : start + held.shape[1], :] = held[place ^ s]
            s += 1


def high_low(values):
    high = values.astype(BF16).astype(F32)
    return [high, values - high]


def prep_kernel(
    n_deals, x_ref, dy_ref, ldt_ref, stept_ref, slot_ref, count_ref, gate_ref,
    cumt_ref, cum_ref, dyt_ref, rows_ref, *rest,
):
    length, width = x_ref.shape
    heads = ldt_ref.shape[0]
    size = width // heads
    picked(x_ref, dy_ref, slot_ref, count_ref, gate_ref, rows_ref, rest)
    cumt = dot(ldt_ref[...], triangle(length, lambda a, b: a <= b), 1, 0, HI)
    cumt_ref[...] = cumt
    pad = jnp.zeros((LANES - heads, length), F32)
    cum_ref[...] = jnp.concatenate([cumt - jnp.log(stept_ref[...]), pad], axis=0).T
    start = jnp.exp(jnp.concatenate([cumt, pad], axis=0).T)
    table = halves(start)
    for j in range(width // LANES):
        span = slice(j * LANES, (j + 1) * LANES)
        dys = dy_ref[:, span].astype(F32) * dot(table, to_lanes(j, size), 1, 0)
        dyt_ref[span, :] = dys.T.astype(BF16)
    decay = jnp.broadcast_to(jnp.exp(cumt[:, length - 1 : length]), (heads, LANES))
    dyt_ref[width : width + 2 * heads, :] = jnp.concatenate(high_low(decay), axis=0).astype(BF16)


def scale_kernel(x_ref, dy_ref, h_ref, cumt_ref, cum_ref, xs_ref, carried_ref, token_ref, *rest):
    outs, xt_ref = rest[:-1], rest[-1]
    length, width = x_ref.shape
    heads = cumt_ref.shape[0]
    size = width // heads
    _, chip, n_chip = core_and_chip()
    pad = jnp.zeros((LANES - heads, length), F32)
    cum = jnp.concatenate([cumt_ref[...], pad], axis=0).T
    into_end = jnp.exp(cum[length - 1 : length] - cum_ref[...])
    table = jnp.concatenate([halves(jnp.exp(cum)), halves(into_end)], axis=0)
    carried = jnp.zeros(carried_ref.shape, F32)
    for j in range(width // LANES):
        span = slice(j * LANES, (j + 1) * LANES)
        scale = dot(table, to_lanes(j, size), 1, 0)
        x_f = x_ref[:, span].astype(F32)
        xt_ref[span, :] = x_f.T.astype(BF16)
        xs_ref[:, span] = (x_f * scale[length:]).astype(BF16)
        dys = (dy_ref[:, span].astype(F32) * scale[:length]).astype(BF16)
        carried = carried + dot(dys, h_ref[span, :], 1, 0)
    carried_ref[...] = carried
    token_ref[...] = jnp.zeros_like(token_ref)
    block = width // n_chip
    s = 0
    for out in outs:
        for start in range(0, out.shape[0], block):
            out[start : start + block, :] = xt_ref[rows_at(chip ^ s, block), :]
            s += 1


def join_kernel(ranges, *refs):
    out, at = refs[-1], 0
    for ref, (start, stop) in zip(refs, ranges):
        out[at : at + stop - start] = ref[start:stop]
        at += stop - start


def joined(arrays, after=(), ranges=None, cost=0.2):
    ranges = ranges or [(0, a.shape[0]) for a in arrays]
    dims = (sum(stop - start for start, stop in ranges), *arrays[0].shape[1:])
    return call(
        lambda *refs: join_kernel(ranges, *refs),
        [shape(dims, arrays[0].dtype)],
        cost,
        tuple(arrays),
        after=after,
    )[0]


def stacked(arrays, after=(), ranges=None, cost=0.2):
    count = len(arrays)
    out = joined(arrays, after, ranges, cost)
    return out.reshape(count, out.shape[0] // count, *out.shape[1:])


def project_kernel(n_mine, many, *refs):
    x_ref, dyt_ref, own_ref = refs[:3]
    mine, other = refs[3 : 3 + n_mine], refs[3 + n_mine]
    w_ref, bc_ref, keep_ref, send_ref = refs[4 + n_mine :]
    core, _, _ = core_and_chip()
    place, n_dp = lax.axis_index("dp"), lax.axis_size("dp")
    share = own_ref.shape[0]
    half = share // 2
    w_ref[rows_at(place, share), :] = own_ref[...]
    for i in range(n_mine):
        source = place ^ (i + 1)
        w_ref[rows_at(source * 2 + core, half), :] = mine[i][...]
        w_ref[rows_at(source * 2 + 1 - core, half), :] = other[i]
    bc = dot(x_ref[...], w_ref[...], 1, 0).astype(BF16)
    bc_ref[...] = bc
    c_rows = bc[:, LANES:]
    width = x_ref.shape[1]
    part = width // 2
    for ref, index in ((keep_ref, core), (send_ref, 1 - core)):
        ref[:part, :] = dot(dyt_ref[rows_at(index, part), :], c_rows, 1, 0).astype(BF16)
        table = dyt_ref[width : width + 4 * many, :].astype(F32)
        quarter = [table[i * many : (i + 1) * many] for i in range(4)]
        high = jnp.where(index == 0, quarter[0], quarter[1])
        low = jnp.where(index == 0, quarter[2], quarter[3])
        fill = jnp.zeros((ref.shape[0] - part - 2 * many, LANES), F32)
        ref[part:, :] = jnp.concatenate([high, low, fill], axis=0).astype(BF16)


def pair(keep_ref, recv_ref, many, size, head):
    core, _, _ = core_and_chip()
    part = many * size
    both = []
    for ref in (keep_ref, recv_ref):
        extra = ref[part:, :].astype(F32)
        decay = extra[head : head + 1] + extra[many + head : many + head + 1]
        both.append((ref[head * size : (head + 1) * size, :].astype(F32), decay))
    first = jax.tree.map(lambda a, b: jnp.where(core == 0, a, b), both[0], both[1])
    second = jax.tree.map(lambda a, b: jnp.where(core == 0, b, a), both[0], both[1])
    return first, second


def payload(ref, many, states, decays):
    size = states[0].shape[0]
    for head, state in enumerate(states):
        ref[head * size : (head + 1) * size, :] = state.astype(BF16)
    decay = jnp.concatenate(decays, axis=0)
    high = decay.astype(BF16).astype(F32)
    fill = jnp.zeros((ref.shape[0] - many * size - 2 * many, LANES), F32)
    extra = jnp.concatenate([high, decay - high, fill], axis=0)
    ref[many * size :, :] = extra.astype(BF16)


def loaded(ref, many, size, head):
    extra = ref[many * size :, :].astype(F32)
    decay = extra[head : head + 1] + extra[many + head : many + head + 1]
    return ref[head * size : (head + 1) * size, :].astype(F32), decay


def combine_kernel(many, size, keep_ref, recv_ref, out_ref):
    states, decays = [], []
    for head in range(many):
        (g0, a0), (g1, a1) = pair(keep_ref, recv_ref, many, size, head)
        states.append(g0 + a0 * g1)
        decays.append(a0 * a1)
    payload(out_ref, many, states, decays)


def pick_side(upper, mine, theirs):
    return jnp.where(upper, theirs, mine), jnp.where(upper, mine, theirs)


def climb_kernel(many, size, bit, mine_ref, recv_ref, out_ref):
    _, chip, _ = core_and_chip()
    upper = lax.rem(lax.div(chip, bit), 2) == 1
    states, decays = [], []
    for head in range(many):
        t_mine, a_mine = loaded(mine_ref, many, size, head)
        t_recv, a_recv = loaded(recv_ref, many, size, head)
        t_low, t_high = pick_side(upper, t_mine, t_recv)
        a_low, a_high = pick_side(upper, a_mine, a_recv)
        states.append(t_low + a_low * t_high)
        decays.append(a_low * a_high)
    payload(out_ref, many, states, decays)


def carry_kernel(many, size, levels, *refs):
    core, chip, _ = core_and_chip()
    recvs = refs[:levels]
    keep_ref, recv_ref, own_ref, send_ref = refs[levels:]
    for head in range(many):
        span = slice(head * size, (head + 1) * size)
        carry, reach = None, None
        for level, ref in enumerate(recvs):
            state, decay = loaded(ref, many, size, head)
            lower = lax.rem(lax.div(chip, 2**level), 2) == 0
            state = jnp.where(lower, state, 0.0)
            decay = jnp.where(lower, decay, 1.0)
            carry = state if carry is None else carry + reach * state
            reach = decay if reach is None else reach * decay
        _, (g1, a1) = pair(keep_ref, recv_ref, many, size, head)
        second = carry
        first = g1 + a1 * second
        own_ref[span, :] = jnp.where(core == 0, first, second).astype(BF16)
        send_ref[span, :] = jnp.where(core == 0, second, first).astype(BF16)


def intra_kernel(
    first, many, x_ref, dy_ref, bc_ref, cumt_ref, cum_ref, h_ref, before_ref,
    dx_ref, mixed_ref, ex_ref, own_ref, rowm_ref,
):
    length, width = x_ref.shape
    heads = cumt_ref.shape[0]
    size = width // heads
    per = LANES // size
    upper = iota((length, length), 0) <= iota((length, length), 1)
    b_rows, c_rows = bc_ref[:, :LANES], bc_ref[:, LANES:]
    scores = dot(b_rows, c_rows, 1, 1)
    lane = iota((1, LANES), 1)
    lane_bf = [where_one(lane // size == i).astype(BF16) for i in range(per)]
    mixed = before_ref[...]
    own = jnp.zeros((length, LANES), F32)
    reach = jnp.zeros((heads, length), F32)
    for j in range(first, first + many):
        span = slice(j * LANES, (j + 1) * LANES)
        out_span = slice((j - first) * LANES, (j - first + 1) * LANES)
        x_p = x_ref[:, span]
        dy_p = dy_ref[:, span]
        dy_h = jnp.concatenate([dy_p * m for m in lane_bf], axis=0)
        cross = dot(x_p, dy_h, 1, 1)
        kern = []
        for i in range(per):
            h = j * per + i
            diff = cumt_ref[h : h + 1, :] - cum_ref[:, h : h + 1]
            seg = jnp.exp(jnp.where(upper, diff, -1e30))
            part = cross[:, i * length : (i + 1) * length]
            mixed = mixed + seg * part
            seg = seg * scores
            kern.append(seg.astype(BF16))
            full = seg * part
            rowm_ref[h : h + 1, :] = jnp.sum(full, axis=0, keepdims=True)
            own = jnp.where(lane == h, jnp.sum(full, axis=1, keepdims=True), own)
        dx_ref[:, out_span] = dot(jnp.concatenate(kern, axis=1), dy_h, 1, 0)
        seen = dy_p.astype(F32) * dot(c_rows, h_ref[span, :], 1, 1)
        reach = reach + dot(to_heads(j, heads, size), halves(seen), 1, 1)
    mixed_ref[...] = mixed
    rows = slice(first * per, (first + many) * per)
    own = own.T[rows]
    own_ref[...] = own
    ex_ref[...] = rowm_ref[rows, :] + jnp.exp(cumt_ref[rows, :]) * reach[rows] - own


def close_kernel(mixed_ref, bc_ref, carried_ref, db_ref, dc_ref):
    mixed = mixed_ref[...].astype(BF16)
    db_ref[...] = dot(mixed, bc_ref[:, LANES:], 1, 0)
    dc_ref[...] = (dot(mixed, bc_ref[:, :LANES], 0, 0) + carried_ref[...]).astype(BF16)


def db_kernel(xs_ref, own_ref, recv_ref, db_ref, dc_ref, out_ref):
    core, _, _ = core_and_chip()
    half = db_ref.shape[1]
    part = own_ref.shape[0]
    total = db_ref[...]
    for ref, index in ((own_ref, core), (recv_ref, 1 - core)):
        total = total + dot(xs_ref[:, rows_at(index, part, LANES)], ref[...], 1, 0)
    out_ref[:, :half] = total.astype(BF16)
    out_ref[:, half:] = dc_ref[...]


def finish_kernel(parts, *refs):
    (x_ref, bc_ref, cumt_ref, stept_ref, cum_ref, h_ref, own_ref, recv_ref,
     w_ref, dbc_ref) = refs[:10]
    dx_refs, ex_refs, st_refs = (refs[10 + i * parts : 10 + (i + 1) * parts] for i in range(3))
    in_ref, decay_ref, grad_ref, token_ref, r_ref, edge_ref = refs[10 + 3 * parts :]
    token_ref[...] = jnp.zeros_like(token_ref)
    core, _, _ = core_and_chip()
    length, width = x_ref.shape
    heads = cumt_ref.shape[0]
    size = width // heads
    part = width // 2
    r_ref[rows_at(core, part), :] = own_ref[...]
    r_ref[rows_at(1 - core, part), :] = recv_ref[...]
    pad = jnp.zeros((LANES - heads, length), F32)
    total = jnp.concatenate([cumt_ref[...], pad], axis=0).T[length - 1 : length]
    table = halves(jnp.exp(total - cum_ref[...]))
    seen = jnp.zeros((heads, length), F32)
    b_rows = bc_ref[:, :LANES]
    d_bc = dbc_ref[...]
    for j in range(width // LANES):
        span = slice(j * LANES, (j + 1) * LANES)
        local = dx_refs[j * LANES // (width // parts)]
        start = j * LANES % (width // parts)
        r_tile = r_ref[span, :]
        reach = dot(b_rows, r_tile, 1, 1)
        d_in = local[:, start : start + LANES] + dot(table, to_lanes(j, size), 1, 0) * reach
        d_in = d_in + dot(d_bc, w_ref[span, :], 1, 1)
        in_ref[:, span] = d_in.astype(BF16)
        product = x_ref[:, span].astype(F32) * reach
        seen = seen + dot(to_heads(j, heads, size), halves(product), 1, 1)
        edge = r_tile.astype(F32) * h_ref[span, :].astype(F32)
        for i in range(LANES // size):
            h = j * (LANES // size) + i
            edge_ref[h : h + 1, :] = jnp.sum(
                edge[i * size : (i + 1) * size], axis=0, keepdims=True
            )
    cumt = cumt_ref[...]
    total = cumt[:, length - 1 : length]
    to_end = jnp.exp(total - cumt)
    step = stept_ref[...]
    own = jnp.concatenate([r[...] for r in st_refs], axis=0)
    excess = jnp.concatenate([r[...] for r in ex_refs], axis=0)
    grad_ref[...] = own / step + to_end * seen
    edge = jnp.exp(total) * jnp.sum(edge_ref[...], axis=1, keepdims=True)
    decay_ref[...] = (
        dot(excess, triangle(length, lambda a, b: a >= b), 1, 0, HI)
        + dot(to_end * step * seen, triangle(length, lambda a, b: a < b), 1, 0, HI)
        + edge
    )


def term_kernel(places, n_columns, *refs):
    columns, pieces = refs[:n_columns], refs[n_columns:-3]
    keep_ref, send_ref, held = refs[-3:]
    pieces = [(p, i) for p in pieces for i in range(p.shape[0])]
    rows = 2 * keep_ref.shape[0]
    core, _, _ = core_and_chip()
    total = None
    for (a, start), (b, i) in zip(places, pieces):
        part = dot(columns[a][start : start + rows, :], b[i], 1, 0)
        total = part if total is None else total + part
    block = keep_ref.shape[0]
    held[0] = total[:block]
    held[1] = total[block:]
    keep_ref[...] = held[core]
    send_ref[...] = held[1 - core].astype(BF16)


def deal_kernel(keep_ref, recv_ref, own_ref, *refs):
    outs, held = refs[:-1], refs[-1]
    place, n_dp = lax.axis_index("dp"), lax.axis_size("dp")
    total = keep_ref[...] + recv_ref[...].astype(F32)
    share = own_ref.shape[0]
    for i in range(n_dp):
        held[i] = total[i * share : (i + 1) * share]
    own_ref[...] = held[place]
    for s, out in enumerate(outs):
        out[...] = held[place ^ (s + 1)].astype(BF16)


def sum_kernel(*refs):
    total = refs[0][...]
    for ref in refs[1:-1]:
        total = total + ref[...].astype(F32)
    refs[-1][...] = total


def expert_kernel(flip, slots, a_ref, b_ref, gate_ref, up_ref, out_ref, *scratch):
    rows_ref, gate_acc, up_acc = scratch
    step = pl.program_id(0)
    n_chip = a_ref.shape[0]

    @pl.when(step == 0)
    def _():
        for half, ref in enumerate((a_ref, b_ref)):
            for i in range(n_chip):
                row = (half * n_chip + i) * slots
                for t in range(rows_ref.shape[1] // LANES):
                    rows_ref[row : row + slots, t * LANES : (t + 1) * LANES] = ref[
                        i, t * slots : (t + 1) * slots, :
                    ]
        gate_acc[...] = jnp.zeros_like(gate_acc)
        up_acc[...] = jnp.zeros_like(up_acc)

    depth = gate_ref.shape[0]
    rows = rows_ref[:, rows_at(step, depth, LANES)]
    gate_acc[...] += dot(rows, gate_ref[...], 1, 0)
    up_acc[...] += dot(rows, up_ref[...], 1, 0)

    @pl.when(step == pl.num_programs(0) - 1)
    def _():
        weighted = jax.nn.silu(gate_acc[...]) * up_acc[...]
        out_ref[...] = (weighted.T if flip else weighted).astype(BF16)


def expert(a, b, w_gate, w_up, slots, flip, after):
    n_chip = a.shape[0]
    total = 2 * n_chip * slots
    width, hidden = w_gate.shape
    depth = 512
    out = (hidden, total) if flip else (total, hidden)

    def body(*refs):
        expert_kernel(flip, slots, *refs[:4], *refs[4 + len(after) :])

    whole = pl.BlockSpec(a.shape, lambda i: (0, 0, 0))
    block = pl.BlockSpec((depth, hidden), lambda i: (i, 0))
    return pl.pallas_call(
        body,
        out_shape=shape(out, BF16),
        grid=(width // depth,),
        in_specs=[whole, whole, block, block]
        + [pl.BlockSpec(memory_space=pl.ANY)] * len(after),
        out_specs=pl.BlockSpec(out, lambda i: (0, 0)),
        scratch_shapes=[
            pltpu.VMEM((total, width), BF16),
            pltpu.VMEM((total, hidden), F32),
            pltpu.VMEM((total, hidden), F32),
        ],
        cost_estimate=pl.CostEstimate(
            flops=int(1e9), bytes_accessed=1000, transcendentals=0
        ),
        compiler_params=pltpu.CompilerParams(vmem_limit_bytes=20 * 1024 * 1024),
    )(a, b, w_gate, w_up, *after)


def down_kernel(n_dp, flip, slots, grad_rows, *refs):
    pieces = refs[:n_dp]
    a_ref, b_ref, out_ref, token_ref = refs[n_dp:]
    token_ref[...] = jnp.zeros_like(token_ref)
    n_chip = a_ref.shape[0]
    piece = out_ref.shape[1]
    base = a_ref.shape[1] - n_dp * grad_rows
    total = None
    for s in range(n_dp):
        columns = []
        for t in range(grad_rows // slots):
            row = base + s * grad_rows + t * slots
            blocks = [r[i, row : row + slots, :] for r in (a_ref, b_ref) for i in range(n_chip)]
            columns.append(jnp.concatenate(blocks, axis=0))
        right = jnp.concatenate(columns, axis=1)[:, :piece]
        part = dot(pieces[s][...], right, 1 if flip else 0, 0)
        total = part if total is None else total + part
    out_ref[...] = total.astype(BF16)


def xored(array, axis, mask):
    count = lax.axis_size(axis)
    return lax.ppermute(array, axis, [(i, i ^ mask) for i in range(count)])


def swapped(array):
    return xored(array, "tm", 1)


def chips(arrays):
    return [arrays[0]] + [xored(a, "tm", 2 * s) for s, a in enumerate(arrays) if s]


def gathered(array, axis, count):
    if count == 1:
        return [array]
    far = xored(array, axis, count // 2)
    return gathered(array, axis, count // 2) + gathered(far, axis, count // 2)


def per_device(
    layer_in,
    out_grad,
    w_bc,
    log_decay,
    step,
    saved_states,
    w_gate,
    w_up,
    slot_rows,
    slot_counts,
    slot_gates,
):
    n_dp = lax.axis_size("dp")
    core, chip, n_chip = core_and_chip()
    x = layer_in[0]
    dy = out_grad[0]
    length, width = x.shape
    heads = log_decay.shape[2]
    size = width // heads
    share, columns = w_bc.shape
    half = columns // 2
    ldt = log_decay[0].T
    stept = step[0].T
    h_in = saved_states[0, 0].reshape(width, half)
    capacity = slot_rows.shape[2]
    piece = width // n_dp
    part = width // 2
    many = heads // 2
    flip = w_gate.shape[2] % LANES == 0

    grad_rows = -(-piece // LANES) * capacity
    w_half = lax.dynamic_slice_in_dim(w_bc, core * (share // 2), share // 2, 0)

    in_rows = width // LANES * capacity
    blocks = [1, 1, 2] if n_chip == 4 else [1] * n_chip
    groups = [2, 2] if n_dp == 4 else [1] * n_dp
    cumt, cum, dyt, rows, *deals = call(
        lambda *refs: prep_kernel(len(groups), *refs),
        [
            shape((heads, length), F32),
            shape((length, LANES), F32),
            shape((width + up16(2 * heads), length), BF16),
            shape((in_rows, LANES), BF16),
        ]
        + [shape((k * grad_rows, LANES), BF16) for k in groups],
        1.5,
        (x, dy, ldt, stept, slot_rows[0], slot_counts, slot_gates[0]),
        scratch=[pltpu.VMEM((n_dp, grad_rows, LANES), BF16)],
        fetch=(0, 1, 2, 3),
        limit=60,
    )
    rows_in = chips([rows] * n_chip)
    w_far = xored(w_half, "dp", n_dp // 2)
    mine = gathered(w_half, "dp", n_dp // 2)[1:]
    w_copy = joined([w_far], after=(rows,))
    mine += gathered(w_copy, "dp", n_dp // 2)
    xs, carried, scaled, *xt = call(
        scale_kernel,
        [shape((length, width), BF16), shape((length, half), F32), shape((8, LANES), F32)]
        + [shape((k * width // n_chip, length), BF16) for k in blocks],
        1.5,
        (x, dy, h_in, cumt, cum),
        after=(rows,),
        scratch=[pltpu.VMEM((width, length), BF16)],
        fetch=(0, 1, 2, 3, 4),
        limit=60,
    )
    if n_dp == 4:
        one = (0, grad_rows), (grad_rows, 2 * grad_rows)
        over_2 = xored(deals[1], "dp", 2)
        early = (over_2,)
    else:
        early = ()
        source, spans = deals[:1] + [xored(d, "dp", s + 1) for s, d in enumerate(deals[1:])], None
    other = swapped(stacked(mine, after=(*rows_in[1:4], scaled), cost=1.0))
    w_whole, bc, keep, send = call(
        lambda *refs: project_kernel(n_dp - 1, many, *refs),
        [
            shape((width, columns), BF16),
            shape((length, columns), BF16),
            shape((part + up16(2 * many), half), BF16),
            shape((part + up16(2 * many), half), BF16),
        ],
        1.0,
        (x, dyt, w_bc, *mine, other),
    )
    recv = swapped(send)
    hidden = w_gate.shape[2]
    climbs = [
        call(
            lambda *refs: combine_kernel(many, size, *refs),
            [shape((part + up16(2 * many), half), BF16)],
            0.5,
            (keep, recv),
        )[0]
    ]
    rows_a = stacked(rows_in, after=(climbs[0],))
    rows_b = swapped(rows_a)
    weighted = expert(rows_a, rows_b, w_gate[0], w_up[0], capacity, flip, (climbs[0],))
    if n_chip == 4:
        x_rows = width // n_chip
        over_y = xored(xt[2], "tm", 4)

    parts = 2
    tiles = width // LANES // parts
    dxs, exs, owns = [], [], []
    held = (weighted, *early)
    arrived = []
    bit = 1
    while bit < n_chip:
        last = bit * 2 == n_chip
        moves = [(k, k ^ (2 * bit)) for k in range(2 * n_chip)]
        arrived.append(lax.ppermute(climbs[-1], "tm", moves))
        if not last:
            climbs.append(
                call(
                    lambda *refs, bit=bit: climb_kernel(many, size, bit, *refs),
                    [shape((part + up16(2 * many), half), BF16)],
                    0.5,
                    (climbs[-1], arrived[-1]),
                    after=held,
                )[0]
            )
        bit *= 2
    later = (climbs[-1],)
    mixed = jnp.zeros((length, length), F32)
    for i in range(parts):
        dx, mixed, ex, own = call(
            lambda *refs, i=i: intra_kernel(i * tiles, tiles, *refs),
            [
                shape((length, width // parts), F32),
                shape((length, length), F32),
                shape((heads // parts, length), F32),
                shape((heads // parts, length), F32),
            ],
            0.7,
            (x, dy, bc, cumt, cum, h_in, mixed),
            after=later,
            scratch=[pltpu.VMEM((heads, length), F32)],
        )
        dxs.append(dx)
        exs.append(ex)
        owns.append(own)
    db, dc = call(
        close_kernel,
        [shape((length, half), F32), shape((length, half), BF16)],
        0.3,
        (mixed, bc, carried),
    )

    held = (dc,)
    if n_dp == 4:
        over_1 = xored(joined([deals[0], over_2], later, [one[1], one[1]]), "dp", 1)
        source, spans = [deals[0], over_1, over_2, over_1], [one[0], one[0], one[0], one[1]]
    dealt = joined(source, later, spans)
    held += (dealt,)
    if n_chip == 4:
        over_x = xored(joined([xt[1], over_y], later, [(0, x_rows), (x_rows, 2 * x_rows)]), "tm", 2)
        columns_in = [xt[0], over_x, over_y]
        places = [(0, 0), (1, 0), (2, 0), (1, x_rows)]
        held += (over_x,)
    else:
        columns_in = chips(xt)
        places = [(i, 0) for i in range(n_chip)]
    far = xored(weighted, "dp", n_dp // 2)
    near = gathered(weighted, "dp", n_dp // 2)
    held += (far, *near[1:])
    r_own, r_send = call(
        lambda *refs: carry_kernel(many, size, len(arrived), *refs),
        [shape((part, half), BF16)] * 2,
        0.5,
        (*arrived, keep, recv),
        after=held,
    )
    r_recv = swapped(r_send)
    if n_chip == 4:
        grads_y = xored(dealt, "tm", 4)
        rest = dealt.shape[0]
        spans = [(0, rest), (0, rest), (0, rest), (rest, 2 * rest)]
    else:
        grads, spans = chips([dealt] * n_chip), None
    fars = gathered(joined([far], (r_own,)), "dp", n_dp // 2)
    d_bc = call(db_kernel, [shape((length, columns), BF16)], 0.3, (xs, r_own, r_recv, db, dc))[0]
    d_bcs = [d_bc.reshape(1, length, columns)]
    while 2 ** (len(d_bcs) - 1) < n_chip:
        level = 2 ** (len(d_bcs) - 1)
        sent = d_bcs[0] if level == 1 else joined(d_bcs)
        d_bcs.append(xored(sent, "tm", 2 * level))
    d_in, d_decay, d_step, token = call(
        lambda *refs: finish_kernel(parts, *refs),
        [
            shape((length, width), BF16),
            shape((heads, length), F32),
            shape((heads, length), F32),
            shape((8, LANES), F32),
        ],
        3.0,
        (x, bc, cumt, stept, cum, h_in, r_own, r_recv, w_whole, d_bc,
         *dxs, *exs, *owns),
        after=tuple(fars[1:]),
        scratch=[pltpu.VMEM((width, half), BF16), pltpu.VMEM((heads, half), F32)],
    )
    w_rows = width // (2 * n_chip)
    term, term_send = call(
        lambda *refs: term_kernel(places, len(columns_in), *refs),
        [shape((w_rows, columns), F32), shape((w_rows, columns), BF16)],
        0.5,
        (*columns_in, *d_bcs),
        after=(token,),
        scratch=[pltpu.VMEM((2, w_rows, columns), F32)],
    )
    final = call(
        deal_kernel,
        [shape((w_rows // n_dp, columns), F32)]
        + [shape((w_rows // n_dp, columns), BF16)] * (n_dp - 1),
        0.3,
        (term, swapped(term_send)),
        scratch=[pltpu.VMEM((n_dp, w_rows // n_dp, columns), F32)],
    )
    final = list(final[:1]) + [xored(f, "dp", s + 1) for s, f in enumerate(final[1:])]

    if n_chip == 4:
        grads_x = xored(joined([dealt, grads_y], (sent,)), "tm", 2)
        grads = [dealt, grads_x, grads_y, grads_x]
    grads_a = stacked(grads, (term,), spans)
    grads_b = swapped(grads_a)
    w_down_grad, done = call(
        lambda *refs: down_kernel(n_dp, flip, capacity, grad_rows, *refs),
        [shape((hidden, piece), BF16), shape((8, LANES), F32)],
        1.0,
        (*near, *fars, grads_a, grads_b),
        after=(final[0],),
    )
    w_bc_grad = call(sum_kernel, [shape(final[0].shape, F32)], 0.1, final, (done,))[0]
    return (d_in[None], d_decay.T[None], d_step.T[None], w_bc_grad, w_down_grad[None])


def solution(mesh):
    in_specs = (
        P("dp", "tm", None),
        P("dp", "tm", None),
        P("dp", None),
        P("dp", "tm", None),
        P("dp", "tm", None),
        P("dp", "tm", None, None, None),
        P(None, None, "tm"),
        P(None, None, "tm"),
        P("dp", None, "tm"),
        P("dp", "tm"),
        P("dp", None, "tm"),
    )
    out_specs = (
        P("dp", "tm", None),
        P("dp", "tm", None),
        P("dp", "tm", None),
        P(("tm", "dp"), None),
        P(None, "tm", "dp"),
    )
    return jax.shard_map(
        per_device, mesh=mesh, in_specs=in_specs, out_specs=out_specs, check_vma=False
    )
```

```python
import jax
import jax.numpy as jnp
from jax import lax
from jax.experimental import pallas as pl
from jax.experimental.pallas import tpu as pltpu
from jax.sharding import PartitionSpec as P

HI = lax.Precision.HIGHEST
F32 = jnp.float32
BF16 = jnp.bfloat16
LANES = 128


def dot(a, b, ca, cb, precision=None):
    return lax.dot_general(
        a, b, (((ca,), (cb,)), ((), ())), precision=precision, preferred_element_type=F32
    )


def iota(dims, axis):
    return lax.broadcasted_iota(jnp.int32, dims, axis)


def where_one(mask):
    return jnp.where(mask, 1.0, 0.0)


def triangle(n, keep):
    return where_one(keep(iota((n, n), 0), iota((n, n), 1))).astype(F32)


def halves(values, axis=1):
    high = values.astype(BF16)
    low = (values - high.astype(F32)).astype(BF16)
    return jnp.concatenate([high, low], axis=axis)


def to_lanes(j, size):
    dims = (LANES, LANES)
    one = where_one(iota(dims, 0) == iota(dims, 1) // size + j * (LANES // size)).astype(BF16)
    return jnp.concatenate([one, one], axis=0)


def to_heads(j, heads, size):
    dims = (heads, LANES)
    one = where_one(iota(dims, 0) == iota(dims, 1) // size + j * (LANES // size)).astype(BF16)
    return jnp.concatenate([one, one], axis=1)


def up16(n):
    return -(-n // 16) * 16


def call(kernel, outs, cost, args, after=(), scratch=(), limit=14, fetch=()):
    n_in, n_after, n_out = len(args), len(after), len(outs)
    fetch = tuple(fetch)

    def body(*refs):
        ins = list(refs[:n_in])
        rest = refs[n_in + n_after :]
        if fetch:
            sems = rest[-1]
            held = rest[len(rest) - 1 - len(fetch) : -1]
            rest = rest[: len(rest) - 1 - len(fetch)]
            copies = []
            for i, (index, ref) in enumerate(zip(fetch, held)):
                copies.append(pltpu.make_async_copy(ins[index], ref, sems.at[i]))
                ins[index] = ref
            for copy in copies:
                copy.start()
            for copy in copies:
                copy.wait()
        kernel(*ins, *rest)

    specs = [
        pl.BlockSpec(memory_space=pltpu.HBM if i in fetch else pltpu.VMEM) for i in range(n_in)
    ]
    held = [pltpu.VMEM(args[i].shape, args[i].dtype) for i in fetch]
    if fetch:
        held.append(pltpu.SemaphoreType.DMA((len(fetch),)))
    return pl.pallas_call(
        body,
        out_shape=outs,
        in_specs=specs + [pl.BlockSpec(memory_space=pl.ANY)] * n_after,
        out_specs=[pl.BlockSpec(memory_space=pltpu.VMEM)] * n_out,
        scratch_shapes=list(scratch) + held,
        cost_estimate=pl.CostEstimate(
            flops=int(cost * 3e9), bytes_accessed=1000, transcendentals=0
        ),
        compiler_params=pltpu.CompilerParams(vmem_limit_bytes=limit * 1024 * 1024),
    )(*args, *after)


def shape(dims, kind):
    return jax.ShapeDtypeStruct(dims, kind)


def core_and_chip():
    place = lax.axis_index("tm")
    return lax.rem(place, 2), lax.div(place, 2), lax.axis_size("tm") // 2


def rows_at(index, size, align=16):
    return pl.ds(pl.multiple_of(index * size, align), size)


def picked(x_ref, dy_ref, slot_ref, count_ref, gate_ref, rows_ref, out_refs):
    length, width = x_ref.shape
    slots = slot_ref.shape[1]
    hit = iota((length, slots), 0) == slot_ref[...]
    live = iota((1, slots), 1) < count_ref[...]
    weight = jnp.where(live, gate_ref[...].astype(F32), 0.0)
    rows = dot(where_one(hit).astype(BF16), x_ref[...], 0, 0).astype(BF16)
    for t in range(width // LANES):
        rows_ref[t * slots : (t + 1) * slots, :] = rows[:, t * LANES : (t + 1) * LANES]
    grads = dot(jnp.where(hit, weight, 0.0).astype(BF16), dy_ref[...], 0, 0).astype(BF16)
    held = out_refs[-1]
    n_dp = held.shape[0]
    piece = width // n_dp
    for i in range(n_dp):
        for t, low in enumerate(range(i * piece, (i + 1) * piece, LANES)):
            block = grads[:, low : min(low + LANES, (i + 1) * piece)]
            if block.shape[1] < LANES:
                fill = jnp.zeros((slots, LANES - block.shape[1]), BF16)
                block = jnp.concatenate([block, fill], axis=1)
            held[i, t * slots : (t + 1) * slots, :] = block
    place = lax.axis_index("dp")
    s = 0
    for out in out_refs[:-1]:
        for start in range(0, out.shape[0], held.shape[1]):
            out[start : start + held.shape[1], :] = held[place ^ s]
            s += 1


def high_low(values):
    high = values.astype(BF16).astype(F32)
    return [high, values - high]


def prep_kernel(
    n_deals, x_ref, dy_ref, ldt_ref, stept_ref, slot_ref, count_ref, gate_ref,
    cumt_ref, cum_ref, dyt_ref, rows_ref, *rest,
):
    length, width = x_ref.shape
    heads = ldt_ref.shape[0]
    size = width // heads
    picked(x_ref, dy_ref, slot_ref, count_ref, gate_ref, rows_ref, rest)
    cumt = dot(ldt_ref[...], triangle(length, lambda a, b: a <= b), 1, 0, HI)
    cumt_ref[...] = cumt
    pad = jnp.zeros((LANES - heads, length), F32)
    cum_ref[...] = jnp.concatenate([cumt - jnp.log(stept_ref[...]), pad], axis=0).T
    start = jnp.exp(jnp.concatenate([cumt, pad], axis=0).T)
    table = halves(start)
    for j in range(width // LANES):
        span = slice(j * LANES, (j + 1) * LANES)
        dys = dy_ref[:, span].astype(F32) * dot(table, to_lanes(j, size), 1, 0)
        dyt_ref[span, :] = dys.T.astype(BF16)
    decay = jnp.broadcast_to(jnp.exp(cumt[:, length - 1 : length]), (heads, LANES))
    dyt_ref[width : width + 2 * heads, :] = jnp.concatenate(high_low(decay), axis=0).astype(BF16)


def scale_kernel(x_ref, dy_ref, h_ref, cumt_ref, cum_ref, xs_ref, carried_ref, token_ref, *rest):
    outs, xt_ref = rest[:-1], rest[-1]
    length, width = x_ref.shape
    heads = cumt_ref.shape[0]
    size = width // heads
    _, chip, n_chip = core_and_chip()
    pad = jnp.zeros((LANES - heads, length), F32)
    cum = jnp.concatenate([cumt_ref[...], pad], axis=0).T
    into_end = jnp.exp(cum[length - 1 : length] - cum_ref[...])
    table = jnp.concatenate([halves(jnp.exp(cum)), halves(into_end)], axis=0)
    carried = jnp.zeros(carried_ref.shape, F32)
    for j in range(width // LANES):
        span = slice(j * LANES, (j + 1) * LANES)
        scale = dot(table, to_lanes(j, size), 1, 0)
        x_f = x_ref[:, span].astype(F32)
        xt_ref[span, :] = x_f.T.astype(BF16)
        xs_ref[:, span] = (x_f * scale[length:]).astype(BF16)
        dys = (dy_ref[:, span].astype(F32) * scale[:length]).astype(BF16)
        carried = carried + dot(dys, h_ref[span, :], 1, 0)
    carried_ref[...] = carried
    token_ref[...] = jnp.zeros_like(token_ref)
    block = width // n_chip
    s = 0
    for out in outs:
        for start in range(0, out.shape[0], block):
            out[start : start + block, :] = xt_ref[rows_at(chip ^ s, block), :]
            s += 1


def join_kernel(ranges, *refs):
    out, at = refs[-1], 0
    for ref, (start, stop) in zip(refs, ranges):
        out[at : at + stop - start] = ref[start:stop]
        at += stop - start


def joined(arrays, after=(), ranges=None, cost=0.2):
    ranges = ranges or [(0, a.shape[0]) for a in arrays]
    dims = (sum(stop - start for start, stop in ranges), *arrays[0].shape[1:])
    return call(
        lambda *refs: join_kernel(ranges, *refs),
        [shape(dims, arrays[0].dtype)],
        cost,
        tuple(arrays),
        after=after,
    )[0]


def stacked(arrays, after=(), ranges=None, cost=0.2):
    count = len(arrays)
    out = joined(arrays, after, ranges, cost)
    return out.reshape(count, out.shape[0] // count, *out.shape[1:])


def project_kernel(n_mine, many, *refs):
    x_ref, dyt_ref, own_ref = refs[:3]
    mine, other = refs[3 : 3 + n_mine], refs[3 + n_mine]
    w_ref, bc_ref, keep_ref, send_ref = refs[4 + n_mine :]
    core, _, _ = core_and_chip()
    place, n_dp = lax.axis_index("dp"), lax.axis_size("dp")
    share = own_ref.shape[0]
    half = share // 2
    w_ref[rows_at(place, share), :] = own_ref[...]
    for i in range(n_mine):
        source = place ^ (i + 1)
        w_ref[rows_at(source * 2 + core, half), :] = mine[i][...]
        w_ref[rows_at(source * 2 + 1 - core, half), :] = other[i]
    bc = dot(x_ref[...], w_ref[...], 1, 0).astype(BF16)
    bc_ref[...] = bc
    c_rows = bc[:, LANES:]
    width = x_ref.shape[1]
    part = width // 2
    for ref, index in ((keep_ref, core), (send_ref, 1 - core)):
        ref[:part, :] = dot(dyt_ref[rows_at(index, part), :], c_rows, 1, 0).astype(BF16)
        table = dyt_ref[width : width + 4 * many, :].astype(F32)
        quarter = [table[i * many : (i + 1) * many] for i in range(4)]
        high = jnp.where(index == 0, quarter[0], quarter[1])
        low = jnp.where(index == 0, quarter[2], quarter[3])
        fill = jnp.zeros((ref.shape[0] - part - 2 * many, LANES), F32)
        ref[part:, :] = jnp.concatenate([high, low, fill], axis=0).astype(BF16)


def pair(keep_ref, recv_ref, many, size, head):
    core, _, _ = core_and_chip()
    part = many * size
    both = []
    for ref in (keep_ref, recv_ref):
        extra = ref[part:, :].astype(F32)
        decay = extra[head : head + 1] + extra[many + head : many + head + 1]
        both.append((ref[head * size : (head + 1) * size, :].astype(F32), decay))
    first = jax.tree.map(lambda a, b: jnp.where(core == 0, a, b), both[0], both[1])
    second = jax.tree.map(lambda a, b: jnp.where(core == 0, b, a), both[0], both[1])
    return first, second


def payload(ref, many, states, decays):
    size = states[0].shape[0]
    for head, state in enumerate(states):
        ref[head * size : (head + 1) * size, :] = state.astype(BF16)
    decay = jnp.concatenate(decays, axis=0)
    high = decay.astype(BF16).astype(F32)
    fill = jnp.zeros((ref.shape[0] - many * size - 2 * many, LANES), F32)
    extra = jnp.concatenate([high, decay - high, fill], axis=0)
    ref[many * size :, :] = extra.astype(BF16)


def loaded(ref, many, size, head):
    extra = ref[many * size :, :].astype(F32)
    decay = extra[head : head + 1] + extra[many + head : many + head + 1]
    return ref[head * size : (head + 1) * size, :].astype(F32), decay


def combine_kernel(many, size, keep_ref, recv_ref, out_ref):
    states, decays = [], []
    for head in range(many):
        (g0, a0), (g1, a1) = pair(keep_ref, recv_ref, many, size, head)
        states.append(g0 + a0 * g1)
        decays.append(a0 * a1)
    payload(out_ref, many, states, decays)


def pick_side(upper, mine, theirs):
    return jnp.where(upper, theirs, mine), jnp.where(upper, mine, theirs)


def climb_kernel(many, size, bit, mine_ref, recv_ref, out_ref):
    _, chip, _ = core_and_chip()
    upper = lax.rem(lax.div(chip, bit), 2) == 1
    states, decays = [], []
    for head in range(many):
        t_mine, a_mine = loaded(mine_ref, many, size, head)
        t_recv, a_recv = loaded(recv_ref, many, size, head)
        t_low, t_high = pick_side(upper, t_mine, t_recv)
        a_low, a_high = pick_side(upper, a_mine, a_recv)
        states.append(t_low + a_low * t_high)
        decays.append(a_low * a_high)
    payload(out_ref, many, states, decays)


def carry_kernel(many, size, levels, *refs):
    core, chip, _ = core_and_chip()
    recvs = refs[:levels]
    keep_ref, recv_ref, own_ref, send_ref = refs[levels:]
    for head in range(many):
        span = slice(head * size, (head + 1) * size)
        carry, reach = None, None
        for level, ref in enumerate(recvs):
            state, decay = loaded(ref, many, size, head)
            lower = lax.rem(lax.div(chip, 2**level), 2) == 0
            state = jnp.where(lower, state, 0.0)
            decay = jnp.where(lower, decay, 1.0)
            carry = state if carry is None else carry + reach * state
            reach = decay if reach is None else reach * decay
        _, (g1, a1) = pair(keep_ref, recv_ref, many, size, head)
        second = carry
        first = g1 + a1 * second
        own_ref[span, :] = jnp.where(core == 0, first, second).astype(BF16)
        send_ref[span, :] = jnp.where(core == 0, second, first).astype(BF16)


def intra_kernel(
    first, many, x_ref, dy_ref, bc_ref, cumt_ref, cum_ref, h_ref, before_ref,
    dx_ref, mixed_ref, ex_ref, own_ref, rowm_ref,
):
    length, width = x_ref.shape
    heads = cumt_ref.shape[0]
    size = width // heads
    per = LANES // size
    upper = iota((length, length), 0) <= iota((length, length), 1)
    b_rows, c_rows = bc_ref[:, :LANES], bc_ref[:, LANES:]
    scores = dot(b_rows, c_rows, 1, 1)
    lane = iota((1, LANES), 1)
    lane_bf = [where_one(lane // size == i).astype(BF16) for i in range(per)]
    mixed = before_ref[...]
    own = jnp.zeros((length, LANES), F32)
    reach = jnp.zeros((heads, length), F32)
    for j in range(first, first + many):
        span = slice(j * LANES, (j + 1) * LANES)
        out_span = slice((j - first) * LANES, (j - first + 1) * LANES)
        x_p = x_ref[:, span]
        dy_p = dy_ref[:, span]
        dy_h = jnp.concatenate([dy_p * m for m in lane_bf], axis=0)
        cross = dot(x_p, dy_h, 1, 1)
        kern = []
        for i in range(per):
            h = j * per + i
            diff = cumt_ref[h : h + 1, :] - cum_ref[:, h : h + 1]
            seg = jnp.exp(jnp.where(upper, diff, -1e30))
            part = cross[:, i * length : (i + 1) * length]
            mixed = mixed + seg * part
            seg = seg * scores
            kern.append(seg.astype(BF16))
            full = seg * part
            rowm_ref[h : h + 1, :] = jnp.sum(full, axis=0, keepdims=True)
            own = jnp.where(lane == h, jnp.sum(full, axis=1, keepdims=True), own)
        dx_ref[:, out_span] = dot(jnp.concatenate(kern, axis=1), dy_h, 1, 0)
        seen = dy_p.astype(F32) * dot(c_rows, h_ref[span, :], 1, 1)
        reach = reach + dot(to_heads(j, heads, size), halves(seen), 1, 1)
    mixed_ref[...] = mixed
    rows = slice(first * per, (first + many) * per)
    own = own.T[rows]
    own_ref[...] = own
    ex_ref[...] = rowm_ref[rows, :] + jnp.exp(cumt_ref[rows, :]) * reach[rows] - own


def close_kernel(mixed_ref, bc_ref, carried_ref, db_ref, dc_ref):
    mixed = mixed_ref[...].astype(BF16)
    db_ref[...] = dot(mixed, bc_ref[:, LANES:], 1, 0)
    dc_ref[...] = (dot(mixed, bc_ref[:, :LANES], 0, 0) + carried_ref[...]).astype(BF16)


def db_kernel(xs_ref, own_ref, recv_ref, db_ref, dc_ref, out_ref):
    core, _, _ = core_and_chip()
    half = db_ref.shape[1]
    part = own_ref.shape[0]
    total = db_ref[...]
    for ref, index in ((own_ref, core), (recv_ref, 1 - core)):
        total = total + dot(xs_ref[:, rows_at(index, part, LANES)], ref[...], 1, 0)
    out_ref[:, :half] = total.astype(BF16)
    out_ref[:, half:] = dc_ref[...]


def finish_kernel(parts, *refs):
    (x_ref, bc_ref, cumt_ref, stept_ref, cum_ref, h_ref, own_ref, recv_ref,
     w_ref, dbc_ref) = refs[:10]
    dx_refs, ex_refs, st_refs = (refs[10 + i * parts : 10 + (i + 1) * parts] for i in range(3))
    in_ref, decay_ref, grad_ref, token_ref, r_ref, edge_ref = refs[10 + 3 * parts :]
    token_ref[...] = jnp.zeros_like(token_ref)
    core, _, _ = core_and_chip()
    length, width = x_ref.shape
    heads = cumt_ref.shape[0]
    size = width // heads
    part = width // 2
    r_ref[rows_at(core, part), :] = own_ref[...]
    r_ref[rows_at(1 - core, part), :] = recv_ref[...]
    pad = jnp.zeros((LANES - heads, length), F32)
    total = jnp.concatenate([cumt_ref[...], pad], axis=0).T[length - 1 : length]
    table = halves(jnp.exp(total - cum_ref[...]))
    seen = jnp.zeros((heads, length), F32)
    b_rows = bc_ref[:, :LANES]
    d_bc = dbc_ref[...]
    for j in range(width // LANES):
        span = slice(j * LANES, (j + 1) * LANES)
        local = dx_refs[j * LANES // (width // parts)]
        start = j * LANES % (width // parts)
        r_tile = r_ref[span, :]
        reach = dot(b_rows, r_tile, 1, 1)
        d_in = local[:, start : start + LANES] + dot(table, to_lanes(j, size), 1, 0) * reach
        d_in = d_in + dot(d_bc, w_ref[span, :], 1, 1)
        in_ref[:, span] = d_in.astype(BF16)
        product = x_ref[:, span].astype(F32) * reach
        seen = seen + dot(to_heads(j, heads, size), halves(product), 1, 1)
        edge = r_tile.astype(F32) * h_ref[span, :].astype(F32)
        for i in range(LANES // size):
            h = j * (LANES // size) + i
            edge_ref[h : h + 1, :] = jnp.sum(
                edge[i * size : (i + 1) * size], axis=0, keepdims=True
            )
    cumt = cumt_ref[...]
    total = cumt[:, length - 1 : length]
    to_end = jnp.exp(total - cumt)
    step = stept_ref[...]
    own = jnp.concatenate([r[...] for r in st_refs], axis=0)
    excess = jnp.concatenate([r[...] for r in ex_refs], axis=0)
    grad_ref[...] = own / step + to_end * seen
    edge = jnp.exp(total) * jnp.sum(edge_ref[...], axis=1, keepdims=True)
    decay_ref[...] = (
        dot(excess, triangle(length, lambda a, b: a >= b), 1, 0, HI)
        + dot(to_end * step * seen, triangle(length, lambda a, b: a < b), 1, 0, HI)
        + edge
    )


def term_kernel(places, n_columns, *refs):
    columns, pieces = refs[:n_columns], refs[n_columns:-3]
    keep_ref, send_ref, held = refs[-3:]
    pieces = [(p, i) for p in pieces for i in range(p.shape[0])]
    rows = 2 * keep_ref.shape[0]
    core, _, _ = core_and_chip()
    total = None
    for (a, start), (b, i) in zip(places, pieces):
        part = dot(columns[a][start : start + rows, :], b[i], 1, 0)
        total = part if total is None else total + part
    block = keep_ref.shape[0]
    held[0] = total[:block]
    held[1] = total[block:]
    keep_ref[...] = held[core]
    send_ref[...] = held[1 - core].astype(BF16)


def deal_kernel(keep_ref, recv_ref, own_ref, *refs):
    outs, held = refs[:-1], refs[-1]
    place, n_dp = lax.axis_index("dp"), lax.axis_size("dp")
    total = keep_ref[...] + recv_ref[...].astype(F32)
    share = own_ref.shape[0]
    for i in range(n_dp):
        held[i] = total[i * share : (i + 1) * share]
    own_ref[...] = held[place]
    for s, out in enumerate(outs):
        out[...] = held[place ^ (s + 1)].astype(BF16)


def sum_kernel(*refs):
    total = refs[0][...]
    for ref in refs[1:-1]:
        total = total + ref[...].astype(F32)
    refs[-1][...] = total


def expert_kernel(flip, slots, a_ref, b_ref, gate_ref, up_ref, out_ref, *scratch):
    rows_ref, gate_acc, up_acc = scratch
    step = pl.program_id(0)
    n_chip = a_ref.shape[0]

    @pl.when(step == 0)
    def _():
        for half, ref in enumerate((a_ref, b_ref)):
            for i in range(n_chip):
                row = (half * n_chip + i) * slots
                for t in range(rows_ref.shape[1] // LANES):
                    rows_ref[row : row + slots, t * LANES : (t + 1) * LANES] = ref[
                        i, t * slots : (t + 1) * slots, :
                    ]
        gate_acc[...] = jnp.zeros_like(gate_acc)
        up_acc[...] = jnp.zeros_like(up_acc)

    depth = gate_ref.shape[0]
    rows = rows_ref[:, rows_at(step, depth, LANES)]
    gate_acc[...] += dot(rows, gate_ref[...], 1, 0)
    up_acc[...] += dot(rows, up_ref[...], 1, 0)

    @pl.when(step == pl.num_programs(0) - 1)
    def _():
        weighted = jax.nn.silu(gate_acc[...]) * up_acc[...]
        out_ref[...] = (weighted.T if flip else weighted).astype(BF16)


def expert(a, b, w_gate, w_up, slots, flip, after):
    n_chip = a.shape[0]
    total = 2 * n_chip * slots
    width, hidden = w_gate.shape
    depth = 512
    out = (hidden, total) if flip else (total, hidden)

    def body(*refs):
        expert_kernel(flip, slots, *refs[:4], *refs[4 + len(after) :])

    whole = pl.BlockSpec(a.shape, lambda i: (0, 0, 0))
    block = pl.BlockSpec((depth, hidden), lambda i: (i, 0))
    return pl.pallas_call(
        body,
        out_shape=shape(out, BF16),
        grid=(width // depth,),
        in_specs=[whole, whole, block, block]
        + [pl.BlockSpec(memory_space=pl.ANY)] * len(after),
        out_specs=pl.BlockSpec(out, lambda i: (0, 0)),
        scratch_shapes=[
            pltpu.VMEM((total, width), BF16),
            pltpu.VMEM((total, hidden), F32),
            pltpu.VMEM((total, hidden), F32),
        ],
        cost_estimate=pl.CostEstimate(
            flops=int(1e9), bytes_accessed=1000, transcendentals=0
        ),
        compiler_params=pltpu.CompilerParams(vmem_limit_bytes=20 * 1024 * 1024),
    )(a, b, w_gate, w_up, *after)


def down_kernel(n_dp, flip, slots, grad_rows, *refs):
    pieces = refs[:n_dp]
    g_ref, out_ref, token_ref = refs[n_dp:]
    token_ref[...] = jnp.zeros_like(token_ref)
    n_chip = g_ref.shape[0]
    piece = out_ref.shape[1]
    total = None
    for s in range(n_dp):
        columns = []
        for t in range(grad_rows // slots):
            row = s * grad_rows + t * slots
            blocks = [
                g_ref[i, half + row : half + row + slots, :]
                for half in (0, n_dp * grad_rows)
                for i in range(n_chip)
            ]
            columns.append(jnp.concatenate(blocks, axis=0))
        right = jnp.concatenate(columns, axis=1)[:, :piece]
        part = dot(pieces[s][...], right, 1 if flip else 0, 0)
        total = part if total is None else total + part
    out_ref[...] = total.astype(BF16)


def xored(array, axis, mask):
    count = lax.axis_size(axis)
    return lax.ppermute(array, axis, [(i, i ^ mask) for i in range(count)])


def swapped(array):
    return xored(array, "tm", 1)


def chips(arrays):
    return [arrays[0]] + [xored(a, "tm", 2 * s) for s, a in enumerate(arrays) if s]


def gathered(array, axis, count):
    if count == 1:
        return [array]
    far = xored(array, axis, count // 2)
    return gathered(array, axis, count // 2) + gathered(far, axis, count // 2)


def per_device(
    layer_in,
    out_grad,
    w_bc,
    log_decay,
    step,
    saved_states,
    w_gate,
    w_up,
    slot_rows,
    slot_counts,
    slot_gates,
):
    n_dp = lax.axis_size("dp")
    core, chip, n_chip = core_and_chip()
    x = layer_in[0]
    dy = out_grad[0]
    length, width = x.shape
    heads = log_decay.shape[2]
    size = width // heads
    share, columns = w_bc.shape
    half = columns // 2
    ldt = log_decay[0].T
    stept = step[0].T
    h_in = saved_states[0, 0].reshape(width, half)
    capacity = slot_rows.shape[2]
    piece = width // n_dp
    part = width // 2
    many = heads // 2
    flip = w_gate.shape[2] % LANES == 0

    grad_rows = -(-piece // LANES) * capacity
    w_half = lax.dynamic_slice_in_dim(w_bc, core * (share // 2), share // 2, 0)

    in_rows = width // LANES * capacity
    blocks = [1, 1, 2] if n_chip == 4 else [1] * n_chip
    groups = [2, 2] if n_dp == 4 else [1] * n_dp
    cumt, cum, dyt, rows, *deals = call(
        lambda *refs: prep_kernel(len(groups), *refs),
        [
            shape((heads, length), F32),
            shape((length, LANES), F32),
            shape((width + up16(2 * heads), length), BF16),
            shape((in_rows, LANES), BF16),
        ]
        + [shape((k * grad_rows, LANES), BF16) for k in groups],
        1.5,
        (x, dy, ldt, stept, slot_rows[0], slot_counts, slot_gates[0]),
        scratch=[pltpu.VMEM((n_dp, grad_rows, LANES), BF16)],
        fetch=(0, 1, 2, 3),
        limit=60,
    )
    rows_in = chips([rows] * n_chip)
    w_far = xored(w_half, "dp", n_dp // 2)
    mine = gathered(w_half, "dp", n_dp // 2)[1:]
    w_copy = joined([w_far], after=(rows,))
    mine += gathered(w_copy, "dp", n_dp // 2)
    xs, carried, scaled, *xt = call(
        scale_kernel,
        [shape((length, width), BF16), shape((length, half), F32), shape((8, LANES), F32)]
        + [shape((k * width // n_chip, length), BF16) for k in blocks],
        1.5,
        (x, dy, h_in, cumt, cum),
        after=(rows,),
        scratch=[pltpu.VMEM((width, length), BF16)],
        fetch=(0, 1, 2, 3, 4),
        limit=60,
    )
    if n_dp == 4:
        one = (0, grad_rows), (grad_rows, 2 * grad_rows)
        over_2 = xored(deals[1], "dp", 2)
        early = (over_2,)
    else:
        early = ()
        source, spans = deals[:1] + [xored(d, "dp", s + 1) for s, d in enumerate(deals[1:])], None
    other = swapped(stacked(mine, after=(*rows_in[1:4], scaled), cost=1.0))
    w_whole, bc, keep, send = call(
        lambda *refs: project_kernel(n_dp - 1, many, *refs),
        [
            shape((width, columns), BF16),
            shape((length, columns), BF16),
            shape((part + up16(2 * many), half), BF16),
            shape((part + up16(2 * many), half), BF16),
        ],
        1.0,
        (x, dyt, w_bc, *mine, other),
    )
    recv = swapped(send)
    hidden = w_gate.shape[2]
    climbs = [
        call(
            lambda *refs: combine_kernel(many, size, *refs),
            [shape((part + up16(2 * many), half), BF16)],
            0.5,
            (keep, recv),
        )[0]
    ]
    rows_a = stacked(rows_in, after=(climbs[0],))
    rows_b = swapped(rows_a)
    weighted = expert(rows_a, rows_b, w_gate[0], w_up[0], capacity, flip, (climbs[0],))
    if n_chip == 4:
        x_rows = width // n_chip
        over_y = xored(xt[2], "tm", 4)

    parts = 2
    tiles = width // LANES // parts
    dxs, exs, owns = [], [], []
    if n_dp == 4:
        over_1 = xored(joined([deals[0], over_2], (weighted,), [one[1], one[1]]), "dp", 1)
        early += (over_1,)
        source, spans = [deals[0], over_1, over_2, over_1], [one[0], one[0], one[0], one[1]]
    held = (weighted, *early)
    arrived = []
    bit = 1
    while bit < n_chip:
        last = bit * 2 == n_chip
        moves = [(k, k ^ (2 * bit)) for k in range(2 * n_chip)]
        arrived.append(lax.ppermute(climbs[-1], "tm", moves))
        if not last:
            climbs.append(
                call(
                    lambda *refs, bit=bit: climb_kernel(many, size, bit, *refs),
                    [shape((part + up16(2 * many), half), BF16)],
                    0.5,
                    (climbs[-1], arrived[-1]),
                    after=held,
                )[0]
            )
        bit *= 2
    later = (climbs[-1],)
    mixed = jnp.zeros((length, length), F32)
    for i in range(parts):
        dx, mixed, ex, own = call(
            lambda *refs, i=i: intra_kernel(i * tiles, tiles, *refs),
            [
                shape((length, width // parts), F32),
                shape((length, length), F32),
                shape((heads // parts, length), F32),
                shape((heads // parts, length), F32),
            ],
            0.7,
            (x, dy, bc, cumt, cum, h_in, mixed),
            after=later,
            scratch=[pltpu.VMEM((heads, length), F32)],
        )
        dxs.append(dx)
        exs.append(ex)
        owns.append(own)
    db, dc = call(
        close_kernel,
        [shape((length, half), F32), shape((length, half), BF16)],
        0.3,
        (mixed, bc, carried),
    )

    held = (dc,)
    dealt = joined(source, later, spans)
    dealt_all = joined([dealt, swapped(dealt)])
    held += (dealt_all,)
    if n_chip == 4:
        over_x = xored(joined([xt[1], over_y], later, [(0, x_rows), (x_rows, 2 * x_rows)]), "tm", 2)
        columns_in = [xt[0], over_x, over_y]
        places = [(0, 0), (1, 0), (2, 0), (1, x_rows)]
        held += (over_x,)
    else:
        columns_in = chips(xt)
        places = [(i, 0) for i in range(n_chip)]
    far = xored(weighted, "dp", n_dp // 2)
    near = gathered(weighted, "dp", n_dp // 2)
    held += (far, *near[1:])
    r_own, r_send = call(
        lambda *refs: carry_kernel(many, size, len(arrived), *refs),
        [shape((part, half), BF16)] * 2,
        0.5,
        (*arrived, keep, recv),
        after=held,
    )
    r_recv = swapped(r_send)
    fars = gathered(joined([far], (r_own,)), "dp", n_dp // 2)
    d_bc = call(db_kernel, [shape((length, columns), BF16)], 0.3, (xs, r_own, r_recv, db, dc))[0]
    d_bcs = [d_bc.reshape(1, length, columns)]
    if n_chip == 4:
        grads_y = xored(dealt_all, "tm", 4)
    while 2 ** (len(d_bcs) - 1) < n_chip:
        level = 2 ** (len(d_bcs) - 1)
        sent = d_bcs[0] if level == 1 else joined(d_bcs)
        d_bcs.append(xored(sent, "tm", 2 * level))
    both = ()
    if n_chip == 4:
        both = (joined([dealt_all, grads_y], (sent,)),)
        grads_x = xored(both[0], "tm", 2)
        rest = dealt_all.shape[0]
        grads = [dealt_all, grads_x, grads_y, grads_x]
        spans = [(0, rest), (0, rest), (0, rest), (rest, 2 * rest)]
    else:
        grads, spans = chips([dealt_all] * n_chip), None
    d_in, d_decay, d_step, token = call(
        lambda *refs: finish_kernel(parts, *refs),
        [
            shape((length, width), BF16),
            shape((heads, length), F32),
            shape((heads, length), F32),
            shape((8, LANES), F32),
        ],
        1.0,
        (x, bc, cumt, stept, cum, h_in, r_own, r_recv, w_whole, d_bc,
         *dxs, *exs, *owns),
        after=(*fars[1:], *both),
        scratch=[pltpu.VMEM((width, half), BF16), pltpu.VMEM((heads, half), F32)],
    )
    w_rows = width // (2 * n_chip)
    term, term_send = call(
        lambda *refs: term_kernel(places, len(columns_in), *refs),
        [shape((w_rows, columns), F32), shape((w_rows, columns), BF16)],
        0.5,
        (*columns_in, *d_bcs),
        after=(token,),
        scratch=[pltpu.VMEM((2, w_rows, columns), F32)],
    )
    final = call(
        deal_kernel,
        [shape((w_rows // n_dp, columns), F32)]
        + [shape((w_rows // n_dp, columns), BF16)] * (n_dp - 1),
        0.3,
        (term, swapped(term_send)),
        scratch=[pltpu.VMEM((n_dp, w_rows // n_dp, columns), F32)],
    )
    final = list(final[:1]) + [xored(f, "dp", s + 1) for s, f in enumerate(final[1:])]

    grads = stacked(grads, (term,), spans)
    w_down_grad, done = call(
        lambda *refs: down_kernel(n_dp, flip, capacity, grad_rows, *refs),
        [shape((hidden, piece), BF16), shape((8, LANES), F32)],
        1.0,
        (*near, *fars, grads),
        after=(final[0],),
    )
    w_bc_grad = call(sum_kernel, [shape(final[0].shape, F32)], 0.1, final, (done,))[0]
    return (d_in[None], d_decay.T[None], d_step.T[None], w_bc_grad, w_down_grad[None])


def solution(mesh):
    in_specs = (
        P("dp", "tm", None),
        P("dp", "tm", None),
        P("dp", None),
        P("dp", "tm", None),
        P("dp", "tm", None),
        P("dp", "tm", None, None, None),
        P(None, None, "tm"),
        P(None, None, "tm"),
        P("dp", None, "tm"),
        P("dp", "tm"),
        P("dp", None, "tm"),
    )
    out_specs = (
        P("dp", "tm", None),
        P("dp", "tm", None),
        P("dp", "tm", None),
        P(("tm", "dp"), None),
        P(None, "tm", "dp"),
    )
    return jax.shard_map(
        per_device, mesh=mesh, in_specs=in_specs, out_specs=out_specs, check_vma=False
    )
```

```python
import jax
import jax.numpy as jnp
from jax import lax
from jax.experimental import pallas as pl
from jax.experimental.pallas import tpu as pltpu
from jax.sharding import PartitionSpec as P

HI = lax.Precision.HIGHEST
F32 = jnp.float32
BF16 = jnp.bfloat16
LANES = 128


def dot(a, b, ca, cb, precision=None):
    return lax.dot_general(
        a, b, (((ca,), (cb,)), ((), ())), precision=precision, preferred_element_type=F32
    )


def iota(dims, axis):
    return lax.broadcasted_iota(jnp.int32, dims, axis)


def where_one(mask):
    return jnp.where(mask, 1.0, 0.0)


def triangle(n, keep):
    return where_one(keep(iota((n, n), 0), iota((n, n), 1))).astype(F32)


def halves(values, axis=1):
    high = values.astype(BF16)
    low = (values - high.astype(F32)).astype(BF16)
    return jnp.concatenate([high, low], axis=axis)


def to_lanes(j, size):
    dims = (LANES, LANES)
    one = where_one(iota(dims, 0) == iota(dims, 1) // size + j * (LANES // size)).astype(BF16)
    return jnp.concatenate([one, one], axis=0)


def to_heads(j, heads, size):
    dims = (heads, LANES)
    one = where_one(iota(dims, 0) == iota(dims, 1) // size + j * (LANES // size)).astype(BF16)
    return jnp.concatenate([one, one], axis=1)


def up16(n):
    return -(-n // 16) * 16


def call(kernel, outs, cost, args, after=(), scratch=(), limit=14, fetch=()):
    n_in, n_after, n_out = len(args), len(after), len(outs)
    fetch = tuple(fetch)

    def body(*refs):
        ins = list(refs[:n_in])
        rest = refs[n_in + n_after :]
        if fetch:
            sems = rest[-1]
            held = rest[len(rest) - 1 - len(fetch) : -1]
            rest = rest[: len(rest) - 1 - len(fetch)]
            copies = []
            for i, (index, ref) in enumerate(zip(fetch, held)):
                copies.append(pltpu.make_async_copy(ins[index], ref, sems.at[i]))
                ins[index] = ref
            for copy in copies:
                copy.start()
            for copy in copies:
                copy.wait()
        kernel(*ins, *rest)

    specs = [
        pl.BlockSpec(memory_space=pltpu.HBM if i in fetch else pltpu.VMEM) for i in range(n_in)
    ]
    held = [pltpu.VMEM(args[i].shape, args[i].dtype) for i in fetch]
    if fetch:
        held.append(pltpu.SemaphoreType.DMA((len(fetch),)))
    return pl.pallas_call(
        body,
        out_shape=outs,
        in_specs=specs + [pl.BlockSpec(memory_space=pl.ANY)] * n_after,
        out_specs=[pl.BlockSpec(memory_space=pltpu.VMEM)] * n_out,
        scratch_shapes=list(scratch) + held,
        cost_estimate=pl.CostEstimate(
            flops=int(cost * 3e9), bytes_accessed=1000, transcendentals=0
        ),
        compiler_params=pltpu.CompilerParams(vmem_limit_bytes=limit * 1024 * 1024),
    )(*args, *after)


def shape(dims, kind):
    return jax.ShapeDtypeStruct(dims, kind)


def core_and_chip():
    place = lax.axis_index("tm")
    return lax.rem(place, 2), lax.div(place, 2), lax.axis_size("tm") // 2


def rows_at(index, size, align=16):
    return pl.ds(pl.multiple_of(index * size, align), size)


def picked(x_ref, dy_ref, slot_ref, count_ref, gate_ref, rows_ref, out_refs):
    length, width = x_ref.shape
    slots = slot_ref.shape[1]
    hit = iota((length, slots), 0) == slot_ref[...]
    live = iota((1, slots), 1) < count_ref[...]
    weight = jnp.where(live, gate_ref[...].astype(F32), 0.0)
    rows = dot(where_one(hit).astype(BF16), x_ref[...], 0, 0).astype(BF16)
    for t in range(width // LANES):
        rows_ref[t * slots : (t + 1) * slots, :] = rows[:, t * LANES : (t + 1) * LANES]
    grads = dot(jnp.where(hit, weight, 0.0).astype(BF16), dy_ref[...], 0, 0).astype(BF16)
    held = out_refs[-1]
    n_dp = held.shape[0]
    piece = width // n_dp
    for i in range(n_dp):
        for t, low in enumerate(range(i * piece, (i + 1) * piece, LANES)):
            block = grads[:, low : min(low + LANES, (i + 1) * piece)]
            if block.shape[1] < LANES:
                fill = jnp.zeros((slots, LANES - block.shape[1]), BF16)
                block = jnp.concatenate([block, fill], axis=1)
            held[i, t * slots : (t + 1) * slots, :] = block
    place = lax.axis_index("dp")
    s = 0
    for out in out_refs[:-1]:
        for start in range(0, out.shape[0], held.shape[1]):
            out[start : start + held.shape[1], :] = held[place ^ s]
            s += 1


def high_low(values):
    high = values.astype(BF16).astype(F32)
    return [high, values - high]


def prep_kernel(
    n_deals, x_ref, dy_ref, ldt_ref, stept_ref, slot_ref, count_ref, gate_ref,
    cumt_ref, cum_ref, dyt_ref, rows_ref, *rest,
):
    length, width = x_ref.shape
    heads = ldt_ref.shape[0]
    size = width // heads
    picked(x_ref, dy_ref, slot_ref, count_ref, gate_ref, rows_ref, rest)
    cumt = dot(ldt_ref[...], triangle(length, lambda a, b: a <= b), 1, 0, HI)
    cumt_ref[...] = cumt
    pad = jnp.zeros((LANES - heads, length), F32)
    cum_ref[...] = jnp.concatenate([cumt - jnp.log(stept_ref[...]), pad], axis=0).T
    start = jnp.exp(jnp.concatenate([cumt, pad], axis=0).T)
    table = halves(start)
    for j in range(width // LANES):
        span = slice(j * LANES, (j + 1) * LANES)
        dys = dy_ref[:, span].astype(F32) * dot(table, to_lanes(j, size), 1, 0)
        dyt_ref[span, :] = dys.T.astype(BF16)
    decay = jnp.broadcast_to(jnp.exp(cumt[:, length - 1 : length]), (heads, LANES))
    dyt_ref[width : width + 2 * heads, :] = jnp.concatenate(high_low(decay), axis=0).astype(BF16)


def scale_kernel(x_ref, dy_ref, h_ref, cumt_ref, cum_ref, xs_ref, carried_ref, token_ref, *rest):
    outs, xt_ref = rest[:-1], rest[-1]
    length, width = x_ref.shape
    heads = cumt_ref.shape[0]
    size = width // heads
    _, chip, n_chip = core_and_chip()
    pad = jnp.zeros((LANES - heads, length), F32)
    cum = jnp.concatenate([cumt_ref[...], pad], axis=0).T
    into_end = jnp.exp(cum[length - 1 : length] - cum_ref[...])
    table = jnp.concatenate([halves(jnp.exp(cum)), halves(into_end)], axis=0)
    carried = jnp.zeros(carried_ref.shape, F32)
    for j in range(width // LANES):
        span = slice(j * LANES, (j + 1) * LANES)
        scale = dot(table, to_lanes(j, size), 1, 0)
        x_f = x_ref[:, span].astype(F32)
        xt_ref[span, :] = x_f.T.astype(BF16)
        xs_ref[:, span] = (x_f * scale[length:]).astype(BF16)
        dys = (dy_ref[:, span].astype(F32) * scale[:length]).astype(BF16)
        carried = carried + dot(dys, h_ref[span, :], 1, 0)
    carried_ref[...] = carried
    token_ref[...] = jnp.zeros_like(token_ref)
    block = width // n_chip
    s = 0
    for out in outs:
        for start in range(0, out.shape[0], block):
            out[start : start + block, :] = xt_ref[rows_at(chip ^ s, block), :]
            s += 1


def join_kernel(ranges, *refs):
    out, at = refs[-1], 0
    for ref, (start, stop) in zip(refs, ranges):
        out[at : at + stop - start] = ref[start:stop]
        at += stop - start


def joined(arrays, after=(), ranges=None, cost=0.2):
    ranges = ranges or [(0, a.shape[0]) for a in arrays]
    dims = (sum(stop - start for start, stop in ranges), *arrays[0].shape[1:])
    return call(
        lambda *refs: join_kernel(ranges, *refs),
        [shape(dims, arrays[0].dtype)],
        cost,
        tuple(arrays),
        after=after,
    )[0]


def stacked(arrays, after=(), ranges=None, cost=0.2):
    count = len(arrays)
    out = joined(arrays, after, ranges, cost)
    return out.reshape(count, out.shape[0] // count, *out.shape[1:])


def project_kernel(n_mine, many, *refs):
    x_ref, dyt_ref, own_ref = refs[:3]
    mine, other = refs[3 : 3 + n_mine], refs[3 + n_mine]
    w_ref, bc_ref, keep_ref, send_ref = refs[4 + n_mine :]
    core, _, _ = core_and_chip()
    place, n_dp = lax.axis_index("dp"), lax.axis_size("dp")
    share = own_ref.shape[0]
    half = share // 2
    w_ref[rows_at(place, share), :] = own_ref[...]
    for i in range(n_mine):
        source = place ^ (i + 1)
        w_ref[rows_at(source * 2 + core, half), :] = mine[i][...]
        w_ref[rows_at(source * 2 + 1 - core, half), :] = other[i]
    bc = dot(x_ref[...], w_ref[...], 1, 0).astype(BF16)
    bc_ref[...] = bc
    c_rows = bc[:, LANES:]
    width = x_ref.shape[1]
    part = width // 2
    for ref, index in ((keep_ref, core), (send_ref, 1 - core)):
        ref[:part, :] = dot(dyt_ref[rows_at(index, part), :], c_rows, 1, 0).astype(BF16)
        table = dyt_ref[width : width + 4 * many, :].astype(F32)
        quarter = [table[i * many : (i + 1) * many] for i in range(4)]
        high = jnp.where(index == 0, quarter[0], quarter[1])
        low = jnp.where(index == 0, quarter[2], quarter[3])
        fill = jnp.zeros((ref.shape[0] - part - 2 * many, LANES), F32)
        ref[part:, :] = jnp.concatenate([high, low, fill], axis=0).astype(BF16)


def pair(keep_ref, recv_ref, many, size, head):
    core, _, _ = core_and_chip()
    part = many * size
    both = []
    for ref in (keep_ref, recv_ref):
        extra = ref[part:, :].astype(F32)
        decay = extra[head : head + 1] + extra[many + head : many + head + 1]
        both.append((ref[head * size : (head + 1) * size, :].astype(F32), decay))
    first = jax.tree.map(lambda a, b: jnp.where(core == 0, a, b), both[0], both[1])
    second = jax.tree.map(lambda a, b: jnp.where(core == 0, b, a), both[0], both[1])
    return first, second


def payload(ref, many, states, decays):
    size = states[0].shape[0]
    for head, state in enumerate(states):
        ref[head * size : (head + 1) * size, :] = state.astype(BF16)
    decay = jnp.concatenate(decays, axis=0)
    high = decay.astype(BF16).astype(F32)
    fill = jnp.zeros((ref.shape[0] - many * size - 2 * many, LANES), F32)
    extra = jnp.concatenate([high, decay - high, fill], axis=0)
    ref[many * size :, :] = extra.astype(BF16)


def loaded(ref, many, size, head):
    extra = ref[many * size :, :].astype(F32)
    decay = extra[head : head + 1] + extra[many + head : many + head + 1]
    return ref[head * size : (head + 1) * size, :].astype(F32), decay


def combine_kernel(many, size, keep_ref, recv_ref, out_ref):
    states, decays = [], []
    for head in range(many):
        (g0, a0), (g1, a1) = pair(keep_ref, recv_ref, many, size, head)
        states.append(g0 + a0 * g1)
        decays.append(a0 * a1)
    payload(out_ref, many, states, decays)


def pick_side(upper, mine, theirs):
    return jnp.where(upper, theirs, mine), jnp.where(upper, mine, theirs)


def climb_kernel(many, size, bit, mine_ref, recv_ref, out_ref):
    _, chip, _ = core_and_chip()
    upper = lax.rem(lax.div(chip, bit), 2) == 1
    states, decays = [], []
    for head in range(many):
        t_mine, a_mine = loaded(mine_ref, many, size, head)
        t_recv, a_recv = loaded(recv_ref, many, size, head)
        t_low, t_high = pick_side(upper, t_mine, t_recv)
        a_low, a_high = pick_side(upper, a_mine, a_recv)
        states.append(t_low + a_low * t_high)
        decays.append(a_low * a_high)
    payload(out_ref, many, states, decays)


def carry_kernel(many, size, levels, *refs):
    core, chip, _ = core_and_chip()
    recvs = refs[:levels]
    keep_ref, recv_ref, own_ref, send_ref = refs[levels:]
    for head in range(many):
        span = slice(head * size, (head + 1) * size)
        carry, reach = None, None
        for level, ref in enumerate(recvs):
            state, decay = loaded(ref, many, size, head)
            lower = lax.rem(lax.div(chip, 2**level), 2) == 0
            state = jnp.where(lower, state, 0.0)
            decay = jnp.where(lower, decay, 1.0)
            carry = state if carry is None else carry + reach * state
            reach = decay if reach is None else reach * decay
        _, (g1, a1) = pair(keep_ref, recv_ref, many, size, head)
        second = carry
        first = g1 + a1 * second
        own_ref[span, :] = jnp.where(core == 0, first, second).astype(BF16)
        send_ref[span, :] = jnp.where(core == 0, second, first).astype(BF16)


def intra_kernel(
    first, many, x_ref, dy_ref, bc_ref, cumt_ref, cum_ref, h_ref, before_ref,
    dx_ref, mixed_ref, ex_ref, own_ref, rowm_ref,
):
    length, width = x_ref.shape
    heads = cumt_ref.shape[0]
    size = width // heads
    per = LANES // size
    upper = iota((length, length), 0) <= iota((length, length), 1)
    b_rows, c_rows = bc_ref[:, :LANES], bc_ref[:, LANES:]
    scores = dot(b_rows, c_rows, 1, 1)
    lane = iota((1, LANES), 1)
    lane_bf = [where_one(lane // size == i).astype(BF16) for i in range(per)]
    mixed = before_ref[...]
    own = jnp.zeros((length, LANES), F32)
    reach = jnp.zeros((heads, length), F32)
    for j in range(first, first + many):
        span = slice(j * LANES, (j + 1) * LANES)
        out_span = slice((j - first) * LANES, (j - first + 1) * LANES)
        x_p = x_ref[:, span]
        dy_p = dy_ref[:, span]
        dy_h = jnp.concatenate([dy_p * m for m in lane_bf], axis=0)
        cross = dot(x_p, dy_h, 1, 1)
        kern = []
        for i in range(per):
            h = j * per + i
            diff = cumt_ref[h : h + 1, :] - cum_ref[:, h : h + 1]
            seg = jnp.exp(jnp.where(upper, diff, -1e30))
            part = cross[:, i * length : (i + 1) * length]
            mixed = mixed + seg * part
            seg = seg * scores
            kern.append(seg.astype(BF16))
            full = seg * part
            rowm_ref[h : h + 1, :] = jnp.sum(full, axis=0, keepdims=True)
            own = jnp.where(lane == h, jnp.sum(full, axis=1, keepdims=True), own)
        dx_ref[:, out_span] = dot(jnp.concatenate(kern, axis=1), dy_h, 1, 0)
        seen = dy_p.astype(F32) * dot(c_rows, h_ref[span, :], 1, 1)
        reach = reach + dot(to_heads(j, heads, size), halves(seen), 1, 1)
    mixed_ref[...] = mixed
    rows = slice(first * per, (first + many) * per)
    own = own.T[rows]
    own_ref[...] = own
    ex_ref[...] = rowm_ref[rows, :] + jnp.exp(cumt_ref[rows, :]) * reach[rows] - own


def close_kernel(mixed_ref, bc_ref, carried_ref, db_ref, dc_ref):
    mixed = mixed_ref[...].astype(BF16)
    db_ref[...] = dot(mixed, bc_ref[:, LANES:], 1, 0)
    dc_ref[...] = (dot(mixed, bc_ref[:, :LANES], 0, 0) + carried_ref[...]).astype(BF16)


def db_kernel(xs_ref, own_ref, recv_ref, db_ref, dc_ref, out_ref):
    core, _, _ = core_and_chip()
    half = db_ref.shape[1]
    part = own_ref.shape[0]
    total = db_ref[...]
    for ref, index in ((own_ref, core), (recv_ref, 1 - core)):
        total = total + dot(xs_ref[:, rows_at(index, part, LANES)], ref[...], 1, 0)
    out_ref[:, :half] = total.astype(BF16)
    out_ref[:, half:] = dc_ref[...]


def finish_kernel(parts, *refs):
    (x_ref, bc_ref, cumt_ref, stept_ref, cum_ref, h_ref, own_ref, recv_ref,
     w_ref, dbc_ref) = refs[:10]
    dx_refs, ex_refs, st_refs = (refs[10 + i * parts : 10 + (i + 1) * parts] for i in range(3))
    in_ref, decay_ref, grad_ref, token_ref, r_ref, edge_ref = refs[10 + 3 * parts :]
    token_ref[...] = jnp.zeros_like(token_ref)
    core, _, _ = core_and_chip()
    length, width = x_ref.shape
    heads = cumt_ref.shape[0]
    size = width // heads
    part = width // 2
    r_ref[rows_at(core, part), :] = own_ref[...]
    r_ref[rows_at(1 - core, part), :] = recv_ref[...]
    pad = jnp.zeros((LANES - heads, length), F32)
    total = jnp.concatenate([cumt_ref[...], pad], axis=0).T[length - 1 : length]
    table = halves(jnp.exp(total - cum_ref[...]))
    seen = jnp.zeros((heads, length), F32)
    b_rows = bc_ref[:, :LANES]
    d_bc = dbc_ref[...]
    for j in range(width // LANES):
        span = slice(j * LANES, (j + 1) * LANES)
        local = dx_refs[j * LANES // (width // parts)]
        start = j * LANES % (width // parts)
        r_tile = r_ref[span, :]
        reach = dot(b_rows, r_tile, 1, 1)
        d_in = local[:, start : start + LANES] + dot(table, to_lanes(j, size), 1, 0) * reach
        d_in = d_in + dot(d_bc, w_ref[span, :], 1, 1)
        in_ref[:, span] = d_in.astype(BF16)
        product = x_ref[:, span].astype(F32) * reach
        seen = seen + dot(to_heads(j, heads, size), halves(product), 1, 1)
        edge = r_tile.astype(F32) * h_ref[span, :].astype(F32)
        for i in range(LANES // size):
            h = j * (LANES // size) + i
            edge_ref[h : h + 1, :] = jnp.sum(
                edge[i * size : (i + 1) * size], axis=0, keepdims=True
            )
    cumt = cumt_ref[...]
    total = cumt[:, length - 1 : length]
    to_end = jnp.exp(total - cumt)
    step = stept_ref[...]
    own = jnp.concatenate([r[...] for r in st_refs], axis=0)
    excess = jnp.concatenate([r[...] for r in ex_refs], axis=0)
    grad_ref[...] = own / step + to_end * seen
    edge = jnp.exp(total) * jnp.sum(edge_ref[...], axis=1, keepdims=True)
    decay_ref[...] = (
        dot(excess, triangle(length, lambda a, b: a >= b), 1, 0, HI)
        + dot(to_end * step * seen, triangle(length, lambda a, b: a < b), 1, 0, HI)
        + edge
    )


def term_kernel(places, n_columns, *refs):
    columns, pieces = refs[:n_columns], refs[n_columns:-3]
    keep_ref, send_ref, held = refs[-3:]
    pieces = [(p, i) for p in pieces for i in range(p.shape[0])]
    rows = 2 * keep_ref.shape[0]
    core, _, _ = core_and_chip()
    total = None
    for (a, start), (b, i) in zip(places, pieces):
        part = dot(columns[a][start : start + rows, :], b[i], 1, 0)
        total = part if total is None else total + part
    block = keep_ref.shape[0]
    held[0] = total[:block]
    held[1] = total[block:]
    keep_ref[...] = held[core]
    send_ref[...] = held[1 - core].astype(BF16)


def deal_kernel(keep_ref, recv_ref, own_ref, *refs):
    outs, held = refs[:-1], refs[-1]
    place, n_dp = lax.axis_index("dp"), lax.axis_size("dp")
    total = keep_ref[...] + recv_ref[...].astype(F32)
    share = own_ref.shape[0]
    for i in range(n_dp):
        held[i] = total[i * share : (i + 1) * share]
    own_ref[...] = held[place]
    for s, out in enumerate(outs):
        out[...] = held[place ^ (s + 1)].astype(BF16)


def sum_kernel(*refs):
    total = refs[0][...]
    for ref in refs[1:-1]:
        total = total + ref[...].astype(F32)
    refs[-1][...] = total


def expert_kernel(flip, slots, a_ref, b_ref, gate_ref, up_ref, out_ref, *scratch):
    rows_ref, gate_acc, up_acc = scratch
    step = pl.program_id(0)
    n_chip = a_ref.shape[0]

    @pl.when(step == 0)
    def _():
        for half, ref in enumerate((a_ref, b_ref)):
            for i in range(n_chip):
                row = (half * n_chip + i) * slots
                for t in range(rows_ref.shape[1] // LANES):
                    rows_ref[row : row + slots, t * LANES : (t + 1) * LANES] = ref[
                        i, t * slots : (t + 1) * slots, :
                    ]
        gate_acc[...] = jnp.zeros_like(gate_acc)
        up_acc[...] = jnp.zeros_like(up_acc)

    depth = gate_ref.shape[0]
    rows = rows_ref[:, rows_at(step, depth, LANES)]
    gate_acc[...] += dot(rows, gate_ref[...], 1, 0)
    up_acc[...] += dot(rows, up_ref[...], 1, 0)

    @pl.when(step == pl.num_programs(0) - 1)
    def _():
        weighted = jax.nn.silu(gate_acc[...]) * up_acc[...]
        out_ref[...] = (weighted.T if flip else weighted).astype(BF16)


def expert(a, b, w_gate, w_up, slots, flip, after):
    n_chip = a.shape[0]
    total = 2 * n_chip * slots
    width, hidden = w_gate.shape
    depth = 512
    out = (hidden, total) if flip else (total, hidden)

    def body(*refs):
        expert_kernel(flip, slots, *refs[:4], *refs[4 + len(after) :])

    whole = pl.BlockSpec(a.shape, lambda i: (0, 0, 0))
    block = pl.BlockSpec((depth, hidden), lambda i: (i, 0))
    return pl.pallas_call(
        body,
        out_shape=shape(out, BF16),
        grid=(width // depth,),
        in_specs=[whole, whole, block, block]
        + [pl.BlockSpec(memory_space=pl.ANY)] * len(after),
        out_specs=pl.BlockSpec(out, lambda i: (0, 0)),
        scratch_shapes=[
            pltpu.VMEM((total, width), BF16),
            pltpu.VMEM((total, hidden), F32),
            pltpu.VMEM((total, hidden), F32),
        ],
        cost_estimate=pl.CostEstimate(
            flops=int(1e9), bytes_accessed=1000, transcendentals=0
        ),
        compiler_params=pltpu.CompilerParams(vmem_limit_bytes=20 * 1024 * 1024),
    )(a, b, w_gate, w_up, *after)


def down_kernel(n_dp, flip, slots, grad_rows, *refs):
    pieces = refs[:n_dp]
    g_ref, out_ref, token_ref = refs[n_dp:]
    token_ref[...] = jnp.zeros_like(token_ref)
    n_chip = g_ref.shape[0]
    piece = out_ref.shape[1]
    total = None
    for s in range(n_dp):
        columns = []
        for t in range(grad_rows // slots):
            row = s * grad_rows + t * slots
            blocks = [
                g_ref[i, half + row : half + row + slots, :]
                for half in (0, n_dp * grad_rows)
                for i in range(n_chip)
            ]
            columns.append(jnp.concatenate(blocks, axis=0))
        right = jnp.concatenate(columns, axis=1)[:, :piece]
        part = dot(pieces[s][...], right, 1 if flip else 0, 0)
        total = part if total is None else total + part
    out_ref[...] = total.astype(BF16)


def xored(array, axis, mask):
    count = lax.axis_size(axis)
    return lax.ppermute(array, axis, [(i, i ^ mask) for i in range(count)])


def swapped(array):
    return xored(array, "tm", 1)


def chips(arrays):
    return [arrays[0]] + [xored(a, "tm", 2 * s) for s, a in enumerate(arrays) if s]


def gathered(array, axis, count):
    if count == 1:
        return [array]
    far = xored(array, axis, count // 2)
    return gathered(array, axis, count // 2) + gathered(far, axis, count // 2)


def per_device(
    layer_in,
    out_grad,
    w_bc,
    log_decay,
    step,
    saved_states,
    w_gate,
    w_up,
    slot_rows,
    slot_counts,
    slot_gates,
):
    n_dp = lax.axis_size("dp")
    core, chip, n_chip = core_and_chip()
    x = layer_in[0]
    dy = out_grad[0]
    length, width = x.shape
    heads = log_decay.shape[2]
    size = width // heads
    share, columns = w_bc.shape
    half = columns // 2
    ldt = log_decay[0].T
    stept = step[0].T
    h_in = saved_states[0, 0].reshape(width, half)
    capacity = slot_rows.shape[2]
    piece = width // n_dp
    part = width // 2
    many = heads // 2
    flip = w_gate.shape[2] % LANES == 0

    grad_rows = -(-piece // LANES) * capacity
    w_half = lax.dynamic_slice_in_dim(w_bc, core * (share // 2), share // 2, 0)

    in_rows = width // LANES * capacity
    blocks = [1, 1, 2] if n_chip == 4 else [1] * n_chip
    groups = [2, 2] if n_dp == 4 else [1] * n_dp
    cumt, cum, dyt, rows, *deals = call(
        lambda *refs: prep_kernel(len(groups), *refs),
        [
            shape((heads, length), F32),
            shape((length, LANES), F32),
            shape((width + up16(2 * heads), length), BF16),
            shape((in_rows, LANES), BF16),
        ]
        + [shape((k * grad_rows, LANES), BF16) for k in groups],
        1.5,
        (x, dy, ldt, stept, slot_rows[0], slot_counts, slot_gates[0]),
        scratch=[pltpu.VMEM((n_dp, grad_rows, LANES), BF16)],
        fetch=(0, 1, 2, 3),
        limit=60,
    )
    w_far = xored(w_half, "dp", n_dp // 2)
    mine = gathered(w_half, "dp", n_dp // 2)[1:]
    w_copy = joined([w_far], after=(rows,))
    mine += gathered(w_copy, "dp", n_dp // 2)
    rows_in = [rows]
    while 2 ** (len(rows_in) - 1) < n_chip:
        rows_sent = joined(rows_in, (w_copy,)) if rows_in[1:] else rows
        rows_in.append(xored(rows_sent, "tm", 2 ** len(rows_in)))
    xs, carried, scaled, *xt = call(
        scale_kernel,
        [shape((length, width), BF16), shape((length, half), F32), shape((8, LANES), F32)]
        + [shape((k * width // n_chip, length), BF16) for k in blocks],
        1.5,
        (x, dy, h_in, cumt, cum),
        after=(rows,),
        scratch=[pltpu.VMEM((width, length), BF16)],
        fetch=(0, 1, 2, 3, 4),
        limit=60,
    )
    if n_dp == 4:
        one = (0, grad_rows), (grad_rows, 2 * grad_rows)
        over_2 = xored(deals[1], "dp", 2)
        early = (over_2,)
    else:
        early = ()
        source, spans = deals[:1] + [xored(d, "dp", s + 1) for s, d in enumerate(deals[1:])], None
    other = swapped(stacked(mine, after=(rows_in[-1], scaled), cost=1.0))
    w_whole, bc, keep, send = call(
        lambda *refs: project_kernel(n_dp - 1, many, *refs),
        [
            shape((width, columns), BF16),
            shape((length, columns), BF16),
            shape((part + up16(2 * many), half), BF16),
            shape((part + up16(2 * many), half), BF16),
        ],
        1.0,
        (x, dyt, w_bc, *mine, other),
    )
    recv = swapped(send)
    hidden = w_gate.shape[2]
    climbs = [
        call(
            lambda *refs: combine_kernel(many, size, *refs),
            [shape((part + up16(2 * many), half), BF16)],
            0.5,
            (keep, recv),
        )[0]
    ]
    rows_a = joined(rows_in, (climbs[0],)).reshape(n_chip, in_rows, LANES)
    rows_b = swapped(rows_a)
    weighted = expert(rows_a, rows_b, w_gate[0], w_up[0], capacity, flip, (climbs[0],))
    if n_chip == 4:
        x_rows = width // n_chip
        over_y = xored(xt[2], "tm", 4)

    parts = 2
    tiles = width // LANES // parts
    dxs, exs, owns = [], [], []
    if n_dp == 4:
        over_1 = xored(joined([deals[0], over_2], (weighted,), [one[1], one[1]]), "dp", 1)
        early += (over_1,)
        source, spans = [deals[0], over_1, over_2, over_1], [one[0], one[0], one[0], one[1]]
    held = (weighted, *early)
    arrived = []
    bit = 1
    while bit < n_chip:
        last = bit * 2 == n_chip
        moves = [(k, k ^ (2 * bit)) for k in range(2 * n_chip)]
        arrived.append(lax.ppermute(climbs[-1], "tm", moves))
        if not last:
            climbs.append(
                call(
                    lambda *refs, bit=bit: climb_kernel(many, size, bit, *refs),
                    [shape((part + up16(2 * many), half), BF16)],
                    0.5,
                    (climbs[-1], arrived[-1]),
                    after=held,
                )[0]
            )
        bit *= 2
    later = (climbs[-1],)
    mixed = jnp.zeros((length, length), F32)
    for i in range(parts):
        dx, mixed, ex, own = call(
            lambda *refs, i=i: intra_kernel(i * tiles, tiles, *refs),
            [
                shape((length, width // parts), F32),
                shape((length, length), F32),
                shape((heads // parts, length), F32),
                shape((heads // parts, length), F32),
            ],
            0.7,
            (x, dy, bc, cumt, cum, h_in, mixed),
            after=later,
            scratch=[pltpu.VMEM((heads, length), F32)],
        )
        dxs.append(dx)
        exs.append(ex)
        owns.append(own)
    db, dc = call(
        close_kernel,
        [shape((length, half), F32), shape((length, half), BF16)],
        0.3,
        (mixed, bc, carried),
    )

    held = (dc,)
    dealt = joined(source, later, spans)
    dealt_all = joined([dealt, swapped(dealt)])
    held += (dealt_all,)
    if n_chip == 4:
        over_x = xored(joined([xt[1], over_y], later, [(0, x_rows), (x_rows, 2 * x_rows)]), "tm", 2)
        columns_in = [xt[0], over_x, over_y]
        places = [(0, 0), (1, 0), (2, 0), (1, x_rows)]
        held += (over_x,)
    else:
        columns_in = chips(xt)
        places = [(i, 0) for i in range(n_chip)]
    far = xored(weighted, "dp", n_dp // 2)
    near = gathered(weighted, "dp", n_dp // 2)
    held += (far, *near[1:])
    r_own, r_send = call(
        lambda *refs: carry_kernel(many, size, len(arrived), *refs),
        [shape((part, half), BF16)] * 2,
        0.5,
        (*arrived, keep, recv),
        after=held,
    )
    r_recv = swapped(r_send)
    d_bc = call(db_kernel, [shape((length, columns), BF16)], 0.3, (xs, r_own, r_recv, db, dc))[0]
    fars = gathered(joined([far], (d_bc,)), "dp", n_dp // 2)
    d_bcs = [d_bc.reshape(1, length, columns)]
    if n_chip == 4:
        grads_y = xored(dealt_all, "tm", 4)
    while 2 ** (len(d_bcs) - 1) < n_chip:
        level = 2 ** (len(d_bcs) - 1)
        sent = d_bcs[0] if level == 1 else joined(d_bcs)
        d_bcs.append(xored(sent, "tm", 2 * level))
    both = ()
    if n_chip == 4:
        both = (joined([dealt_all, grads_y], (sent,)),)
        grads_x = xored(both[0], "tm", 2)
        rest = dealt_all.shape[0]
        grads = [dealt_all, grads_x, grads_y, grads_x]
        spans = [(0, rest), (0, rest), (0, rest), (rest, 2 * rest)]
    else:
        grads, spans = chips([dealt_all] * n_chip), None
    d_in, d_decay, d_step, token = call(
        lambda *refs: finish_kernel(parts, *refs),
        [
            shape((length, width), BF16),
            shape((heads, length), F32),
            shape((heads, length), F32),
            shape((8, LANES), F32),
        ],
        1.0,
        (x, bc, cumt, stept, cum, h_in, r_own, r_recv, w_whole, d_bc,
         *dxs, *exs, *owns),
        after=both,
        scratch=[pltpu.VMEM((width, half), BF16), pltpu.VMEM((heads, half), F32)],
    )
    w_rows = width // (2 * n_chip)
    term, term_send = call(
        lambda *refs: term_kernel(places, len(columns_in), *refs),
        [shape((w_rows, columns), F32), shape((w_rows, columns), BF16)],
        0.5,
        (*columns_in, *d_bcs),
        after=(token, *fars[1:]),
        scratch=[pltpu.VMEM((2, w_rows, columns), F32)],
    )
    final = call(
        deal_kernel,
        [shape((w_rows // n_dp, columns), F32)]
        + [shape((w_rows // n_dp, columns), BF16)] * (n_dp - 1),
        0.3,
        (term, swapped(term_send)),
        scratch=[pltpu.VMEM((n_dp, w_rows // n_dp, columns), F32)],
    )
    final = list(final[:1]) + [xored(f, "dp", s + 1) for s, f in enumerate(final[1:])]

    grads = stacked(grads, (final[0],), spans)
    w_down_grad, done = call(
        lambda *refs: down_kernel(n_dp, flip, capacity, grad_rows, *refs),
        [shape((hidden, piece), BF16), shape((8, LANES), F32)],
        1.0,
        (*near, *fars, grads),
        after=(final[0],),
    )
    w_bc_grad = call(sum_kernel, [shape(final[0].shape, F32)], 0.1, final, (done,))[0]
    return (d_in[None], d_decay.T[None], d_step.T[None], w_bc_grad, w_down_grad[None])


def solution(mesh):
    in_specs = (
        P("dp", "tm", None),
        P("dp", "tm", None),
        P("dp", None),
        P("dp", "tm", None),
        P("dp", "tm", None),
        P("dp", "tm", None, None, None),
        P(None, None, "tm"),
        P(None, None, "tm"),
        P("dp", None, "tm"),
        P("dp", "tm"),
        P("dp", None, "tm"),
    )
    out_specs = (
        P("dp", "tm", None),
        P("dp", "tm", None),
        P("dp", "tm", None),
        P(("tm", "dp"), None),
        P(None, "tm", "dp"),
    )
    return jax.shard_map(
        per_device, mesh=mesh, in_specs=in_specs, out_specs=out_specs, check_vma=False
    )
```

```python
import jax
import jax.numpy as jnp
from jax import lax
from jax.experimental import pallas as pl
from jax.experimental.pallas import tpu as pltpu
from jax.sharding import PartitionSpec as P

HI = lax.Precision.HIGHEST
F32 = jnp.float32
BF16 = jnp.bfloat16
LANES = 128


def dot(a, b, ca, cb, precision=None):
    return lax.dot_general(
        a, b, (((ca,), (cb,)), ((), ())), precision=precision, preferred_element_type=F32
    )


def iota(dims, axis):
    return lax.broadcasted_iota(jnp.int32, dims, axis)


def where_one(mask):
    return jnp.where(mask, 1.0, 0.0)


def triangle(n, keep):
    return where_one(keep(iota((n, n), 0), iota((n, n), 1))).astype(F32)


def halves(values, axis=1):
    high = values.astype(BF16)
    low = (values - high.astype(F32)).astype(BF16)
    return jnp.concatenate([high, low], axis=axis)


def to_lanes(j, size):
    dims = (LANES, LANES)
    one = where_one(iota(dims, 0) == iota(dims, 1) // size + j * (LANES // size)).astype(BF16)
    return jnp.concatenate([one, one], axis=0)


def to_heads(j, heads, size):
    dims = (heads, LANES)
    one = where_one(iota(dims, 0) == iota(dims, 1) // size + j * (LANES // size)).astype(BF16)
    return jnp.concatenate([one, one], axis=1)


def up16(n):
    return -(-n // 16) * 16


def call(kernel, outs, cost, args, after=(), scratch=(), limit=14, fetch=()):
    n_in, n_after, n_out = len(args), len(after), len(outs)
    fetch = tuple(fetch)

    def body(*refs):
        ins = list(refs[:n_in])
        rest = refs[n_in + n_after :]
        if fetch:
            sems = rest[-1]
            held = rest[len(rest) - 1 - len(fetch) : -1]
            rest = rest[: len(rest) - 1 - len(fetch)]
            copies = []
            for i, (index, ref) in enumerate(zip(fetch, held)):
                copies.append(pltpu.make_async_copy(ins[index], ref, sems.at[i]))
                ins[index] = ref
            for copy in copies:
                copy.start()
            for copy in copies:
                copy.wait()
        kernel(*ins, *rest)

    specs = [
        pl.BlockSpec(memory_space=pltpu.HBM if i in fetch else pltpu.VMEM) for i in range(n_in)
    ]
    held = [pltpu.VMEM(args[i].shape, args[i].dtype) for i in fetch]
    if fetch:
        held.append(pltpu.SemaphoreType.DMA((len(fetch),)))
    return pl.pallas_call(
        body,
        out_shape=outs,
        in_specs=specs + [pl.BlockSpec(memory_space=pl.ANY)] * n_after,
        out_specs=[pl.BlockSpec(memory_space=pltpu.VMEM)] * n_out,
        scratch_shapes=list(scratch) + held,
        cost_estimate=pl.CostEstimate(
            flops=int(cost * 3e9), bytes_accessed=1000, transcendentals=0
        ),
        compiler_params=pltpu.CompilerParams(vmem_limit_bytes=limit * 1024 * 1024),
    )(*args, *after)


def shape(dims, kind):
    return jax.ShapeDtypeStruct(dims, kind)


def core_and_chip():
    place = lax.axis_index("tm")
    return lax.rem(place, 2), lax.div(place, 2), lax.axis_size("tm") // 2


def rows_at(index, size, align=16):
    return pl.ds(pl.multiple_of(index * size, align), size)


def dealt_blocks(grads, held, out_refs):
    slots, width = grads.shape
    n_dp = held.shape[0]
    piece = width // n_dp
    for i in range(n_dp):
        for t, low in enumerate(range(i * piece, (i + 1) * piece, LANES)):
            block = grads[:, low : min(low + LANES, (i + 1) * piece)]
            if block.shape[1] < LANES:
                fill = jnp.zeros((slots, LANES - block.shape[1]), BF16)
                block = jnp.concatenate([block, fill], axis=1)
            held[i, t * slots : (t + 1) * slots, :] = block
    place = lax.axis_index("dp")
    s = 0
    for out in out_refs:
        for start in range(0, out.shape[0], held.shape[1]):
            out[start : start + held.shape[1], :] = held[place ^ s]
            s += 1


def columns_of(ref, index, wide):
    return ref.at[:, pl.ds(pl.multiple_of(index * wide, LANES), wide)]


def rows_of(ref, index, high):
    return ref.at[pl.ds(pl.multiple_of(index * high, LANES), high), :]


def high_low(values):
    high = values.astype(BF16).astype(F32)
    return [high, values - high]


def prep_kernel(
    n_deals, x_hbm, dy_hbm, ldt_ref, stept_ref, slot_ref, count_ref, gate_ref,
    cumt_ref, cum_ref, dyt_hbm, rows_ref, *rest,
):
    deal_refs = rest[:n_deals]
    held_ref, x_buf, dy_buf, dyt_buf, extra_buf, in_sems, out_sems = rest[n_deals:]
    parts, length, wide = x_buf.shape
    arrivals = []
    for c in range(parts):
        pair = [
            pltpu.make_async_copy(columns_of(ref, c, wide), buf.at[c], in_sems.at[k, c])
            for k, (ref, buf) in enumerate(((x_hbm, x_buf), (dy_hbm, dy_buf)))
        ]
        for copy in pair:
            copy.start()
        arrivals.append(pair)
    heads = ldt_ref.shape[0]
    size = parts * wide // heads
    slots = slot_ref.shape[1]
    hit = iota((length, slots), 0) == slot_ref[...]
    live = iota((1, slots), 1) < count_ref[...]
    weight = jnp.where(live, gate_ref[...].astype(F32), 0.0)
    pick = where_one(hit).astype(BF16)
    scaled = jnp.where(hit, weight, 0.0).astype(BF16)
    cumt = dot(ldt_ref[...], triangle(length, lambda a, b: a <= b), 1, 0, HI)
    cumt_ref[...] = cumt
    pad = jnp.zeros((LANES - heads, length), F32)
    cum_ref[...] = jnp.concatenate([cumt - jnp.log(stept_ref[...]), pad], axis=0).T
    table = halves(jnp.exp(jnp.concatenate([cumt, pad], axis=0).T))
    decay = jnp.broadcast_to(jnp.exp(cumt[:, length - 1 : length]), (heads, LANES))
    extra_buf[...] = jnp.concatenate(high_low(decay), axis=0).astype(BF16)
    leaving = [
        pltpu.make_async_copy(
            extra_buf, dyt_hbm.at[pl.ds(parts * wide, 2 * heads), :], out_sems.at[parts]
        )
    ]
    leaving[0].start()
    grads = []
    for c in range(parts):
        arrivals[c][0].wait()
        rows = dot(pick, x_buf[c], 0, 0).astype(BF16)
        for t in range(wide // LANES):
            at = (c * (wide // LANES) + t) * slots
            rows_ref[at : at + slots, :] = rows[:, t * LANES : (t + 1) * LANES]
        arrivals[c][1].wait()
        grads.append(dot(scaled, dy_buf[c], 0, 0).astype(BF16))
        for t in range(wide // LANES):
            span = slice(t * LANES, (t + 1) * LANES)
            wanted = to_lanes(c * (wide // LANES) + t, size)
            dys = dy_buf[c, :, span].astype(F32) * dot(table, wanted, 1, 0)
            dyt_buf[c, span, :] = dys.T.astype(BF16)
        copy = pltpu.make_async_copy(dyt_buf.at[c], rows_of(dyt_hbm, c, wide), out_sems.at[c])
        copy.start()
        leaving.append(copy)
    dealt_blocks(jnp.concatenate(grads, axis=1), held_ref, deal_refs)
    for copy in leaving:
        copy.wait()


def scale_kernel(x_ref, dy_ref, h_ref, cumt_ref, cum_ref, xs_ref, carried_ref, token_ref, *rest):
    outs, xt_ref = rest[:-1], rest[-1]
    length, width = x_ref.shape
    heads = cumt_ref.shape[0]
    size = width // heads
    _, chip, n_chip = core_and_chip()
    pad = jnp.zeros((LANES - heads, length), F32)
    cum = jnp.concatenate([cumt_ref[...], pad], axis=0).T
    into_end = jnp.exp(cum[length - 1 : length] - cum_ref[...])
    table = jnp.concatenate([halves(jnp.exp(cum)), halves(into_end)], axis=0)
    carried = jnp.zeros(carried_ref.shape, F32)
    for j in range(width // LANES):
        span = slice(j * LANES, (j + 1) * LANES)
        scale = dot(table, to_lanes(j, size), 1, 0)
        x_f = x_ref[:, span].astype(F32)
        xt_ref[span, :] = x_f.T.astype(BF16)
        xs_ref[:, span] = (x_f * scale[length:]).astype(BF16)
        dys = (dy_ref[:, span].astype(F32) * scale[:length]).astype(BF16)
        carried = carried + dot(dys, h_ref[span, :], 1, 0)
    carried_ref[...] = carried
    token_ref[...] = jnp.zeros_like(token_ref)
    block = width // n_chip
    s = 0
    for out in outs:
        for start in range(0, out.shape[0], block):
            out[start : start + block, :] = xt_ref[rows_at(chip ^ s, block), :]
            s += 1


def scale4_kernel(
    x_hbm, dy_hbm, h_hbm, cumt_ref, cum_ref, xs_hbm, carried_ref, token_ref, *rest
):
    outs = rest[:-8]
    x_buf, dy_buf, h_buf, xs_buf, xt_buf, in_sems, xs_sems, xt_sems = rest[-8:]
    parts, length, wide = x_buf.shape
    _, chip, _ = core_and_chip()
    arrivals = []
    for s in range(parts):
        sources = (
            (columns_of(x_hbm, chip ^ s, wide), x_buf),
            (columns_of(dy_hbm, chip ^ s, wide), dy_buf),
            (rows_of(h_hbm, chip ^ s, wide), h_buf),
        )
        three = [
            pltpu.make_async_copy(source, buf.at[s], in_sems.at[k, s])
            for k, (source, buf) in enumerate(sources)
        ]
        for copy in three:
            copy.start()
        arrivals.append(three)
    heads = cumt_ref.shape[0]
    size = parts * wide // heads
    pad = jnp.zeros((LANES - heads, length), F32)
    cum = jnp.concatenate([cumt_ref[...], pad], axis=0).T
    into_end = jnp.exp(cum[length - 1 : length] - cum_ref[...])
    table = jnp.concatenate([halves(jnp.exp(cum)), halves(into_end)], axis=0)
    carried = jnp.zeros(carried_ref.shape, F32)
    token_ref[...] = jnp.zeros_like(token_ref)
    targets = [(out, at) for out in outs for at in range(0, out.shape[0], wide)]
    leaving = []
    for s in range(parts):
        for copy in arrivals[s]:
            copy.wait()
        for t in range(wide // LANES):
            span = slice(t * LANES, (t + 1) * LANES)
            scale = dot(table, to_lanes((chip ^ s) * (wide // LANES) + t, size), 1, 0)
            x_f = x_buf[s, :, span].astype(F32)
            xt_buf[s, span, :] = x_f.T.astype(BF16)
            xs_buf[s, :, span] = (x_f * scale[length:]).astype(BF16)
            dys = (dy_buf[s, :, span].astype(F32) * scale[:length]).astype(BF16)
            carried = carried + dot(dys, h_buf[s, span, :], 1, 0)
        out, at = targets[s]
        pair = [
            pltpu.make_async_copy(xs_buf.at[s], columns_of(xs_hbm, chip ^ s, wide), xs_sems.at[s]),
            pltpu.make_async_copy(xt_buf.at[s], out.at[pl.ds(at, wide), :], xt_sems.at[s]),
        ]
        for copy in pair:
            copy.start()
        leaving += pair
    carried_ref[...] = carried
    for copy in leaving:
        copy.wait()


def early(kernel, outs, raw_outs, cost, args, raw_args, scratch):
    def spec(raw):
        return pl.BlockSpec(memory_space=pl.ANY if raw else pltpu.VMEM)

    return pl.pallas_call(
        kernel,
        out_shape=outs,
        in_specs=[spec(i in raw_args) for i in range(len(args))],
        out_specs=[spec(i in raw_outs) for i in range(len(outs))],
        scratch_shapes=scratch,
        cost_estimate=pl.CostEstimate(
            flops=int(cost * 3e9), bytes_accessed=1000, transcendentals=0
        ),
        compiler_params=pltpu.CompilerParams(vmem_limit_bytes=60 * 1024 * 1024),
    )(*args)


def join_kernel(ranges, *refs):
    out, at = refs[-1], 0
    for ref, (start, stop) in zip(refs, ranges):
        out[at : at + stop - start] = ref[start:stop]
        at += stop - start


def joined(arrays, after=(), ranges=None, cost=0.2):
    ranges = ranges or [(0, a.shape[0]) for a in arrays]
    dims = (sum(stop - start for start, stop in ranges), *arrays[0].shape[1:])
    return call(
        lambda *refs: join_kernel(ranges, *refs),
        [shape(dims, arrays[0].dtype)],
        cost,
        tuple(arrays),
        after=after,
    )[0]


def stacked(arrays, after=(), ranges=None, cost=0.2):
    count = len(arrays)
    out = joined(arrays, after, ranges, cost)
    return out.reshape(count, out.shape[0] // count, *out.shape[1:])


def project_kernel(n_mine, many, *refs):
    x_ref, dyt_ref, own_ref = refs[:3]
    mine, other = refs[3 : 3 + n_mine], refs[3 + n_mine]
    w_ref, bc_ref, keep_ref, send_ref = refs[4 + n_mine :]
    core, _, _ = core_and_chip()
    place, n_dp = lax.axis_index("dp"), lax.axis_size("dp")
    share = own_ref.shape[0]
    half = share // 2
    w_ref[rows_at(place, share), :] = own_ref[...]
    for i in range(n_mine):
        source = place ^ (i + 1)
        w_ref[rows_at(source * 2 + core, half), :] = mine[i][...]
        w_ref[rows_at(source * 2 + 1 - core, half), :] = other[i]
    bc = dot(x_ref[...], w_ref[...], 1, 0).astype(BF16)
    bc_ref[...] = bc
    c_rows = bc[:, LANES:]
    width = x_ref.shape[1]
    part = width // 2
    for ref, index in ((keep_ref, core), (send_ref, 1 - core)):
        ref[:part, :] = dot(dyt_ref[rows_at(index, part), :], c_rows, 1, 0).astype(BF16)
        table = dyt_ref[width : width + 4 * many, :].astype(F32)
        quarter = [table[i * many : (i + 1) * many] for i in range(4)]
        high = jnp.where(index == 0, quarter[0], quarter[1])
        low = jnp.where(index == 0, quarter[2], quarter[3])
        fill = jnp.zeros((ref.shape[0] - part - 2 * many, LANES), F32)
        ref[part:, :] = jnp.concatenate([high, low, fill], axis=0).astype(BF16)


def pair(keep_ref, recv_ref, many, size, head):
    core, _, _ = core_and_chip()
    part = many * size
    both = []
    for ref in (keep_ref, recv_ref):
        extra = ref[part:, :].astype(F32)
        decay = extra[head : head + 1] + extra[many + head : many + head + 1]
        both.append((ref[head * size : (head + 1) * size, :].astype(F32), decay))
    first = jax.tree.map(lambda a, b: jnp.where(core == 0, a, b), both[0], both[1])
    second = jax.tree.map(lambda a, b: jnp.where(core == 0, b, a), both[0], both[1])
    return first, second


def payload(ref, many, states, decays):
    size = states[0].shape[0]
    for head, state in enumerate(states):
        ref[head * size : (head + 1) * size, :] = state.astype(BF16)
    decay = jnp.concatenate(decays, axis=0)
    high = decay.astype(BF16).astype(F32)
    fill = jnp.zeros((ref.shape[0] - many * size - 2 * many, LANES), F32)
    extra = jnp.concatenate([high, decay - high, fill], axis=0)
    ref[many * size :, :] = extra.astype(BF16)


def loaded(ref, many, size, head):
    extra = ref[many * size :, :].astype(F32)
    decay = extra[head : head + 1] + extra[many + head : many + head + 1]
    return ref[head * size : (head + 1) * size, :].astype(F32), decay


def combine_kernel(many, size, keep_ref, recv_ref, out_ref):
    states, decays = [], []
    for head in range(many):
        (g0, a0), (g1, a1) = pair(keep_ref, recv_ref, many, size, head)
        states.append(g0 + a0 * g1)
        decays.append(a0 * a1)
    payload(out_ref, many, states, decays)


def pick_side(upper, mine, theirs):
    return jnp.where(upper, theirs, mine), jnp.where(upper, mine, theirs)


def climb_kernel(many, size, bit, mine_ref, recv_ref, out_ref):
    _, chip, _ = core_and_chip()
    upper = lax.rem(lax.div(chip, bit), 2) == 1
    states, decays = [], []
    for head in range(many):
        t_mine, a_mine = loaded(mine_ref, many, size, head)
        t_recv, a_recv = loaded(recv_ref, many, size, head)
        t_low, t_high = pick_side(upper, t_mine, t_recv)
        a_low, a_high = pick_side(upper, a_mine, a_recv)
        states.append(t_low + a_low * t_high)
        decays.append(a_low * a_high)
    payload(out_ref, many, states, decays)


def carry_kernel(many, size, levels, *refs):
    core, chip, _ = core_and_chip()
    recvs = refs[:levels]
    keep_ref, recv_ref, own_ref, send_ref = refs[levels:]
    for head in range(many):
        span = slice(head * size, (head + 1) * size)
        carry, reach = None, None
        for level, ref in enumerate(recvs):
            state, decay = loaded(ref, many, size, head)
            lower = lax.rem(lax.div(chip, 2**level), 2) == 0
            state = jnp.where(lower, state, 0.0)
            decay = jnp.where(lower, decay, 1.0)
            carry = state if carry is None else carry + reach * state
            reach = decay if reach is None else reach * decay
        _, (g1, a1) = pair(keep_ref, recv_ref, many, size, head)
        second = carry
        first = g1 + a1 * second
        own_ref[span, :] = jnp.where(core == 0, first, second).astype(BF16)
        send_ref[span, :] = jnp.where(core == 0, second, first).astype(BF16)


def intra_kernel(
    first, many, x_ref, dy_ref, bc_ref, cumt_ref, cum_ref, h_ref, before_ref,
    dx_ref, mixed_ref, ex_ref, own_ref, rowm_ref,
):
    length, width = x_ref.shape
    heads = cumt_ref.shape[0]
    size = width // heads
    per = LANES // size
    upper = iota((length, length), 0) <= iota((length, length), 1)
    b_rows, c_rows = bc_ref[:, :LANES], bc_ref[:, LANES:]
    scores = dot(b_rows, c_rows, 1, 1)
    lane = iota((1, LANES), 1)
    lane_bf = [where_one(lane // size == i).astype(BF16) for i in range(per)]
    mixed = before_ref[...]
    own = jnp.zeros((length, LANES), F32)
    reach = jnp.zeros((heads, length), F32)
    for j in range(first, first + many):
        span = slice(j * LANES, (j + 1) * LANES)
        out_span = slice((j - first) * LANES, (j - first + 1) * LANES)
        x_p = x_ref[:, span]
        dy_p = dy_ref[:, span]
        dy_h = jnp.concatenate([dy_p * m for m in lane_bf], axis=0)
        cross = dot(x_p, dy_h, 1, 1)
        kern = []
        for i in range(per):
            h = j * per + i
            diff = cumt_ref[h : h + 1, :] - cum_ref[:, h : h + 1]
            seg = jnp.exp(jnp.where(upper, diff, -1e30))
            part = cross[:, i * length : (i + 1) * length]
            mixed = mixed + seg * part
            seg = seg * scores
            kern.append(seg.astype(BF16))
            full = seg * part
            rowm_ref[h : h + 1, :] = jnp.sum(full, axis=0, keepdims=True)
            own = jnp.where(lane == h, jnp.sum(full, axis=1, keepdims=True), own)
        dx_ref[:, out_span] = dot(jnp.concatenate(kern, axis=1), dy_h, 1, 0)
        seen = dy_p.astype(F32) * dot(c_rows, h_ref[span, :], 1, 1)
        reach = reach + dot(to_heads(j, heads, size), halves(seen), 1, 1)
    mixed_ref[...] = mixed
    rows = slice(first * per, (first + many) * per)
    own = own.T[rows]
    own_ref[...] = own
    ex_ref[...] = rowm_ref[rows, :] + jnp.exp(cumt_ref[rows, :]) * reach[rows] - own


def close_kernel(mixed_ref, bc_ref, carried_ref, db_ref, dc_ref):
    mixed = mixed_ref[...].astype(BF16)
    db_ref[...] = dot(mixed, bc_ref[:, LANES:], 1, 0)
    dc_ref[...] = (dot(mixed, bc_ref[:, :LANES], 0, 0) + carried_ref[...]).astype(BF16)


def db_kernel(xs_ref, own_ref, recv_ref, db_ref, dc_ref, out_ref):
    core, _, _ = core_and_chip()
    half = db_ref.shape[1]
    part = own_ref.shape[0]
    total = db_ref[...]
    for ref, index in ((own_ref, core), (recv_ref, 1 - core)):
        total = total + dot(xs_ref[:, rows_at(index, part, LANES)], ref[...], 1, 0)
    out_ref[:, :half] = total.astype(BF16)
    out_ref[:, half:] = dc_ref[...]


def finish_kernel(parts, *refs):
    (x_ref, bc_ref, cumt_ref, stept_ref, cum_ref, h_ref, own_ref, recv_ref,
     w_ref, dbc_ref) = refs[:10]
    dx_refs, ex_refs, st_refs = (refs[10 + i * parts : 10 + (i + 1) * parts] for i in range(3))
    in_ref, decay_ref, grad_ref, token_ref, r_ref, edge_ref = refs[10 + 3 * parts :]
    token_ref[...] = jnp.zeros_like(token_ref)
    core, _, _ = core_and_chip()
    length, width = x_ref.shape
    heads = cumt_ref.shape[0]
    size = width // heads
    part = width // 2
    r_ref[rows_at(core, part), :] = own_ref[...]
    r_ref[rows_at(1 - core, part), :] = recv_ref[...]
    pad = jnp.zeros((LANES - heads, length), F32)
    total = jnp.concatenate([cumt_ref[...], pad], axis=0).T[length - 1 : length]
    table = halves(jnp.exp(total - cum_ref[...]))
    seen = jnp.zeros((heads, length), F32)
    b_rows = bc_ref[:, :LANES]
    d_bc = dbc_ref[...]
    for j in range(width // LANES):
        span = slice(j * LANES, (j + 1) * LANES)
        local = dx_refs[j * LANES // (width // parts)]
        start = j * LANES % (width // parts)
        r_tile = r_ref[span, :]
        reach = dot(b_rows, r_tile, 1, 1)
        d_in = local[:, start : start + LANES] + dot(table, to_lanes(j, size), 1, 0) * reach
        d_in = d_in + dot(d_bc, w_ref[span, :], 1, 1)
        in_ref[:, span] = d_in.astype(BF16)
        product = x_ref[:, span].astype(F32) * reach
        seen = seen + dot(to_heads(j, heads, size), halves(product), 1, 1)
        edge = r_tile.astype(F32) * h_ref[span, :].astype(F32)
        for i in range(LANES // size):
            h = j * (LANES // size) + i
            edge_ref[h : h + 1, :] = jnp.sum(
                edge[i * size : (i + 1) * size], axis=0, keepdims=True
            )
    cumt = cumt_ref[...]
    total = cumt[:, length - 1 : length]
    to_end = jnp.exp(total - cumt)
    step = stept_ref[...]
    own = jnp.concatenate([r[...] for r in st_refs], axis=0)
    excess = jnp.concatenate([r[...] for r in ex_refs], axis=0)
    grad_ref[...] = own / step + to_end * seen
    edge = jnp.exp(total) * jnp.sum(edge_ref[...], axis=1, keepdims=True)
    decay_ref[...] = (
        dot(excess, triangle(length, lambda a, b: a >= b), 1, 0, HI)
        + dot(to_end * step * seen, triangle(length, lambda a, b: a < b), 1, 0, HI)
        + edge
    )


def term_kernel(places, n_columns, *refs):
    columns, pieces = refs[:n_columns], refs[n_columns:-3]
    keep_ref, send_ref, held = refs[-3:]
    pieces = [(p, i) for p in pieces for i in range(p.shape[0])]
    rows = 2 * keep_ref.shape[0]
    core, _, _ = core_and_chip()
    total = None
    for (a, start), (b, i) in zip(places, pieces):
        part = dot(columns[a][start : start + rows, :], b[i], 1, 0)
        total = part if total is None else total + part
    block = keep_ref.shape[0]
    held[0] = total[:block]
    held[1] = total[block:]
    keep_ref[...] = held[core]
    send_ref[...] = held[1 - core].astype(BF16)


def deal_kernel(keep_ref, recv_ref, own_ref, *refs):
    outs, held = refs[:-1], refs[-1]
    place, n_dp = lax.axis_index("dp"), lax.axis_size("dp")
    total = keep_ref[...] + recv_ref[...].astype(F32)
    share = own_ref.shape[0]
    for i in range(n_dp):
        held[i] = total[i * share : (i + 1) * share]
    own_ref[...] = held[place]
    for s, out in enumerate(outs):
        out[...] = held[place ^ (s + 1)].astype(BF16)


def sum_kernel(*refs):
    total = refs[0][...]
    for ref in refs[1:-1]:
        total = total + ref[...].astype(F32)
    refs[-1][...] = total


def expert_kernel(flip, slots, a_ref, b_ref, gate_ref, up_ref, out_ref, *scratch):
    rows_ref, gate_acc, up_acc = scratch
    step = pl.program_id(0)
    n_chip = a_ref.shape[0]

    @pl.when(step == 0)
    def _():
        for half, ref in enumerate((a_ref, b_ref)):
            for i in range(n_chip):
                row = (half * n_chip + i) * slots
                for t in range(rows_ref.shape[1] // LANES):
                    rows_ref[row : row + slots, t * LANES : (t + 1) * LANES] = ref[
                        i, t * slots : (t + 1) * slots, :
                    ]
        gate_acc[...] = jnp.zeros_like(gate_acc)
        up_acc[...] = jnp.zeros_like(up_acc)

    depth = gate_ref.shape[0]
    rows = rows_ref[:, rows_at(step, depth, LANES)]
    gate_acc[...] += dot(rows, gate_ref[...], 1, 0)
    up_acc[...] += dot(rows, up_ref[...], 1, 0)

    @pl.when(step == pl.num_programs(0) - 1)
    def _():
        weighted = jax.nn.silu(gate_acc[...]) * up_acc[...]
        out_ref[...] = (weighted.T if flip else weighted).astype(BF16)


def expert(a, b, w_gate, w_up, slots, flip, after):
    n_chip = a.shape[0]
    total = 2 * n_chip * slots
    width, hidden = w_gate.shape
    depth = 512
    out = (hidden, total) if flip else (total, hidden)

    def body(*refs):
        expert_kernel(flip, slots, *refs[:4], *refs[4 + len(after) :])

    whole = pl.BlockSpec(a.shape, lambda i: (0, 0, 0))
    block = pl.BlockSpec((depth, hidden), lambda i: (i, 0))
    return pl.pallas_call(
        body,
        out_shape=shape(out, BF16),
        grid=(width // depth,),
        in_specs=[whole, whole, block, block]
        + [pl.BlockSpec(memory_space=pl.ANY)] * len(after),
        out_specs=pl.BlockSpec(out, lambda i: (0, 0)),
        scratch_shapes=[
            pltpu.VMEM((total, width), BF16),
            pltpu.VMEM((total, hidden), F32),
            pltpu.VMEM((total, hidden), F32),
        ],
        cost_estimate=pl.CostEstimate(
            flops=int(1e9), bytes_accessed=1000, transcendentals=0
        ),
        compiler_params=pltpu.CompilerParams(vmem_limit_bytes=20 * 1024 * 1024),
    )(a, b, w_gate, w_up, *after)


def down_kernel(n_dp, flip, slots, grad_rows, *refs):
    pieces = refs[:n_dp]
    g_ref, out_ref, token_ref = refs[n_dp:]
    token_ref[...] = jnp.zeros_like(token_ref)
    n_chip = g_ref.shape[0]
    piece = out_ref.shape[1]
    total = None
    for s in range(n_dp):
        columns = []
        for t in range(grad_rows // slots):
            row = s * grad_rows + t * slots
            blocks = [
                g_ref[i, half + row : half + row + slots, :]
                for half in (0, n_dp * grad_rows)
                for i in range(n_chip)
            ]
            columns.append(jnp.concatenate(blocks, axis=0))
        right = jnp.concatenate(columns, axis=1)[:, :piece]
        part = dot(pieces[s][...], right, 1 if flip else 0, 0)
        total = part if total is None else total + part
    out_ref[...] = total.astype(BF16)


def xored(array, axis, mask):
    count = lax.axis_size(axis)
    return lax.ppermute(array, axis, [(i, i ^ mask) for i in range(count)])


def swapped(array):
    return xored(array, "tm", 1)


def chips(arrays):
    return [arrays[0]] + [xored(a, "tm", 2 * s) for s, a in enumerate(arrays) if s]


def gathered(array, axis, count):
    if count == 1:
        return [array]
    far = xored(array, axis, count // 2)
    return gathered(array, axis, count // 2) + gathered(far, axis, count // 2)


def per_device(
    layer_in,
    out_grad,
    w_bc,
    log_decay,
    step,
    saved_states,
    w_gate,
    w_up,
    slot_rows,
    slot_counts,
    slot_gates,
):
    n_dp = lax.axis_size("dp")
    core, chip, n_chip = core_and_chip()
    x = layer_in[0]
    dy = out_grad[0]
    length, width = x.shape
    heads = log_decay.shape[2]
    size = width // heads
    share, columns = w_bc.shape
    half = columns // 2
    ldt = log_decay[0].T
    stept = step[0].T
    h_in = saved_states[0, 0].reshape(width, half)
    capacity = slot_rows.shape[2]
    piece = width // n_dp
    part = width // 2
    many = heads // 2
    flip = w_gate.shape[2] % LANES == 0

    grad_rows = -(-piece // LANES) * capacity
    w_half = lax.dynamic_slice_in_dim(w_bc, core * (share // 2), share // 2, 0)

    in_rows = width // LANES * capacity
    blocks = [1, 1, 2] if n_chip == 4 else [1] * n_chip
    groups = [2, 2] if n_dp == 4 else [1] * n_dp
    cuts = 4
    wide = width // cuts
    dma = pltpu.SemaphoreType.DMA
    cumt, cum, dyt, rows, *deals = early(
        lambda *refs: prep_kernel(len(groups), *refs),
        [
            shape((heads, length), F32),
            shape((length, LANES), F32),
            shape((width + up16(2 * heads), length), BF16),
            shape((in_rows, LANES), BF16),
        ]
        + [shape((k * grad_rows, LANES), BF16) for k in groups],
        (2,),
        1.5,
        (x, dy, ldt, stept, slot_rows[0], slot_counts, slot_gates[0]),
        (0, 1),
        [
            pltpu.VMEM((n_dp, grad_rows, LANES), BF16),
            pltpu.VMEM((cuts, length, wide), BF16),
            pltpu.VMEM((cuts, length, wide), BF16),
            pltpu.VMEM((cuts, wide, length), BF16),
            pltpu.VMEM((2 * heads, LANES), BF16),
            dma((2, cuts)),
            dma((cuts + 1,)),
        ],
    )
    w_far = xored(w_half, "dp", n_dp // 2)
    mine = gathered(w_half, "dp", n_dp // 2)[1:]
    w_copy = joined([w_far], after=(rows,))
    mine += gathered(w_copy, "dp", n_dp // 2)
    rows_in = [rows]
    while 2 ** (len(rows_in) - 1) < n_chip:
        rows_sent = joined(rows_in, (w_copy,)) if rows_in[1:] else rows
        rows_in.append(xored(rows_sent, "tm", 2 ** len(rows_in)))
    scale_outs = [shape((length, width), BF16), shape((length, half), F32), shape((8, LANES), F32)]
    scale_outs += [shape((k * width // n_chip, length), BF16) for k in blocks]
    if n_chip == cuts:
        xs, carried, scaled, *xt = early(
            scale4_kernel,
            scale_outs,
            (0, 3, 4, 5),
            1.5,
            (x, dy, h_in, cumt, cum),
            (0, 1, 2),
            [
                pltpu.VMEM((cuts, length, wide), BF16),
                pltpu.VMEM((cuts, length, wide), BF16),
                pltpu.VMEM((cuts, wide, half), BF16),
                pltpu.VMEM((cuts, length, wide), BF16),
                pltpu.VMEM((cuts, wide, length), BF16),
                dma((3, cuts)),
                dma((cuts,)),
                dma((cuts,)),
            ],
        )
    else:
        xs, carried, scaled, *xt = call(
            scale_kernel,
            scale_outs,
            1.5,
            (x, dy, h_in, cumt, cum),
            scratch=[pltpu.VMEM((width, length), BF16)],
            fetch=(0, 1, 2, 3, 4),
            limit=60,
        )
    if n_dp == 4:
        one = (0, grad_rows), (grad_rows, 2 * grad_rows)
        over_2 = xored(deals[1], "dp", 2)
        hops = (over_2,)
    else:
        hops = ()
        source, spans = deals[:1] + [xored(d, "dp", s + 1) for s, d in enumerate(deals[1:])], None
    other = swapped(stacked(mine, after=(rows_in[-1], scaled), cost=1.0))
    w_whole, bc, keep, send = call(
        lambda *refs: project_kernel(n_dp - 1, many, *refs),
        [
            shape((width, columns), BF16),
            shape((length, columns), BF16),
            shape((part + up16(2 * many), half), BF16),
            shape((part + up16(2 * many), half), BF16),
        ],
        1.0,
        (x, dyt, w_bc, *mine, other),
    )
    recv = swapped(send)
    hidden = w_gate.shape[2]
    climbs = [
        call(
            lambda *refs: combine_kernel(many, size, *refs),
            [shape((part + up16(2 * many), half), BF16)],
            0.5,
            (keep, recv),
        )[0]
    ]
    rows_a = joined(rows_in, (climbs[0],)).reshape(n_chip, in_rows, LANES)
    rows_b = swapped(rows_a)
    weighted = expert(rows_a, rows_b, w_gate[0], w_up[0], capacity, flip, (climbs[0],))
    if n_chip == 4:
        x_rows = width // n_chip
        over_y = xored(xt[2], "tm", 4)

    parts = 2
    tiles = width // LANES // parts
    dxs, exs, owns = [], [], []
    if n_dp == 4:
        over_1 = xored(joined([deals[0], over_2], (weighted,), [one[1], one[1]]), "dp", 1)
        hops += (over_1,)
        source, spans = [deals[0], over_1, over_2, over_1], [one[0], one[0], one[0], one[1]]
    held = (weighted, *hops)
    arrived = []
    bit = 1
    while bit < n_chip:
        last = bit * 2 == n_chip
        moves = [(k, k ^ (2 * bit)) for k in range(2 * n_chip)]
        arrived.append(lax.ppermute(climbs[-1], "tm", moves))
        if not last:
            climbs.append(
                call(
                    lambda *refs, bit=bit: climb_kernel(many, size, bit, *refs),
                    [shape((part + up16(2 * many), half), BF16)],
                    0.5,
                    (climbs[-1], arrived[-1]),
                    after=held,
                )[0]
            )
        bit *= 2
    later = (climbs[-1],)
    mixed = jnp.zeros((length, length), F32)
    for i in range(parts):
        dx, mixed, ex, own = call(
            lambda *refs, i=i: intra_kernel(i * tiles, tiles, *refs),
            [
                shape((length, width // parts), F32),
                shape((length, length), F32),
                shape((heads // parts, length), F32),
                shape((heads // parts, length), F32),
            ],
            0.7,
            (x, dy, bc, cumt, cum, h_in, mixed),
            after=later,
            scratch=[pltpu.VMEM((heads, length), F32)],
        )
        dxs.append(dx)
        exs.append(ex)
        owns.append(own)
    db, dc = call(
        close_kernel,
        [shape((length, half), F32), shape((length, half), BF16)],
        0.3,
        (mixed, bc, carried),
    )

    held = (dc,)
    dealt = joined(source, later, spans)
    dealt_all = joined([dealt, swapped(dealt)])
    held += (dealt_all,)
    if n_chip == 4:
        over_x = xored(joined([xt[1], over_y], later, [(0, x_rows), (x_rows, 2 * x_rows)]), "tm", 2)
        columns_in = [xt[0], over_x, over_y]
        places = [(0, 0), (1, 0), (2, 0), (1, x_rows)]
        held += (over_x,)
    else:
        columns_in = chips(xt)
        places = [(i, 0) for i in range(n_chip)]
    far = xored(weighted, "dp", n_dp // 2)
    near = gathered(weighted, "dp", n_dp // 2)
    held += (far, *near[1:])
    r_own, r_send = call(
        lambda *refs: carry_kernel(many, size, len(arrived), *refs),
        [shape((part, half), BF16)] * 2,
        0.5,
        (*arrived, keep, recv),
        after=held,
    )
    r_recv = swapped(r_send)
    d_bc = call(db_kernel, [shape((length, columns), BF16)], 0.3, (xs, r_own, r_recv, db, dc))[0]
    fars = gathered(joined([far], (d_bc,)), "dp", n_dp // 2)
    d_bcs = [d_bc.reshape(1, length, columns)]
    if n_chip == 4:
        grads_y = xored(dealt_all, "tm", 4)
    while 2 ** (len(d_bcs) - 1) < n_chip:
        level = 2 ** (len(d_bcs) - 1)
        sent = d_bcs[0] if level == 1 else joined(d_bcs)
        d_bcs.append(xored(sent, "tm", 2 * level))
    both = ()
    if n_chip == 4:
        both = (joined([dealt_all, grads_y], (sent,)),)
        grads_x = xored(both[0], "tm", 2)
        rest = dealt_all.shape[0]
        grads = [dealt_all, grads_x, grads_y, grads_x]
        spans = [(0, rest), (0, rest), (0, rest), (rest, 2 * rest)]
    else:
        grads, spans = chips([dealt_all] * n_chip), None
    d_in, d_decay, d_step, token = call(
        lambda *refs: finish_kernel(parts, *refs),
        [
            shape((length, width), BF16),
            shape((heads, length), F32),
            shape((heads, length), F32),
            shape((8, LANES), F32),
        ],
        1.0,
        (x, bc, cumt, stept, cum, h_in, r_own, r_recv, w_whole, d_bc,
         *dxs, *exs, *owns),
        after=both,
        scratch=[pltpu.VMEM((width, half), BF16), pltpu.VMEM((heads, half), F32)],
    )
    w_rows = width // (2 * n_chip)
    term, term_send = call(
        lambda *refs: term_kernel(places, len(columns_in), *refs),
        [shape((w_rows, columns), F32), shape((w_rows, columns), BF16)],
        0.5,
        (*columns_in, *d_bcs),
        after=(token, *fars[1:]),
        scratch=[pltpu.VMEM((2, w_rows, columns), F32)],
    )
    final = call(
        deal_kernel,
        [shape((w_rows // n_dp, columns), F32)]
        + [shape((w_rows // n_dp, columns), BF16)] * (n_dp - 1),
        0.3,
        (term, swapped(term_send)),
        scratch=[pltpu.VMEM((n_dp, w_rows // n_dp, columns), F32)],
    )
    final = list(final[:1]) + [xored(f, "dp", s + 1) for s, f in enumerate(final[1:])]

    grads = stacked(grads, (final[0],), spans)
    w_down_grad, done = call(
        lambda *refs: down_kernel(n_dp, flip, capacity, grad_rows, *refs),
        [shape((hidden, piece), BF16), shape((8, LANES), F32)],
        1.0,
        (*near, *fars, grads),
        after=(final[0],),
    )
    w_bc_grad = call(sum_kernel, [shape(final[0].shape, F32)], 0.1, final, (done,))[0]
    return (d_in[None], d_decay.T[None], d_step.T[None], w_bc_grad, w_down_grad[None])


def solution(mesh):
    in_specs = (
        P("dp", "tm", None),
        P("dp", "tm", None),
        P("dp", None),
        P("dp", "tm", None),
        P("dp", "tm", None),
        P("dp", "tm", None, None, None),
        P(None, None, "tm"),
        P(None, None, "tm"),
        P("dp", None, "tm"),
        P("dp", "tm"),
        P("dp", None, "tm"),
    )
    out_specs = (
        P("dp", "tm", None),
        P("dp", "tm", None),
        P("dp", "tm", None),
        P(("tm", "dp"), None),
        P(None, "tm", "dp"),
    )
    return jax.shard_map(
        per_device, mesh=mesh, in_specs=in_specs, out_specs=out_specs, check_vma=False
    )
```

```python
import jax
import jax.numpy as jnp
from jax import lax
from jax.experimental import pallas as pl
from jax.experimental.pallas import tpu as pltpu
from jax.sharding import PartitionSpec as P

HI = lax.Precision.HIGHEST
F32 = jnp.float32
BF16 = jnp.bfloat16
LANES = 128


def dot(a, b, ca, cb, precision=None):
    return lax.dot_general(
        a, b, (((ca,), (cb,)), ((), ())), precision=precision, preferred_element_type=F32
    )


def iota(dims, axis):
    return lax.broadcasted_iota(jnp.int32, dims, axis)


def where_one(mask):
    return jnp.where(mask, 1.0, 0.0)


def triangle(n, keep):
    return where_one(keep(iota((n, n), 0), iota((n, n), 1))).astype(F32)


def halves(values, axis=1):
    high = values.astype(BF16)
    low = (values - high.astype(F32)).astype(BF16)
    return jnp.concatenate([high, low], axis=axis)


def to_lanes(j, size):
    dims = (LANES, LANES)
    one = where_one(iota(dims, 0) == iota(dims, 1) // size + j * (LANES // size)).astype(BF16)
    return jnp.concatenate([one, one], axis=0)


def to_heads(j, heads, size):
    dims = (heads, LANES)
    one = where_one(iota(dims, 0) == iota(dims, 1) // size + j * (LANES // size)).astype(BF16)
    return jnp.concatenate([one, one], axis=1)


def up16(n):
    return -(-n // 16) * 16


def call(kernel, outs, cost, args, after=(), scratch=(), limit=14, fetch=()):
    n_in, n_after, n_out = len(args), len(after), len(outs)
    fetch = tuple(fetch)

    def body(*refs):
        ins = list(refs[:n_in])
        rest = refs[n_in + n_after :]
        if fetch:
            sems = rest[-1]
            held = rest[len(rest) - 1 - len(fetch) : -1]
            rest = rest[: len(rest) - 1 - len(fetch)]
            copies = []
            for i, (index, ref) in enumerate(zip(fetch, held)):
                copies.append(pltpu.make_async_copy(ins[index], ref, sems.at[i]))
                ins[index] = ref
            for copy in copies:
                copy.start()
            for copy in copies:
                copy.wait()
        kernel(*ins, *rest)

    specs = [
        pl.BlockSpec(memory_space=pltpu.HBM if i in fetch else pltpu.VMEM) for i in range(n_in)
    ]
    held = [pltpu.VMEM(args[i].shape, args[i].dtype) for i in fetch]
    if fetch:
        held.append(pltpu.SemaphoreType.DMA((len(fetch),)))
    return pl.pallas_call(
        body,
        out_shape=outs,
        in_specs=specs + [pl.BlockSpec(memory_space=pl.ANY)] * n_after,
        out_specs=[pl.BlockSpec(memory_space=pltpu.VMEM)] * n_out,
        scratch_shapes=list(scratch) + held,
        cost_estimate=pl.CostEstimate(
            flops=int(cost * 3e9), bytes_accessed=1000, transcendentals=0
        ),
        compiler_params=pltpu.CompilerParams(vmem_limit_bytes=limit * 1024 * 1024),
    )(*args, *after)


def shape(dims, kind):
    return jax.ShapeDtypeStruct(dims, kind)


def core_and_chip():
    place = lax.axis_index("tm")
    return lax.rem(place, 2), lax.div(place, 2), lax.axis_size("tm") // 2


def rows_at(index, size, align=16):
    return pl.ds(pl.multiple_of(index * size, align), size)


def picked(x_ref, dy_ref, slot_ref, count_ref, gate_ref, rows_ref, out_refs):
    length, width = x_ref.shape
    slots = slot_ref.shape[1]
    hit = iota((length, slots), 0) == slot_ref[...]
    live = iota((1, slots), 1) < count_ref[...]
    weight = jnp.where(live, gate_ref[...].astype(F32), 0.0)
    rows = dot(where_one(hit).astype(BF16), x_ref[...], 0, 0).astype(BF16)
    for t in range(width // LANES):
        rows_ref[t * slots : (t + 1) * slots, :] = rows[:, t * LANES : (t + 1) * LANES]
    grads = dot(jnp.where(hit, weight, 0.0).astype(BF16), dy_ref[...], 0, 0).astype(BF16)
    held = out_refs[-1]
    n_dp = held.shape[0]
    piece = width // n_dp
    for i in range(n_dp):
        for t, low in enumerate(range(i * piece, (i + 1) * piece, LANES)):
            block = grads[:, low : min(low + LANES, (i + 1) * piece)]
            if block.shape[1] < LANES:
                fill = jnp.zeros((slots, LANES - block.shape[1]), BF16)
                block = jnp.concatenate([block, fill], axis=1)
            held[i, t * slots : (t + 1) * slots, :] = block
    place = lax.axis_index("dp")
    s = 0
    for out in out_refs[:-1]:
        for start in range(0, out.shape[0], held.shape[1]):
            out[start : start + held.shape[1], :] = held[place ^ s]
            s += 1


def high_low(values):
    high = values.astype(BF16).astype(F32)
    return [high, values - high]


def prep_kernel(
    n_deals, x_ref, dy_ref, ldt_ref, stept_ref, slot_ref, count_ref, gate_ref,
    cumt_ref, cum_ref, dyt_ref, rows_ref, *rest,
):
    length, width = x_ref.shape
    heads = ldt_ref.shape[0]
    size = width // heads
    picked(x_ref, dy_ref, slot_ref, count_ref, gate_ref, rows_ref, rest)
    cumt = dot(ldt_ref[...], triangle(length, lambda a, b: a <= b), 1, 0, HI)
    cumt_ref[...] = cumt
    pad = jnp.zeros((LANES - heads, length), F32)
    cum_ref[...] = jnp.concatenate([cumt - jnp.log(stept_ref[...]), pad], axis=0).T
    start = jnp.exp(jnp.concatenate([cumt, pad], axis=0).T)
    table = halves(start)
    for j in range(width // LANES):
        span = slice(j * LANES, (j + 1) * LANES)
        dys = dy_ref[:, span].astype(F32) * dot(table, to_lanes(j, size), 1, 0)
        dyt_ref[span, :] = dys.T.astype(BF16)
    decay = jnp.broadcast_to(jnp.exp(cumt[:, length - 1 : length]), (heads, LANES))
    dyt_ref[width : width + 2 * heads, :] = jnp.concatenate(high_low(decay), axis=0).astype(BF16)


def scale_kernel(x_ref, dy_ref, h_ref, cumt_ref, cum_ref, xs_ref, carried_ref, token_ref, *rest):
    outs, xt_ref = rest[:-1], rest[-1]
    length, width = x_ref.shape
    heads = cumt_ref.shape[0]
    size = width // heads
    _, chip, n_chip = core_and_chip()
    pad = jnp.zeros((LANES - heads, length), F32)
    cum = jnp.concatenate([cumt_ref[...], pad], axis=0).T
    into_end = jnp.exp(cum[length - 1 : length] - cum_ref[...])
    table = jnp.concatenate([halves(jnp.exp(cum)), halves(into_end)], axis=0)
    carried = jnp.zeros(carried_ref.shape, F32)
    for j in range(width // LANES):
        span = slice(j * LANES, (j + 1) * LANES)
        scale = dot(table, to_lanes(j, size), 1, 0)
        x_f = x_ref[:, span].astype(F32)
        xt_ref[span, :] = x_f.T.astype(BF16)
        xs_ref[:, span] = (x_f * scale[length:]).astype(BF16)
        dys = (dy_ref[:, span].astype(F32) * scale[:length]).astype(BF16)
        carried = carried + dot(dys, h_ref[span, :], 1, 0)
    carried_ref[...] = carried
    token_ref[...] = jnp.zeros_like(token_ref)
    block = width // n_chip
    s = 0
    for out in outs:
        for start in range(0, out.shape[0], block):
            out[start : start + block, :] = xt_ref[rows_at(chip ^ s, block), :]
            s += 1


def join_kernel(ranges, *refs):
    out, at = refs[-1], 0
    for ref, (start, stop) in zip(refs, ranges):
        out[at : at + stop - start] = ref[start:stop]
        at += stop - start


def joined(arrays, after=(), ranges=None, cost=0.2):
    ranges = ranges or [(0, a.shape[0]) for a in arrays]
    dims = (sum(stop - start for start, stop in ranges), *arrays[0].shape[1:])
    return call(
        lambda *refs: join_kernel(ranges, *refs),
        [shape(dims, arrays[0].dtype)],
        cost,
        tuple(arrays),
        after=after,
    )[0]


def stacked(arrays, after=(), ranges=None, cost=0.2):
    count = len(arrays)
    out = joined(arrays, after, ranges, cost)
    return out.reshape(count, out.shape[0] // count, *out.shape[1:])


def project_kernel(n_mine, many, *refs):
    x_ref, dyt_ref, own_ref = refs[:3]
    mine, other = refs[3 : 3 + n_mine], refs[3 + n_mine]
    w_ref, bc_ref, keep_ref, send_ref = refs[4 + n_mine :]
    core, _, _ = core_and_chip()
    place, n_dp = lax.axis_index("dp"), lax.axis_size("dp")
    share = own_ref.shape[0]
    half = share // 2
    w_ref[rows_at(place, share), :] = own_ref[...]
    for i in range(n_mine):
        source = place ^ (i + 1)
        w_ref[rows_at(source * 2 + core, half), :] = mine[i][...]
        w_ref[rows_at(source * 2 + 1 - core, half), :] = other[i]
    bc = dot(x_ref[...], w_ref[...], 1, 0).astype(BF16)
    bc_ref[...] = bc
    c_rows = bc[:, LANES:]
    width = x_ref.shape[1]
    part = width // 2
    for ref, index in ((keep_ref, core), (send_ref, 1 - core)):
        ref[:part, :] = dot(dyt_ref[rows_at(index, part), :], c_rows, 1, 0).astype(BF16)
        table = dyt_ref[width : width + 4 * many, :].astype(F32)
        quarter = [table[i * many : (i + 1) * many] for i in range(4)]
        high = jnp.where(index == 0, quarter[0], quarter[1])
        low = jnp.where(index == 0, quarter[2], quarter[3])
        fill = jnp.zeros((ref.shape[0] - part - 2 * many, LANES), F32)
        ref[part:, :] = jnp.concatenate([high, low, fill], axis=0).astype(BF16)


def pair(keep_ref, recv_ref, many, size, head):
    core, _, _ = core_and_chip()
    part = many * size
    both = []
    for ref in (keep_ref, recv_ref):
        extra = ref[part:, :].astype(F32)
        decay = extra[head : head + 1] + extra[many + head : many + head + 1]
        both.append((ref[head * size : (head + 1) * size, :].astype(F32), decay))
    first = jax.tree.map(lambda a, b: jnp.where(core == 0, a, b), both[0], both[1])
    second = jax.tree.map(lambda a, b: jnp.where(core == 0, b, a), both[0], both[1])
    return first, second


def payload(ref, many, states, decays):
    size = states[0].shape[0]
    for head, state in enumerate(states):
        ref[head * size : (head + 1) * size, :] = state.astype(BF16)
    decay = jnp.concatenate(decays, axis=0)
    high = decay.astype(BF16).astype(F32)
    fill = jnp.zeros((ref.shape[0] - many * size - 2 * many, LANES), F32)
    extra = jnp.concatenate([high, decay - high, fill], axis=0)
    ref[many * size :, :] = extra.astype(BF16)


def loaded(ref, many, size, head):
    extra = ref[many * size :, :].astype(F32)
    decay = extra[head : head + 1] + extra[many + head : many + head + 1]
    return ref[head * size : (head + 1) * size, :].astype(F32), decay


def combine_kernel(many, size, keep_ref, recv_ref, out_ref):
    states, decays = [], []
    for head in range(many):
        (g0, a0), (g1, a1) = pair(keep_ref, recv_ref, many, size, head)
        states.append(g0 + a0 * g1)
        decays.append(a0 * a1)
    payload(out_ref, many, states, decays)


def pick_side(upper, mine, theirs):
    return jnp.where(upper, theirs, mine), jnp.where(upper, mine, theirs)


def climb_kernel(many, size, bit, mine_ref, recv_ref, out_ref):
    _, chip, _ = core_and_chip()
    upper = lax.rem(lax.div(chip, bit), 2) == 1
    states, decays = [], []
    for head in range(many):
        t_mine, a_mine = loaded(mine_ref, many, size, head)
        t_recv, a_recv = loaded(recv_ref, many, size, head)
        t_low, t_high = pick_side(upper, t_mine, t_recv)
        a_low, a_high = pick_side(upper, a_mine, a_recv)
        states.append(t_low + a_low * t_high)
        decays.append(a_low * a_high)
    payload(out_ref, many, states, decays)


def carry_kernel(many, size, levels, *refs):
    core, chip, _ = core_and_chip()
    recvs = refs[:levels]
    keep_ref, recv_ref, own_ref, send_ref = refs[levels:]
    for head in range(many):
        span = slice(head * size, (head + 1) * size)
        carry, reach = None, None
        for level, ref in enumerate(recvs):
            state, decay = loaded(ref, many, size, head)
            lower = lax.rem(lax.div(chip, 2**level), 2) == 0
            state = jnp.where(lower, state, 0.0)
            decay = jnp.where(lower, decay, 1.0)
            carry = state if carry is None else carry + reach * state
            reach = decay if reach is None else reach * decay
        _, (g1, a1) = pair(keep_ref, recv_ref, many, size, head)
        second = carry
        first = g1 + a1 * second
        own_ref[span, :] = jnp.where(core == 0, first, second).astype(BF16)
        send_ref[span, :] = jnp.where(core == 0, second, first).astype(BF16)


def intra_kernel(
    first, many, x_ref, dy_ref, bc_ref, cumt_ref, cum_ref, h_ref, before_ref,
    dx_ref, mixed_ref, ex_ref, own_ref, rowm_ref,
):
    length, width = x_ref.shape
    heads = cumt_ref.shape[0]
    size = width // heads
    per = LANES // size
    upper = iota((length, length), 0) <= iota((length, length), 1)
    b_rows, c_rows = bc_ref[:, :LANES], bc_ref[:, LANES:]
    scores = dot(b_rows, c_rows, 1, 1)
    lane = iota((1, LANES), 1)
    lane_bf = [where_one(lane // size == i).astype(BF16) for i in range(per)]
    mixed = before_ref[...]
    own = jnp.zeros((length, LANES), F32)
    reach = jnp.zeros((heads, length), F32)
    for j in range(first, first + many):
        span = slice(j * LANES, (j + 1) * LANES)
        out_span = slice((j - first) * LANES, (j - first + 1) * LANES)
        x_p = x_ref[:, span]
        dy_p = dy_ref[:, span]
        dy_h = jnp.concatenate([dy_p * m for m in lane_bf], axis=0)
        cross = dot(x_p, dy_h, 1, 1)
        kern = []
        for i in range(per):
            h = j * per + i
            diff = cumt_ref[h : h + 1, :] - cum_ref[:, h : h + 1]
            seg = jnp.exp(jnp.where(upper, diff, -1e30))
            part = cross[:, i * length : (i + 1) * length]
            mixed = mixed + seg * part
            seg = seg * scores
            kern.append(seg.astype(BF16))
            full = seg * part
            rowm_ref[h : h + 1, :] = jnp.sum(full, axis=0, keepdims=True)
            own = jnp.where(lane == h, jnp.sum(full, axis=1, keepdims=True), own)
        dx_ref[:, out_span] = dot(jnp.concatenate(kern, axis=1), dy_h, 1, 0)
        seen = dy_p.astype(F32) * dot(c_rows, h_ref[span, :], 1, 1)
        reach = reach + dot(to_heads(j, heads, size), halves(seen), 1, 1)
    mixed_ref[...] = mixed
    rows = slice(first * per, (first + many) * per)
    own = own.T[rows]
    own_ref[...] = own
    ex_ref[...] = rowm_ref[rows, :] + jnp.exp(cumt_ref[rows, :]) * reach[rows] - own


def close_kernel(mixed_ref, bc_ref, carried_ref, db_ref, dc_ref):
    mixed = mixed_ref[...].astype(BF16)
    db_ref[...] = dot(mixed, bc_ref[:, LANES:], 1, 0)
    dc_ref[...] = (dot(mixed, bc_ref[:, :LANES], 0, 0) + carried_ref[...]).astype(BF16)


def db_kernel(xs_ref, own_ref, recv_ref, db_ref, dc_ref, out_ref):
    core, _, _ = core_and_chip()
    half = db_ref.shape[1]
    part = own_ref.shape[0]
    total = db_ref[...]
    for ref, index in ((own_ref, core), (recv_ref, 1 - core)):
        total = total + dot(xs_ref[:, rows_at(index, part, LANES)], ref[...], 1, 0)
    out_ref[:, :half] = total.astype(BF16)
    out_ref[:, half:] = dc_ref[...]


def finish_kernel(parts, *refs):
    (x_ref, bc_ref, cumt_ref, stept_ref, cum_ref, h_ref, own_ref, recv_ref,
     w_ref, dbc_ref) = refs[:10]
    dx_refs, ex_refs, st_refs = (refs[10 + i * parts : 10 + (i + 1) * parts] for i in range(3))
    in_ref, decay_ref, grad_ref, token_ref, r_ref, edge_ref = refs[10 + 3 * parts :]
    token_ref[...] = jnp.zeros_like(token_ref)
    core, _, _ = core_and_chip()
    length, width = x_ref.shape
    heads = cumt_ref.shape[0]
    size = width // heads
    part = width // 2
    r_ref[rows_at(core, part), :] = own_ref[...]
    r_ref[rows_at(1 - core, part), :] = recv_ref[...]
    pad = jnp.zeros((LANES - heads, length), F32)
    total = jnp.concatenate([cumt_ref[...], pad], axis=0).T[length - 1 : length]
    table = halves(jnp.exp(total - cum_ref[...]))
    seen = jnp.zeros((heads, length), F32)
    b_rows = bc_ref[:, :LANES]
    d_bc = dbc_ref[...]
    for j in range(width // LANES):
        span = slice(j * LANES, (j + 1) * LANES)
        local = dx_refs[j * LANES // (width // parts)]
        start = j * LANES % (width // parts)
        r_tile = r_ref[span, :]
        reach = dot(b_rows, r_tile, 1, 1)
        d_in = local[:, start : start + LANES] + dot(table, to_lanes(j, size), 1, 0) * reach
        d_in = d_in + dot(d_bc, w_ref[span, :], 1, 1)
        in_ref[:, span] = d_in.astype(BF16)
        product = x_ref[:, span].astype(F32) * reach
        seen = seen + dot(to_heads(j, heads, size), halves(product), 1, 1)
        edge = r_tile.astype(F32) * h_ref[span, :].astype(F32)
        for i in range(LANES // size):
            h = j * (LANES // size) + i
            edge_ref[h : h + 1, :] = jnp.sum(
                edge[i * size : (i + 1) * size], axis=0, keepdims=True
            )
    cumt = cumt_ref[...]
    total = cumt[:, length - 1 : length]
    to_end = jnp.exp(total - cumt)
    step = stept_ref[...]
    own = jnp.concatenate([r[...] for r in st_refs], axis=0)
    excess = jnp.concatenate([r[...] for r in ex_refs], axis=0)
    grad_ref[...] = own / step + to_end * seen
    edge = jnp.exp(total) * jnp.sum(edge_ref[...], axis=1, keepdims=True)
    decay_ref[...] = (
        dot(excess, triangle(length, lambda a, b: a >= b), 1, 0, HI)
        + dot(to_end * step * seen, triangle(length, lambda a, b: a < b), 1, 0, HI)
        + edge
    )


def term_kernel(places, n_columns, *refs):
    columns, pieces = refs[:n_columns], refs[n_columns:-3]
    keep_ref, send_ref, held = refs[-3:]
    pieces = [(p, i) for p in pieces for i in range(p.shape[0])]
    rows = 2 * keep_ref.shape[0]
    core, _, _ = core_and_chip()
    total = None
    for (a, start), (b, i) in zip(places, pieces):
        part = dot(columns[a][start : start + rows, :], b[i], 1, 0)
        total = part if total is None else total + part
    block = keep_ref.shape[0]
    held[0] = total[:block]
    held[1] = total[block:]
    keep_ref[...] = held[core]
    send_ref[...] = held[1 - core].astype(BF16)


def deal_kernel(keep_ref, recv_ref, own_ref, *refs):
    outs, held = refs[:-1], refs[-1]
    place, n_dp = lax.axis_index("dp"), lax.axis_size("dp")
    total = keep_ref[...] + recv_ref[...].astype(F32)
    share = own_ref.shape[0]
    for i in range(n_dp):
        held[i] = total[i * share : (i + 1) * share]
    own_ref[...] = held[place]
    for s, out in enumerate(outs):
        out[...] = held[place ^ (s + 1)].astype(BF16)


def sum_kernel(*refs):
    total = refs[0][...]
    for ref in refs[1:-1]:
        total = total + ref[...].astype(F32)
    refs[-1][...] = total


def expert_kernel(flip, slots, a_ref, b_ref, gate_ref, up_ref, out_ref, rows_ref):
    n_chip = a_ref.shape[0]
    width = rows_ref.shape[1]
    for half, ref in enumerate((a_ref, b_ref)):
        for i in range(n_chip):
            row = (half * n_chip + i) * slots
            for t in range(width // LANES):
                rows_ref[row : row + slots, t * LANES : (t + 1) * LANES] = ref[
                    i, t * slots : (t + 1) * slots, :
                ]
    gate = dot(rows_ref[...], gate_ref[...], 1, 0)
    up = dot(rows_ref[...], up_ref[...], 1, 0)
    weighted = jax.nn.silu(gate) * up
    out_ref[...] = (weighted.T if flip else weighted).astype(BF16)


def expert(a, b, w_gate, w_up, slots, flip, after):
    total = 2 * a.shape[0] * slots
    width, hidden = w_gate.shape
    out = (hidden, total) if flip else (total, hidden)
    return call(
        lambda *refs: expert_kernel(flip, slots, *refs),
        [shape(out, BF16)],
        0.35,
        (a, b, w_gate, w_up),
        after,
        [pltpu.VMEM((total, width), BF16)],
        limit=24,
    )[0]


def down_kernel(n_dp, flip, slots, grad_rows, *refs):
    pieces = refs[:n_dp]
    g_ref, out_ref, token_ref = refs[n_dp:]
    token_ref[...] = jnp.zeros_like(token_ref)
    n_chip = g_ref.shape[0]
    piece = out_ref.shape[1]
    total = None
    for s in range(n_dp):
        columns = []
        for t in range(grad_rows // slots):
            row = s * grad_rows + t * slots
            blocks = [
                g_ref[i, half + row : half + row + slots, :]
                for half in (0, n_dp * grad_rows)
                for i in range(n_chip)
            ]
            columns.append(jnp.concatenate(blocks, axis=0))
        right = jnp.concatenate(columns, axis=1)[:, :piece]
        part = dot(pieces[s][...], right, 1 if flip else 0, 0)
        total = part if total is None else total + part
    out_ref[...] = total.astype(BF16)


def xored(array, axis, mask):
    count = lax.axis_size(axis)
    return lax.ppermute(array, axis, [(i, i ^ mask) for i in range(count)])


def swapped(array):
    return xored(array, "tm", 1)


def chips(arrays):
    return [arrays[0]] + [xored(a, "tm", 2 * s) for s, a in enumerate(arrays) if s]


def gathered(array, axis, count):
    if count == 1:
        return [array]
    far = xored(array, axis, count // 2)
    return gathered(array, axis, count // 2) + gathered(far, axis, count // 2)


def per_device(
    layer_in,
    out_grad,
    w_bc,
    log_decay,
    step,
    saved_states,
    w_gate,
    w_up,
    slot_rows,
    slot_counts,
    slot_gates,
):
    n_dp = lax.axis_size("dp")
    core, chip, n_chip = core_and_chip()
    x = layer_in[0]
    dy = out_grad[0]
    length, width = x.shape
    heads = log_decay.shape[2]
    size = width // heads
    share, columns = w_bc.shape
    half = columns // 2
    ldt = log_decay[0].T
    stept = step[0].T
    h_in = saved_states[0, 0].reshape(width, half)
    capacity = slot_rows.shape[2]
    piece = width // n_dp
    part = width // 2
    many = heads // 2
    flip = w_gate.shape[2] % LANES == 0

    grad_rows = -(-piece // LANES) * capacity
    w_half = lax.dynamic_slice_in_dim(w_bc, core * (share // 2), share // 2, 0)

    in_rows = width // LANES * capacity
    blocks = [1, 1, 2] if n_chip == 4 else [1] * n_chip
    groups = [2, 2] if n_dp == 4 else [1] * n_dp
    cumt, cum, dyt, rows, *deals = call(
        lambda *refs: prep_kernel(len(groups), *refs),
        [
            shape((heads, length), F32),
            shape((length, LANES), F32),
            shape((width + up16(2 * heads), length), BF16),
            shape((in_rows, LANES), BF16),
        ]
        + [shape((k * grad_rows, LANES), BF16) for k in groups],
        1.5,
        (x, dy, ldt, stept, slot_rows[0], slot_counts, slot_gates[0]),
        scratch=[pltpu.VMEM((n_dp, grad_rows, LANES), BF16)],
        fetch=(0, 1, 2, 3),
        limit=60,
    )
    rows_in = chips([rows] * n_chip)
    w_far = xored(w_half, "dp", n_dp // 2)
    mine = gathered(w_half, "dp", n_dp // 2)[1:]
    w_copy = joined([w_far], after=(rows,))
    mine += gathered(w_copy, "dp", n_dp // 2)
    xs, carried, scaled, *xt = call(
        scale_kernel,
        [shape((length, width), BF16), shape((length, half), F32), shape((8, LANES), F32)]
        + [shape((k * width // n_chip, length), BF16) for k in blocks],
        1.5,
        (x, dy, h_in, cumt, cum),
        after=(rows,),
        scratch=[pltpu.VMEM((width, length), BF16)],
        fetch=(0, 1, 2, 3, 4),
        limit=60,
    )
    if n_dp == 4:
        one = (0, grad_rows), (grad_rows, 2 * grad_rows)
        over_2 = xored(deals[1], "dp", 2)
        early = (over_2,)
    else:
        early = ()
        source, spans = deals[:1] + [xored(d, "dp", s + 1) for s, d in enumerate(deals[1:])], None
    other = swapped(stacked(mine, after=(*rows_in[1:4], scaled), cost=1.0))
    w_whole, bc, keep, send = call(
        lambda *refs: project_kernel(n_dp - 1, many, *refs),
        [
            shape((width, columns), BF16),
            shape((length, columns), BF16),
            shape((part + up16(2 * many), half), BF16),
            shape((part + up16(2 * many), half), BF16),
        ],
        1.0,
        (x, dyt, w_bc, *mine, other),
    )
    recv = swapped(send)
    hidden = w_gate.shape[2]
    climbs = [
        call(
            lambda *refs: combine_kernel(many, size, *refs),
            [shape((part + up16(2 * many), half), BF16)],
            0.5,
            (keep, recv),
        )[0]
    ]
    rows_a = stacked(rows_in, after=(climbs[0],))
    rows_b = swapped(rows_a)
    weighted = expert(rows_a, rows_b, w_gate[0], w_up[0], capacity, flip, (climbs[0],))
    if n_chip == 4:
        x_rows = width // n_chip
        over_y = xored(xt[2], "tm", 4)

    parts = 2
    tiles = width // LANES // parts
    dxs, exs, owns = [], [], []
    if n_dp == 4:
        over_1 = xored(joined([deals[0], over_2], (weighted,), [one[1], one[1]]), "dp", 1)
        early += (over_1,)
        source, spans = [deals[0], over_1, over_2, over_1], [one[0], one[0], one[0], one[1]]
    held = (weighted, *early)
    arrived = []
    bit = 1
    while bit < n_chip:
        last = bit * 2 == n_chip
        moves = [(k, k ^ (2 * bit)) for k in range(2 * n_chip)]
        arrived.append(lax.ppermute(climbs[-1], "tm", moves))
        if not last:
            climbs.append(
                call(
                    lambda *refs, bit=bit: climb_kernel(many, size, bit, *refs),
                    [shape((part + up16(2 * many), half), BF16)],
                    0.5,
                    (climbs[-1], arrived[-1]),
                    after=held,
                )[0]
            )
        bit *= 2
    later = (climbs[-1],)
    mixed = jnp.zeros((length, length), F32)
    for i in range(parts):
        dx, mixed, ex, own = call(
            lambda *refs, i=i: intra_kernel(i * tiles, tiles, *refs),
            [
                shape((length, width // parts), F32),
                shape((length, length), F32),
                shape((heads // parts, length), F32),
                shape((heads // parts, length), F32),
            ],
            0.7,
            (x, dy, bc, cumt, cum, h_in, mixed),
            after=later,
            scratch=[pltpu.VMEM((heads, length), F32)],
        )
        dxs.append(dx)
        exs.append(ex)
        owns.append(own)
    db, dc = call(
        close_kernel,
        [shape((length, half), F32), shape((length, half), BF16)],
        0.3,
        (mixed, bc, carried),
    )

    held = (dc,)
    dealt = joined(source, later, spans)
    dealt_all = joined([dealt, swapped(dealt)])
    held += (dealt_all,)
    if n_chip == 4:
        over_x = xored(joined([xt[1], over_y], later, [(0, x_rows), (x_rows, 2 * x_rows)]), "tm", 2)
        columns_in = [xt[0], over_x, over_y]
        places = [(0, 0), (1, 0), (2, 0), (1, x_rows)]
        held += (over_x,)
    else:
        columns_in = chips(xt)
        places = [(i, 0) for i in range(n_chip)]
    far = xored(weighted, "dp", n_dp // 2)
    near = gathered(weighted, "dp", n_dp // 2)
    held += (far, *near[1:])
    r_own, r_send = call(
        lambda *refs: carry_kernel(many, size, len(arrived), *refs),
        [shape((part, half), BF16)] * 2,
        0.5,
        (*arrived, keep, recv),
        after=held,
    )
    r_recv = swapped(r_send)
    fars = gathered(joined([far], (r_own,)), "dp", n_dp // 2)
    d_bc = call(db_kernel, [shape((length, columns), BF16)], 0.3, (xs, r_own, r_recv, db, dc))[0]
    d_bcs = [d_bc.reshape(1, length, columns)]
    if n_chip == 4:
        grads_y = xored(dealt_all, "tm", 4)
    while 2 ** (len(d_bcs) - 1) < n_chip:
        level = 2 ** (len(d_bcs) - 1)
        sent = d_bcs[0] if level == 1 else joined(d_bcs)
        d_bcs.append(xored(sent, "tm", 2 * level))
    both = ()
    if n_chip == 4:
        both = (joined([dealt_all, grads_y], (sent,)),)
        grads_x = xored(both[0], "tm", 2)
        rest = dealt_all.shape[0]
        grads = [dealt_all, grads_x, grads_y, grads_x]
        spans = [(0, rest), (0, rest), (0, rest), (rest, 2 * rest)]
    else:
        grads, spans = chips([dealt_all] * n_chip), None
    d_in, d_decay, d_step, token = call(
        lambda *refs: finish_kernel(parts, *refs),
        [
            shape((length, width), BF16),
            shape((heads, length), F32),
            shape((heads, length), F32),
            shape((8, LANES), F32),
        ],
        1.0,
        (x, bc, cumt, stept, cum, h_in, r_own, r_recv, w_whole, d_bc,
         *dxs, *exs, *owns),
        after=(*fars[1:], *both),
        scratch=[pltpu.VMEM((width, half), BF16), pltpu.VMEM((heads, half), F32)],
    )
    w_rows = width // (2 * n_chip)
    term, term_send = call(
        lambda *refs: term_kernel(places, len(columns_in), *refs),
        [shape((w_rows, columns), F32), shape((w_rows, columns), BF16)],
        0.5,
        (*columns_in, *d_bcs),
        after=(token,),
        scratch=[pltpu.VMEM((2, w_rows, columns), F32)],
    )
    final = call(
        deal_kernel,
        [shape((w_rows // n_dp, columns), F32)]
        + [shape((w_rows // n_dp, columns), BF16)] * (n_dp - 1),
        0.3,
        (term, swapped(term_send)),
        scratch=[pltpu.VMEM((n_dp, w_rows // n_dp, columns), F32)],
    )
    final = [final[0]] + [xored(final[s], "dp", s) for s in reversed(range(1, n_dp))]

    grads = stacked(grads, (term,), spans)
    w_down_grad, done = call(
        lambda *refs: down_kernel(n_dp, flip, capacity, grad_rows, *refs),
        [shape((hidden, piece), BF16), shape((8, LANES), F32)],
        1.0,
        (*near, *fars, grads),
        after=(final[0],),
    )
    w_bc_grad = call(sum_kernel, [shape(final[0].shape, F32)], 0.1, final, (done,))[0]
    return (d_in[None], d_decay.T[None], d_step.T[None], w_bc_grad, w_down_grad[None])


def solution(mesh):
    in_specs = (
        P("dp", "tm", None),
        P("dp", "tm", None),
        P("dp", None),
        P("dp", "tm", None),
        P("dp", "tm", None),
        P("dp", "tm", None, None, None),
        P(None, None, "tm"),
        P(None, None, "tm"),
        P("dp", None, "tm"),
        P("dp", "tm"),
        P("dp", None, "tm"),
    )
    out_specs = (
        P("dp", "tm", None),
        P("dp", "tm", None),
        P("dp", "tm", None),
        P(("tm", "dp"), None),
        P(None, "tm", "dp"),
    )
    return jax.shard_map(
        per_device, mesh=mesh, in_specs=in_specs, out_specs=out_specs, check_vma=False
    )
```

```python
import jax
import jax.numpy as jnp
from jax import lax
from jax.experimental import pallas as pl
from jax.experimental.pallas import tpu as pltpu
from jax.sharding import PartitionSpec as P

HI = lax.Precision.HIGHEST
F32 = jnp.float32
BF16 = jnp.bfloat16
LANES = 128


def dot(a, b, ca, cb, precision=None):
    return lax.dot_general(
        a, b, (((ca,), (cb,)), ((), ())), precision=precision, preferred_element_type=F32
    )


def iota(dims, axis):
    return lax.broadcasted_iota(jnp.int32, dims, axis)


def where_one(mask):
    return jnp.where(mask, 1.0, 0.0)


def triangle(n, keep):
    return where_one(keep(iota((n, n), 0), iota((n, n), 1))).astype(F32)


def halves(values, axis=1):
    high = values.astype(BF16)
    low = (values - high.astype(F32)).astype(BF16)
    return jnp.concatenate([high, low], axis=axis)


def to_lanes(j, size):
    dims = (LANES, LANES)
    one = where_one(iota(dims, 0) == iota(dims, 1) // size + j * (LANES // size)).astype(BF16)
    return jnp.concatenate([one, one], axis=0)


def to_heads(j, heads, size):
    dims = (heads, LANES)
    one = where_one(iota(dims, 0) == iota(dims, 1) // size + j * (LANES // size)).astype(BF16)
    return jnp.concatenate([one, one], axis=1)


def up16(n):
    return -(-n // 16) * 16


def call(kernel, outs, cost, args, after=(), scratch=(), limit=14, fetch=()):
    n_in, n_after, n_out = len(args), len(after), len(outs)
    fetch = tuple(fetch)

    def body(*refs):
        ins = list(refs[:n_in])
        rest = refs[n_in + n_after :]
        if fetch:
            sems = rest[-1]
            held = rest[len(rest) - 1 - len(fetch) : -1]
            rest = rest[: len(rest) - 1 - len(fetch)]
            copies = []
            for i, (index, ref) in enumerate(zip(fetch, held)):
                copies.append(pltpu.make_async_copy(ins[index], ref, sems.at[i]))
                ins[index] = ref
            for copy in copies:
                copy.start()
            for copy in copies:
                copy.wait()
        kernel(*ins, *rest)

    specs = [
        pl.BlockSpec(memory_space=pltpu.HBM if i in fetch else pltpu.VMEM) for i in range(n_in)
    ]
    held = [pltpu.VMEM(args[i].shape, args[i].dtype) for i in fetch]
    if fetch:
        held.append(pltpu.SemaphoreType.DMA((len(fetch),)))
    return pl.pallas_call(
        body,
        out_shape=outs,
        in_specs=specs + [pl.BlockSpec(memory_space=pl.ANY)] * n_after,
        out_specs=[pl.BlockSpec(memory_space=pltpu.VMEM)] * n_out,
        scratch_shapes=list(scratch) + held,
        cost_estimate=pl.CostEstimate(
            flops=int(cost * 3e9), bytes_accessed=1000, transcendentals=0
        ),
        compiler_params=pltpu.CompilerParams(vmem_limit_bytes=limit * 1024 * 1024),
    )(*args, *after)


def shape(dims, kind):
    return jax.ShapeDtypeStruct(dims, kind)


def core_and_chip():
    place = lax.axis_index("tm")
    return lax.rem(place, 2), lax.div(place, 2), lax.axis_size("tm") // 2


def rows_at(index, size, align=16):
    return pl.ds(pl.multiple_of(index * size, align), size)


def picked(x_ref, dy_ref, slot_ref, count_ref, gate_ref, rows_ref, out_refs):
    length, width = x_ref.shape
    slots = slot_ref.shape[1]
    hit = iota((length, slots), 0) == slot_ref[...]
    live = iota((1, slots), 1) < count_ref[...]
    weight = jnp.where(live, gate_ref[...].astype(F32), 0.0)
    rows = dot(where_one(hit).astype(BF16), x_ref[...], 0, 0).astype(BF16)
    for t in range(width // LANES):
        rows_ref[t * slots : (t + 1) * slots, :] = rows[:, t * LANES : (t + 1) * LANES]
    grads = dot(jnp.where(hit, weight, 0.0).astype(BF16), dy_ref[...], 0, 0).astype(BF16)
    held = out_refs[-1]
    n_dp = held.shape[0]
    piece = width // n_dp
    for i in range(n_dp):
        for t, low in enumerate(range(i * piece, (i + 1) * piece, LANES)):
            block = grads[:, low : min(low + LANES, (i + 1) * piece)]
            if block.shape[1] < LANES:
                fill = jnp.zeros((slots, LANES - block.shape[1]), BF16)
                block = jnp.concatenate([block, fill], axis=1)
            held[i, t * slots : (t + 1) * slots, :] = block
    place = lax.axis_index("dp")
    s = 0
    for out in out_refs[:-1]:
        for start in range(0, out.shape[0], held.shape[1]):
            out[start : start + held.shape[1], :] = held[place ^ s]
            s += 1


def high_low(values):
    high = values.astype(BF16).astype(F32)
    return [high, values - high]


def prep_kernel(
    n_deals, x_ref, dy_ref, ldt_ref, stept_ref, slot_ref, count_ref, gate_ref,
    cumt_ref, cum_ref, dyt_ref, rows_ref, *rest,
):
    length, width = x_ref.shape
    heads = ldt_ref.shape[0]
    size = width // heads
    picked(x_ref, dy_ref, slot_ref, count_ref, gate_ref, rows_ref, rest)
    cumt = dot(ldt_ref[...], triangle(length, lambda a, b: a <= b), 1, 0, HI)
    cumt_ref[...] = cumt
    pad = jnp.zeros((LANES - heads, length), F32)
    cum_ref[...] = jnp.concatenate([cumt - jnp.log(stept_ref[...]), pad], axis=0).T
    start = jnp.exp(jnp.concatenate([cumt, pad], axis=0).T)
    table = halves(start)
    for j in range(width // LANES):
        span = slice(j * LANES, (j + 1) * LANES)
        dys = dy_ref[:, span].astype(F32) * dot(table, to_lanes(j, size), 1, 0)
        dyt_ref[span, :] = dys.astype(BF16).T
    decay = jnp.broadcast_to(jnp.exp(cumt[:, length - 1 : length]), (heads, LANES))
    dyt_ref[width : width + 2 * heads, :] = jnp.concatenate(high_low(decay), axis=0).astype(BF16)


def scale_kernel(x_ref, dy_ref, h_ref, cumt_ref, cum_ref, xs_ref, carried_ref, token_ref, *rest):
    outs, xt_ref = rest[:-1], rest[-1]
    length, width = x_ref.shape
    heads = cumt_ref.shape[0]
    size = width // heads
    _, chip, n_chip = core_and_chip()
    pad = jnp.zeros((LANES - heads, length), F32)
    cum = jnp.concatenate([cumt_ref[...], pad], axis=0).T
    into_end = jnp.exp(cum[length - 1 : length] - cum_ref[...])
    table = jnp.concatenate([halves(jnp.exp(cum)), halves(into_end)], axis=0)
    carried = jnp.zeros(carried_ref.shape, F32)
    for j in range(width // LANES):
        span = slice(j * LANES, (j + 1) * LANES)
        scale = dot(table, to_lanes(j, size), 1, 0)
        x_f = x_ref[:, span].astype(F32)
        xt_ref[span, :] = x_ref[:, span].T
        xs_ref[:, span] = (x_f * scale[length:]).astype(BF16)
        dys = (dy_ref[:, span].astype(F32) * scale[:length]).astype(BF16)
        carried = carried + dot(dys, h_ref[span, :], 1, 0)
    carried_ref[...] = carried
    token_ref[...] = jnp.zeros_like(token_ref)
    block = width // n_chip
    s = 0
    for out in outs:
        for start in range(0, out.shape[0], block):
            out[start : start + block, :] = xt_ref[rows_at(chip ^ s, block), :]
            s += 1


def join_kernel(ranges, *refs):
    out, at = refs[-1], 0
    for ref, (start, stop) in zip(refs, ranges):
        out[at : at + stop - start] = ref[start:stop]
        at += stop - start


def joined(arrays, after=(), ranges=None, cost=0.2):
    ranges = ranges or [(0, a.shape[0]) for a in arrays]
    dims = (sum(stop - start for start, stop in ranges), *arrays[0].shape[1:])
    return call(
        lambda *refs: join_kernel(ranges, *refs),
        [shape(dims, arrays[0].dtype)],
        cost,
        tuple(arrays),
        after=after,
    )[0]


def stacked(arrays, after=(), ranges=None, cost=0.2):
    count = len(arrays)
    out = joined(arrays, after, ranges, cost)
    return out.reshape(count, out.shape[0] // count, *out.shape[1:])


def project_kernel(n_mine, many, *refs):
    x_ref, dyt_ref, own_ref = refs[:3]
    mine, other = refs[3 : 3 + n_mine], refs[3 + n_mine]
    w_ref, bc_ref, keep_ref, send_ref = refs[4 + n_mine :]
    core, _, _ = core_and_chip()
    place, n_dp = lax.axis_index("dp"), lax.axis_size("dp")
    share = own_ref.shape[0]
    half = share // 2
    w_ref[rows_at(place, share), :] = own_ref[...]
    for i in range(n_mine):
        source = place ^ (i + 1)
        w_ref[rows_at(source * 2 + core, half), :] = mine[i][...]
        w_ref[rows_at(source * 2 + 1 - core, half), :] = other[i]
    bc = dot(x_ref[...], w_ref[...], 1, 0).astype(BF16)
    bc_ref[...] = bc
    c_rows = bc[:, LANES:]
    width = x_ref.shape[1]
    part = width // 2
    for ref, index in ((keep_ref, core), (send_ref, 1 - core)):
        ref[:part, :] = dot(dyt_ref[rows_at(index, part), :], c_rows, 1, 0).astype(BF16)
        table = dyt_ref[width : width + 4 * many, :].astype(F32)
        quarter = [table[i * many : (i + 1) * many] for i in range(4)]
        high = jnp.where(index == 0, quarter[0], quarter[1])
        low = jnp.where(index == 0, quarter[2], quarter[3])
        fill = jnp.zeros((ref.shape[0] - part - 2 * many, LANES), F32)
        ref[part:, :] = jnp.concatenate([high, low, fill], axis=0).astype(BF16)


def pair(keep_ref, recv_ref, many, size, head):
    core, _, _ = core_and_chip()
    part = many * size
    both = []
    for ref in (keep_ref, recv_ref):
        extra = ref[part:, :].astype(F32)
        decay = extra[head : head + 1] + extra[many + head : many + head + 1]
        both.append((ref[head * size : (head + 1) * size, :].astype(F32), decay))
    first = jax.tree.map(lambda a, b: jnp.where(core == 0, a, b), both[0], both[1])
    second = jax.tree.map(lambda a, b: jnp.where(core == 0, b, a), both[0], both[1])
    return first, second


def payload(ref, many, states, decays):
    size = states[0].shape[0]
    for head, state in enumerate(states):
        ref[head * size : (head + 1) * size, :] = state.astype(BF16)
    decay = jnp.concatenate(decays, axis=0)
    high = decay.astype(BF16).astype(F32)
    fill = jnp.zeros((ref.shape[0] - many * size - 2 * many, LANES), F32)
    extra = jnp.concatenate([high, decay - high, fill], axis=0)
    ref[many * size :, :] = extra.astype(BF16)


def loaded(ref, many, size, head):
    extra = ref[many * size :, :].astype(F32)
    decay = extra[head : head + 1] + extra[many + head : many + head + 1]
    return ref[head * size : (head + 1) * size, :].astype(F32), decay


def combine_kernel(many, size, keep_ref, recv_ref, out_ref):
    states, decays = [], []
    for head in range(many):
        (g0, a0), (g1, a1) = pair(keep_ref, recv_ref, many, size, head)
        states.append(g0 + a0 * g1)
        decays.append(a0 * a1)
    payload(out_ref, many, states, decays)


def pick_side(upper, mine, theirs):
    return jnp.where(upper, theirs, mine), jnp.where(upper, mine, theirs)


def climb_kernel(many, size, bit, mine_ref, recv_ref, out_ref):
    _, chip, _ = core_and_chip()
    upper = lax.rem(lax.div(chip, bit), 2) == 1
    states, decays = [], []
    for head in range(many):
        t_mine, a_mine = loaded(mine_ref, many, size, head)
        t_recv, a_recv = loaded(recv_ref, many, size, head)
        t_low, t_high = pick_side(upper, t_mine, t_recv)
        a_low, a_high = pick_side(upper, a_mine, a_recv)
        states.append(t_low + a_low * t_high)
        decays.append(a_low * a_high)
    payload(out_ref, many, states, decays)


def carry_kernel(many, size, levels, *refs):
    core, chip, _ = core_and_chip()
    recvs = refs[:levels]
    keep_ref, recv_ref, own_ref, send_ref = refs[levels:]
    for head in range(many):
        span = slice(head * size, (head + 1) * size)
        carry, reach = None, None
        for level, ref in enumerate(recvs):
            state, decay = loaded(ref, many, size, head)
            lower = lax.rem(lax.div(chip, 2**level), 2) == 0
            state = jnp.where(lower, state, 0.0)
            decay = jnp.where(lower, decay, 1.0)
            carry = state if carry is None else carry + reach * state
            reach = decay if reach is None else reach * decay
        _, (g1, a1) = pair(keep_ref, recv_ref, many, size, head)
        second = carry
        first = g1 + a1 * second
        own_ref[span, :] = jnp.where(core == 0, first, second).astype(BF16)
        send_ref[span, :] = jnp.where(core == 0, second, first).astype(BF16)


def intra_kernel(
    first, many, x_ref, dy_ref, bc_ref, cumt_ref, cum_ref, h_ref, before_ref,
    dx_ref, mixed_ref, ex_ref, own_ref, rowm_ref,
):
    length, width = x_ref.shape
    heads = cumt_ref.shape[0]
    size = width // heads
    per = LANES // size
    upper = iota((length, length), 0) <= iota((length, length), 1)
    b_rows, c_rows = bc_ref[:, :LANES], bc_ref[:, LANES:]
    scores = dot(b_rows, c_rows, 1, 1)
    lane = iota((1, LANES), 1)
    lane_bf = [where_one(lane // size == i).astype(BF16) for i in range(per)]
    mixed = before_ref[...]
    own = jnp.zeros((length, LANES), F32)
    reach = jnp.zeros((heads, length), F32)
    for j in range(first, first + many):
        span = slice(j * LANES, (j + 1) * LANES)
        out_span = slice((j - first) * LANES, (j - first + 1) * LANES)
        x_p = x_ref[:, span]
        dy_p = dy_ref[:, span]
        dy_h = jnp.concatenate([dy_p * m for m in lane_bf], axis=0)
        cross = dot(x_p, dy_h, 1, 1)
        kern = []
        for i in range(per):
            h = j * per + i
            diff = cumt_ref[h : h + 1, :] - cum_ref[:, h : h + 1]
            seg = jnp.exp(jnp.where(upper, diff, -1e30))
            part = cross[:, i * length : (i + 1) * length]
            mixed = mixed + seg * part
            seg = seg * scores
            kern.append(seg.astype(BF16))
            full = seg * part
            rowm_ref[h : h + 1, :] = jnp.sum(full, axis=0, keepdims=True)
            own = jnp.where(lane == h, jnp.sum(full, axis=1, keepdims=True), own)
        dx_ref[:, out_span] = dot(jnp.concatenate(kern, axis=1), dy_h, 1, 0)
        seen = dy_p.astype(F32) * dot(c_rows, h_ref[span, :], 1, 1)
        reach = reach + dot(to_heads(j, heads, size), halves(seen), 1, 1)
    mixed_ref[...] = mixed
    rows = slice(first * per, (first + many) * per)
    own = own.T[rows]
    own_ref[...] = own
    ex_ref[...] = rowm_ref[rows, :] + jnp.exp(cumt_ref[rows, :]) * reach[rows] - own


def close_kernel(mixed_ref, bc_ref, carried_ref, db_ref, dc_ref):
    mixed = mixed_ref[...].astype(BF16)
    db_ref[...] = dot(mixed, bc_ref[:, LANES:], 1, 0)
    dc_ref[...] = (dot(mixed, bc_ref[:, :LANES], 0, 0) + carried_ref[...]).astype(BF16)


def db_kernel(xs_ref, own_ref, recv_ref, db_ref, dc_ref, out_ref):
    core, _, _ = core_and_chip()
    half = db_ref.shape[1]
    part = own_ref.shape[0]
    total = db_ref[...]
    for ref, index in ((own_ref, core), (recv_ref, 1 - core)):
        total = total + dot(xs_ref[:, rows_at(index, part, LANES)], ref[...], 1, 0)
    out_ref[:, :half] = total.astype(BF16)
    out_ref[:, half:] = dc_ref[...]


def finish_kernel(parts, *refs):
    (x_ref, bc_ref, cumt_ref, stept_ref, cum_ref, h_ref, own_ref, recv_ref,
     w_ref, dbc_ref) = refs[:10]
    dx_refs, ex_refs, st_refs = (refs[10 + i * parts : 10 + (i + 1) * parts] for i in range(3))
    in_ref, decay_ref, grad_ref, token_ref, r_ref, edge_ref = refs[10 + 3 * parts :]
    token_ref[...] = jnp.zeros_like(token_ref)
    core, _, _ = core_and_chip()
    length, width = x_ref.shape
    heads = cumt_ref.shape[0]
    size = width // heads
    part = width // 2
    r_ref[rows_at(core, part), :] = own_ref[...]
    r_ref[rows_at(1 - core, part), :] = recv_ref[...]
    pad = jnp.zeros((LANES - heads, length), F32)
    total = jnp.concatenate([cumt_ref[...], pad], axis=0).T[length - 1 : length]
    table = halves(jnp.exp(total - cum_ref[...]))
    seen = jnp.zeros((heads, length), F32)
    b_rows = bc_ref[:, :LANES]
    d_bc = dbc_ref[...]
    for j in range(width // LANES):
        span = slice(j * LANES, (j + 1) * LANES)
        local = dx_refs[j * LANES // (width // parts)]
        start = j * LANES % (width // parts)
        r_tile = r_ref[span, :]
        reach = dot(b_rows, r_tile, 1, 1)
        d_in = local[:, start : start + LANES] + dot(table, to_lanes(j, size), 1, 0) * reach
        d_in = d_in + dot(d_bc, w_ref[span, :], 1, 1)
        in_ref[:, span] = d_in.astype(BF16)
        product = x_ref[:, span].astype(F32) * reach
        seen = seen + dot(to_heads(j, heads, size), halves(product), 1, 1)
        edge = r_tile.astype(F32) * h_ref[span, :].astype(F32)
        for i in range(LANES // size):
            h = j * (LANES // size) + i
            edge_ref[h : h + 1, :] = jnp.sum(
                edge[i * size : (i + 1) * size], axis=0, keepdims=True
            )
    cumt = cumt_ref[...]
    total = cumt[:, length - 1 : length]
    to_end = jnp.exp(total - cumt)
    step = stept_ref[...]
    own = jnp.concatenate([r[...] for r in st_refs], axis=0)
    excess = jnp.concatenate([r[...] for r in ex_refs], axis=0)
    grad_ref[...] = own / step + to_end * seen
    edge = jnp.exp(total) * jnp.sum(edge_ref[...], axis=1, keepdims=True)
    decay_ref[...] = (
        dot(excess, triangle(length, lambda a, b: a >= b), 1, 0, HI)
        + dot(to_end * step * seen, triangle(length, lambda a, b: a < b), 1, 0, HI)
        + edge
    )


def term_kernel(places, n_columns, *refs):
    columns, pieces = refs[:n_columns], refs[n_columns:-3]
    keep_ref, send_ref, held = refs[-3:]
    pieces = [(p, i) for p in pieces for i in range(p.shape[0])]
    rows = 2 * keep_ref.shape[0]
    core, _, _ = core_and_chip()
    total = None
    for (a, start), (b, i) in zip(places, pieces):
        part = dot(columns[a][start : start + rows, :], b[i], 1, 0)
        total = part if total is None else total + part
    block = keep_ref.shape[0]
    held[0] = total[:block]
    held[1] = total[block:]
    keep_ref[...] = held[core]
    send_ref[...] = held[1 - core].astype(BF16)


def deal_kernel(keep_ref, recv_ref, own_ref, *refs):
    outs, held = refs[:-1], refs[-1]
    place, n_dp = lax.axis_index("dp"), lax.axis_size("dp")
    total = keep_ref[...] + recv_ref[...].astype(F32)
    share = own_ref.shape[0]
    for i in range(n_dp):
        held[i] = total[i * share : (i + 1) * share]
    own_ref[...] = held[place]
    for s, out in enumerate(outs):
        out[...] = held[place ^ (s + 1)].astype(BF16)


def sum_kernel(*refs):
    total = refs[0][...]
    for ref in refs[1:-1]:
        total = total + ref[...].astype(F32)
    refs[-1][...] = total


def expert_kernel(flip, slots, a_ref, b_ref, gate_ref, up_ref, out_ref, rows_ref):
    n_chip = a_ref.shape[0]
    width = rows_ref.shape[1]
    for half, ref in enumerate((a_ref, b_ref)):
        for i in range(n_chip):
            row = (half * n_chip + i) * slots
            for t in range(width // LANES):
                rows_ref[row : row + slots, t * LANES : (t + 1) * LANES] = ref[
                    i, t * slots : (t + 1) * slots, :
                ]
    gate = dot(rows_ref[...], gate_ref[...], 1, 0)
    up = dot(rows_ref[...], up_ref[...], 1, 0)
    weighted = jax.nn.silu(gate) * up
    weighted = weighted.astype(BF16)
    out_ref[...] = weighted.T if flip else weighted


def expert(a, b, w_gate, w_up, slots, flip, after):
    total = 2 * a.shape[0] * slots
    width, hidden = w_gate.shape
    out = (hidden, total) if flip else (total, hidden)
    return call(
        lambda *refs: expert_kernel(flip, slots, *refs),
        [shape(out, BF16)],
        0.35,
        (a, b, w_gate, w_up),
        after,
        [pltpu.VMEM((total, width), BF16)],
        limit=24,
    )[0]


def down_kernel(n_dp, flip, slots, grad_rows, *refs):
    pieces = refs[:n_dp]
    g_ref, out_ref, token_ref = refs[n_dp:]
    token_ref[...] = jnp.zeros_like(token_ref)
    n_chip = g_ref.shape[0]
    piece = out_ref.shape[1]
    total = None
    for s in range(n_dp):
        columns = []
        for t in range(grad_rows // slots):
            row = s * grad_rows + t * slots
            blocks = [
                g_ref[i, half + row : half + row + slots, :]
                for half in (0, n_dp * grad_rows)
                for i in range(n_chip)
            ]
            columns.append(jnp.concatenate(blocks, axis=0))
        right = jnp.concatenate(columns, axis=1)[:, :piece]
        part = dot(pieces[s][...], right, 1 if flip else 0, 0)
        total = part if total is None else total + part
    out_ref[...] = total.astype(BF16)


def xored(array, axis, mask):
    count = lax.axis_size(axis)
    return lax.ppermute(array, axis, [(i, i ^ mask) for i in range(count)])


def swapped(array):
    return xored(array, "tm", 1)


def chips(arrays):
    return [arrays[0]] + [xored(a, "tm", 2 * s) for s, a in enumerate(arrays) if s]


def gathered(array, axis, count):
    if count == 1:
        return [array]
    far = xored(array, axis, count // 2)
    return gathered(array, axis, count // 2) + gathered(far, axis, count // 2)


def per_device(
    layer_in,
    out_grad,
    w_bc,
    log_decay,
    step,
    saved_states,
    w_gate,
    w_up,
    slot_rows,
    slot_counts,
    slot_gates,
):
    n_dp = lax.axis_size("dp")
    core, chip, n_chip = core_and_chip()
    x = layer_in[0]
    dy = out_grad[0]
    length, width = x.shape
    heads = log_decay.shape[2]
    size = width // heads
    share, columns = w_bc.shape
    half = columns // 2
    ldt = log_decay[0].T
    stept = step[0].T
    h_in = saved_states[0, 0].reshape(width, half)
    capacity = slot_rows.shape[2]
    piece = width // n_dp
    part = width // 2
    many = heads // 2
    flip = w_gate.shape[2] % LANES == 0

    grad_rows = -(-piece // LANES) * capacity
    w_half = lax.dynamic_slice_in_dim(w_bc, core * (share // 2), share // 2, 0)

    in_rows = width // LANES * capacity
    blocks = [1, 1, 2] if n_chip == 4 else [1] * n_chip
    groups = [2, 2] if n_dp == 4 else [1] * n_dp
    cumt, cum, dyt, rows, *deals = call(
        lambda *refs: prep_kernel(len(groups), *refs),
        [
            shape((heads, length), F32),
            shape((length, LANES), F32),
            shape((width + up16(2 * heads), length), BF16),
            shape((in_rows, LANES), BF16),
        ]
        + [shape((k * grad_rows, LANES), BF16) for k in groups],
        1.5,
        (x, dy, ldt, stept, slot_rows[0], slot_counts, slot_gates[0]),
        scratch=[pltpu.VMEM((n_dp, grad_rows, LANES), BF16)],
        fetch=(0, 1, 2, 3),
        limit=60,
    )
    rows_in = chips([rows] * n_chip)
    w_far = xored(w_half, "dp", n_dp // 2)
    mine = gathered(w_half, "dp", n_dp // 2)[1:]
    w_copy = joined([w_far], after=(rows,))
    mine += gathered(w_copy, "dp", n_dp // 2)
    xs, carried, scaled, *xt = call(
        scale_kernel,
        [shape((length, width), BF16), shape((length, half), F32), shape((8, LANES), F32)]
        + [shape((k * width // n_chip, length), BF16) for k in blocks],
        1.5,
        (x, dy, h_in, cumt, cum),
        after=(rows,),
        scratch=[pltpu.VMEM((width, length), BF16)],
        fetch=(0, 1, 2, 3, 4),
        limit=60,
    )
    if n_dp == 4:
        one = (0, grad_rows), (grad_rows, 2 * grad_rows)
        over_2 = xored(deals[1], "dp", 2)
        early = (over_2,)
    else:
        early = ()
        source, spans = deals[:1] + [xored(d, "dp", s + 1) for s, d in enumerate(deals[1:])], None
    other = swapped(stacked(mine, after=(*rows_in[1:4], scaled), cost=1.0))
    w_whole, bc, keep, send = call(
        lambda *refs: project_kernel(n_dp - 1, many, *refs),
        [
            shape((width, columns), BF16),
            shape((length, columns), BF16),
            shape((part + up16(2 * many), half), BF16),
            shape((part + up16(2 * many), half), BF16),
        ],
        1.0,
        (x, dyt, w_bc, *mine, other),
    )
    recv = swapped(send)
    hidden = w_gate.shape[2]
    climbs = [
        call(
            lambda *refs: combine_kernel(many, size, *refs),
            [shape((part + up16(2 * many), half), BF16)],
            0.5,
            (keep, recv),
        )[0]
    ]
    rows_a = stacked(rows_in, after=(climbs[0],))
    rows_b = swapped(rows_a)
    weighted = expert(rows_a, rows_b, w_gate[0], w_up[0], capacity, flip, (climbs[0],))
    if n_chip == 4:
        x_rows = width // n_chip
        over_y = xored(xt[2], "tm", 4)

    parts = 2
    tiles = width // LANES // parts
    dxs, exs, owns = [], [], []
    if n_dp == 4:
        over_1 = xored(joined([deals[0], over_2], (weighted,), [one[1], one[1]]), "dp", 1)
        early += (over_1,)
        source, spans = [deals[0], over_1, over_2, over_1], [one[0], one[0], one[0], one[1]]
    held = (weighted, *early)
    arrived = []
    bit = 1
    while bit < n_chip:
        last = bit * 2 == n_chip
        moves = [(k, k ^ (2 * bit)) for k in range(2 * n_chip)]
        arrived.append(lax.ppermute(climbs[-1], "tm", moves))
        if not last:
            climbs.append(
                call(
                    lambda *refs, bit=bit: climb_kernel(many, size, bit, *refs),
                    [shape((part + up16(2 * many), half), BF16)],
                    0.5,
                    (climbs[-1], arrived[-1]),
                    after=held,
                )[0]
            )
        bit *= 2
    later = (climbs[-1],)
    mixed = jnp.zeros((length, length), F32)
    for i in range(parts):
        dx, mixed, ex, own = call(
            lambda *refs, i=i: intra_kernel(i * tiles, tiles, *refs),
            [
                shape((length, width // parts), F32),
                shape((length, length), F32),
                shape((heads // parts, length), F32),
                shape((heads // parts, length), F32),
            ],
            0.7,
            (x, dy, bc, cumt, cum, h_in, mixed),
            after=later,
            scratch=[pltpu.VMEM((heads, length), F32)],
        )
        dxs.append(dx)
        exs.append(ex)
        owns.append(own)
    db, dc = call(
        close_kernel,
        [shape((length, half), F32), shape((length, half), BF16)],
        0.3,
        (mixed, bc, carried),
    )

    held = (dc,)
    dealt = joined(source, later, spans)
    dealt_all = joined([dealt, swapped(dealt)])
    held += (dealt_all,)
    if n_chip == 4:
        over_x = xored(joined([xt[1], over_y], later, [(0, x_rows), (x_rows, 2 * x_rows)]), "tm", 2)
        columns_in = [xt[0], over_x, over_y]
        places = [(0, 0), (1, 0), (2, 0), (1, x_rows)]
        held += (over_x,)
    else:
        columns_in = chips(xt)
        places = [(i, 0) for i in range(n_chip)]
    far = xored(weighted, "dp", n_dp // 2)
    near = gathered(weighted, "dp", n_dp // 2)
    held += (far, *near[1:])
    r_own, r_send = call(
        lambda *refs: carry_kernel(many, size, len(arrived), *refs),
        [shape((part, half), BF16)] * 2,
        0.5,
        (*arrived, keep, recv),
        after=held,
    )
    r_recv = swapped(r_send)
    fars = gathered(joined([far], (r_own,)), "dp", n_dp // 2)
    d_bc = call(db_kernel, [shape((length, columns), BF16)], 0.3, (xs, r_own, r_recv, db, dc))[0]
    d_bcs = [d_bc.reshape(1, length, columns)]
    if n_chip == 4:
        grads_y = xored(dealt_all, "tm", 4)
    while 2 ** (len(d_bcs) - 1) < n_chip:
        level = 2 ** (len(d_bcs) - 1)
        sent = d_bcs[0] if level == 1 else joined(d_bcs)
        d_bcs.append(xored(sent, "tm", 2 * level))
    both = ()
    if n_chip == 4:
        both = (joined([dealt_all, grads_y], (sent,)),)
        grads_x = xored(both[0], "tm", 2)
        rest = dealt_all.shape[0]
        grads = [dealt_all, grads_x, grads_y, grads_x]
        spans = [(0, rest), (0, rest), (0, rest), (rest, 2 * rest)]
    else:
        grads, spans = chips([dealt_all] * n_chip), None
    d_in, d_decay, d_step, token = call(
        lambda *refs: finish_kernel(parts, *refs),
        [
            shape((length, width), BF16),
            shape((heads, length), F32),
            shape((heads, length), F32),
            shape((8, LANES), F32),
        ],
        1.0,
        (x, bc, cumt, stept, cum, h_in, r_own, r_recv, w_whole, d_bc,
         *dxs, *exs, *owns),
        after=(*fars[1:], *both),
        scratch=[pltpu.VMEM((width, half), BF16), pltpu.VMEM((heads, half), F32)],
    )
    w_rows = width // (2 * n_chip)
    term, term_send = call(
        lambda *refs: term_kernel(places, len(columns_in), *refs),
        [shape((w_rows, columns), F32), shape((w_rows, columns), BF16)],
        0.5,
        (*columns_in, *d_bcs),
        after=(token,),
        scratch=[pltpu.VMEM((2, w_rows, columns), F32)],
    )
    final = call(
        deal_kernel,
        [shape((w_rows // n_dp, columns), F32)]
        + [shape((w_rows // n_dp, columns), BF16)] * (n_dp - 1),
        0.3,
        (term, swapped(term_send)),
        scratch=[pltpu.VMEM((n_dp, w_rows // n_dp, columns), F32)],
    )
    final = [final[0]] + [xored(final[s], "dp", s) for s in reversed(range(1, n_dp))]

    grads = stacked(grads, (term,), spans)
    w_down_grad, done = call(
        lambda *refs: down_kernel(n_dp, flip, capacity, grad_rows, *refs),
        [shape((hidden, piece), BF16), shape((8, LANES), F32)],
        1.0,
        (*near, *fars, grads),
        after=(final[0],),
    )
    w_bc_grad = call(sum_kernel, [shape(final[0].shape, F32)], 0.1, final, (done,))[0]
    return (d_in[None], d_decay.T[None], d_step.T[None], w_bc_grad, w_down_grad[None])


def solution(mesh):
    in_specs = (
        P("dp", "tm", None),
        P("dp", "tm", None),
        P("dp", None),
        P("dp", "tm", None),
        P("dp", "tm", None),
        P("dp", "tm", None, None, None),
        P(None, None, "tm"),
        P(None, None, "tm"),
        P("dp", None, "tm"),
        P("dp", "tm"),
        P("dp", None, "tm"),
    )
    out_specs = (
        P("dp", "tm", None),
        P("dp", "tm", None),
        P("dp", "tm", None),
        P(("tm", "dp"), None),
        P(None, "tm", "dp"),
    )
    return jax.shard_map(
        per_device, mesh=mesh, in_specs=in_specs, out_specs=out_specs, check_vma=False
    )
```

```python
import jax
import jax.numpy as jnp
from jax import lax
from jax.experimental import pallas as pl
from jax.experimental.pallas import tpu as pltpu
from jax.sharding import PartitionSpec as P

HI = lax.Precision.HIGHEST
F32 = jnp.float32
BF16 = jnp.bfloat16
LANES = 128


def dot(a, b, ca, cb, precision=None):
    return lax.dot_general(
        a, b, (((ca,), (cb,)), ((), ())), precision=precision, preferred_element_type=F32
    )


def iota(dims, axis):
    return lax.broadcasted_iota(jnp.int32, dims, axis)


def where_one(mask):
    return jnp.where(mask, 1.0, 0.0)


def triangle(n, keep):
    return where_one(keep(iota((n, n), 0), iota((n, n), 1))).astype(F32)


def halves(values, axis=1):
    high = values.astype(BF16)
    low = (values - high.astype(F32)).astype(BF16)
    return jnp.concatenate([high, low], axis=axis)


def to_lanes(j, size):
    dims = (LANES, LANES)
    one = where_one(iota(dims, 0) == iota(dims, 1) // size + j * (LANES // size)).astype(BF16)
    return jnp.concatenate([one, one], axis=0)


def to_heads(j, heads, size):
    dims = (heads, LANES)
    one = where_one(iota(dims, 0) == iota(dims, 1) // size + j * (LANES // size)).astype(BF16)
    return jnp.concatenate([one, one], axis=1)


def up16(n):
    return -(-n // 16) * 16


def call(kernel, outs, cost, args, after=(), scratch=(), limit=14, fetch=()):
    n_in, n_after, n_out = len(args), len(after), len(outs)
    fetch = tuple(fetch)

    def body(*refs):
        ins = list(refs[:n_in])
        rest = refs[n_in + n_after :]
        if fetch:
            sems = rest[-1]
            held = rest[len(rest) - 1 - len(fetch) : -1]
            rest = rest[: len(rest) - 1 - len(fetch)]
            copies = []
            for i, (index, ref) in enumerate(zip(fetch, held)):
                copies.append(pltpu.make_async_copy(ins[index], ref, sems.at[i]))
                ins[index] = ref
            for copy in copies:
                copy.start()
            for copy in copies:
                copy.wait()
        kernel(*ins, *rest)

    specs = [
        pl.BlockSpec(memory_space=pltpu.HBM if i in fetch else pltpu.VMEM) for i in range(n_in)
    ]
    held = [pltpu.VMEM(args[i].shape, args[i].dtype) for i in fetch]
    if fetch:
        held.append(pltpu.SemaphoreType.DMA((len(fetch),)))
    return pl.pallas_call(
        body,
        out_shape=outs,
        in_specs=specs + [pl.BlockSpec(memory_space=pl.ANY)] * n_after,
        out_specs=[pl.BlockSpec(memory_space=pltpu.VMEM)] * n_out,
        scratch_shapes=list(scratch) + held,
        cost_estimate=pl.CostEstimate(
            flops=int(cost * 3e9), bytes_accessed=1000, transcendentals=0
        ),
        compiler_params=pltpu.CompilerParams(vmem_limit_bytes=limit * 1024 * 1024),
    )(*args, *after)


def shape(dims, kind):
    return jax.ShapeDtypeStruct(dims, kind)


def core_and_chip():
    place = lax.axis_index("tm")
    return lax.rem(place, 2), lax.div(place, 2), lax.axis_size("tm") // 2


def rows_at(index, size, align=16):
    return pl.ds(pl.multiple_of(index * size, align), size)


def picked(x_ref, dy_ref, slot_ref, count_ref, gate_ref, rows_ref, out_refs):
    length, width = x_ref.shape
    slots = slot_ref.shape[1]
    hit = iota((length, slots), 0) == slot_ref[...]
    live = iota((1, slots), 1) < count_ref[...]
    weight = jnp.where(live, gate_ref[...].astype(F32), 0.0)
    rows = dot(where_one(hit).astype(BF16), x_ref[...], 0, 0).astype(BF16)
    for t in range(width // LANES):
        rows_ref[t * slots : (t + 1) * slots, :] = rows[:, t * LANES : (t + 1) * LANES]
    grads = dot(jnp.where(hit, weight, 0.0).astype(BF16), dy_ref[...], 0, 0).astype(BF16)
    held = out_refs[-1]
    n_dp = held.shape[0]
    piece = width // n_dp
    for i in range(n_dp):
        for t, low in enumerate(range(i * piece, (i + 1) * piece, LANES)):
            block = grads[:, low : min(low + LANES, (i + 1) * piece)]
            if block.shape[1] < LANES:
                fill = jnp.zeros((slots, LANES - block.shape[1]), BF16)
                block = jnp.concatenate([block, fill], axis=1)
            held[i, t * slots : (t + 1) * slots, :] = block
    place = lax.axis_index("dp")
    s = 0
    for out in out_refs[:-1]:
        for start in range(0, out.shape[0], held.shape[1]):
            out[start : start + held.shape[1], :] = held[place ^ s]
            s += 1


def high_low(values):
    high = values.astype(BF16).astype(F32)
    return [high, values - high]


def prep_kernel(
    n_deals, x_ref, dy_ref, ldt_ref, stept_ref, slot_ref, count_ref, gate_ref,
    cumt_ref, cum_ref, dyt_ref, rows_ref, *rest,
):
    length, width = x_ref.shape
    heads = ldt_ref.shape[0]
    size = width // heads
    picked(x_ref, dy_ref, slot_ref, count_ref, gate_ref, rows_ref, rest)
    cumt = dot(ldt_ref[...], triangle(length, lambda a, b: a <= b), 1, 0, HI)
    cumt_ref[...] = cumt
    pad = jnp.zeros((LANES - heads, length), F32)
    cum_ref[...] = jnp.concatenate([cumt - jnp.log(stept_ref[...]), pad], axis=0).T
    start = jnp.exp(jnp.concatenate([cumt, pad], axis=0).T)
    table = halves(start)
    for j in range(width // LANES):
        span = slice(j * LANES, (j + 1) * LANES)
        dys = dy_ref[:, span].astype(F32) * dot(table, to_lanes(j, size), 1, 0)
        dyt_ref[span, :] = dys.astype(BF16).T
    decay = jnp.broadcast_to(jnp.exp(cumt[:, length - 1 : length]), (heads, LANES))
    dyt_ref[width : width + 2 * heads, :] = jnp.concatenate(high_low(decay), axis=0).astype(BF16)


def scale_kernel(x_ref, cumt_ref, cum_ref, xs_ref, token_ref, *rest):
    outs, xt_ref = rest[:-1], rest[-1]
    length, width = x_ref.shape
    heads = cumt_ref.shape[0]
    size = width // heads
    _, chip, n_chip = core_and_chip()
    pad = jnp.zeros((LANES - heads, length), F32)
    cum = jnp.concatenate([cumt_ref[...], pad], axis=0).T
    into_end = jnp.exp(cum[length - 1 : length] - cum_ref[...])
    table = halves(into_end)
    for j in range(width // LANES):
        span = slice(j * LANES, (j + 1) * LANES)
        scale = dot(table, to_lanes(j, size), 1, 0)
        xt_ref[span, :] = x_ref[:, span].T
        xs_ref[:, span] = (x_ref[:, span].astype(F32) * scale).astype(BF16)
    token_ref[...] = jnp.zeros_like(token_ref)
    block = width // n_chip
    s = 0
    for out in outs:
        for start in range(0, out.shape[0], block):
            out[start : start + block, :] = xt_ref[rows_at(chip ^ s, block), :]
            s += 1


def join_kernel(ranges, *refs):
    out, at = refs[-1], 0
    for ref, (start, stop) in zip(refs, ranges):
        out[at : at + stop - start] = ref[start:stop]
        at += stop - start


def joined(arrays, after=(), ranges=None, cost=0.2):
    ranges = ranges or [(0, a.shape[0]) for a in arrays]
    dims = (sum(stop - start for start, stop in ranges), *arrays[0].shape[1:])
    return call(
        lambda *refs: join_kernel(ranges, *refs),
        [shape(dims, arrays[0].dtype)],
        cost,
        tuple(arrays),
        after=after,
    )[0]


def stacked(arrays, after=(), ranges=None, cost=0.2):
    count = len(arrays)
    out = joined(arrays, after, ranges, cost)
    return out.reshape(count, out.shape[0] // count, *out.shape[1:])


def project_kernel(n_mine, many, *refs):
    x_ref, dyt_ref, own_ref = refs[:3]
    mine, other = refs[3 : 3 + n_mine], refs[3 + n_mine]
    w_ref, bc_ref, keep_ref, send_ref = refs[4 + n_mine :]
    core, _, _ = core_and_chip()
    place, n_dp = lax.axis_index("dp"), lax.axis_size("dp")
    share = own_ref.shape[0]
    half = share // 2
    w_ref[rows_at(place, share), :] = own_ref[...]
    for i in range(n_mine):
        source = place ^ (i + 1)
        w_ref[rows_at(source * 2 + core, half), :] = mine[i][...]
        w_ref[rows_at(source * 2 + 1 - core, half), :] = other[i]
    bc = dot(x_ref[...], w_ref[...], 1, 0).astype(BF16)
    bc_ref[...] = bc
    c_rows = bc[:, LANES:]
    width = x_ref.shape[1]
    part = width // 2
    for ref, index in ((keep_ref, core), (send_ref, 1 - core)):
        ref[:part, :] = dot(dyt_ref[rows_at(index, part), :], c_rows, 1, 0).astype(BF16)
        table = dyt_ref[width : width + 4 * many, :].astype(F32)
        quarter = [table[i * many : (i + 1) * many] for i in range(4)]
        high = jnp.where(index == 0, quarter[0], quarter[1])
        low = jnp.where(index == 0, quarter[2], quarter[3])
        fill = jnp.zeros((ref.shape[0] - part - 2 * many, LANES), F32)
        ref[part:, :] = jnp.concatenate([high, low, fill], axis=0).astype(BF16)


def pair(keep_ref, recv_ref, many, size, head):
    core, _, _ = core_and_chip()
    part = many * size
    both = []
    for ref in (keep_ref, recv_ref):
        extra = ref[part:, :].astype(F32)
        decay = extra[head : head + 1] + extra[many + head : many + head + 1]
        both.append((ref[head * size : (head + 1) * size, :].astype(F32), decay))
    first = jax.tree.map(lambda a, b: jnp.where(core == 0, a, b), both[0], both[1])
    second = jax.tree.map(lambda a, b: jnp.where(core == 0, b, a), both[0], both[1])
    return first, second


def payload(ref, many, states, decays):
    size = states[0].shape[0]
    for head, state in enumerate(states):
        ref[head * size : (head + 1) * size, :] = state.astype(BF16)
    decay = jnp.concatenate(decays, axis=0)
    high = decay.astype(BF16).astype(F32)
    fill = jnp.zeros((ref.shape[0] - many * size - 2 * many, LANES), F32)
    extra = jnp.concatenate([high, decay - high, fill], axis=0)
    ref[many * size :, :] = extra.astype(BF16)


def loaded(ref, many, size, head):
    extra = ref[many * size :, :].astype(F32)
    decay = extra[head : head + 1] + extra[many + head : many + head + 1]
    return ref[head * size : (head + 1) * size, :].astype(F32), decay


def combine_kernel(many, size, keep_ref, recv_ref, out_ref):
    states, decays = [], []
    for head in range(many):
        (g0, a0), (g1, a1) = pair(keep_ref, recv_ref, many, size, head)
        states.append(g0 + a0 * g1)
        decays.append(a0 * a1)
    payload(out_ref, many, states, decays)


def pick_side(upper, mine, theirs):
    return jnp.where(upper, theirs, mine), jnp.where(upper, mine, theirs)


def climb_kernel(many, size, bit, mine_ref, recv_ref, out_ref):
    _, chip, _ = core_and_chip()
    upper = lax.rem(lax.div(chip, bit), 2) == 1
    states, decays = [], []
    for head in range(many):
        t_mine, a_mine = loaded(mine_ref, many, size, head)
        t_recv, a_recv = loaded(recv_ref, many, size, head)
        t_low, t_high = pick_side(upper, t_mine, t_recv)
        a_low, a_high = pick_side(upper, a_mine, a_recv)
        states.append(t_low + a_low * t_high)
        decays.append(a_low * a_high)
    payload(out_ref, many, states, decays)


def carry_kernel(many, size, levels, *refs):
    core, chip, _ = core_and_chip()
    recvs = refs[:levels]
    keep_ref, recv_ref, own_ref, send_ref = refs[levels:]
    for head in range(many):
        span = slice(head * size, (head + 1) * size)
        carry, reach = None, None
        for level, ref in enumerate(recvs):
            state, decay = loaded(ref, many, size, head)
            lower = lax.rem(lax.div(chip, 2**level), 2) == 0
            state = jnp.where(lower, state, 0.0)
            decay = jnp.where(lower, decay, 1.0)
            carry = state if carry is None else carry + reach * state
            reach = decay if reach is None else reach * decay
        _, (g1, a1) = pair(keep_ref, recv_ref, many, size, head)
        second = carry
        first = g1 + a1 * second
        own_ref[span, :] = jnp.where(core == 0, first, second).astype(BF16)
        send_ref[span, :] = jnp.where(core == 0, second, first).astype(BF16)


def intra_kernel(
    first, many, x_ref, dy_ref, bc_ref, cumt_ref, cum_ref, h_ref, before_ref,
    dx_ref, mixed_ref, ex_ref, own_ref, rowm_ref,
):
    length, width = x_ref.shape
    heads = cumt_ref.shape[0]
    size = width // heads
    per = LANES // size
    upper = iota((length, length), 0) <= iota((length, length), 1)
    b_rows, c_rows = bc_ref[:, :LANES], bc_ref[:, LANES:]
    scores = dot(b_rows, c_rows, 1, 1)
    lane = iota((1, LANES), 1)
    lane_bf = [where_one(lane // size == i).astype(BF16) for i in range(per)]
    mixed = before_ref[...]
    own = jnp.zeros((length, LANES), F32)
    reach = jnp.zeros((heads, length), F32)
    for j in range(first, first + many):
        span = slice(j * LANES, (j + 1) * LANES)
        out_span = slice((j - first) * LANES, (j - first + 1) * LANES)
        x_p = x_ref[:, span]
        dy_p = dy_ref[:, span]
        dy_h = jnp.concatenate([dy_p * m for m in lane_bf], axis=0)
        cross = dot(x_p, dy_h, 1, 1)
        kern = []
        for i in range(per):
            h = j * per + i
            diff = cumt_ref[h : h + 1, :] - cum_ref[:, h : h + 1]
            seg = jnp.exp(jnp.where(upper, diff, -1e30))
            part = cross[:, i * length : (i + 1) * length]
            mixed = mixed + seg * part
            seg = seg * scores
            kern.append(seg.astype(BF16))
            full = seg * part
            rowm_ref[h : h + 1, :] = jnp.sum(full, axis=0, keepdims=True)
            own = jnp.where(lane == h, jnp.sum(full, axis=1, keepdims=True), own)
        dx_ref[:, out_span] = dot(jnp.concatenate(kern, axis=1), dy_h, 1, 0)
        seen = dy_p.astype(F32) * dot(c_rows, h_ref[span, :], 1, 1)
        reach = reach + dot(to_heads(j, heads, size), halves(seen), 1, 1)
    mixed_ref[...] = mixed
    rows = slice(first * per, (first + many) * per)
    own = own.T[rows]
    own_ref[...] = own
    ex_ref[...] = rowm_ref[rows, :] + jnp.exp(cumt_ref[rows, :]) * reach[rows] - own


def close_kernel(mixed_ref, bc_ref, dyt_ref, h_ref, db_ref, dc_ref):
    carried = dot(dyt_ref[: h_ref.shape[0], :], h_ref[...], 0, 0)
    mixed = mixed_ref[...].astype(BF16)
    db_ref[...] = dot(mixed, bc_ref[:, LANES:], 1, 0)
    dc_ref[...] = (dot(mixed, bc_ref[:, :LANES], 0, 0) + carried).astype(BF16)


def db_kernel(xs_ref, own_ref, recv_ref, db_ref, dc_ref, out_ref):
    core, _, _ = core_and_chip()
    half = db_ref.shape[1]
    part = own_ref.shape[0]
    total = db_ref[...]
    for ref, index in ((own_ref, core), (recv_ref, 1 - core)):
        total = total + dot(xs_ref[:, rows_at(index, part, LANES)], ref[...], 1, 0)
    out_ref[:, :half] = total.astype(BF16)
    out_ref[:, half:] = dc_ref[...]


def finish_kernel(parts, *refs):
    (x_ref, bc_ref, cumt_ref, stept_ref, cum_ref, h_ref, own_ref, recv_ref,
     w_ref, dbc_ref) = refs[:10]
    dx_refs, ex_refs, st_refs = (refs[10 + i * parts : 10 + (i + 1) * parts] for i in range(3))
    in_ref, decay_ref, grad_ref, token_ref, r_ref, edge_ref = refs[10 + 3 * parts :]
    token_ref[...] = jnp.zeros_like(token_ref)
    core, _, _ = core_and_chip()
    length, width = x_ref.shape
    heads = cumt_ref.shape[0]
    size = width // heads
    part = width // 2
    r_ref[rows_at(core, part), :] = own_ref[...]
    r_ref[rows_at(1 - core, part), :] = recv_ref[...]
    pad = jnp.zeros((LANES - heads, length), F32)
    total = jnp.concatenate([cumt_ref[...], pad], axis=0).T[length - 1 : length]
    table = halves(jnp.exp(total - cum_ref[...]))
    seen = jnp.zeros((heads, length), F32)
    b_rows = bc_ref[:, :LANES]
    d_bc = dbc_ref[...]
    for j in range(width // LANES):
        span = slice(j * LANES, (j + 1) * LANES)
        local = dx_refs[j * LANES // (width // parts)]
        start = j * LANES % (width // parts)
        r_tile = r_ref[span, :]
        reach = dot(b_rows, r_tile, 1, 1)
        d_in = local[:, start : start + LANES] + dot(table, to_lanes(j, size), 1, 0) * reach
        d_in = d_in + dot(d_bc, w_ref[span, :], 1, 1)
        in_ref[:, span] = d_in.astype(BF16)
        product = x_ref[:, span].astype(F32) * reach
        seen = seen + dot(to_heads(j, heads, size), halves(product), 1, 1)
        edge = r_tile.astype(F32) * h_ref[span, :].astype(F32)
        for i in range(LANES // size):
            h = j * (LANES // size) + i
            edge_ref[h : h + 1, :] = jnp.sum(
                edge[i * size : (i + 1) * size], axis=0, keepdims=True
            )
    cumt = cumt_ref[...]
    total = cumt[:, length - 1 : length]
    to_end = jnp.exp(total - cumt)
    step = stept_ref[...]
    own = jnp.concatenate([r[...] for r in st_refs], axis=0)
    excess = jnp.concatenate([r[...] for r in ex_refs], axis=0)
    grad_ref[...] = own / step + to_end * seen
    edge = jnp.exp(total) * jnp.sum(edge_ref[...], axis=1, keepdims=True)
    decay_ref[...] = (
        dot(excess, triangle(length, lambda a, b: a >= b), 1, 0, HI)
        + dot(to_end * step * seen, triangle(length, lambda a, b: a < b), 1, 0, HI)
        + edge
    )


def term_kernel(places, n_columns, *refs):
    columns, pieces = refs[:n_columns], refs[n_columns:-3]
    keep_ref, send_ref, held = refs[-3:]
    pieces = [(p, i) for p in pieces for i in range(p.shape[0])]
    rows = 2 * keep_ref.shape[0]
    core, _, _ = core_and_chip()
    total = None
    for (a, start), (b, i) in zip(places, pieces):
        part = dot(columns[a][start : start + rows, :], b[i], 1, 0)
        total = part if total is None else total + part
    block = keep_ref.shape[0]
    held[0] = total[:block]
    held[1] = total[block:]
    keep_ref[...] = held[core]
    send_ref[...] = held[1 - core].astype(BF16)


def deal_kernel(keep_ref, recv_ref, own_ref, *refs):
    outs, held = refs[:-1], refs[-1]
    place, n_dp = lax.axis_index("dp"), lax.axis_size("dp")
    total = keep_ref[...] + recv_ref[...].astype(F32)
    share = own_ref.shape[0]
    for i in range(n_dp):
        held[i] = total[i * share : (i + 1) * share]
    own_ref[...] = held[place]
    for s, out in enumerate(outs):
        out[...] = held[place ^ (s + 1)].astype(BF16)


def sum_kernel(*refs):
    total = refs[0][...]
    for ref in refs[1:-1]:
        total = total + ref[...].astype(F32)
    refs[-1][...] = total


def expert_kernel(flip, slots, a_ref, b_ref, gate_ref, up_ref, out_ref, rows_ref):
    n_chip = a_ref.shape[0]
    width = rows_ref.shape[1]
    for half, ref in enumerate((a_ref, b_ref)):
        for i in range(n_chip):
            row = (half * n_chip + i) * slots
            for t in range(width // LANES):
                rows_ref[row : row + slots, t * LANES : (t + 1) * LANES] = ref[
                    i, t * slots : (t + 1) * slots, :
                ]
    gate = dot(rows_ref[...], gate_ref[...], 1, 0)
    up = dot(rows_ref[...], up_ref[...], 1, 0)
    weighted = jax.nn.silu(gate) * up
    weighted = weighted.astype(BF16)
    out_ref[...] = weighted.T if flip else weighted


def expert(a, b, w_gate, w_up, slots, flip, after):
    total = 2 * a.shape[0] * slots
    width, hidden = w_gate.shape
    out = (hidden, total) if flip else (total, hidden)
    return call(
        lambda *refs: expert_kernel(flip, slots, *refs),
        [shape(out, BF16)],
        0.35,
        (a, b, w_gate, w_up),
        after,
        [pltpu.VMEM((total, width), BF16)],
        limit=24,
    )[0]


def down_kernel(n_dp, flip, slots, grad_rows, *refs):
    pieces = refs[:n_dp]
    g_ref, out_ref, token_ref = refs[n_dp:]
    token_ref[...] = jnp.zeros_like(token_ref)
    n_chip = g_ref.shape[0]
    piece = out_ref.shape[1]
    total = None
    for s in range(n_dp):
        columns = []
        for t in range(grad_rows // slots):
            row = s * grad_rows + t * slots
            blocks = [
                g_ref[i, half + row : half + row + slots, :]
                for half in (0, n_dp * grad_rows)
                for i in range(n_chip)
            ]
            columns.append(jnp.concatenate(blocks, axis=0))
        right = jnp.concatenate(columns, axis=1)[:, :piece]
        part = dot(pieces[s][...], right, 1 if flip else 0, 0)
        total = part if total is None else total + part
    out_ref[...] = total.astype(BF16)


def xored(array, axis, mask):
    count = lax.axis_size(axis)
    return lax.ppermute(array, axis, [(i, i ^ mask) for i in range(count)])


def swapped(array):
    return xored(array, "tm", 1)


def chips(arrays):
    return [arrays[0]] + [xored(a, "tm", 2 * s) for s, a in enumerate(arrays) if s]


def gathered(array, axis, count):
    if count == 1:
        return [array]
    far = xored(array, axis, count // 2)
    return gathered(array, axis, count // 2) + gathered(far, axis, count // 2)


def per_device(
    layer_in,
    out_grad,
    w_bc,
    log_decay,
    step,
    saved_states,
    w_gate,
    w_up,
    slot_rows,
    slot_counts,
    slot_gates,
):
    n_dp = lax.axis_size("dp")
    core, chip, n_chip = core_and_chip()
    x = layer_in[0]
    dy = out_grad[0]
    length, width = x.shape
    heads = log_decay.shape[2]
    size = width // heads
    share, columns = w_bc.shape
    half = columns // 2
    ldt = log_decay[0].T
    stept = step[0].T
    h_in = saved_states[0, 0].reshape(width, half)
    capacity = slot_rows.shape[2]
    piece = width // n_dp
    part = width // 2
    many = heads // 2
    flip = w_gate.shape[2] % LANES == 0

    grad_rows = -(-piece // LANES) * capacity
    w_half = lax.dynamic_slice_in_dim(w_bc, core * (share // 2), share // 2, 0)

    in_rows = width // LANES * capacity
    blocks = [1, 1, 2] if n_chip == 4 else [1] * n_chip
    groups = [2, 2] if n_dp == 4 else [1] * n_dp
    cumt, cum, dyt, rows, *deals = call(
        lambda *refs: prep_kernel(len(groups), *refs),
        [
            shape((heads, length), F32),
            shape((length, LANES), F32),
            shape((width + up16(2 * heads), length), BF16),
            shape((in_rows, LANES), BF16),
        ]
        + [shape((k * grad_rows, LANES), BF16) for k in groups],
        1.5,
        (x, dy, ldt, stept, slot_rows[0], slot_counts, slot_gates[0]),
        scratch=[pltpu.VMEM((n_dp, grad_rows, LANES), BF16)],
        fetch=(0, 1, 2, 3),
        limit=60,
    )
    rows_in = chips([rows] * n_chip)
    w_far = xored(w_half, "dp", n_dp // 2)
    mine = gathered(w_half, "dp", n_dp // 2)[1:]
    w_copy = joined([w_far], after=(rows,))
    mine += gathered(w_copy, "dp", n_dp // 2)
    xs, scaled, *xt = call(
        scale_kernel,
        [shape((length, width), BF16), shape((8, LANES), F32)]
        + [shape((k * width // n_chip, length), BF16) for k in blocks],
        1.5,
        (x, cumt, cum),
        after=(rows,),
        scratch=[pltpu.VMEM((width, length), BF16)],
        fetch=(0, 1, 2),
        limit=60,
    )
    if n_dp == 4:
        one = (0, grad_rows), (grad_rows, 2 * grad_rows)
        over_2 = xored(deals[1], "dp", 2)
        early = (over_2,)
    else:
        early = ()
        source, spans = deals[:1] + [xored(d, "dp", s + 1) for s, d in enumerate(deals[1:])], None
    other = swapped(stacked(mine, after=(*rows_in[1:4], scaled), cost=1.0))
    w_whole, bc, keep, send = call(
        lambda *refs: project_kernel(n_dp - 1, many, *refs),
        [
            shape((width, columns), BF16),
            shape((length, columns), BF16),
            shape((part + up16(2 * many), half), BF16),
            shape((part + up16(2 * many), half), BF16),
        ],
        1.0,
        (x, dyt, w_bc, *mine, other),
    )
    recv = swapped(send)
    hidden = w_gate.shape[2]
    climbs = [
        call(
            lambda *refs: combine_kernel(many, size, *refs),
            [shape((part + up16(2 * many), half), BF16)],
            0.5,
            (keep, recv),
        )[0]
    ]
    rows_a = stacked(rows_in, after=(climbs[0],))
    rows_b = swapped(rows_a)
    weighted = expert(rows_a, rows_b, w_gate[0], w_up[0], capacity, flip, (climbs[0],))
    if n_chip == 4:
        x_rows = width // n_chip
        over_y = xored(xt[2], "tm", 4)

    parts = 2
    tiles = width // LANES // parts
    dxs, exs, owns = [], [], []
    if n_dp == 4:
        over_1 = xored(joined([deals[0], over_2], (weighted,), [one[1], one[1]]), "dp", 1)
        early += (over_1,)
        source, spans = [deals[0], over_1, over_2, over_1], [one[0], one[0], one[0], one[1]]
    held = (weighted, *early)
    arrived = []
    bit = 1
    while bit < n_chip:
        last = bit * 2 == n_chip
        moves = [(k, k ^ (2 * bit)) for k in range(2 * n_chip)]
        arrived.append(lax.ppermute(climbs[-1], "tm", moves))
        if not last:
            climbs.append(
                call(
                    lambda *refs, bit=bit: climb_kernel(many, size, bit, *refs),
                    [shape((part + up16(2 * many), half), BF16)],
                    0.5,
                    (climbs[-1], arrived[-1]),
                    after=held,
                )[0]
            )
        bit *= 2
    later = (climbs[-1],)
    mixed = jnp.zeros((length, length), F32)
    for i in range(parts):
        dx, mixed, ex, own = call(
            lambda *refs, i=i: intra_kernel(i * tiles, tiles, *refs),
            [
                shape((length, width // parts), F32),
                shape((length, length), F32),
                shape((heads // parts, length), F32),
                shape((heads // parts, length), F32),
            ],
            0.7,
            (x, dy, bc, cumt, cum, h_in, mixed),
            after=later,
            scratch=[pltpu.VMEM((heads, length), F32)],
        )
        dxs.append(dx)
        exs.append(ex)
        owns.append(own)
    db, dc = call(
        close_kernel,
        [shape((length, half), F32), shape((length, half), BF16)],
        0.3,
        (mixed, bc, dyt, h_in),
    )

    held = (dc,)
    dealt = joined(source, later, spans)
    dealt_all = joined([dealt, swapped(dealt)])
    held += (dealt_all,)
    if n_chip == 4:
        over_x = xored(joined([xt[1], over_y], later, [(0, x_rows), (x_rows, 2 * x_rows)]), "tm", 2)
        columns_in = [xt[0], over_x, over_y]
        places = [(0, 0), (1, 0), (2, 0), (1, x_rows)]
        held += (over_x,)
    else:
        columns_in = chips(xt)
        places = [(i, 0) for i in range(n_chip)]
    far = xored(weighted, "dp", n_dp // 2)
    near = gathered(weighted, "dp", n_dp // 2)
    held += (far, *near[1:])
    r_own, r_send = call(
        lambda *refs: carry_kernel(many, size, len(arrived), *refs),
        [shape((part, half), BF16)] * 2,
        0.5,
        (*arrived, keep, recv),
        after=held,
    )
    r_recv = swapped(r_send)
    fars = gathered(joined([far], (r_own,)), "dp", n_dp // 2)
    d_bc = call(db_kernel, [shape((length, columns), BF16)], 0.3, (xs, r_own, r_recv, db, dc))[0]
    d_bcs = [d_bc.reshape(1, length, columns)]
    if n_chip == 4:
        grads_y = xored(dealt_all, "tm", 4)
    while 2 ** (len(d_bcs) - 1) < n_chip:
        level = 2 ** (len(d_bcs) - 1)
        sent = d_bcs[0] if level == 1 else joined(d_bcs)
        d_bcs.append(xored(sent, "tm", 2 * level))
    both = ()
    if n_chip == 4:
        both = (joined([dealt_all, grads_y], (sent,)),)
        grads_x = xored(both[0], "tm", 2)
        rest = dealt_all.shape[0]
        grads = [dealt_all, grads_x, grads_y, grads_x]
        spans = [(0, rest), (0, rest), (0, rest), (rest, 2 * rest)]
    else:
        grads, spans = chips([dealt_all] * n_chip), None
    d_in, d_decay, d_step, token = call(
        lambda *refs: finish_kernel(parts, *refs),
        [
            shape((length, width), BF16),
            shape((heads, length), F32),
            shape((heads, length), F32),
            shape((8, LANES), F32),
        ],
        1.0,
        (x, bc, cumt, stept, cum, h_in, r_own, r_recv, w_whole, d_bc,
         *dxs, *exs, *owns),
        after=(*fars[1:], *both),
        scratch=[pltpu.VMEM((width, half), BF16), pltpu.VMEM((heads, half), F32)],
    )
    w_rows = width // (2 * n_chip)
    term, term_send = call(
        lambda *refs: term_kernel(places, len(columns_in), *refs),
        [shape((w_rows, columns), F32), shape((w_rows, columns), BF16)],
        0.5,
        (*columns_in, *d_bcs),
        after=(token,),
        scratch=[pltpu.VMEM((2, w_rows, columns), F32)],
    )
    final = call(
        deal_kernel,
        [shape((w_rows // n_dp, columns), F32)]
        + [shape((w_rows // n_dp, columns), BF16)] * (n_dp - 1),
        0.3,
        (term, swapped(term_send)),
        scratch=[pltpu.VMEM((n_dp, w_rows // n_dp, columns), F32)],
    )
    final = [final[0]] + [xored(final[s], "dp", s) for s in reversed(range(1, n_dp))]

    grads = stacked(grads, (term,), spans)
    w_down_grad, done = call(
        lambda *refs: down_kernel(n_dp, flip, capacity, grad_rows, *refs),
        [shape((hidden, piece), BF16), shape((8, LANES), F32)],
        1.0,
        (*near, *fars, grads),
        after=(final[0],),
    )
    w_bc_grad = call(sum_kernel, [shape(final[0].shape, F32)], 0.1, final, (done,))[0]
    return (d_in[None], d_decay.T[None], d_step.T[None], w_bc_grad, w_down_grad[None])


def solution(mesh):
    in_specs = (
        P("dp", "tm", None),
        P("dp", "tm", None),
        P("dp", None),
        P("dp", "tm", None),
        P("dp", "tm", None),
        P("dp", "tm", None, None, None),
        P(None, None, "tm"),
        P(None, None, "tm"),
        P("dp", None, "tm"),
        P("dp", "tm"),
        P("dp", None, "tm"),
    )
    out_specs = (
        P("dp", "tm", None),
        P("dp", "tm", None),
        P("dp", "tm", None),
        P(("tm", "dp"), None),
        P(None, "tm", "dp"),
    )
    return jax.shard_map(
        per_device, mesh=mesh, in_specs=in_specs, out_specs=out_specs, check_vma=False
    )
```
